32 devices in a mesh: section: 8 (over z, x), dp: 4 (over y, core).
Axes of the slice: x: 2, y: 2, z: 4, core: 2. Of those that a mesh axis runs over, the one named last changes fastest.
Arguments:
- clean_nodes: bfloat16 [8, 64, 512], P('dp'), may hold values from -6 to 6
- noise_nodes: bfloat16 [8, 64, 512], P('dp'), may hold values from -6 to 6
- edge_feats: bfloat16 [8, 64, 60, 192], P('dp'), may hold values from -6 to 6
- neighbours: int32 [8, 64, 60], P('dp'), may hold values from 0 to 63, as said below
- time_bins: int32 [8], P('dp'), may hold values from 0 to 99
- cotangent: bfloat16 [8, 64, 512], P('dp'), may hold values from -6 to 6
- pair_weight: bfloat16 [8, 512, 1024], P('section'), may hold values from -0.25 to 0.25
- message_edge: bfloat16 [8, 192, 512], P('section'), may hold values from -0.4375 to 0.4375
- message_out: bfloat16 [8, 512, 512], P('section'), may hold values from -0.25 to 0.25
- ffn_in: bfloat16 [8, 512, 2048], P('section'), may hold values from -0.25 to 0.25
- ffn_out: bfloat16 [8, 2048, 512], P('section'), may hold values from -0.125 to 0.125
- edge_pair: bfloat16 [8, 512, 384], P('section'), may hold values from -0.25 to 0.25
- edge_self: bfloat16 [8, 192, 192], P('section'), may hold values from -0.4375 to 0.4375
- edge_out: bfloat16 [8, 192, 192], P('section'), may hold values from -0.4375 to 0.4375
- norm_gain: float32 [8, 3, 512], P('section'), may hold values from 0.25 to 1.75
- norm_shift: float32 [8, 3, 512], P('section'), may hold values from -1.8 to 1.8
- node_bias: float32 [8, 3, 512], P('section'), may hold values from -1.8 to 1.8
- ffn_bias: float32 [8, 2048], P('section'), may hold values from -1.8 to 1.8
- edge_bias: float32 [8, 2, 192], P('section'), may hold values from -1.8 to 1.8
Outputs:
- activations: bfloat16 [8, 8, 64, 512], P('section', 'dp')
- input_grads: bfloat16 [8, 8, 64, 512], P('section', 'dp')
- grad_pair_weight: float32 [8, 512, 1024], P('section')
- grad_message_edge: float32 [8, 192, 512], P('section')
- grad_message_out: float32 [8, 512, 512], P('section')
- grad_ffn_in: float32 [8, 512, 2048], P('section')
- grad_ffn_out: float32 [8, 2048, 512], P('section')
- grad_edge_pair: float32 [8, 512, 384], P('section')
- grad_edge_self: float32 [8, 192, 192], P('section')
- grad_edge_out: float32 [8, 192, 192], P('section')
- grad_norm_gain: float32 [8, 3, 512], P('section')
- grad_norm_shift: float32 [8, 3, 512], P('section')
- grad_node_bias: float32 [8, 3, 512], P('section')
- grad_ffn_bias: float32 [8, 2048], P('section')
- grad_edge_bias: float32 [8, 2, 192], P('section')
The draws below stay inside these ranges and needn't reach their ends.
Inputs may be any that keep to these rules, and one draw needn't show every extreme that they name: Each node's 60 neighbours are distinct nodes of its own protein other than itself.
All inputs are finite; a program needn't handle non-finite values.
Results may differ from the reference program's by a relative error of at most 0.029.
Values may be sent and summed in bfloat16 or wider, within the bound.
A program may use at most 192 MiB of HBM per device.

```python
import math
import jax
import jax.numpy as jnp
from jax import lax

D = 512
DE = 192
FF = 2048
K = 60
TBINS = 100
NODES = 64
PROTEINS = 8
N_SECTION = 8


def draw_neighbours(key, part):
    key = jax.random.fold_in(key, 7)
    total = PROTEINS * NODES
    keys = jax.random.split(key, total)
    chosen = jax.vmap(lambda single: jax.random.permutation(single, NODES - 1)[:K])(keys)
    itself = (jnp.arange(total, dtype=jnp.int32) % NODES)[:, None]
    result = chosen + (chosen >= itself).astype(jnp.int32)
    return result.reshape(PROTEINS, NODES, K).astype(jnp.int32)


def place_ends(drawn, key, least, high):
    longest = drawn.shape.index(max(drawn.shape))
    spots = []
    for shift in (0, 1):
        where = [jax.random.randint(jax.random.fold_in(key, axis), (), 0, length) for axis, length in enumerate(drawn.shape)]
        where[longest] = (where[longest] + shift) % drawn.shape[longest]
        spots.append(tuple(where))
    return drawn.at[spots[0]].set(least).at[spots[1]].set(high)


def levels(stream_key, extent, shards, smallest, top_value):
    def one(dim, parts):
        heights = jax.random.uniform(jax.random.fold_in(jax.random.fold_in(stream_key, 6), dim), (parts,), jnp.float32, smallest / len(shards), top_value / len(shards))
        return jnp.repeat(jnp.exp(heights), extent[dim] // parts).reshape((-1,) + (1,) * (len(extent) - dim - 1))

    loudness = one(*shards[0])
    for cut in shards[1:]:
        loudness = loudness * one(*cut)
    return loudness


def noise(rng, dims, scale, limit, cuts=(), held_as=jnp.bfloat16):
    values = scale * jax.random.normal(rng, dims, jnp.float32)
    if cuts:
        values = values * levels(rng, dims, cuts, -0.22, 0.18)
    return jnp.clip(values, -limit, limit).astype(held_as)


def setup_inputs(seed: int = 0) -> dict:
    key_list = jax.random.split(jax.random.key(seed), 20)
    return {
        "clean_nodes": noise(key_list[0], (PROTEINS, NODES, D), 1.0, 6.0, ((0, 4),)),
        "noise_nodes": noise(key_list[1], (PROTEINS, NODES, D), 1.0, 6.0, ((0, 4),)),
        "edge_feats": noise(key_list[2], (PROTEINS, NODES, K, DE), 1.0, 6.0, ((0, 4),)),
        "neighbours": draw_neighbours(jax.random.fold_in(key_list[19], 71), 0),
        "time_bins": place_ends(jax.random.randint(key_list[4], (PROTEINS,), 0, TBINS), jax.random.fold_in(key_list[4], 1), 0, TBINS - 1).astype(jnp.int32),
        "cotangent": noise(key_list[5], (PROTEINS, NODES, D), 1.0, 6.0, ((0, 4),)),
        "pair_weight": noise(key_list[6], (N_SECTION, D, 2 * D), D ** -0.5, 0.25, ((0, 8),)),
        "message_edge": noise(key_list[7], (N_SECTION, DE, D), DE ** -0.5, 0.4375, ((0, 8),)),
        "message_out": noise(key_list[8], (N_SECTION, D, D), D ** -0.5, 0.25, ((0, 8),)),
        "ffn_in": noise(key_list[9], (N_SECTION, D, FF), D ** -0.5, 0.25, ((0, 8),)),
        "ffn_out": noise(key_list[10], (N_SECTION, FF, D), FF ** -0.5, 0.125, ((0, 8),)),
        "edge_pair": noise(key_list[11], (N_SECTION, D, 2 * DE), D ** -0.5, 0.25, ((0, 8),)),
        "edge_self": noise(key_list[12], (N_SECTION, DE, DE), DE ** -0.5, 0.4375, ((0, 8),)),
        "edge_out": noise(key_list[13], (N_SECTION, DE, DE), DE ** -0.5, 0.4375, ((0, 8),)),
        "norm_gain": jnp.clip(1.0 + 0.15 * jax.random.normal(key_list[14], (N_SECTION, 3, D), jnp.float32), 0.25, 1.75),
        "norm_shift": noise(key_list[15], (N_SECTION, 3, D), 0.3, 1.8, ((0, 8),), jnp.float32),
        "node_bias": noise(key_list[16], (N_SECTION, 3, D), 0.3, 1.8, ((0, 8),), jnp.float32),
        "ffn_bias": noise(key_list[17], (N_SECTION, FF), 0.3, 1.8, ((0, 8),), jnp.float32),
        "edge_bias": noise(key_list[18], (N_SECTION, 2, DE), 0.3, 1.8, ((0, 8),), jnp.float32),
    }


@jax.custom_vjp
def low(v):
    return lax.optimization_barrier(v.astype(jnp.bfloat16)).astype(jnp.float32)

@jax.custom_vjp
def low_back(v):
    return v

def low_keep(v):
    return (low(v), None)

def low_pass(kept, grad):
    return (grad,)

def back_keep(v):
    return (v, None)

def back_low(kept, grad):
    return (low(grad),)
low.defvjp(low_keep, low_pass)
low_back.defvjp(back_keep, back_low)

def layer_norm(value, gain, shift):
    centre = lax.optimization_barrier(jnp.mean(value, axis=-1, keepdims=True))
    centred = value - centre
    spread = lax.optimization_barrier(jnp.mean(centred * centred, axis=-1, keepdims=True))
    return centred * lax.rsqrt(spread + 1e-05) * gain + shift

def matmul(left, right):
    return jnp.einsum('...c,cd->...d', left, right, precision=lax.Precision.HIGHEST)

def layer_one(weights, hidden, edge_state, nearest):
    pair_w, msg_edge, msg_out, ffn_w_in, ffn_w_out, edge_pair_w, edge_self_w, edge_out_w, gains, shifts, node_b, ffn_b, edge_b = weights
    width = msg_out.shape[0]
    edge_width = edge_self_w.shape[0]
    normed_one = low(layer_norm(hidden, gains[0], shifts[0]))
    pair_out = low_back(matmul(normed_one, pair_w))
    before_act = low_back(pair_out[:, None, :width] + pair_out[:, width:][nearest] + matmul(edge_state, msg_edge) + node_b[0])
    message_act = low(jax.nn.gelu(before_act))
    message_all = low_back(matmul(message_act, msg_out))
    after_msg = hidden + lax.optimization_barrier(jnp.mean(message_all, axis=1)) + node_b[1]
    normed_two = low(layer_norm(after_msg, gains[1], shifts[1]))
    ffn_pre = low_back(matmul(normed_two, ffn_w_in) + ffn_b)
    ffn_act = low(jax.nn.gelu(ffn_pre))
    ffn_result = low_back(matmul(ffn_act, ffn_w_out))
    after_ffn = after_msg + ffn_result + node_b[2]
    normed_three = low(layer_norm(after_ffn, gains[2], shifts[2]))
    edge_pairs = low_back(matmul(normed_three, edge_pair_w))
    edge_pre = low_back(edge_pairs[:, None, :edge_width] + edge_pairs[:, edge_width:][nearest] + matmul(edge_state, edge_self_w) + edge_b[0])
    edge_act = low(jax.nn.gelu(edge_pre))
    edge_result = low_back(matmul(edge_act, edge_out_w))
    edge_next = edge_state + edge_result + edge_b[1]
    return (after_ffn, edge_next)

def reference(clean_nodes, noise_nodes, edge_feats, neighbours, time_bins, cotangent, pair_weight, message_edge, message_out, ffn_in, ffn_out, edge_pair, edge_self, edge_out, norm_gain, norm_shift, node_bias, ffn_bias, edge_bias):
    weights = tuple((item.astype(jnp.float32) for item in (pair_weight, message_edge, message_out, ffn_in, ffn_out, edge_pair, edge_self, edge_out, norm_gain, norm_shift, node_bias, ffn_bias, edge_bias)))
    phase = (time_bins.astype(jnp.float32) + 0.5) * (math.pi * 0.5 / TBINS)
    start = jnp.cos(phase)[:, None, None] * clean_nodes.astype(jnp.float32) + jnp.sin(phase)[:, None, None] * noise_nodes.astype(jnp.float32)
    edge_start = edge_feats.astype(jnp.float32)
    run_layer = jax.vmap(layer_one, in_axes=(None, 0, 0, 0))

    def first_section(carry, layer_weights):
        hidden, edge_state = carry
        after, edge_next = run_layer(layer_weights, hidden, edge_state, neighbours)
        return ((low(after), low(edge_next)), None)
    (predicted, unused_edges), unused = lax.scan(jax.checkpoint(first_section), (start, edge_start), weights)

    def second_pass(all_weights, probes):

        def section_step(carry, inputs):
            hidden, edge_state = carry
            layer_weights, probe = inputs
            hidden = hidden + probe
            after, edge_next = run_layer(layer_weights, hidden, edge_state, neighbours)
            node_send = low(low_back(after))
            edge_send = low(low_back(edge_next))
            return ((node_send, edge_send), node_send)
        (final_nodes, final_edges), section_outs = lax.scan(jax.checkpoint(section_step), (start + predicted, edge_start), (all_weights, probes))
        return (final_nodes, section_outs)
    probes = jnp.zeros((N_SECTION, PROTEINS, NODES, D), jnp.float32)
    (final_nodes, section_outs), pullback = jax.vjp(second_pass, weights, probes)
    grad_weights, grad_probes = pullback((cotangent.astype(jnp.float32), jnp.zeros_like(section_outs)))
    return (section_outs.astype(jnp.bfloat16), grad_probes.astype(jnp.bfloat16), grad_weights[0], grad_weights[1], grad_weights[2], grad_weights[3], grad_weights[4], grad_weights[5], grad_weights[6], grad_weights[7], grad_weights[8], grad_weights[9], grad_weights[10], grad_weights[11], grad_weights[12])
```

```python
import functools
import math

import jax
import jax.numpy as jnp
from jax import lax
from jax.experimental import pallas as pl
from jax.experimental.pallas import tpu as pltpu
from jax.sharding import PartitionSpec as P

TBINS = 100


def from_behind(block, axis, distance):
    devices = range(lax.axis_size(axis))
    route = [(i - distance, i) for i in devices if i - distance in devices]
    return lax.ppermute(block, axis, route)


def for_sending(value):
    return jax.tree.map(lambda a: a.astype(jnp.bfloat16) if a.dtype == jnp.float32 else a, value)


def layer_norm(value, gain, shift):
    centre = jnp.mean(value, axis=-1, keepdims=True)
    centred = value - centre
    spread = jnp.mean(centred * centred, axis=-1, keepdims=True)
    return centred * lax.rsqrt(spread + 1e-05) * gain + shift


def forward_layer(weights, hidden, edge_state, nearest):
    (
        pair_w,
        msg_edge,
        msg_out,
        ffn_w_in,
        ffn_w_out,
        edge_pair_w,
        edge_self_w,
        edge_out_w,
        gains,
        shifts,
        node_b,
        ffn_b,
        edge_b,
    ) = weights
    width = msg_out.shape[0]
    edge_width = edge_self_w.shape[0]
    normed_one = layer_norm(hidden, gains[0], shifts[0]).astype(jnp.bfloat16)
    pair_out = jnp.dot(normed_one, pair_w, preferred_element_type=jnp.float32)
    before_act = (
        pair_out[:, None, :width]
        + jnp.take(pair_out[:, width:], nearest, axis=0)
        + jnp.einsum("nkc,cd->nkd", edge_state, msg_edge, preferred_element_type=jnp.float32)
        + node_b[0]
    )
    message_act = jax.nn.gelu(before_act).astype(jnp.bfloat16)
    message_all = jnp.einsum(
        "nkc,cd->nkd", message_act, msg_out, preferred_element_type=jnp.float32
    )
    after_msg = hidden + jnp.mean(message_all, axis=1) + node_b[1]
    normed_two = layer_norm(after_msg, gains[1], shifts[1]).astype(jnp.bfloat16)
    ffn_pre = jnp.dot(normed_two, ffn_w_in, preferred_element_type=jnp.float32) + ffn_b
    ffn_act = jax.nn.gelu(ffn_pre).astype(jnp.bfloat16)
    after_ffn = (
        after_msg + jnp.dot(ffn_act, ffn_w_out, preferred_element_type=jnp.float32) + node_b[2]
    )
    normed_three = layer_norm(after_ffn, gains[2], shifts[2]).astype(jnp.bfloat16)
    edge_pairs = jnp.dot(normed_three, edge_pair_w, preferred_element_type=jnp.float32)
    edge_pre = (
        edge_pairs[:, None, :edge_width]
        + jnp.take(edge_pairs[:, edge_width:], nearest, axis=0)
        + jnp.einsum("nkc,cd->nkd", edge_state, edge_self_w, preferred_element_type=jnp.float32)
        + edge_b[0]
    )
    edge_act = jax.nn.gelu(edge_pre).astype(jnp.bfloat16)
    edge_next = (
        edge_state.astype(jnp.float32)
        + jnp.einsum("nkc,cd->nkd", edge_act, edge_out_w, preferred_element_type=jnp.float32)
        + edge_b[1]
    )
    saved = (
        normed_one,
        before_act,
        message_act,
        after_msg,
        normed_two,
        ffn_pre,
        ffn_act,
        after_ffn,
        normed_three,
        edge_pre,
        edge_act,
    )
    return (after_ffn, edge_next, saved)


def backward_layer(weights, hidden, edge_state, nearest, grad_nodes_out, grad_edges_out):
    (
        pair_w,
        msg_edge,
        msg_out,
        ffn_w_in,
        ffn_w_out,
        edge_pair_w,
        edge_self_w,
        edge_out_w,
        gains,
        shifts,
        node_b,
        ffn_b,
        edge_b,
    ) = weights
    unused_nodes, unused_edges, saved = forward_layer(weights, hidden, edge_state, nearest)
    (
        normed_one,
        before_act,
        message_act,
        after_msg,
        normed_two,
        ffn_pre,
        ffn_act,
        after_ffn,
        normed_three,
        edge_pre,
        edge_act,
    ) = saved
    width = msg_out.shape[0]
    edge_width = edge_self_w.shape[0]
    count = nearest.shape[1]
    node_count = hidden.shape[0]
    one_hot = (
        nearest.reshape(-1)[None, :] == jnp.arange(node_count, dtype=jnp.int32)[:, None]
    ).astype(jnp.bfloat16)
    edge_grad_low = grad_edges_out.astype(jnp.bfloat16)
    grad_edge_b1 = jnp.sum(grad_edges_out, axis=(0, 1))
    grad_edge_out_w = jnp.einsum(
        "nkc,nkd->cd", edge_act, edge_grad_low, preferred_element_type=jnp.float32
    )
    edge_act_grad = jnp.einsum(
        "nkd,cd->nkc", edge_grad_low, edge_out_w, preferred_element_type=jnp.float32
    )
    unused_value, gelu_edge = jax.vjp(jax.nn.gelu, edge_pre)
    edge_pre_grad = gelu_edge(edge_act_grad)[0].astype(jnp.bfloat16)
    grad_edge_b0 = jnp.sum(edge_pre_grad, axis=(0, 1), dtype=jnp.float32)
    grad_edge_self_w = jnp.einsum(
        "nkc,nkd->cd", edge_state, edge_pre_grad, preferred_element_type=jnp.float32
    )
    edge_total = grad_edges_out + jnp.einsum(
        "nkd,cd->nkc", edge_pre_grad, edge_self_w, preferred_element_type=jnp.float32
    )
    own_edge = jnp.sum(edge_pre_grad, axis=1, dtype=jnp.float32)
    other_edge = jnp.dot(
        one_hot, edge_pre_grad.reshape(-1, edge_width), preferred_element_type=jnp.float32
    )
    pairs_grad = jnp.concatenate([own_edge, other_edge], axis=-1).astype(jnp.bfloat16)
    grad_edge_pair_w = jnp.einsum(
        "nc,nd->cd", normed_three, pairs_grad, preferred_element_type=jnp.float32
    )
    normed_three_grad = jnp.einsum(
        "nd,cd->nc", pairs_grad, edge_pair_w, preferred_element_type=jnp.float32
    )
    unused_value, norm_three_back = jax.vjp(layer_norm, after_ffn, gains[2], shifts[2])
    ffn_side, gain_three, shift_three = norm_three_back(normed_three_grad)
    after_ffn_grad = grad_nodes_out + ffn_side
    grad_node_b2 = jnp.sum(after_ffn_grad, axis=0)
    ffn_out_grad = after_ffn_grad.astype(jnp.bfloat16)
    grad_ffn_w_out = jnp.einsum(
        "nc,nd->cd", ffn_act, ffn_out_grad, preferred_element_type=jnp.float32
    )
    ffn_act_grad = jnp.einsum(
        "nd,cd->nc", ffn_out_grad, ffn_w_out, preferred_element_type=jnp.float32
    )
    unused_value, gelu_ffn = jax.vjp(jax.nn.gelu, ffn_pre)
    ffn_pre_grad = gelu_ffn(ffn_act_grad)[0].astype(jnp.bfloat16)
    grad_ffn_b = jnp.sum(ffn_pre_grad, axis=0, dtype=jnp.float32)
    grad_ffn_w_in = jnp.einsum(
        "nc,nd->cd", normed_two, ffn_pre_grad, preferred_element_type=jnp.float32
    )
    normed_two_grad = jnp.einsum(
        "nd,cd->nc", ffn_pre_grad, ffn_w_in, preferred_element_type=jnp.float32
    )
    unused_value, norm_two_back = jax.vjp(layer_norm, after_msg, gains[1], shifts[1])
    msg_side, gain_two, shift_two = norm_two_back(normed_two_grad)
    after_msg_grad = after_ffn_grad + msg_side
    grad_node_b1 = jnp.sum(after_msg_grad, axis=0)
    message_grad = (after_msg_grad / count).astype(jnp.bfloat16)
    grad_msg_out = jnp.einsum(
        "nkc,nd->cd", message_act, message_grad, preferred_element_type=jnp.float32
    )
    message_act_grad = jnp.einsum(
        "nd,cd->nc", message_grad, msg_out, preferred_element_type=jnp.float32
    )
    unused_value, gelu_msg = jax.vjp(jax.nn.gelu, before_act)
    before_grad = gelu_msg(jnp.broadcast_to(message_act_grad[:, None, :], before_act.shape))[
        0
    ].astype(jnp.bfloat16)
    grad_node_b0 = jnp.sum(before_grad, axis=(0, 1), dtype=jnp.float32)
    grad_msg_edge = jnp.einsum(
        "nkc,nkd->cd", edge_state, before_grad, preferred_element_type=jnp.float32
    )
    edge_total = edge_total + jnp.einsum(
        "nkd,cd->nkc", before_grad, msg_edge, preferred_element_type=jnp.float32
    )
    own_node = jnp.sum(before_grad, axis=1, dtype=jnp.float32)
    other_node = jnp.dot(
        one_hot, before_grad.reshape(-1, width), preferred_element_type=jnp.float32
    )
    pair_grad = jnp.concatenate([own_node, other_node], axis=-1).astype(jnp.bfloat16)
    grad_pair_w = jnp.einsum("nc,nd->cd", normed_one, pair_grad, preferred_element_type=jnp.float32)
    normed_one_grad = jnp.einsum("nd,cd->nc", pair_grad, pair_w, preferred_element_type=jnp.float32)
    unused_value, norm_one_back = jax.vjp(layer_norm, hidden, gains[0], shifts[0])
    input_side, gain_one, shift_one = norm_one_back(normed_one_grad)
    hidden_grad = after_msg_grad + input_side
    grads = (
        grad_pair_w,
        grad_msg_edge,
        grad_msg_out,
        grad_ffn_w_in,
        grad_ffn_w_out,
        grad_edge_pair_w,
        grad_edge_self_w,
        grad_edge_out_w,
        jnp.stack([gain_one, gain_two, gain_three]),
        jnp.stack([shift_one, shift_two, shift_three]),
        jnp.stack([grad_node_b0, grad_node_b1, grad_node_b2]),
        grad_ffn_b,
        jnp.stack([grad_edge_b0, grad_edge_b1]),
    )
    return (hidden_grad.astype(jnp.bfloat16), edge_total.astype(jnp.bfloat16), grads)


def on_device(
    clean_nodes,
    noise_nodes,
    edge_feats,
    neighbours,
    time_bins,
    cotangent,
    pair_weight,
    message_edge,
    message_out,
    ffn_in,
    ffn_out,
    edge_pair,
    edge_self,
    edge_out,
    norm_gain,
    norm_shift,
    node_bias,
    ffn_bias,
    edge_bias,
):
    sections = lax.axis_size("section")
    place = lax.axis_index("section")
    weights = tuple(
        (
            item[0]
            for item in (
                pair_weight,
                message_edge,
                message_out,
                ffn_in,
                ffn_out,
                edge_pair,
                edge_self,
                edge_out,
                norm_gain,
                norm_shift,
                node_bias,
                ffn_bias,
                edge_bias,
            )
        )
    )
    batches, node_count, width = clean_nodes.shape
    phase = (time_bins.astype(jnp.float32) + 0.5) * (math.pi * 0.5 / TBINS)
    start = jnp.cos(phase)[:, None, None] * clean_nodes.astype(jnp.float32) + jnp.sin(phase)[
        :, None, None
    ] * noise_nodes.astype(jnp.float32)
    zero_nodes = jnp.zeros((node_count, width), jnp.bfloat16)
    zero_edges = jnp.zeros(edge_feats.shape[1:], jnp.bfloat16)
    is_first = place == 0
    is_last = place == sections - 1

    def forward_step(step_index, carry):
        recv_nodes, recv_edges, back_nodes, kept_nodes, kept_edges, section_outs = carry
        item = step_index - place
        first_pass = (item >= 0) & (item < batches)
        second_pass = (item >= sections) & (item < sections + batches)
        index = jnp.clip(jnp.where(second_pass, item - sections, item), 0, batches - 1)
        predicted = back_nodes
        own_start = lax.dynamic_index_in_dim(start, index, 0, keepdims=False)
        lead_nodes = own_start + jnp.where(second_pass, predicted.astype(jnp.float32), 0.0)
        nodes_in = jnp.where(is_first, lead_nodes, recv_nodes.astype(jnp.float32))
        edges_in = jnp.where(
            is_first, lax.dynamic_index_in_dim(edge_feats, index, 0, keepdims=False), recv_edges
        )
        nearest = lax.dynamic_index_in_dim(neighbours, index, 0, keepdims=False)

        def run_layer(operand):
            after, edge_next, saved = forward_layer(weights, operand[0], operand[1], operand[2])
            return (after.astype(jnp.bfloat16), edge_next.astype(jnp.bfloat16))

        def skip_layer(operand):
            return (zero_nodes, zero_edges)

        out_nodes, out_edges = lax.cond(
            first_pass | second_pass, run_layer, skip_layer, (nodes_in, edges_in, nearest)
        )
        kept_nodes = lax.dynamic_update_index_in_dim(
            kept_nodes, jnp.where(second_pass, nodes_in, kept_nodes[index]), index, 0
        )
        kept_edges = lax.dynamic_update_index_in_dim(
            kept_edges, jnp.where(second_pass, edges_in, kept_edges[index]), index, 0
        )
        section_outs = lax.dynamic_update_index_in_dim(
            section_outs, jnp.where(second_pass, out_nodes, section_outs[index]), index, 0
        )
        recv_nodes, recv_edges = from_behind((out_nodes, out_edges), "section", 1)
        back_nodes = from_behind(out_nodes, "section", 1 - sections)
        return (recv_nodes, recv_edges, back_nodes, kept_nodes, kept_edges, section_outs)

    forward_init = (
        zero_nodes,
        zero_edges,
        zero_nodes,
        jnp.zeros((batches, node_count, width), jnp.float32),
        jnp.zeros_like(edge_feats),
        jnp.zeros((batches, node_count, width), jnp.bfloat16),
    )
    unused_nodes, unused_edges, unused_back, kept_nodes, kept_edges, section_outs = lax.fori_loop(
        0, 2 * sections + batches - 1, forward_step, forward_init
    )
    grads_zero = tuple((jnp.zeros(item.shape, jnp.float32) for item in weights))

    def backward_step(step_index, carry):
        recv_grad_nodes, recv_grad_edges, grads, input_grads = carry
        item = step_index - (sections - 1 - place)
        live = (item >= 0) & (item < batches)
        index = jnp.clip(item, 0, batches - 1)
        nodes_grad_out = jnp.where(
            is_last,
            lax.dynamic_index_in_dim(cotangent, index, 0, keepdims=False).astype(jnp.float32),
            recv_grad_nodes.astype(jnp.float32),
        )
        edges_grad_out = jnp.where(is_last, 0.0, recv_grad_edges.astype(jnp.float32))
        nearest = lax.dynamic_index_in_dim(neighbours, index, 0, keepdims=False)

        def run_back(operand):
            return backward_layer(
                weights, operand[0], operand[1], operand[2], operand[3], operand[4]
            )

        def skip_back(operand):
            return (zero_nodes, zero_edges, grads_zero)

        nodes_grad, edges_grad, terms = lax.cond(
            live,
            run_back,
            skip_back,
            (kept_nodes[index], kept_edges[index], nearest, nodes_grad_out, edges_grad_out),
        )
        grads = tuple((total + term for total, term in zip(grads, terms)))
        input_grads = lax.dynamic_update_index_in_dim(
            input_grads, jnp.where(live, nodes_grad, input_grads[index]), index, 0
        )
        recv_grad_nodes, recv_grad_edges = from_behind((nodes_grad, edges_grad), "section", -1)
        return (recv_grad_nodes, recv_grad_edges, grads, input_grads)

    backward_init = (
        zero_nodes,
        zero_edges,
        grads_zero,
        jnp.zeros((batches, node_count, width), jnp.bfloat16),
    )
    unused_grad_nodes, unused_grad_edges, grads, input_grads = lax.fori_loop(
        0, sections + batches - 1, backward_step, backward_init
    )
    totals = jax.tree.map(lambda part: part.astype(jnp.float32), lax.psum(for_sending(grads), "dp"))
    return (
        section_outs[None],
        input_grads[None],
        totals[0][None],
        totals[1][None],
        totals[2][None],
        totals[3][None],
        totals[4][None],
        totals[5][None],
        totals[6][None],
        totals[7][None],
        totals[8][None],
        totals[9][None],
        totals[10][None],
        totals[11][None],
        totals[12][None],
    )


BF16 = jnp.bfloat16
F32 = jnp.float32
MESH = pl.DeviceIdType.MESH
GELU_A = 0.7978845608028654
GELU_B = 0.044715


def gelu(x):
    return 0.5 * x * (1.0 + jnp.tanh(x * (GELU_A + (GELU_A * GELU_B) * (x * x))))


def gelu_both(x):
    square = x * x
    t = jnp.tanh(x * (GELU_A + (GELU_A * GELU_B) * square))
    half = 0.5 * (1.0 + t)
    slope = half + (0.5 * x) * (1.0 - t * t) * (GELU_A + (3.0 * GELU_A * GELU_B) * square)
    return x * half, slope


def mm(a, b):
    return jnp.dot(a, b, preferred_element_type=F32)


def mm_bt(a, b):
    return lax.dot_general(a, b, (((1,), (1,)), ((), ())), preferred_element_type=F32)


def mm_at(a, b):
    return lax.dot_general(a, b, (((0,), (0,)), ((), ())), preferred_element_type=F32)


def stacked(blocks):
    return jnp.concatenate(blocks, axis=0)


def row_mean(x):
    return jnp.mean(x, axis=-1, keepdims=True)


def normed(x):
    centred = x - row_mean(x)
    scale = lax.rsqrt(row_mean(centred * centred) + 1e-05)
    return centred * scale, scale


def norm_back(grad, unit, scale, gain):
    t = grad * gain
    return scale * (t - row_mean(t) - unit * row_mean(t * unit))


def col_sum(x):
    return jnp.sum(x, axis=0, keepdims=True)


def relay_kernel(
    dims,
    ecat0, oht, mix, clean, noise, cot, pw, mo, fi, fo, ep, gains, shifts, node_b, fb, edge_b, we_own, ws_own, wo_own,
    act, ig, g_fwd, g_bwd, g_dpq, g_small, g_edge,
    start, par, eb0, wall, fwd, bwd, sg, eg, eg_r, eg_b, eg_o, eg_f, wo, eb1,
    ecat, wcat, scat, pwn, parn, hin_r, hst, mb_s, mb_r, pq_s, pq_r, rq_s, rq_r,
    un0, un1, un2, hi_s, sc0, sc1, sc2, sci, u_s, slope_s, de, dacc, gp, gpe, dcat, act_t, edge_t,
    x_s, x_r, row_s, row_r, dpqo_r, dmb_s, dmb_r, dh1_s, dh1_r, dh1_f, dh2_s, dn3_s, da2_s, h1_s, a1_s,
    ld_sem, nx_ss, nx_rs, hop_ss, hop_rs,
    pq_ss, pq_rs, ag_ss, ag_rs, rq_ss, rq_rs, ag2_ss, ag2_rs,
    mb_ss, mb_rs, x_ss, x_rs, row_ss, row_rs, dpqo_rs, fw_ss, dmb_ss, dmb_rs, dh_ss, dh_rs,
    e1_ss, e1_rs, e2_ss, e2_rs, g_ss, g_rs, ring_ss, ring_rs, sib_ss, sib_rs,
):
    S, B, N, K, Q, D, DE, EP, FF, C = dims
    BN = B * N
    RB = 16
    top = DE + N
    me_s = lax.axis_index("section")
    me_d = lax.axis_index("dp")
    core = lax.rem(me_d, 2)
    pair = me_d - core
    w = lax.div(me_s, 2)
    q = 2 * lax.rem(me_s, 2) + core
    owner_d = pair + lax.div(w, B)
    slot = lax.rem(w, B)
    my_row = pl.multiple_of(slot * N + q * Q, Q)
    own_rows = pl.ds(top, Q)

    def quarter(j):
        return pl.ds(pl.multiple_of(DE + j * Q, Q), Q)

    def is_me(sec, dpi):
        return (sec == me_s) & (dpi == me_d)

    def far(src, dst, ssem, rsem, sec, dpi):
        return pltpu.make_async_remote_copy(
            src_ref=src, dst_ref=dst, send_sem=ssem, recv_sem=rsem,
            device_id={"section": sec, "dp": dpi}, device_id_type=MESH,
        )

    def push(src, dst, ssem, rsem, sec, dpi):
        lax.cond(
            is_me(sec, dpi),
            lambda: pltpu.make_async_copy(src, dst, rsem).start(),
            lambda: far(src, dst, ssem, rsem, sec, dpi).start(),
        )

    def arrive(ref, sem):
        pltpu.make_async_copy(ref, ref, sem).wait()

    def drain(ref, sem, sec, dpi):
        @pl.when(jnp.logical_not(is_me(sec, dpi)))
        def _():
            arrive(ref, sem)

    def worker_of(p, j):
        return 2 * (core * B + p) + j // 2, pair + j % 2

    def peer(k):
        j = lax.rem(q + k, 4)
        return j, 2 * w + lax.div(j, 2), pair + lax.rem(j, 2)

    works_here = lax.div(w, B) == core

    pairs = [(p, j) for p in range(B) for j in range(4)]

    load = pltpu.make_async_copy(ecat0, ecat.at[0], ld_sem)
    load.start()
    barrier = pltpu.get_barrier_semaphore()
    for sec in range(S):
        for c in range(C):
            near = (c == pair) | (c == pair + 1) | (w == sec // 2)

            @pl.when(near & jnp.logical_not(is_me(sec, c)))
            def _():
                pl.semaphore_signal(
                    barrier, inc=1, device_id={"section": sec, "dp": c}, device_id_type=MESH
                )
    W = D + 2 * EP
    H = wall.shape[1] // 2
    wall[me_s] = jnp.zeros((2 * H, W), BF16)
    wall[me_s, pl.ds(0, DE), pl.ds(0, D)] = we_own[...]
    wall[me_s, pl.ds(0, DE), pl.ds(D, DE)] = ws_own[...]
    wall[me_s, pl.ds(0, DE), pl.ds(D + EP, DE)] = wo_own[...]
    bias = edge_b[pl.ds(1, 1), :]
    high = bias.astype(BF16).astype(F32)
    row = lax.broadcasted_iota(jnp.int32, (16, DE), 0)
    wall[me_s, pl.ds(DE, 16), pl.ds(0, DE)] = jnp.where(
        row == 0, high, jnp.where(row == 1, bias - high, 0.0)
    ).astype(BF16)
    eb0[...] = jnp.zeros_like(eb0)
    eb0[:, pl.ds(0, DE)] = edge_b[pl.ds(0, 1), :]
    par[pl.ds(0, 1), :] = gains[0]
    par[pl.ds(1, 1), :] = shifts[0]
    par[pl.ds(2, 1), :] = node_b[0]
    par[pl.ds(3, 5), :] = jnp.zeros((5, D), F32)
    pl.semaphore_wait(barrier, 2 * S - 1 + 2 * (C - 2))

    def section_at(i):
        i = lax.rem(i + S, S)
        return jnp.where(i < S // 2, 2 * i, 2 * (S - i) - 1)

    place = jnp.where(lax.rem(me_s, 2) == 0, w, S - 1 - w)
    mine = pl.ds(pl.multiple_of(core * H, H), H)
    theirs = pl.ds(pl.multiple_of((1 - core) * H, H), H)
    sides = ((section_at(place + 1), S // 2), (section_at(place - 1), S // 2 - 1))

    def ring_send(layer, side, hop):
        sec, reach = sides[side]
        if hop < reach:
            half = wall.at[layer, mine]
            far(half, half, ring_ss.at[side, hop], ring_rs.at[layer], sec, me_d).start()

    for side in range(2):
        ring_send(me_s, side, 0)
    before = lax.rem(me_s + S - 1, S)
    far(pw, pwn, nx_ss.at[0], nx_rs.at[0], before, me_d).start()
    far(par, parn, nx_ss.at[1], nx_rs.at[1], before, me_d).start()

    for p in range(B):
        rows = pl.ds(p * N, N)
        start[rows, :] = mix[0, p] * clean[rows, :].astype(F32) + mix[1, p] * noise[rows, :].astype(F32)

    def ring():
        for hop in range(1, S // 2 + 1):
            for side in range(2):
                if hop <= sides[side][1]:
                    layer = section_at(place - hop if side == 0 else place + hop)
                    half = wall.at[layer, mine]
                    arrive(half, ring_rs.at[layer])
                    ring_send(layer, side, hop)
                    far(half, half, sib_ss.at[layer], sib_rs.at[layer], me_s, pair + 1 - core).start()

    def ring_drain():
        for side in range(2):
            for hop in range(sides[side][1]):
                arrive(wall.at[me_s, mine], ring_ss.at[side, hop])
        for layer in range(S):
            @pl.when(layer != me_s)
            def _():
                arrive(wall.at[layer, mine], sib_ss.at[layer])

    def unpack(t):
        @pl.when(t != me_s)
        def _():
            arrive(wall.at[t, theirs], sib_rs.at[t])

        wcat[t, pl.ds(0, DE), :] = wall[t, pl.ds(0, DE), pl.ds(0, D)]
        scat[t, pl.ds(0, DE), :] = wall[t, pl.ds(0, DE), pl.ds(D, EP)]
        wo[t, pl.ds(0, DE), :] = wall[t, pl.ds(0, DE), pl.ds(D + EP, EP)]
        wo[t, pl.ds(DE, N), :] = jnp.zeros((N, EP), BF16)
        eb1[t] = wall[t, pl.ds(DE, 16), pl.ds(0, EP)]

    def rows_out(src, dst, ssem, rsem):
        for p, j in pairs:
            sec, dpi = worker_of(p, j)
            push(src.at[pl.ds(p * N + j * Q, Q)], dst, ssem, rsem, sec, dpi)

    def rows_drain(src, ssem):
        lax.cond(
            works_here,
            lambda: arrive(src.at[pl.ds(0, B * N - Q)], ssem),
            lambda: arrive(src, ssem),
        )

    def spread(rows, half, ref, layer, ssem, rsem, rows_sem):
        arrive(rows, rows_sem)
        for k in range(1, 4):
            _, sec, dpi = peer(k)
            far(rows.at[:, pl.ds(half, half)], ref.at[layer, quarter(q)], ssem, rsem, sec, dpi).start()
        ref[layer, own_rows, :] = rows[:, pl.ds(0, half)]
        ref[layer, quarter(q), :] = rows[:, pl.ds(half, half)]

    def spread_wait(ref, layer, sem):
        arrive(ref.at[layer, pl.ds(DE, 3 * Q)], sem)

    def share(group, src, dst):
        for c in range(C):
            push(src, dst.at[me_d], g_ss.at[group, c], g_rs.at[group, me_d], me_s, c)

    def share_wait(group, src, dst):
        for c in range(C):
            arrive(dst.at[c], g_rs.at[group, c])
            drain(src, g_ss.at[group, c], me_s, c)

    steps = 4
    KC = K // steps
    RC = KC * Q

    def messages(t):
        own = wcat[t, own_rows, :].astype(F32)
        total = jnp.zeros((Q, D), F32)
        for i in range(steps):
            pre = mm(ecat[t, pl.ds(i * RC, RC), :], wcat[t, pl.ds(0, top), :])
            for k in range(KC):
                total = total + gelu(pre[k * Q : (k + 1) * Q] + own)
        mb_s[...] = (total * (1.0 / K)).astype(BF16)

    def edge_update(t):
        own = scat[t, own_rows, :].astype(F32)
        bias = eb1[t, pl.ds(0, 1), :].astype(F32) + eb1[t, pl.ds(1, 1), :].astype(F32)
        for i in range(steps):
            pe = mm(ecat[t, pl.ds(i * RC, RC), :], scat[t, pl.ds(0, top), :])
            act_e = stacked([gelu(pe[k * Q : (k + 1) * Q] + own).astype(BF16) for k in range(KC)])
            z = mm(act_e, wo[t])
            for k in range(KC):
                rows = pl.ds(i * RC + k * Q, Q)
                ecat[t + 1, rows, :] = (ecat[t, rows, :].astype(F32) + z[k * Q : (k + 1) * Q] + bias).astype(BF16)

    chunks = 4
    FC = FF // chunks

    def node_forward(step):
        @pl.when(step < S)
        def _():
            arrive(pwn, nx_rs.at[0])
            arrive(parn, nx_rs.at[1])
            arrive(pw, nx_ss.at[0])
            arrive(par, nx_ss.at[1])

        @pl.when(step == 0)
        def _():
            hi_s[...] = start[...]

        @pl.when(step > 0)
        def _():
            arrive(hin_r, hop_rs)
            first = jnp.where(me_s == 0, 1.0, 0.0)
            for i in range(0, BN, RB):
                rows = pl.ds(i, RB)
                hi_s[rows, :] = hin_r[rows, :].astype(F32) + first * start[rows, :]

        arrive(mb_r, mb_rs)
        mean = mm(mb_r[...], mo[...])
        for i in range(0, BN, RB):
            rows = pl.ds(i, RB)
            h1 = hi_s[rows, :] + mean[i : i + RB] + node_b[1]
            h1_s[rows, :] = h1
            unit, scale = normed(h1)
            un1[rows, :] = unit
            sc1[rows, :] = scale
            fwd[rows, pl.ds(2 * D, D)] = (unit * gains[1] + shifts[1]).astype(BF16)
            fwd[rows, pl.ds(D, D)] = mb_r[rows, :]
        a2 = fwd[:, pl.ds(2 * D, D)]
        y = jnp.zeros((BN, D), F32)
        for c in range(chunks):
            cols = pl.ds(c * FC, FC)
            u = mm(a2, fi[:, cols])
            v = []
            for i in range(0, BN, RB):
                rows = pl.ds(i, RB)
                block = u[i : i + RB] + fb[:, cols]
                u_s[rows, cols] = block
                v.append(gelu(block).astype(BF16))
            y = y + mm(stacked(v), fo[cols, :])
        last = jnp.where(me_s == S - 1, 1.0, 0.0)
        for i in range(0, BN, RB):
            rows = pl.ds(i, RB)
            h2 = h1_s[rows, :] + y[i : i + RB] + node_b[2]
            rounded = h2.astype(BF16)
            hst[rows, :] = rounded
            unit, scale = normed(h2)
            un2[rows, :] = unit
            sc2[rows, :] = scale
            fwd[rows, pl.ds(3 * D, D)] = (unit * gains[2] + shifts[2]).astype(BF16)
            pair_norm(rows, rounded.astype(F32) + last * start[rows, :], parn)
        rq = mm(fwd[:, pl.ds(3 * D, D)], ep[...])
        for i in range(0, BN, RB):
            rows = pl.ds(i, RB)
            rq_s[rows, pl.ds(0, EP)] = (rq[i : i + RB, :EP] + eb0[...]).astype(BF16)
            rq_s[rows, pl.ds(EP, EP)] = rq[i : i + RB, EP:].astype(BF16)
        pair_rows(pwn, parn)
        later = lax.rem(me_s + 1, S)

        @pl.when(me_s < S - 1)
        def _():
            rows_out(rq_s, rq_r, rq_ss, rq_rs)

        @pl.when(step < 2 * S - 1)
        def _():
            rows_out(pq_s, pq_r, pq_ss, pq_rs)
            far(hst, hin_r, hop_ss, hop_rs, later, me_d).start()

        @pl.when(step >= S)
        def _():
            act[...] = hst[...]
            for i in range(0, BN, RB):
                rows = pl.ds(i, RB)
                unit, scale = normed(hi_s[rows, :])
                hi_s[rows, :] = unit
                sci[rows, :] = scale
                fwd[rows, pl.ds(0, D)] = (unit * gains[0] + shifts[0]).astype(BF16)
                for c in range(chunks):
                    cols = pl.ds(c * FC, FC)
                    slope_s[rows, cols] = gelu_both(u_s[rows, cols])[1].astype(BF16)
            share(0, fwd, g_fwd)

    def pair_norm(rows, hidden, first):
        unit, scale = normed(hidden)
        un0[rows, :] = unit
        sc0[rows, :] = scale
        a1_s[rows, :] = (unit * first[pl.ds(0, 1), :] + first[pl.ds(1, 1), :]).astype(BF16)

    def pair_rows(weight, first):
        for half in range(2):
            cols = pl.ds(half * D, D)
            value = mm(a1_s[...], weight[:, cols])
            if half == 0:
                value = value + first[pl.ds(2, 1), :]
            pq_s[:, cols] = value.astype(BF16)

    def node_forward_drain():
        arrive(hst, hop_ss)
        rows_drain(pq_s, pq_ss)

        @pl.when(me_s < S - 1)
        def _():
            rows_drain(rq_s, rq_ss)

    @pl.when(me_s == 0)
    def _():
        for i in range(0, BN, RB):
            rows = pl.ds(i, RB)
            pair_norm(rows, start[rows, :], par)
        pair_rows(pw, par)
        rows_out(pq_s, pq_r, pq_ss, pq_rs)

    def message_slope(t):
        own = wcat[t, own_rows, :].astype(F32)
        for i in range(steps):
            pre = mm(ecat[t, pl.ds(i * RC, RC), :], wcat[t, pl.ds(0, top), :])
            for k in range(KC):
                gp[t, pl.ds(i * RC + k * Q, Q), :] = gelu_both(pre[k * Q : (k + 1) * Q] + own)[1].astype(BF16)

    def edge_slope(t):
        own = scat[t, own_rows, :].astype(F32)
        values = []
        for i in range(steps):
            pe = mm(ecat[t, pl.ds(i * RC, RC), :], scat[t, pl.ds(0, top), :])
            for k in range(KC):
                value, slope = gelu_both(pe[k * Q : (k + 1) * Q] + own)
                values.append(value.astype(BF16))
                gpe[t, pl.ds(i * RC + k * Q, Q), :] = slope.astype(BF16)
        act_t[t] = stacked(values).T

    def prepare(t):
        message_slope(t)
        edge_t[t] = ecat[t].T

        @pl.when(t > 0)
        def _():
            edge_slope(t - 1)

    def forward_step(step, carry):
        t = lax.rem(step, S)

        @pl.when(step < S)
        def _():
            unpack(t)

        spread_wait(wcat, t, ag_rs)
        messages(t)
        spread_wait(wcat, t, ag_ss)
        push(mb_s, mb_r.at[pl.ds(my_row, Q)], mb_ss, mb_rs, t, owner_d)

        @pl.when((step == 0) & (me_s == 0))
        def _():
            rows_drain(pq_s, pq_ss)

        @pl.when((step > 0) & (me_s == lax.rem(step + S - 1, S)))
        def _():
            node_forward_drain()

        @pl.when(me_s == t)
        def _():
            node_forward(step)

        @pl.when((me_s != t) & (step >= S))
        def _():
            prepare(t)

        @pl.when(t < S - 1)
        def _():
            spread(rq_r, EP, scat, t, ag2_ss, ag2_rs, rq_rs)

        @pl.when(step < 2 * S - 1)
        def _():
            spread(pq_r, D, wcat, lax.rem(step + 1, S), ag_ss, ag_rs, pq_rs)

        @pl.when(t < S - 1)
        def _():
            spread_wait(scat, t, ag2_rs)
            edge_update(t)
            spread_wait(scat, t, ag2_ss)

        drain(mb_s, mb_ss, t, owner_d)
        return carry

    ring()
    load.wait()
    spread(pq_r, D, wcat, 0, ag_ss, ag_rs, pq_rs)
    lax.fori_loop(0, 2 * S, forward_step, 0)
    ring_drain()

    def edge_back(t):
        b2, n2 = lax.rem(t, 2), lax.rem(t + 1, 2)
        total = jnp.zeros((Q, EP), F32)
        for i in range(steps):
            chunk = pl.ds(i * RC, RC)
            carry = mm_bt(dcat[b2, chunk, pl.ds(0, D)], wcat[t, pl.ds(0, top), :])
            low = []
            for k in range(KC):
                rows = pl.ds(i * RC + k * Q, Q)
                low.append((dacc[rows, :] + carry[k * Q : (k + 1) * Q]).astype(BF16))
                de[n2, rows, :] = low[-1]
            dw = mm_bt(stacked(low), wo[t - 1])
            for k in range(KC):
                rows = pl.ds(i * RC + k * Q, Q)
                d = (gpe[t - 1, rows, :].astype(F32) * dw[k * Q : (k + 1) * Q]).astype(BF16)
                total = total + d.astype(F32)
                dcat[n2, rows, pl.ds(D, EP)] = d
        row_s[:, pl.ds(2 * D, EP)] = total.astype(BF16)
        x_s[:, pl.ds(D, EP)] = mm(oht[...], dcat[n2, :, pl.ds(D, EP)]).astype(BF16)

    def edge_pass(t):
        b3 = lax.rem(t, 2)
        for i in range(steps):
            rows = pl.ds(i * RC, RC)
            d = dcat[b3, rows, pl.ds(D, EP)]
            dacc[rows, :] = de[b3, rows, :].astype(F32) + mm_bt(d, scat[t, pl.ds(0, top), :])

    blocks = 2 * C
    BW = (D + 2 * EP) // blocks
    my_block = lax.rem(me_s, 2) * C + me_d
    my_cols = pl.ds(pl.multiple_of(my_block * BW, BW), BW)

    def edge_grads(t):
        b3 = lax.rem(t, 2)

        @pl.when(t < S - 1)
        def _():
            eg[t, pl.ds(0, DE), pl.ds(0, D + EP)] = mm(edge_t[t, pl.ds(0, DE), :], dcat[b3]).astype(BF16)
            eg[t, pl.ds(0, DE), pl.ds(D + EP, EP)] = mm(act_t[t, pl.ds(0, DE), :], de[b3]).astype(BF16)
            bias = jnp.sum(de[b3].astype(F32), axis=0, keepdims=True)
            eg[t, pl.ds(DE, 16), pl.ds(0, EP)] = jnp.broadcast_to(bias, (16, EP)).astype(BF16)

        @pl.when(t == S - 1)
        def _():
            eg[t, pl.ds(0, DE), pl.ds(0, D)] = mm(edge_t[t, pl.ds(0, DE), :], dcat[b3, :, pl.ds(0, D)]).astype(BF16)
            eg[t, pl.ds(0, DE), pl.ds(D, 2 * EP)] = jnp.zeros((DE, 2 * EP), BF16)
            eg[t, pl.ds(DE, 16), pl.ds(0, EP)] = jnp.zeros((16, EP), BF16)

        eg[t, pl.ds(DE, 16), pl.ds(EP, D + EP)] = jnp.zeros((16, D + EP), BF16)
        for k in range(blocks):
            @pl.when(k != my_block)
            def _():
                far(
                    eg.at[t, :, pl.ds(k * BW, BW)], eg_r.at[t, my_block], e1_ss.at[t, k], e1_rs.at[t, my_block],
                    2 * w + k // C, k % C,
                ).start()

    def edge_grads_sum(t):
        eg_r[t, my_block] = eg[t, :, my_cols]
        for k in range(blocks):
            @pl.when(k != my_block)
            def _():
                arrive(eg_r.at[t, k], e1_rs.at[t, k])
                arrive(eg.at[t, :, pl.ds(k * BW, BW)], e1_ss.at[t, k])
        total = eg_r[t, 0].astype(F32)
        for k in range(1, blocks):
            total = total + eg_r[t, k].astype(F32)
        eg_b[t] = total.astype(BF16)
        push(eg_b.at[t], eg_o.at[me_s], e2_ss.at[t], e2_rs.at[me_s], t, me_d)

    def gather_blocks():
        for k in range(1, 4):
            j, sec, dpi = peer(k)
            rows = pl.ds(pl.multiple_of(j * Q, Q), Q)
            far(x_s.at[rows], x_r.at[q], x_ss, x_rs, sec, dpi).start()
        x_r[q] = x_s[pl.ds(pl.multiple_of(q * Q, Q), Q), :]

    def gather_wait():
        arrive(x_r.at[pl.ds(0, 3)], x_rs)
        arrive(x_s.at[pl.ds(0, 3 * Q)], x_ss)
        total = x_r[0].astype(F32)
        for j in range(1, 4):
            total = total + x_r[j].astype(F32)
        return total

    def message_back(t):
        b2 = lax.rem(t, 2)
        dm = dmb_r[...].astype(F32)
        total = jnp.zeros((Q, D), F32)
        for k in range(K):
            rows = pl.ds(k * Q, Q)
            d = (gp[t, rows, :].astype(F32) * dm).astype(BF16)
            total = total + d.astype(F32)
            dcat[b2, rows, pl.ds(0, D)] = d
        row_s[:, pl.ds(0, D)] = total.astype(BF16)
        x_s[:, pl.ds(0, D)] = mm(oht[...], dcat[b2, :, pl.ds(0, D)]).astype(BF16)

    def node_backward():
        @pl.when(me_s < S - 1)
        def _():
            arrive(dh1_r, dh_rs)
            arrive(row_r, row_rs)
            dn0 = mm_bt(row_r[:, pl.ds(0, 2 * D)], pwn[...])
            dn3 = mm_bt(row_r[:, pl.ds(2 * D, 2 * EP)], ep[...])
            for i in range(0, BN, RB):
                rows = pl.ds(i, RB)
                dn = dn3[i : i + RB]
                dn3_s[rows, :] = dn
                first = norm_back(dn0[i : i + RB], un0[rows, :], sc0[rows, :], parn[pl.ds(0, 1), :])
                dh = (dh1_r[rows, :].astype(F32) + first).astype(BF16).astype(F32)
                dh2_s[rows, :] = dh + norm_back(dn, un2[rows, :], sc2[rows, :], gains[2])

        @pl.when(me_s == S - 1)
        def _():
            dh2_s[...] = cot[...].astype(F32)

        dy = stacked([dh2_s[pl.ds(i, RB), :].astype(BF16) for i in range(0, BN, RB)])
        bwd[:, pl.ds(D, D)] = dy
        da2 = jnp.zeros((BN, D), F32)
        for c in range(chunks):
            cols = pl.ds(c * FC, FC)
            dv = mm_bt(dy, fo[cols, :])
            du = stacked(
                [(slope_s[pl.ds(i, RB), cols].astype(F32) * dv[i : i + RB]).astype(BF16) for i in range(0, BN, RB)]
            )
            da2 = da2 + mm_bt(du, fi[:, cols])
        for i in range(0, BN, RB):
            rows = pl.ds(i, RB)
            block = da2[i : i + RB]
            da2_s[rows, :] = block
            dh1 = dh2_s[rows, :] + norm_back(block, un1[rows, :], sc1[rows, :], gains[1])
            dh1_f[rows, :] = dh1
            bwd[rows, pl.ds(0, D)] = (dh1 * (1.0 / K)).astype(BF16)
        dmb_s[...] = mm_bt(bwd[:, pl.ds(0, D)], mo[...]).astype(BF16)
        rows_out(dmb_s, dmb_r, dmb_ss, dmb_rs)

        @pl.when(me_s > 0)
        def _():
            dh1_s[...] = dh1_f[...].astype(BF16)
            far(dh1_s, dh1_r, dh_ss, dh_rs, me_s - 1, me_d).start()

        @pl.when(me_s < S - 1)
        def _():
            far(row_r.at[:, pl.ds(0, 2 * D)], dpqo_r, fw_ss, dpqo_rs, me_s + 1, me_d).start()
            drs = row_r[:, pl.ds(2 * D, 2 * EP)]
            bwd[:, pl.ds(2 * D, 2 * EP)] = drs
            dn = dn3_s[...]
            sg[pl.ds(11, 1), :] = col_sum(dn * un2[...])
            sg[pl.ds(12, 1), :] = col_sum(dn)
            sg[pl.ds(16, 1), pl.ds(0, EP)] = col_sum(drs[:, :EP].astype(F32))

        @pl.when(me_s == S - 1)
        def _():
            bwd[:, pl.ds(2 * D, 2 * EP)] = jnp.zeros((B * N, 2 * EP), BF16)
            sg[pl.ds(11, 1), :] = jnp.zeros((1, D), F32)
            sg[pl.ds(12, 1), :] = jnp.zeros((1, D), F32)
            sg[pl.ds(16, 1), pl.ds(0, EP)] = jnp.zeros((1, EP), F32)

        share(1, bwd, g_bwd)
        sg[pl.ds(13, 1), :] = col_sum(dh2_s[...])
        sg[pl.ds(8, 1), :] = col_sum(da2_s[...] * un1[...])
        sg[pl.ds(9, 1), :] = col_sum(da2_s[...])
        sg[pl.ds(10, 1), :] = col_sum(dh1_f[...])

    def node_backward_drain():
        rows_drain(dmb_s, dmb_ss)

        @pl.when(me_s > 0)
        def _():
            arrive(dh1_s, dh_ss)

        @pl.when(me_s < S - 1)
        def _():
            arrive(row_r.at[:, pl.ds(0, 2 * D)], fw_ss)

    dacc[...] = jnp.zeros_like(dacc)

    def backward_step(step, carry):
        t = S - 1 - step

        @pl.when(me_s == t)
        def _():
            node_backward()

        @pl.when(((t == S - 1) & (me_s >= S - 2)) | (me_s == t - 2))
        def _():
            prepare(me_s)

        @pl.when(t < S - 1)
        def _():
            edge_pass(t)

        @pl.when(t + 3 < S)
        def _():
            edge_grads_sum(t + 3)

        arrive(dmb_r, dmb_rs)
        message_back(t)

        @pl.when(t > 0)
        def _():
            edge_back(t)

        @pl.when(t == 0)
        def _():
            x_s[:, pl.ds(D, EP)] = jnp.zeros((N, EP), BF16)

        gather_blocks()
        other = gather_wait().astype(BF16)
        row_s[:, pl.ds(D, D)] = other[:, :D]
        row_s[:, pl.ds(2 * D + EP, EP)] = other[:, D:]
        dpq = row_s.at[:, pl.ds(0, 2 * D)]

        @pl.when(t > 0)
        def _():
            push(row_s, row_r.at[pl.ds(my_row, Q)], row_ss, row_rs, t - 1, owner_d)

        @pl.when(t == 0)
        def _():
            push(dpq, dpqo_r.at[pl.ds(my_row, Q)], row_ss, dpqo_rs, t, owner_d)

        edge_grads(t)

        @pl.when(t > 0)
        def _():
            drain(row_s, row_ss, t - 1, owner_d)

        @pl.when(t == 0)
        def _():
            drain(dpq, row_ss, t, owner_d)

        @pl.when(me_s == t)
        def _():
            node_backward_drain()

        return carry

    lax.fori_loop(0, S, backward_step, 0)

    arrive(dpqo_r, dpqo_rs)
    share(2, dpqo_r, g_dpq)
    dpq = dpqo_r[...]
    sg[pl.ds(2, 1), :] = col_sum(dpq[:, :D].astype(F32))
    dn = mm_bt(dpq, pw[...])
    unit = hi_s[...]
    sg[pl.ds(0, 1), :] = col_sum(dn * unit)
    sg[pl.ds(1, 1), :] = col_sum(dn)
    share(3, sg, g_small)
    ig[...] = (dh1_f[...] + norm_back(dn, unit, sci[...], gains[0])).astype(BF16)
    for t in range(min(2, S - 1), -1, -1):
        edge_grads_sum(t)
    for sec in range(S):
        arrive(eg_o.at[sec], e2_rs.at[sec])
    for half in range(2):
        total = eg_o[half].astype(F32)
        for sec in range(half + 2, S, 2):
            total = total + eg_o[sec].astype(F32)
        eg_f[half] = total.astype(BF16)
    share(4, eg_f, g_edge)
    for t in range(S):
        drain(eg_b.at[t], e2_ss.at[t], t, me_d)
    share_wait(0, fwd, g_fwd)
    share_wait(1, bwd, g_bwd)
    share_wait(2, dpqo_r, g_dpq)
    share_wait(3, sg, g_small)
    share_wait(4, eg_f, g_edge)


def run_relay(dims, operands):
    S, B, N, K, Q, D, DE, EP, FF, C = dims
    R = K * Q
    BN = B * N
    tall = DE + N + Q
    vm = pl.BlockSpec(memory_space=pltpu.VMEM)
    hbm = pl.BlockSpec(memory_space=pl.ANY)
    dma = pltpu.SemaphoreType.DMA
    sds = jax.ShapeDtypeStruct
    BW = (D + 2 * EP) // (2 * C)
    tile = 32
    held = -(-(DE + 16) // tile) * tile
    scratch = [
        pltpu.VMEM((BN, D), F32),
        pltpu.VMEM((8, D), F32),
        pltpu.VMEM((1, EP), F32),
        pltpu.VMEM((S, held, D + 2 * EP), BF16),
        pltpu.VMEM((BN, 4 * D), BF16),
        pltpu.VMEM((BN, 2 * D + 2 * EP), BF16),
        pltpu.VMEM((24, D), F32),
        pltpu.VMEM((S, DE + 16, D + 2 * EP), BF16),
        pltpu.VMEM((S, 2 * C, DE + 16, BW), BF16),
        pltpu.VMEM((S, DE + 16, BW), BF16),
        pltpu.VMEM((S, DE + 16, BW), BF16),
        pltpu.VMEM((2, DE + 16, BW), BF16),
        pltpu.VMEM((S, EP, EP), BF16),
        pltpu.VMEM((S, 16, EP), BF16),
        pltpu.VMEM((S, R, EP), BF16),
        pltpu.VMEM((S, tall, D), BF16),
        pltpu.VMEM((S, tall, EP), BF16),
        pltpu.VMEM((D, 2 * D), BF16),
        pltpu.VMEM((8, D), F32),
        pltpu.VMEM((BN, D), BF16),
        pltpu.VMEM((BN, D), BF16),
        pltpu.VMEM((Q, D), BF16),
        pltpu.VMEM((BN, D), BF16),
        pltpu.VMEM((BN, 2 * D), BF16),
        pltpu.VMEM((Q, 2 * D), BF16),
        pltpu.VMEM((BN, 2 * EP), BF16),
        pltpu.VMEM((Q, 2 * EP), BF16),
        pltpu.VMEM((BN, D), F32),
        pltpu.VMEM((BN, D), F32),
        pltpu.VMEM((BN, D), F32),
        pltpu.VMEM((BN, D), F32),
        pltpu.VMEM((BN, 1), F32),
        pltpu.VMEM((BN, 1), F32),
        pltpu.VMEM((BN, 1), F32),
        pltpu.VMEM((BN, 1), F32),
        pltpu.VMEM((BN, FF), F32),
        pltpu.VMEM((BN, FF), BF16),
        pltpu.VMEM((2, R, EP), BF16),
        pltpu.VMEM((R, EP), F32),
        pltpu.VMEM((S, R, D), BF16),
        pltpu.VMEM((S, R, EP), BF16),
        pltpu.VMEM((2, R, D + EP), BF16),
        pltpu.VMEM((S, EP, R), BF16),
        pltpu.VMEM((S, EP, R), BF16),
        pltpu.VMEM((N, D + EP), BF16),
        pltpu.VMEM((4, Q, D + EP), BF16),
        pltpu.VMEM((Q, 2 * D + 2 * EP), BF16),
        pltpu.VMEM((BN, 2 * D + 2 * EP), BF16),
        pltpu.VMEM((BN, 2 * D), BF16),
        pltpu.VMEM((BN, D), BF16),
        pltpu.VMEM((Q, D), BF16),
        pltpu.VMEM((BN, D), BF16),
        pltpu.VMEM((BN, D), BF16),
        pltpu.VMEM((BN, D), F32),
        pltpu.VMEM((BN, D), F32),
        pltpu.VMEM((BN, D), F32),
        pltpu.VMEM((BN, D), F32),
        pltpu.VMEM((BN, D), F32),
        pltpu.VMEM((BN, D), BF16),
        dma, dma((2,)), dma((2,)), dma, dma,
        dma, dma, dma, dma, dma, dma, dma, dma,
        dma, dma, dma, dma, dma, dma, dma,
        dma, dma, dma, dma, dma,
        dma((S, 2 * C)), dma((S, 2 * C)), dma((S,)), dma((S,)), dma((5, C)), dma((5, C)),
        dma((2, S // 2)), dma((S,)), dma((S,)), dma((S,)),
    ]
    return pl.pallas_call(
        functools.partial(relay_kernel, dims),
        out_shape=(
            sds((BN, D), BF16),
            sds((BN, D), BF16),
            sds((C, BN, 4 * D), BF16),
            sds((C, BN, 2 * D + 2 * EP), BF16),
            sds((C, BN, 2 * D), BF16),
            sds((C, 24, D), F32),
            sds((C, 2, DE + 16, BW), BF16),
        ),
        in_specs=[hbm, vm, pl.BlockSpec(memory_space=pltpu.SMEM)] + [vm] * 16,
        out_specs=(vm,) * 2 + (hbm,) * 5,
        scratch_shapes=scratch,
        compiler_params=pltpu.CompilerParams(
            collective_id=0, has_side_effects=True, vmem_limit_bytes=62 * 1024 * 1024
        ),
    )(*operands)


def gradient_kernel(
    dims,
    fwd, bwd, dpq, small, edge, fi, fo, fb, act, ig,
    g_pair, g_edge, g_out, g_fi, g_fo, g_ep, g_self, g_eout, g_gain, g_shift, g_nb, g_fb, g_eb, act_out, ig_out,
    fwd_v, bwd_v, dpq_v, fi_v, fo_v, gfi_v, gfo_v, pair_v, out_v, edge_v, in_sems, sems,
):
    S, B, N, K, Q, D, DE, EP, FF, C = dims
    chunks = 4
    FC = FF // chunks

    def part(c, size=D):
        return pl.ds(c * size, size)

    loads = {}

    def load(name, src, dst):
        loads[name] = pltpu.make_async_copy(src, dst, in_sems.at[len(loads)])
        loads[name].start()

    load("a2", fwd.at[:, part(2)], fwd_v.at[2])
    load("dy", bwd.at[:, part(1)], bwd_v.at[1])
    for c in range(chunks):
        load(("fi", c), fi.at[:, part(c, FC)], fi_v.at[c])
        load(("fo", c), fo.at[part(c, FC)], fo_v.at[c])
    load("a1", fwd.at[:, part(0)], fwd_v.at[0])
    load("dpq0", dpq.at[:, part(0)], dpq_v.at[0])
    load("dpq1", dpq.at[:, part(1)], dpq_v.at[1])
    load("mbar", fwd.at[:, part(1)], fwd_v.at[1])
    load("dmsg", bwd.at[:, part(0)], bwd_v.at[0])
    load("a3", fwd.at[:, part(3)], fwd_v.at[3])
    load("drs", bwd.at[:, part(2)], bwd_v.at[2])
    load("edge", edge, edge_v)
    stores = []

    def out(src, dst):
        copy = pltpu.make_async_copy(src, dst, sems.at[len(stores)])
        copy.start()
        stores.append(copy)

    out(act, act_out)
    out(ig, ig_out)
    loads["a2"].wait()
    loads["dy"].wait()
    a2 = fwd_v[2]
    dy = bwd_v[1]
    for c in range(chunks):
        cols = part(c, FC)
        loads["fi", c].wait()
        loads["fo", c].wait()
        value, slope = gelu_both(mm(a2, fi_v[c]) + fb[:, cols])
        du = (slope * mm_bt(dy, fo_v[c])).astype(BF16)
        g_fb[:, cols] = col_sum(du.astype(F32))
        gfi_v[c] = mm_at(a2, du)
        out(gfi_v.at[c], g_fi.at[0, :, cols])
        gfo_v[c] = mm_at(value.astype(BF16), dy)
        out(gfo_v.at[c], g_fo.at[0, cols])
    loads["a1"].wait()
    for c in range(2):
        loads["dpq%d" % c].wait()
        pair_v[c] = mm_at(fwd_v[0], dpq_v[c])
        out(pair_v.at[c], g_pair.at[0, :, part(c)])
    loads["mbar"].wait()
    loads["dmsg"].wait()
    out_v[...] = mm_at(fwd_v[1], bwd_v[0]) * float(K)
    out(out_v, g_out.at[0])
    loads["a3"].wait()
    loads["drs"].wait()
    ends = mm_at(fwd_v[3], bwd_v[2])
    g_ep[0] = jnp.concatenate([ends[:, :DE], ends[:, EP : EP + DE]], axis=1)
    total = small[0]
    for c in range(1, C):
        total = total + small[c]
    for i, rows in enumerate(((0, 1, 2), (8, 9, 10), (11, 12, 13))):
        g_gain[i] = total[rows[0] : rows[0] + 1]
        g_shift[i] = total[rows[1] : rows[1] + 1]
        g_nb[i] = total[rows[2] : rows[2] + 1]
    g_eb[0, pl.ds(0, 1), :] = total[16:17, :DE]
    loads["edge"].wait()
    BW = (D + 2 * EP) // (2 * C)
    for k in range(2 * C):
        block = edge_v[k % C, k // C].astype(F32)
        first = k * BW
        for array, begin, width in ((g_edge, 0, D), (g_self, D, DE), (g_eout, D + EP, DE)):
            low, high = max(first, begin), min(first + BW, begin + width)
            if low < high:
                array[0, :, pl.ds(low - begin, high - low)] = block[:DE, low - first : high - first]
        low, high = first, min(first + BW, DE)
        if low < high:
            g_eb[0, pl.ds(1, 1), pl.ds(low, high - low)] = block[DE : DE + 1, low - first : high - first]
    for copy in stores:
        copy.wait()


def run_gradients(dims, operands):
    S, B, N, K, Q, D, DE, EP, FF, C = dims
    rows = C * B * N
    BW = (D + 2 * EP) // (2 * C)
    vm = pl.BlockSpec(memory_space=pltpu.VMEM)
    hbm = pl.BlockSpec(memory_space=pl.ANY)
    sds = jax.ShapeDtypeStruct
    shapes = (
        (1, D, 2 * D), (1, DE, D), (1, D, D), (1, D, FF), (1, FF, D), (1, D, 2 * DE), (1, DE, DE), (1, DE, DE),
        (3, 1, D), (3, 1, D), (3, 1, D), (1, FF), (1, 2, DE),
    )
    return pl.pallas_call(
        functools.partial(gradient_kernel, dims),
        out_shape=tuple(sds(shape, F32) for shape in shapes) + (sds((1, B, N, D), BF16),) * 2,
        in_specs=[hbm, hbm, hbm, vm, hbm, hbm, hbm, vm, hbm, hbm],
        out_specs=(hbm, vm, hbm, hbm, hbm) + (vm,) * 8 + (hbm,) * 2,
        scratch_shapes=[
            pltpu.VMEM((4, rows, D), BF16),
            pltpu.VMEM((3, rows, D), BF16),
            pltpu.VMEM((2, rows, D), BF16),
            pltpu.VMEM((4, D, FF // 4), BF16),
            pltpu.VMEM((4, FF // 4, D), BF16),
            pltpu.VMEM((4, D, FF // 4), F32),
            pltpu.VMEM((4, FF // 4, D), F32),
            pltpu.VMEM((2, D, D), F32),
            pltpu.VMEM((D, D), F32),
            pltpu.VMEM((C, 2, DE + 16, BW), BF16),
            pltpu.SemaphoreType.DMA((18,)),
            pltpu.SemaphoreType.DMA((13,)),
        ],
        compiler_params=pltpu.CompilerParams(vmem_limit_bytes=56 * 1024 * 1024),
    )(*operands)


def stationary(
    clean_nodes, noise_nodes, edge_feats, neighbours, time_bins, cotangent,
    pair_weight, message_edge, message_out, ffn_in, ffn_out, edge_pair, edge_self, edge_out,
    norm_gain, norm_shift, node_bias, ffn_bias, edge_bias,
):
    S = lax.axis_size("section")
    place = lax.axis_index("section")
    column = lax.axis_index("dp")
    B, N, D = clean_nodes.shape
    K, DE = edge_feats.shape[2:]
    FF = ffn_in.shape[2]
    Q = N // 4
    EP = DE + N
    core = column % 2
    w = place // 2
    slab = (place % 2) * 2 * Q

    node_ids = jnp.arange(N, dtype=jnp.int32)
    both = [
        lax.dynamic_slice(array, (w % B, slab) + (0,) * (array.ndim - 2), (1, 2 * Q) + array.shape[2:])[0]
        for array in (edge_feats, neighbours)
    ]
    chosen = (both[1][:, :, None] == node_ids).astype(BF16)
    both = jnp.concatenate([both[0], chosen], axis=2)
    mine = lax.dynamic_slice_in_dim(both, core * Q, Q, 0)
    theirs = lax.dynamic_slice_in_dim(both, (1 - core) * Q, Q, 0)
    got = lax.ppermute(theirs, "dp", [(i, i ^ 1) for i in range(lax.axis_size("dp"))])
    ecat0 = jnp.swapaxes(jnp.where(w // B == core, mine, got), 0, 1).reshape(K * Q, EP)
    oht = jnp.transpose(ecat0[:, DE:])
    phase = (time_bins.astype(F32) + 0.5) * (math.pi * 0.5 / TBINS)
    mix = jnp.cos(phase[None] - jnp.array([[0.0], [math.pi * 0.5]], F32))

    def by_rows(array):
        return jnp.transpose(array, (1, 0, 2))

    def widen(array, size, axis=-1):
        extra = [(0, 0)] * array.ndim
        extra[axis] = (0, size - array.shape[axis])
        return jnp.pad(array, extra)

    ep = jnp.concatenate([widen(edge_pair[0, :, :DE], EP), widen(edge_pair[0, :, DE:], EP)], axis=1)
    C = lax.axis_size("dp")
    dims = (S, B, N, K, Q, D, DE, EP, FF, C)
    act, ig, g_fwd, g_bwd, g_dpq, g_small, g_edge = run_relay(
        dims,
        (
            ecat0, oht, mix, clean_nodes.reshape(B * N, D), noise_nodes.reshape(B * N, D),
            cotangent.reshape(B * N, D), pair_weight[0], message_out[0], ffn_in[0], ffn_out[0], ep,
            by_rows(norm_gain), by_rows(norm_shift), by_rows(node_bias), ffn_bias, edge_bias[0],
            message_edge[0], edge_self[0], edge_out[0],
        ),
    )
    grads = run_gradients(
        dims,
        (
            g_fwd.reshape(C * B * N, -1), g_bwd.reshape(C * B * N, -1), g_dpq.reshape(C * B * N, -1),
            g_small, g_edge, ffn_in[0], ffn_out[0], ffn_bias, act.reshape(1, B, N, D), ig.reshape(1, B, N, D),
        ),
    )
    grads, outs = list(grads[:-2]), tuple(grads[-2:])
    grads[8:11] = [by_rows(array) for array in grads[8:11]]
    return outs + tuple(grads)


def solution(mesh):
    sections, copies = mesh.shape["section"], mesh.shape["dp"]

    def body(*args):
        B, N = args[0].shape[:2]
        fits = sections == 4 * B and copies % 2 == 0 and N % 64 == 0
        return stationary(*args) if fits else on_device(*args)

    placed = (
        P("dp", None, None),
        P("dp", None, None),
        P("dp", None, None, None),
        P("dp", None, None),
        P("dp"),
        P("dp", None, None),
        P("section", None, None),
        P("section", None, None),
        P("section", None, None),
        P("section", None, None),
        P("section", None, None),
        P("section", None, None),
        P("section", None, None),
        P("section", None, None),
        P("section", None, None),
        P("section", None, None),
        P("section", None, None),
        P("section", None),
        P("section", None, None),
    )
    return jax.shard_map(
        body,
        mesh=mesh,
        in_specs=placed,
        out_specs=(
            P("section", "dp", None, None),
            P("section", "dp", None, None),
            P("section", None, None),
            P("section", None, None),
            P("section", None, None),
            P("section", None, None),
            P("section", None, None),
            P("section", None, None),
            P("section", None, None),
            P("section", None, None),
            P("section", None, None),
            P("section", None, None),
            P("section", None, None),
            P("section", None),
            P("section", None, None),
        ),
        check_vma=False,
    )
```

```python
import functools
import math

import jax
import jax.numpy as jnp
from jax import lax
from jax.experimental import pallas as pl
from jax.experimental.pallas import tpu as pltpu
from jax.sharding import PartitionSpec as P

TBINS = 100


def from_behind(block, axis, distance):
    devices = range(lax.axis_size(axis))
    route = [(i - distance, i) for i in devices if i - distance in devices]
    return lax.ppermute(block, axis, route)


def for_sending(value):
    return jax.tree.map(lambda a: a.astype(jnp.bfloat16) if a.dtype == jnp.float32 else a, value)


def layer_norm(value, gain, shift):
    centre = jnp.mean(value, axis=-1, keepdims=True)
    centred = value - centre
    spread = jnp.mean(centred * centred, axis=-1, keepdims=True)
    return centred * lax.rsqrt(spread + 1e-05) * gain + shift


def forward_layer(weights, hidden, edge_state, nearest):
    (
        pair_w,
        msg_edge,
        msg_out,
        ffn_w_in,
        ffn_w_out,
        edge_pair_w,
        edge_self_w,
        edge_out_w,
        gains,
        shifts,
        node_b,
        ffn_b,
        edge_b,
    ) = weights
    width = msg_out.shape[0]
    edge_width = edge_self_w.shape[0]
    normed_one = layer_norm(hidden, gains[0], shifts[0]).astype(jnp.bfloat16)
    pair_out = jnp.dot(normed_one, pair_w, preferred_element_type=jnp.float32)
    before_act = (
        pair_out[:, None, :width]
        + jnp.take(pair_out[:, width:], nearest, axis=0)
        + jnp.einsum("nkc,cd->nkd", edge_state, msg_edge, preferred_element_type=jnp.float32)
        + node_b[0]
    )
    message_act = jax.nn.gelu(before_act).astype(jnp.bfloat16)
    message_all = jnp.einsum(
        "nkc,cd->nkd", message_act, msg_out, preferred_element_type=jnp.float32
    )
    after_msg = hidden + jnp.mean(message_all, axis=1) + node_b[1]
    normed_two = layer_norm(after_msg, gains[1], shifts[1]).astype(jnp.bfloat16)
    ffn_pre = jnp.dot(normed_two, ffn_w_in, preferred_element_type=jnp.float32) + ffn_b
    ffn_act = jax.nn.gelu(ffn_pre).astype(jnp.bfloat16)
    after_ffn = (
        after_msg + jnp.dot(ffn_act, ffn_w_out, preferred_element_type=jnp.float32) + node_b[2]
    )
    normed_three = layer_norm(after_ffn, gains[2], shifts[2]).astype(jnp.bfloat16)
    edge_pairs = jnp.dot(normed_three, edge_pair_w, preferred_element_type=jnp.float32)
    edge_pre = (
        edge_pairs[:, None, :edge_width]
        + jnp.take(edge_pairs[:, edge_width:], nearest, axis=0)
        + jnp.einsum("nkc,cd->nkd", edge_state, edge_self_w, preferred_element_type=jnp.float32)
        + edge_b[0]
    )
    edge_act = jax.nn.gelu(edge_pre).astype(jnp.bfloat16)
    edge_next = (
        edge_state.astype(jnp.float32)
        + jnp.einsum("nkc,cd->nkd", edge_act, edge_out_w, preferred_element_type=jnp.float32)
        + edge_b[1]
    )
    saved = (
        normed_one,
        before_act,
        message_act,
        after_msg,
        normed_two,
        ffn_pre,
        ffn_act,
        after_ffn,
        normed_three,
        edge_pre,
        edge_act,
    )
    return (after_ffn, edge_next, saved)


def backward_layer(weights, hidden, edge_state, nearest, grad_nodes_out, grad_edges_out):
    (
        pair_w,
        msg_edge,
        msg_out,
        ffn_w_in,
        ffn_w_out,
        edge_pair_w,
        edge_self_w,
        edge_out_w,
        gains,
        shifts,
        node_b,
        ffn_b,
        edge_b,
    ) = weights
    unused_nodes, unused_edges, saved = forward_layer(weights, hidden, edge_state, nearest)
    (
        normed_one,
        before_act,
        message_act,
        after_msg,
        normed_two,
        ffn_pre,
        ffn_act,
        after_ffn,
        normed_three,
        edge_pre,
        edge_act,
    ) = saved
    width = msg_out.shape[0]
    edge_width = edge_self_w.shape[0]
    count = nearest.shape[1]
    node_count = hidden.shape[0]
    one_hot = (
        nearest.reshape(-1)[None, :] == jnp.arange(node_count, dtype=jnp.int32)[:, None]
    ).astype(jnp.bfloat16)
    edge_grad_low = grad_edges_out.astype(jnp.bfloat16)
    grad_edge_b1 = jnp.sum(grad_edges_out, axis=(0, 1))
    grad_edge_out_w = jnp.einsum(
        "nkc,nkd->cd", edge_act, edge_grad_low, preferred_element_type=jnp.float32
    )
    edge_act_grad = jnp.einsum(
        "nkd,cd->nkc", edge_grad_low, edge_out_w, preferred_element_type=jnp.float32
    )
    unused_value, gelu_edge = jax.vjp(jax.nn.gelu, edge_pre)
    edge_pre_grad = gelu_edge(edge_act_grad)[0].astype(jnp.bfloat16)
    grad_edge_b0 = jnp.sum(edge_pre_grad, axis=(0, 1), dtype=jnp.float32)
    grad_edge_self_w = jnp.einsum(
        "nkc,nkd->cd", edge_state, edge_pre_grad, preferred_element_type=jnp.float32
    )
    edge_total = grad_edges_out + jnp.einsum(
        "nkd,cd->nkc", edge_pre_grad, edge_self_w, preferred_element_type=jnp.float32
    )
    own_edge = jnp.sum(edge_pre_grad, axis=1, dtype=jnp.float32)
    other_edge = jnp.dot(
        one_hot, edge_pre_grad.reshape(-1, edge_width), preferred_element_type=jnp.float32
    )
    pairs_grad = jnp.concatenate([own_edge, other_edge], axis=-1).astype(jnp.bfloat16)
    grad_edge_pair_w = jnp.einsum(
        "nc,nd->cd", normed_three, pairs_grad, preferred_element_type=jnp.float32
    )
    normed_three_grad = jnp.einsum(
        "nd,cd->nc", pairs_grad, edge_pair_w, preferred_element_type=jnp.float32
    )
    unused_value, norm_three_back = jax.vjp(layer_norm, after_ffn, gains[2], shifts[2])
    ffn_side, gain_three, shift_three = norm_three_back(normed_three_grad)
    after_ffn_grad = grad_nodes_out + ffn_side
    grad_node_b2 = jnp.sum(after_ffn_grad, axis=0)
    ffn_out_grad = after_ffn_grad.astype(jnp.bfloat16)
    grad_ffn_w_out = jnp.einsum(
        "nc,nd->cd", ffn_act, ffn_out_grad, preferred_element_type=jnp.float32
    )
    ffn_act_grad = jnp.einsum(
        "nd,cd->nc", ffn_out_grad, ffn_w_out, preferred_element_type=jnp.float32
    )
    unused_value, gelu_ffn = jax.vjp(jax.nn.gelu, ffn_pre)
    ffn_pre_grad = gelu_ffn(ffn_act_grad)[0].astype(jnp.bfloat16)
    grad_ffn_b = jnp.sum(ffn_pre_grad, axis=0, dtype=jnp.float32)
    grad_ffn_w_in = jnp.einsum(
        "nc,nd->cd", normed_two, ffn_pre_grad, preferred_element_type=jnp.float32
    )
    normed_two_grad = jnp.einsum(
        "nd,cd->nc", ffn_pre_grad, ffn_w_in, preferred_element_type=jnp.float32
    )
    unused_value, norm_two_back = jax.vjp(layer_norm, after_msg, gains[1], shifts[1])
    msg_side, gain_two, shift_two = norm_two_back(normed_two_grad)
    after_msg_grad = after_ffn_grad + msg_side
    grad_node_b1 = jnp.sum(after_msg_grad, axis=0)
    message_grad = (after_msg_grad / count).astype(jnp.bfloat16)
    grad_msg_out = jnp.einsum(
        "nkc,nd->cd", message_act, message_grad, preferred_element_type=jnp.float32
    )
    message_act_grad = jnp.einsum(
        "nd,cd->nc", message_grad, msg_out, preferred_element_type=jnp.float32
    )
    unused_value, gelu_msg = jax.vjp(jax.nn.gelu, before_act)
    before_grad = gelu_msg(jnp.broadcast_to(message_act_grad[:, None, :], before_act.shape))[
        0
    ].astype(jnp.bfloat16)
    grad_node_b0 = jnp.sum(before_grad, axis=(0, 1), dtype=jnp.float32)
    grad_msg_edge = jnp.einsum(
        "nkc,nkd->cd", edge_state, before_grad, preferred_element_type=jnp.float32
    )
    edge_total = edge_total + jnp.einsum(
        "nkd,cd->nkc", before_grad, msg_edge, preferred_element_type=jnp.float32
    )
    own_node = jnp.sum(before_grad, axis=1, dtype=jnp.float32)
    other_node = jnp.dot(
        one_hot, before_grad.reshape(-1, width), preferred_element_type=jnp.float32
    )
    pair_grad = jnp.concatenate([own_node, other_node], axis=-1).astype(jnp.bfloat16)
    grad_pair_w = jnp.einsum("nc,nd->cd", normed_one, pair_grad, preferred_element_type=jnp.float32)
    normed_one_grad = jnp.einsum("nd,cd->nc", pair_grad, pair_w, preferred_element_type=jnp.float32)
    unused_value, norm_one_back = jax.vjp(layer_norm, hidden, gains[0], shifts[0])
    input_side, gain_one, shift_one = norm_one_back(normed_one_grad)
    hidden_grad = after_msg_grad + input_side
    grads = (
        grad_pair_w,
        grad_msg_edge,
        grad_msg_out,
        grad_ffn_w_in,
        grad_ffn_w_out,
        grad_edge_pair_w,
        grad_edge_self_w,
        grad_edge_out_w,
        jnp.stack([gain_one, gain_two, gain_three]),
        jnp.stack([shift_one, shift_two, shift_three]),
        jnp.stack([grad_node_b0, grad_node_b1, grad_node_b2]),
        grad_ffn_b,
        jnp.stack([grad_edge_b0, grad_edge_b1]),
    )
    return (hidden_grad.astype(jnp.bfloat16), edge_total.astype(jnp.bfloat16), grads)


def on_device(
    clean_nodes,
    noise_nodes,
    edge_feats,
    neighbours,
    time_bins,
    cotangent,
    pair_weight,
    message_edge,
    message_out,
    ffn_in,
    ffn_out,
    edge_pair,
    edge_self,
    edge_out,
    norm_gain,
    norm_shift,
    node_bias,
    ffn_bias,
    edge_bias,
):
    sections = lax.axis_size("section")
    place = lax.axis_index("section")
    weights = tuple(
        (
            item[0]
            for item in (
                pair_weight,
                message_edge,
                message_out,
                ffn_in,
                ffn_out,
                edge_pair,
                edge_self,
                edge_out,
                norm_gain,
                norm_shift,
                node_bias,
                ffn_bias,
                edge_bias,
            )
        )
    )
    batches, node_count, width = clean_nodes.shape
    phase = (time_bins.astype(jnp.float32) + 0.5) * (math.pi * 0.5 / TBINS)
    start = jnp.cos(phase)[:, None, None] * clean_nodes.astype(jnp.float32) + jnp.sin(phase)[
        :, None, None
    ] * noise_nodes.astype(jnp.float32)
    zero_nodes = jnp.zeros((node_count, width), jnp.bfloat16)
    zero_edges = jnp.zeros(edge_feats.shape[1:], jnp.bfloat16)
    is_first = place == 0
    is_last = place == sections - 1

    def forward_step(step_index, carry):
        recv_nodes, recv_edges, back_nodes, kept_nodes, kept_edges, section_outs = carry
        item = step_index - place
        first_pass = (item >= 0) & (item < batches)
        second_pass = (item >= sections) & (item < sections + batches)
        index = jnp.clip(jnp.where(second_pass, item - sections, item), 0, batches - 1)
        predicted = back_nodes
        own_start = lax.dynamic_index_in_dim(start, index, 0, keepdims=False)
        lead_nodes = own_start + jnp.where(second_pass, predicted.astype(jnp.float32), 0.0)
        nodes_in = jnp.where(is_first, lead_nodes, recv_nodes.astype(jnp.float32))
        edges_in = jnp.where(
            is_first, lax.dynamic_index_in_dim(edge_feats, index, 0, keepdims=False), recv_edges
        )
        nearest = lax.dynamic_index_in_dim(neighbours, index, 0, keepdims=False)

        def run_layer(operand):
            after, edge_next, saved = forward_layer(weights, operand[0], operand[1], operand[2])
            return (after.astype(jnp.bfloat16), edge_next.astype(jnp.bfloat16))

        def skip_layer(operand):
            return (zero_nodes, zero_edges)

        out_nodes, out_edges = lax.cond(
            first_pass | second_pass, run_layer, skip_layer, (nodes_in, edges_in, nearest)
        )
        kept_nodes = lax.dynamic_update_index_in_dim(
            kept_nodes, jnp.where(second_pass, nodes_in, kept_nodes[index]), index, 0
        )
        kept_edges = lax.dynamic_update_index_in_dim(
            kept_edges, jnp.where(second_pass, edges_in, kept_edges[index]), index, 0
        )
        section_outs = lax.dynamic_update_index_in_dim(
            section_outs, jnp.where(second_pass, out_nodes, section_outs[index]), index, 0
        )
        recv_nodes, recv_edges = from_behind((out_nodes, out_edges), "section", 1)
        back_nodes = from_behind(out_nodes, "section", 1 - sections)
        return (recv_nodes, recv_edges, back_nodes, kept_nodes, kept_edges, section_outs)

    forward_init = (
        zero_nodes,
        zero_edges,
        zero_nodes,
        jnp.zeros((batches, node_count, width), jnp.float32),
        jnp.zeros_like(edge_feats),
        jnp.zeros((batches, node_count, width), jnp.bfloat16),
    )
    unused_nodes, unused_edges, unused_back, kept_nodes, kept_edges, section_outs = lax.fori_loop(
        0, 2 * sections + batches - 1, forward_step, forward_init
    )
    grads_zero = tuple((jnp.zeros(item.shape, jnp.float32) for item in weights))

    def backward_step(step_index, carry):
        recv_grad_nodes, recv_grad_edges, grads, input_grads = carry
        item = step_index - (sections - 1 - place)
        live = (item >= 0) & (item < batches)
        index = jnp.clip(item, 0, batches - 1)
        nodes_grad_out = jnp.where(
            is_last,
            lax.dynamic_index_in_dim(cotangent, index, 0, keepdims=False).astype(jnp.float32),
            recv_grad_nodes.astype(jnp.float32),
        )
        edges_grad_out = jnp.where(is_last, 0.0, recv_grad_edges.astype(jnp.float32))
        nearest = lax.dynamic_index_in_dim(neighbours, index, 0, keepdims=False)

        def run_back(operand):
            return backward_layer(
                weights, operand[0], operand[1], operand[2], operand[3], operand[4]
            )

        def skip_back(operand):
            return (zero_nodes, zero_edges, grads_zero)

        nodes_grad, edges_grad, terms = lax.cond(
            live,
            run_back,
            skip_back,
            (kept_nodes[index], kept_edges[index], nearest, nodes_grad_out, edges_grad_out),
        )
        grads = tuple((total + term for total, term in zip(grads, terms)))
        input_grads = lax.dynamic_update_index_in_dim(
            input_grads, jnp.where(live, nodes_grad, input_grads[index]), index, 0
        )
        recv_grad_nodes, recv_grad_edges = from_behind((nodes_grad, edges_grad), "section", -1)
        return (recv_grad_nodes, recv_grad_edges, grads, input_grads)

    backward_init = (
        zero_nodes,
        zero_edges,
        grads_zero,
        jnp.zeros((batches, node_count, width), jnp.bfloat16),
    )
    unused_grad_nodes, unused_grad_edges, grads, input_grads = lax.fori_loop(
        0, sections + batches - 1, backward_step, backward_init
    )
    totals = jax.tree.map(lambda part: part.astype(jnp.float32), lax.psum(for_sending(grads), "dp"))
    return (
        section_outs[None],
        input_grads[None],
        totals[0][None],
        totals[1][None],
        totals[2][None],
        totals[3][None],
        totals[4][None],
        totals[5][None],
        totals[6][None],
        totals[7][None],
        totals[8][None],
        totals[9][None],
        totals[10][None],
        totals[11][None],
        totals[12][None],
    )


BF16 = jnp.bfloat16
F32 = jnp.float32
MESH = pl.DeviceIdType.MESH
GELU_A = 0.7978845608028654
GELU_B = 0.044715


def gelu(x):
    return 0.5 * x * (1.0 + jnp.tanh(x * (GELU_A + (GELU_A * GELU_B) * (x * x))))


def gelu_both(x):
    square = x * x
    t = jnp.tanh(x * (GELU_A + (GELU_A * GELU_B) * square))
    half = 0.5 * (1.0 + t)
    slope = half + (0.5 * x) * (1.0 - t * t) * (GELU_A + (3.0 * GELU_A * GELU_B) * square)
    return x * half, slope


def mm(a, b):
    return jnp.dot(a, b, preferred_element_type=F32)


def mm_bt(a, b):
    return lax.dot_general(a, b, (((1,), (1,)), ((), ())), preferred_element_type=F32)


def mm_at(a, b):
    return lax.dot_general(a, b, (((0,), (0,)), ((), ())), preferred_element_type=F32)


def stacked(blocks):
    return jnp.concatenate(blocks, axis=0)


def row_mean(x):
    return jnp.mean(x, axis=-1, keepdims=True)


def normed(x):
    centred = x - row_mean(x)
    scale = lax.rsqrt(row_mean(centred * centred) + 1e-05)
    return centred * scale, scale


def norm_back(grad, unit, scale, gain):
    t = grad * gain
    return scale * (t - row_mean(t) - unit * row_mean(t * unit))


def col_sum(x):
    return jnp.sum(x, axis=0, keepdims=True)


def relay_kernel(
    dims,
    ecat0, oht, mix, clean, noise, cot, pw, mo, fi, fo, ep, gains, shifts, node_b, fb, edge_b, we_own, ws_own, wo_own,
    act, ig, g_fwd, g_bwd, g_dpq, g_small, g_edge,
    start, par, eb0, wall, fwd, bwd, sg, eg, eg_r, eg_b, eg_o, eg_f, wo, eb1,
    ecat, wcat, scat, pwn, parn, hin_r, hst, mb_s, mb_r, pq_s, pq_r, rq_s, rq_r,
    un0, un1, un2, hi_s, sc0, sc1, sc2, sci, u_s, slope_s, de, dacc, gp, gpe, dcat, act_t, edge_t,
    x_s, x_r, row_s, row_r, dpqo_r, dmb_s, dmb_r, dh1_s, dh1_r, dh1_f, dh2_s, dn3_s, da2_s, h1_s, a1_s,
    ld_sem, nx_ss, nx_rs, hop_ss, hop_rs,
    pq_ss, pq_rs, ag_ss, ag_rs, rq_ss, rq_rs, ag2_ss, ag2_rs,
    mb_ss, mb_rs, x_ss, x_rs, row_ss, row_rs, dpqo_rs, fw_ss, dmb_ss, dmb_rs, dh_ss, dh_rs,
    e1_ss, e1_rs, e2_ss, e2_rs, g_ss, g_rs, ring_ss, ring_rs, sib_ss, sib_rs,
):
    S, B, N, K, Q, D, DE, EP, FF, C = dims
    BN = B * N
    RB = 16
    top = DE + N
    me_s = lax.axis_index("section")
    me_d = lax.axis_index("dp")
    core = lax.rem(me_d, 2)
    pair = me_d - core
    w = lax.div(me_s, 2)
    q = 2 * lax.rem(me_s, 2) + core
    owner_d = pair + lax.div(w, B)
    slot = lax.rem(w, B)
    my_row = pl.multiple_of(slot * N + q * Q, Q)
    own_rows = pl.ds(top, Q)

    def quarter(j):
        return pl.ds(pl.multiple_of(DE + j * Q, Q), Q)

    def is_me(sec, dpi):
        return (sec == me_s) & (dpi == me_d)

    def far(src, dst, ssem, rsem, sec, dpi):
        return pltpu.make_async_remote_copy(
            src_ref=src, dst_ref=dst, send_sem=ssem, recv_sem=rsem,
            device_id={"section": sec, "dp": dpi}, device_id_type=MESH,
        )

    def push(src, dst, ssem, rsem, sec, dpi):
        lax.cond(
            is_me(sec, dpi),
            lambda: pltpu.make_async_copy(src, dst, rsem).start(),
            lambda: far(src, dst, ssem, rsem, sec, dpi).start(),
        )

    def arrive(ref, sem):
        pltpu.make_async_copy(ref, ref, sem).wait()

    def drain(ref, sem, sec, dpi):
        @pl.when(jnp.logical_not(is_me(sec, dpi)))
        def _():
            arrive(ref, sem)

    def worker_of(p, j):
        return 2 * (core * B + p) + j // 2, pair + j % 2

    def peer(k):
        j = lax.rem(q + k, 4)
        return j, 2 * w + lax.div(j, 2), pair + lax.rem(j, 2)

    works_here = lax.div(w, B) == core

    def at(p, first=0, size=16):
        return pl.ds(pl.multiple_of(p * N + first, size), size)

    near = jnp.clip(w - core * B, 0, B - 1)

    load = pltpu.make_async_copy(ecat0, ecat.at[0], ld_sem)
    load.start()
    barrier = pltpu.get_barrier_semaphore()
    for sec in range(S):
        for c in range(C):
            greeted = (c == pair) | (c == pair + 1) | (w == sec // 2)

            @pl.when(greeted & jnp.logical_not(is_me(sec, c)))
            def _():
                pl.semaphore_signal(
                    barrier, inc=1, device_id={"section": sec, "dp": c}, device_id_type=MESH
                )
    W = D + 2 * EP
    H = wall.shape[1] // 2
    wall[me_s] = jnp.zeros((2 * H, W), BF16)
    wall[me_s, pl.ds(0, DE), pl.ds(0, D)] = we_own[...]
    wall[me_s, pl.ds(0, DE), pl.ds(D, DE)] = ws_own[...]
    wall[me_s, pl.ds(0, DE), pl.ds(D + EP, DE)] = wo_own[...]
    bias = edge_b[pl.ds(1, 1), :]
    high = bias.astype(BF16).astype(F32)
    row = lax.broadcasted_iota(jnp.int32, (16, DE), 0)
    wall[me_s, pl.ds(DE, 16), pl.ds(0, DE)] = jnp.where(
        row == 0, high, jnp.where(row == 1, bias - high, 0.0)
    ).astype(BF16)
    eb0[...] = jnp.zeros_like(eb0)
    eb0[:, pl.ds(0, DE)] = edge_b[pl.ds(0, 1), :]
    par[pl.ds(0, 1), :] = gains[0]
    par[pl.ds(1, 1), :] = shifts[0]
    par[pl.ds(2, 1), :] = node_b[0]
    par[pl.ds(3, 5), :] = jnp.zeros((5, D), F32)
    pl.semaphore_wait(barrier, 2 * S - 1 + 2 * (C - 2))

    def section_at(i):
        i = lax.rem(i + S, S)
        return jnp.where(i < S // 2, 2 * i, 2 * (S - i) - 1)

    place = jnp.where(lax.rem(me_s, 2) == 0, w, S - 1 - w)
    mine = pl.ds(pl.multiple_of(core * H, H), H)
    theirs = pl.ds(pl.multiple_of((1 - core) * H, H), H)
    sides = ((section_at(place + 1), S // 2), (section_at(place - 1), S // 2 - 1))

    def ring_send(layer, side, hop):
        sec, reach = sides[side]
        if hop < reach:
            half = wall.at[layer, mine]
            far(half, half, ring_ss.at[side, hop], ring_rs.at[layer], sec, me_d).start()

    for side in range(2):
        ring_send(me_s, side, 0)
    before = lax.rem(me_s + S - 1, S)
    far(pw, pwn, nx_ss.at[0], nx_rs.at[0], before, me_d).start()
    far(par, parn, nx_ss.at[1], nx_rs.at[1], before, me_d).start()

    for p in range(B):
        rows = pl.ds(p * N, N)
        start[rows, :] = mix[0, p] * clean[rows, :].astype(F32) + mix[1, p] * noise[rows, :].astype(F32)

    def ring():
        for hop in range(1, S // 2 + 1):
            for side in range(2):
                if hop <= sides[side][1]:
                    layer = section_at(place - hop if side == 0 else place + hop)
                    half = wall.at[layer, mine]
                    arrive(half, ring_rs.at[layer])
                    ring_send(layer, side, hop)
                    far(half, half, sib_ss.at[layer], sib_rs.at[layer], me_s, pair + 1 - core).start()

    def ring_drain():
        for side in range(2):
            for hop in range(sides[side][1]):
                arrive(wall.at[me_s, mine], ring_ss.at[side, hop])
        for layer in range(S):
            @pl.when(layer != me_s)
            def _():
                arrive(wall.at[layer, mine], sib_ss.at[layer])

    def unpack(t):
        @pl.when(t != me_s)
        def _():
            arrive(wall.at[t, theirs], sib_rs.at[t])

        wcat[t, pl.ds(0, DE), :] = wall[t, pl.ds(0, DE), pl.ds(0, D)]
        scat[t, pl.ds(0, DE), :] = wall[t, pl.ds(0, DE), pl.ds(D, EP)]
        wo[t, pl.ds(0, DE), :] = wall[t, pl.ds(0, DE), pl.ds(D + EP, EP)]
        wo[t, pl.ds(DE, N), :] = jnp.zeros((N, EP), BF16)
        eb1[t] = wall[t, pl.ds(DE, 16), pl.ds(0, EP)]

    def rows_out(p, src, dst, ssem, rsem):
        for j in range(4):
            sec, dpi = worker_of(p, j)
            push(src.at[at(p, j * Q, Q)], dst, ssem, rsem, sec, dpi)

    def rows_drain(src, ssem):
        lax.cond(
            works_here,
            lambda: arrive(src.at[pl.ds(0, B * N - Q)], ssem),
            lambda: arrive(src, ssem),
        )

    def spread(rows, half, ref, layer, ssem, rsem, rows_sem):
        arrive(rows, rows_sem)
        for k in range(1, 4):
            _, sec, dpi = peer(k)
            far(rows.at[:, pl.ds(half, half)], ref.at[layer, quarter(q)], ssem, rsem, sec, dpi).start()
        ref[layer, own_rows, :] = rows[:, pl.ds(0, half)]
        ref[layer, quarter(q), :] = rows[:, pl.ds(half, half)]

    def spread_wait(ref, layer, sem):
        arrive(ref.at[layer, pl.ds(DE, 3 * Q)], sem)

    def share(group, src, dst):
        for c in range(C):
            push(src, dst.at[me_d], g_ss.at[group, c], g_rs.at[group, me_d], me_s, c)

    def share_wait(group, src, dst):
        for c in range(C):
            arrive(dst.at[c], g_rs.at[group, c])
            drain(src, g_ss.at[group, c], me_s, c)

    steps = 4
    KC = K // steps
    RC = KC * Q

    def messages(t):
        own = wcat[t, own_rows, :].astype(F32)
        total = jnp.zeros((Q, D), F32)
        for i in range(steps):
            pre = mm(ecat[t, pl.ds(i * RC, RC), :], wcat[t, pl.ds(0, top), :])
            for k in range(KC):
                total = total + gelu(pre[k * Q : (k + 1) * Q] + own)
        mb_s[...] = (total * (1.0 / K)).astype(BF16)

    def edge_update(t):
        own = scat[t, own_rows, :].astype(F32)
        bias = eb1[t, pl.ds(0, 1), :].astype(F32) + eb1[t, pl.ds(1, 1), :].astype(F32)
        for i in range(steps):
            pe = mm(ecat[t, pl.ds(i * RC, RC), :], scat[t, pl.ds(0, top), :])
            act_e = stacked([gelu(pe[k * Q : (k + 1) * Q] + own).astype(BF16) for k in range(KC)])
            z = mm(act_e, wo[t])
            for k in range(KC):
                rows = pl.ds(i * RC + k * Q, Q)
                ecat[t + 1, rows, :] = (ecat[t, rows, :].astype(F32) + z[k * Q : (k + 1) * Q] + bias).astype(BF16)

    chunks = 4
    FC = FF // chunks

    def node_forward(step):
        @pl.when(step < S)
        def _():
            arrive(pwn, nx_rs.at[0])
            arrive(parn, nx_rs.at[1])
            arrive(pw, nx_ss.at[0])
            arrive(par, nx_ss.at[1])

        @pl.when(step == 0)
        def _():
            hi_s[...] = start[...]

        @pl.when(step > 0)
        def _():
            arrive(hin_r, hop_rs)
            first = jnp.where(me_s == 0, 1.0, 0.0)
            for i in range(0, BN, RB):
                rows = pl.ds(i, RB)
                hi_s[rows, :] = hin_r[rows, :].astype(F32) + first * start[rows, :]

        later = lax.rem(me_s + 1, S)

        def turn(n, carry):
            p = lax.rem(near + n, B)
            whole = at(p, 0, N)
            arrive(mb_r.at[whole], mb_rs.at[p])
            mean = mm(mb_r[whole, :], mo[...])
            for i in range(0, N, RB):
                rows = at(p, i)
                h1 = hi_s[rows, :] + mean[i : i + RB] + node_b[1]
                h1_s[rows, :] = h1
                unit, scale = normed(h1)
                un1[rows, :] = unit
                sc1[rows, :] = scale
                fwd[rows, pl.ds(2 * D, D)] = (unit * gains[1] + shifts[1]).astype(BF16)
                fwd[rows, pl.ds(D, D)] = mb_r[rows, :]
            a2 = fwd[whole, pl.ds(2 * D, D)]
            y = jnp.zeros((N, D), F32)
            for c in range(chunks):
                cols = pl.ds(c * FC, FC)
                u = mm(a2, fi[:, cols])
                v = []
                for i in range(0, N, RB):
                    block = u[i : i + RB] + fb[:, cols]
                    u_s[at(p, i), cols] = block
                    v.append(gelu(block).astype(BF16))
                y = y + mm(stacked(v), fo[cols, :])
            last = jnp.where(me_s == S - 1, 1.0, 0.0)
            for i in range(0, N, RB):
                rows = at(p, i)
                h2 = h1_s[rows, :] + y[i : i + RB] + node_b[2]
                rounded = h2.astype(BF16)
                hst[rows, :] = rounded
                unit, scale = normed(h2)
                un2[rows, :] = unit
                sc2[rows, :] = scale
                fwd[rows, pl.ds(3 * D, D)] = (unit * gains[2] + shifts[2]).astype(BF16)
                pair_norm(rows, rounded.astype(F32) + last * start[rows, :], parn)
            rq = mm(fwd[whole, pl.ds(3 * D, D)], ep[...])
            for i in range(0, N, RB):
                rows = at(p, i)
                rq_s[rows, pl.ds(0, EP)] = (rq[i : i + RB, :EP] + eb0[...]).astype(BF16)
                rq_s[rows, pl.ds(EP, EP)] = rq[i : i + RB, EP:].astype(BF16)
            pair_rows(p, pwn, parn)

            @pl.when(me_s < S - 1)
            def _():
                rows_out(p, rq_s, rq_r, rq_ss, rq_rs)

            @pl.when(step < 2 * S - 1)
            def _():
                rows_out(p, pq_s, pq_r, pq_ss, pq_rs)

            @pl.when((n == 0) & works_here)
            def _():
                pass_on(step)

            return carry

        lax.fori_loop(0, B, turn, 0)

        @pl.when(step < 2 * S - 1)
        def _():
            far(hst, hin_r, hop_ss, hop_rs, later, me_d).start()

        @pl.when(step >= S)
        def _():
            act[...] = hst[...]
            for i in range(0, BN, RB):
                rows = pl.ds(i, RB)
                unit, scale = normed(hi_s[rows, :])
                hi_s[rows, :] = unit
                sci[rows, :] = scale
                fwd[rows, pl.ds(0, D)] = (unit * gains[0] + shifts[0]).astype(BF16)
                for c in range(chunks):
                    cols = pl.ds(c * FC, FC)
                    slope_s[rows, cols] = gelu_both(u_s[rows, cols])[1].astype(BF16)
            share(0, fwd, g_fwd)

    def pair_norm(rows, hidden, first):
        unit, scale = normed(hidden)
        un0[rows, :] = unit
        sc0[rows, :] = scale
        a1_s[rows, :] = (unit * first[pl.ds(0, 1), :] + first[pl.ds(1, 1), :]).astype(BF16)

    def pair_rows(p, weight, first):
        whole = at(p, 0, N)
        for half in range(2):
            cols = pl.ds(half * D, D)
            value = mm(a1_s[whole, :], weight[:, cols])
            if half == 0:
                value = value + first[pl.ds(2, 1), :]
            pq_s[whole, cols] = value.astype(BF16)

    def pass_on(step):
        t = lax.rem(step, S)

        @pl.when(t < S - 1)
        def _():
            spread(rq_r, EP, scat, t, ag2_ss, ag2_rs, rq_rs)

        @pl.when(step < 2 * S - 1)
        def _():
            spread(pq_r, D, wcat, lax.rem(step + 1, S), ag_ss, ag_rs, pq_rs)

    def node_forward_drain():
        arrive(hst, hop_ss)
        rows_drain(pq_s, pq_ss)

        @pl.when(me_s < S - 1)
        def _():
            rows_drain(rq_s, rq_ss)

    @pl.when(me_s == 0)
    def _():
        for i in range(0, BN, RB):
            rows = pl.ds(i, RB)
            pair_norm(rows, start[rows, :], par)
        for p in range(B):
            pair_rows(p, pw, par)
            rows_out(p, pq_s, pq_r, pq_ss, pq_rs)

    def message_slope(t):
        own = wcat[t, own_rows, :].astype(F32)
        for i in range(steps):
            pre = mm(ecat[t, pl.ds(i * RC, RC), :], wcat[t, pl.ds(0, top), :])
            for k in range(KC):
                gp[t, pl.ds(i * RC + k * Q, Q), :] = gelu_both(pre[k * Q : (k + 1) * Q] + own)[1].astype(BF16)

    def edge_slope(t):
        own = scat[t, own_rows, :].astype(F32)
        values = []
        for i in range(steps):
            pe = mm(ecat[t, pl.ds(i * RC, RC), :], scat[t, pl.ds(0, top), :])
            for k in range(KC):
                value, slope = gelu_both(pe[k * Q : (k + 1) * Q] + own)
                values.append(value.astype(BF16))
                gpe[t, pl.ds(i * RC + k * Q, Q), :] = slope.astype(BF16)
        act_t[t] = stacked(values).T

    def prepare(t):
        message_slope(t)
        edge_t[t] = ecat[t].T

        @pl.when(t > 0)
        def _():
            edge_slope(t - 1)

    def forward_step(step, carry):
        t = lax.rem(step, S)

        @pl.when(step < S)
        def _():
            unpack(t)

        spread_wait(wcat, t, ag_rs)
        messages(t)
        spread_wait(wcat, t, ag_ss)
        push(mb_s, mb_r.at[pl.ds(my_row, Q)], mb_ss, mb_rs.at[slot], t, owner_d)

        @pl.when((step == 0) & (me_s == 0))
        def _():
            rows_drain(pq_s, pq_ss)

        @pl.when((step > 0) & (me_s == lax.rem(step + S - 1, S)))
        def _():
            node_forward_drain()

        @pl.when(me_s == t)
        def _():
            node_forward(step)

        @pl.when((me_s != t) & (step >= S))
        def _():
            prepare(t)

        @pl.when(jnp.logical_not((me_s == t) & works_here))
        def _():
            pass_on(step)

        @pl.when(t < S - 1)
        def _():
            spread_wait(scat, t, ag2_rs)
            edge_update(t)
            spread_wait(scat, t, ag2_ss)

        drain(mb_s, mb_ss, t, owner_d)
        return carry

    ring()
    load.wait()
    spread(pq_r, D, wcat, 0, ag_ss, ag_rs, pq_rs)
    lax.fori_loop(0, 2 * S, forward_step, 0)
    ring_drain()

    def edge_back(t):
        b2, n2 = lax.rem(t, 2), lax.rem(t + 1, 2)
        total = jnp.zeros((Q, EP), F32)
        for i in range(steps):
            chunk = pl.ds(i * RC, RC)
            carry = mm_bt(dcat[b2, chunk, pl.ds(0, D)], wcat[t, pl.ds(0, top), :])
            low = []
            for k in range(KC):
                rows = pl.ds(i * RC + k * Q, Q)
                low.append((dacc[rows, :] + carry[k * Q : (k + 1) * Q]).astype(BF16))
                de[n2, rows, :] = low[-1]
            dw = mm_bt(stacked(low), wo[t - 1])
            for k in range(KC):
                rows = pl.ds(i * RC + k * Q, Q)
                d = (gpe[t - 1, rows, :].astype(F32) * dw[k * Q : (k + 1) * Q]).astype(BF16)
                total = total + d.astype(F32)
                dcat[n2, rows, pl.ds(D, EP)] = d
        row_s[:, pl.ds(2 * D, EP)] = total.astype(BF16)
        x_s[:, pl.ds(D, EP)] = mm(oht[...], dcat[n2, :, pl.ds(D, EP)]).astype(BF16)

    def edge_pass(t):
        b3 = lax.rem(t, 2)
        for i in range(steps):
            rows = pl.ds(i * RC, RC)
            d = dcat[b3, rows, pl.ds(D, EP)]
            dacc[rows, :] = de[b3, rows, :].astype(F32) + mm_bt(d, scat[t, pl.ds(0, top), :])

    blocks = 2 * C
    BW = (D + 2 * EP) // blocks
    my_block = lax.rem(me_s, 2) * C + me_d
    my_cols = pl.ds(pl.multiple_of(my_block * BW, BW), BW)

    def edge_grads(t):
        b3 = lax.rem(t, 2)

        @pl.when(t < S - 1)
        def _():
            eg[t, pl.ds(0, DE), pl.ds(0, D + EP)] = mm(edge_t[t, pl.ds(0, DE), :], dcat[b3]).astype(BF16)
            eg[t, pl.ds(0, DE), pl.ds(D + EP, EP)] = mm(act_t[t, pl.ds(0, DE), :], de[b3]).astype(BF16)
            bias = jnp.sum(de[b3].astype(F32), axis=0, keepdims=True)
            eg[t, pl.ds(DE, 16), pl.ds(0, EP)] = jnp.broadcast_to(bias, (16, EP)).astype(BF16)

        @pl.when(t == S - 1)
        def _():
            eg[t, pl.ds(0, DE), pl.ds(0, D)] = mm(edge_t[t, pl.ds(0, DE), :], dcat[b3, :, pl.ds(0, D)]).astype(BF16)
            eg[t, pl.ds(0, DE), pl.ds(D, 2 * EP)] = jnp.zeros((DE, 2 * EP), BF16)
            eg[t, pl.ds(DE, 16), pl.ds(0, EP)] = jnp.zeros((16, EP), BF16)

        eg[t, pl.ds(DE, 16), pl.ds(EP, D + EP)] = jnp.zeros((16, D + EP), BF16)
        for k in range(blocks):
            @pl.when(k != my_block)
            def _():
                far(
                    eg.at[t, :, pl.ds(k * BW, BW)], eg_r.at[t, my_block], e1_ss.at[t, k], e1_rs.at[t, my_block],
                    2 * w + k // C, k % C,
                ).start()

    def edge_grads_sum(t):
        eg_r[t, my_block] = eg[t, :, my_cols]
        for k in range(blocks):
            @pl.when(k != my_block)
            def _():
                arrive(eg_r.at[t, k], e1_rs.at[t, k])
                arrive(eg.at[t, :, pl.ds(k * BW, BW)], e1_ss.at[t, k])
        total = eg_r[t, 0].astype(F32)
        for k in range(1, blocks):
            total = total + eg_r[t, k].astype(F32)
        eg_b[t] = total.astype(BF16)
        push(eg_b.at[t], eg_o.at[me_s], e2_ss.at[t], e2_rs.at[me_s], t, me_d)

    def gather_blocks():
        for k in range(1, 4):
            j, sec, dpi = peer(k)
            rows = pl.ds(pl.multiple_of(j * Q, Q), Q)
            far(x_s.at[rows], x_r.at[q], x_ss, x_rs, sec, dpi).start()
        x_r[q] = x_s[pl.ds(pl.multiple_of(q * Q, Q), Q), :]

    def gather_wait():
        arrive(x_r.at[pl.ds(0, 3)], x_rs)
        arrive(x_s.at[pl.ds(0, 3 * Q)], x_ss)
        total = x_r[0].astype(F32)
        for j in range(1, 4):
            total = total + x_r[j].astype(F32)
        return total

    def message_back(t):
        b2 = lax.rem(t, 2)
        dm = dmb_r[...].astype(F32)
        total = jnp.zeros((Q, D), F32)
        for k in range(K):
            rows = pl.ds(k * Q, Q)
            d = (gp[t, rows, :].astype(F32) * dm).astype(BF16)
            total = total + d.astype(F32)
            dcat[b2, rows, pl.ds(0, D)] = d
        row_s[:, pl.ds(0, D)] = total.astype(BF16)
        x_s[:, pl.ds(0, D)] = mm(oht[...], dcat[b2, :, pl.ds(0, D)]).astype(BF16)

    def node_backward():
        @pl.when(me_s < S - 1)
        def _():
            arrive(dh1_r, dh_rs)

        def turn(n, carry):
            p = lax.rem(near + n, B)
            whole = at(p, 0, N)

            @pl.when(me_s < S - 1)
            def _():
                arrive(row_r.at[whole], row_rs.at[p])
                dn0 = mm_bt(row_r[whole, pl.ds(0, 2 * D)], pwn[...])
                dn3 = mm_bt(row_r[whole, pl.ds(2 * D, 2 * EP)], ep[...])
                for i in range(0, N, RB):
                    rows = at(p, i)
                    dn = dn3[i : i + RB]
                    dn3_s[rows, :] = dn
                    first = norm_back(dn0[i : i + RB], un0[rows, :], sc0[rows, :], parn[pl.ds(0, 1), :])
                    dh = (dh1_r[rows, :].astype(F32) + first).astype(BF16).astype(F32)
                    dh2_s[rows, :] = dh + norm_back(dn, un2[rows, :], sc2[rows, :], gains[2])

            @pl.when(me_s == S - 1)
            def _():
                dh2_s[whole, :] = cot[whole, :].astype(F32)

            dy = dh2_s[whole, :].astype(BF16)
            bwd[whole, pl.ds(D, D)] = dy
            da2 = jnp.zeros((N, D), F32)
            for c in range(chunks):
                cols = pl.ds(c * FC, FC)
                dv = mm_bt(dy, fo[cols, :])
                du = stacked(
                    [(slope_s[at(p, i), cols].astype(F32) * dv[i : i + RB]).astype(BF16) for i in range(0, N, RB)]
                )
                da2 = da2 + mm_bt(du, fi[:, cols])
            for i in range(0, N, RB):
                rows = at(p, i)
                block = da2[i : i + RB]
                da2_s[rows, :] = block
                dh1 = dh2_s[rows, :] + norm_back(block, un1[rows, :], sc1[rows, :], gains[1])
                dh1_f[rows, :] = dh1
                bwd[rows, pl.ds(0, D)] = (dh1 * (1.0 / K)).astype(BF16)
            dmb_s[whole, :] = mm_bt(bwd[whole, pl.ds(0, D)], mo[...]).astype(BF16)
            rows_out(p, dmb_s, dmb_r, dmb_ss, dmb_rs)
            return carry

        lax.fori_loop(0, B, turn, 0)

        @pl.when(me_s > 0)
        def _():
            dh1_s[...] = dh1_f[...].astype(BF16)
            far(dh1_s, dh1_r, dh_ss, dh_rs, me_s - 1, me_d).start()

        @pl.when(me_s < S - 1)
        def _():
            far(row_r.at[:, pl.ds(0, 2 * D)], dpqo_r, fw_ss, dpqo_rs, me_s + 1, me_d).start()
            drs = row_r[:, pl.ds(2 * D, 2 * EP)]
            bwd[:, pl.ds(2 * D, 2 * EP)] = drs
            dn = dn3_s[...]
            sg[pl.ds(11, 1), :] = col_sum(dn * un2[...])
            sg[pl.ds(12, 1), :] = col_sum(dn)
            sg[pl.ds(16, 1), pl.ds(0, EP)] = col_sum(drs[:, :EP].astype(F32))

        @pl.when(me_s == S - 1)
        def _():
            bwd[:, pl.ds(2 * D, 2 * EP)] = jnp.zeros((B * N, 2 * EP), BF16)
            sg[pl.ds(11, 1), :] = jnp.zeros((1, D), F32)
            sg[pl.ds(12, 1), :] = jnp.zeros((1, D), F32)
            sg[pl.ds(16, 1), pl.ds(0, EP)] = jnp.zeros((1, EP), F32)

        share(1, bwd, g_bwd)
        sg[pl.ds(13, 1), :] = col_sum(dh2_s[...])
        sg[pl.ds(8, 1), :] = col_sum(da2_s[...] * un1[...])
        sg[pl.ds(9, 1), :] = col_sum(da2_s[...])
        sg[pl.ds(10, 1), :] = col_sum(dh1_f[...])

    def node_backward_drain():
        rows_drain(dmb_s, dmb_ss)

        @pl.when(me_s > 0)
        def _():
            arrive(dh1_s, dh_ss)

        @pl.when(me_s < S - 1)
        def _():
            arrive(row_r.at[:, pl.ds(0, 2 * D)], fw_ss)

    dacc[...] = jnp.zeros_like(dacc)

    def backward_step(step, carry):
        t = S - 1 - step

        @pl.when(me_s == t)
        def _():
            node_backward()

        @pl.when(((t == S - 1) & (me_s >= S - 2)) | (me_s == t - 2))
        def _():
            prepare(me_s)

        @pl.when(t < S - 1)
        def _():
            edge_pass(t)

        @pl.when(t + 3 < S)
        def _():
            edge_grads_sum(t + 3)

        arrive(dmb_r, dmb_rs)
        message_back(t)

        @pl.when(t > 0)
        def _():
            edge_back(t)

        @pl.when(t == 0)
        def _():
            x_s[:, pl.ds(D, EP)] = jnp.zeros((N, EP), BF16)

        gather_blocks()
        other = gather_wait().astype(BF16)
        row_s[:, pl.ds(D, D)] = other[:, :D]
        row_s[:, pl.ds(2 * D + EP, EP)] = other[:, D:]
        dpq = row_s.at[:, pl.ds(0, 2 * D)]

        @pl.when(t > 0)
        def _():
            push(row_s, row_r.at[pl.ds(my_row, Q)], row_ss, row_rs.at[slot], t - 1, owner_d)

        @pl.when(t == 0)
        def _():
            push(dpq, dpqo_r.at[pl.ds(my_row, Q)], row_ss, dpqo_rs, t, owner_d)

        edge_grads(t)

        @pl.when(t > 0)
        def _():
            drain(row_s, row_ss, t - 1, owner_d)

        @pl.when(t == 0)
        def _():
            drain(dpq, row_ss, t, owner_d)

        @pl.when(me_s == t)
        def _():
            node_backward_drain()

        return carry

    lax.fori_loop(0, S, backward_step, 0)

    arrive(dpqo_r, dpqo_rs)
    share(2, dpqo_r, g_dpq)
    dpq = dpqo_r[...]
    sg[pl.ds(2, 1), :] = col_sum(dpq[:, :D].astype(F32))
    dn = mm_bt(dpq, pw[...])
    unit = hi_s[...]
    sg[pl.ds(0, 1), :] = col_sum(dn * unit)
    sg[pl.ds(1, 1), :] = col_sum(dn)
    share(3, sg, g_small)
    ig[...] = (dh1_f[...] + norm_back(dn, unit, sci[...], gains[0])).astype(BF16)
    for t in range(min(2, S - 1), -1, -1):
        edge_grads_sum(t)
    for sec in range(S):
        arrive(eg_o.at[sec], e2_rs.at[sec])
    for half in range(2):
        total = eg_o[half].astype(F32)
        for sec in range(half + 2, S, 2):
            total = total + eg_o[sec].astype(F32)
        eg_f[half] = total.astype(BF16)
    share(4, eg_f, g_edge)
    for t in range(S):
        drain(eg_b.at[t], e2_ss.at[t], t, me_d)
    share_wait(0, fwd, g_fwd)
    share_wait(1, bwd, g_bwd)
    share_wait(2, dpqo_r, g_dpq)
    share_wait(3, sg, g_small)
    share_wait(4, eg_f, g_edge)


def run_relay(dims, operands):
    S, B, N, K, Q, D, DE, EP, FF, C = dims
    R = K * Q
    BN = B * N
    tall = DE + N + Q
    vm = pl.BlockSpec(memory_space=pltpu.VMEM)
    hbm = pl.BlockSpec(memory_space=pl.ANY)
    dma = pltpu.SemaphoreType.DMA
    sds = jax.ShapeDtypeStruct
    BW = (D + 2 * EP) // (2 * C)
    tile = 32
    held = -(-(DE + 16) // tile) * tile
    scratch = [
        pltpu.VMEM((BN, D), F32),
        pltpu.VMEM((8, D), F32),
        pltpu.VMEM((1, EP), F32),
        pltpu.VMEM((S, held, D + 2 * EP), BF16),
        pltpu.VMEM((BN, 4 * D), BF16),
        pltpu.VMEM((BN, 2 * D + 2 * EP), BF16),
        pltpu.VMEM((24, D), F32),
        pltpu.VMEM((S, DE + 16, D + 2 * EP), BF16),
        pltpu.VMEM((S, 2 * C, DE + 16, BW), BF16),
        pltpu.VMEM((S, DE + 16, BW), BF16),
        pltpu.VMEM((S, DE + 16, BW), BF16),
        pltpu.VMEM((2, DE + 16, BW), BF16),
        pltpu.VMEM((S, EP, EP), BF16),
        pltpu.VMEM((S, 16, EP), BF16),
        pltpu.VMEM((S, R, EP), BF16),
        pltpu.VMEM((S, tall, D), BF16),
        pltpu.VMEM((S, tall, EP), BF16),
        pltpu.VMEM((D, 2 * D), BF16),
        pltpu.VMEM((8, D), F32),
        pltpu.VMEM((BN, D), BF16),
        pltpu.VMEM((BN, D), BF16),
        pltpu.VMEM((Q, D), BF16),
        pltpu.VMEM((BN, D), BF16),
        pltpu.VMEM((BN, 2 * D), BF16),
        pltpu.VMEM((Q, 2 * D), BF16),
        pltpu.VMEM((BN, 2 * EP), BF16),
        pltpu.VMEM((Q, 2 * EP), BF16),
        pltpu.VMEM((BN, D), F32),
        pltpu.VMEM((BN, D), F32),
        pltpu.VMEM((BN, D), F32),
        pltpu.VMEM((BN, D), F32),
        pltpu.VMEM((BN, 1), F32),
        pltpu.VMEM((BN, 1), F32),
        pltpu.VMEM((BN, 1), F32),
        pltpu.VMEM((BN, 1), F32),
        pltpu.VMEM((BN, FF), F32),
        pltpu.VMEM((BN, FF), BF16),
        pltpu.VMEM((2, R, EP), BF16),
        pltpu.VMEM((R, EP), F32),
        pltpu.VMEM((S, R, D), BF16),
        pltpu.VMEM((S, R, EP), BF16),
        pltpu.VMEM((2, R, D + EP), BF16),
        pltpu.VMEM((S, EP, R), BF16),
        pltpu.VMEM((S, EP, R), BF16),
        pltpu.VMEM((N, D + EP), BF16),
        pltpu.VMEM((4, Q, D + EP), BF16),
        pltpu.VMEM((Q, 2 * D + 2 * EP), BF16),
        pltpu.VMEM((BN, 2 * D + 2 * EP), BF16),
        pltpu.VMEM((BN, 2 * D), BF16),
        pltpu.VMEM((BN, D), BF16),
        pltpu.VMEM((Q, D), BF16),
        pltpu.VMEM((BN, D), BF16),
        pltpu.VMEM((BN, D), BF16),
        pltpu.VMEM((BN, D), F32),
        pltpu.VMEM((BN, D), F32),
        pltpu.VMEM((BN, D), F32),
        pltpu.VMEM((BN, D), F32),
        pltpu.VMEM((BN, D), F32),
        pltpu.VMEM((BN, D), BF16),
        dma, dma((2,)), dma((2,)), dma, dma,
        dma, dma, dma, dma, dma, dma, dma, dma,
        dma, dma((B,)), dma, dma, dma, dma((B,)), dma,
        dma, dma, dma, dma, dma,
        dma((S, 2 * C)), dma((S, 2 * C)), dma((S,)), dma((S,)), dma((5, C)), dma((5, C)),
        dma((2, S // 2)), dma((S,)), dma((S,)), dma((S,)),
    ]
    return pl.pallas_call(
        functools.partial(relay_kernel, dims),
        out_shape=(
            sds((BN, D), BF16),
            sds((BN, D), BF16),
            sds((C, BN, 4 * D), BF16),
            sds((C, BN, 2 * D + 2 * EP), BF16),
            sds((C, BN, 2 * D), BF16),
            sds((C, 24, D), F32),
            sds((C, 2, DE + 16, BW), BF16),
        ),
        in_specs=[hbm, vm, pl.BlockSpec(memory_space=pltpu.SMEM)] + [vm] * 16,
        out_specs=(vm,) * 2 + (hbm,) * 5,
        scratch_shapes=scratch,
        compiler_params=pltpu.CompilerParams(
            collective_id=0, has_side_effects=True, vmem_limit_bytes=62 * 1024 * 1024
        ),
    )(*operands)


def gradient_kernel(
    dims,
    fwd, bwd, dpq, small, edge, fi, fo, fb, act, ig,
    g_pair, g_edge, g_out, g_fi, g_fo, g_ep, g_self, g_eout, g_gain, g_shift, g_nb, g_fb, g_eb, act_out, ig_out,
    fwd_v, bwd_v, dpq_v, fi_v, fo_v, gfi_v, gfo_v, pair_v, out_v, edge_v, in_sems, sems,
):
    S, B, N, K, Q, D, DE, EP, FF, C = dims
    chunks = 4
    FC = FF // chunks

    def part(c, size=D):
        return pl.ds(c * size, size)

    loads = {}

    def load(name, src, dst):
        loads[name] = pltpu.make_async_copy(src, dst, in_sems.at[len(loads)])
        loads[name].start()

    load("a2", fwd.at[:, part(2)], fwd_v.at[2])
    load("dy", bwd.at[:, part(1)], bwd_v.at[1])
    for c in range(chunks):
        load(("fi", c), fi.at[:, part(c, FC)], fi_v.at[c])
        load(("fo", c), fo.at[part(c, FC)], fo_v.at[c])
    load("a1", fwd.at[:, part(0)], fwd_v.at[0])
    load("dpq0", dpq.at[:, part(0)], dpq_v.at[0])
    load("dpq1", dpq.at[:, part(1)], dpq_v.at[1])
    load("mbar", fwd.at[:, part(1)], fwd_v.at[1])
    load("dmsg", bwd.at[:, part(0)], bwd_v.at[0])
    load("a3", fwd.at[:, part(3)], fwd_v.at[3])
    load("drs", bwd.at[:, part(2)], bwd_v.at[2])
    load("edge", edge, edge_v)
    stores = []

    def out(src, dst):
        copy = pltpu.make_async_copy(src, dst, sems.at[len(stores)])
        copy.start()
        stores.append(copy)

    out(act, act_out)
    out(ig, ig_out)
    loads["a2"].wait()
    loads["dy"].wait()
    a2 = fwd_v[2]
    dy = bwd_v[1]
    for c in range(chunks):
        cols = part(c, FC)
        loads["fi", c].wait()
        loads["fo", c].wait()
        value, slope = gelu_both(mm(a2, fi_v[c]) + fb[:, cols])
        du = (slope * mm_bt(dy, fo_v[c])).astype(BF16)
        g_fb[:, cols] = col_sum(du.astype(F32))
        gfi_v[c] = mm_at(a2, du)
        out(gfi_v.at[c], g_fi.at[0, :, cols])
        gfo_v[c] = mm_at(value.astype(BF16), dy)
        out(gfo_v.at[c], g_fo.at[0, cols])
    loads["a1"].wait()
    for c in range(2):
        loads["dpq%d" % c].wait()
        pair_v[c] = mm_at(fwd_v[0], dpq_v[c])
        out(pair_v.at[c], g_pair.at[0, :, part(c)])
    loads["mbar"].wait()
    loads["dmsg"].wait()
    out_v[...] = mm_at(fwd_v[1], bwd_v[0]) * float(K)
    out(out_v, g_out.at[0])
    loads["a3"].wait()
    loads["drs"].wait()
    ends = mm_at(fwd_v[3], bwd_v[2])
    g_ep[0] = jnp.concatenate([ends[:, :DE], ends[:, EP : EP + DE]], axis=1)
    total = small[0]
    for c in range(1, C):
        total = total + small[c]
    for i, rows in enumerate(((0, 1, 2), (8, 9, 10), (11, 12, 13))):
        g_gain[i] = total[rows[0] : rows[0] + 1]
        g_shift[i] = total[rows[1] : rows[1] + 1]
        g_nb[i] = total[rows[2] : rows[2] + 1]
    g_eb[0, pl.ds(0, 1), :] = total[16:17, :DE]
    loads["edge"].wait()
    BW = (D + 2 * EP) // (2 * C)
    for k in range(2 * C):
        block = edge_v[k % C, k // C].astype(F32)
        first = k * BW
        for array, begin, width in ((g_edge, 0, D), (g_self, D, DE), (g_eout, D + EP, DE)):
            low, high = max(first, begin), min(first + BW, begin + width)
            if low < high:
                array[0, :, pl.ds(low - begin, high - low)] = block[:DE, low - first : high - first]
        low, high = first, min(first + BW, DE)
        if low < high:
            g_eb[0, pl.ds(1, 1), pl.ds(low, high - low)] = block[DE : DE + 1, low - first : high - first]
    for copy in stores:
        copy.wait()


def run_gradients(dims, operands):
    S, B, N, K, Q, D, DE, EP, FF, C = dims
    rows = C * B * N
    BW = (D + 2 * EP) // (2 * C)
    vm = pl.BlockSpec(memory_space=pltpu.VMEM)
    hbm = pl.BlockSpec(memory_space=pl.ANY)
    sds = jax.ShapeDtypeStruct
    shapes = (
        (1, D, 2 * D), (1, DE, D), (1, D, D), (1, D, FF), (1, FF, D), (1, D, 2 * DE), (1, DE, DE), (1, DE, DE),
        (3, 1, D), (3, 1, D), (3, 1, D), (1, FF), (1, 2, DE),
    )
    return pl.pallas_call(
        functools.partial(gradient_kernel, dims),
        out_shape=tuple(sds(shape, F32) for shape in shapes) + (sds((1, B, N, D), BF16),) * 2,
        in_specs=[hbm, hbm, hbm, vm, hbm, hbm, hbm, vm, hbm, hbm],
        out_specs=(hbm, vm, hbm, hbm, hbm) + (vm,) * 8 + (hbm,) * 2,
        scratch_shapes=[
            pltpu.VMEM((4, rows, D), BF16),
            pltpu.VMEM((3, rows, D), BF16),
            pltpu.VMEM((2, rows, D), BF16),
            pltpu.VMEM((4, D, FF // 4), BF16),
            pltpu.VMEM((4, FF // 4, D), BF16),
            pltpu.VMEM((4, D, FF // 4), F32),
            pltpu.VMEM((4, FF // 4, D), F32),
            pltpu.VMEM((2, D, D), F32),
            pltpu.VMEM((D, D), F32),
            pltpu.VMEM((C, 2, DE + 16, BW), BF16),
            pltpu.SemaphoreType.DMA((18,)),
            pltpu.SemaphoreType.DMA((13,)),
        ],
        compiler_params=pltpu.CompilerParams(vmem_limit_bytes=56 * 1024 * 1024),
    )(*operands)


def stationary(
    clean_nodes, noise_nodes, edge_feats, neighbours, time_bins, cotangent,
    pair_weight, message_edge, message_out, ffn_in, ffn_out, edge_pair, edge_self, edge_out,
    norm_gain, norm_shift, node_bias, ffn_bias, edge_bias,
):
    S = lax.axis_size("section")
    place = lax.axis_index("section")
    column = lax.axis_index("dp")
    B, N, D = clean_nodes.shape
    K, DE = edge_feats.shape[2:]
    FF = ffn_in.shape[2]
    Q = N // 4
    EP = DE + N
    core = column % 2
    w = place // 2
    slab = (place % 2) * 2 * Q

    node_ids = jnp.arange(N, dtype=jnp.int32)
    both = [
        lax.dynamic_slice(array, (w % B, slab) + (0,) * (array.ndim - 2), (1, 2 * Q) + array.shape[2:])[0]
        for array in (edge_feats, neighbours)
    ]
    chosen = (both[1][:, :, None] == node_ids).astype(BF16)
    both = jnp.concatenate([both[0], chosen], axis=2)
    mine = lax.dynamic_slice_in_dim(both, core * Q, Q, 0)
    theirs = lax.dynamic_slice_in_dim(both, (1 - core) * Q, Q, 0)
    got = lax.ppermute(theirs, "dp", [(i, i ^ 1) for i in range(lax.axis_size("dp"))])
    ecat0 = jnp.swapaxes(jnp.where(w // B == core, mine, got), 0, 1).reshape(K * Q, EP)
    oht = jnp.transpose(ecat0[:, DE:])
    phase = (time_bins.astype(F32) + 0.5) * (math.pi * 0.5 / TBINS)
    mix = jnp.cos(phase[None] - jnp.array([[0.0], [math.pi * 0.5]], F32))

    def by_rows(array):
        return jnp.transpose(array, (1, 0, 2))

    def widen(array, size, axis=-1):
        extra = [(0, 0)] * array.ndim
        extra[axis] = (0, size - array.shape[axis])
        return jnp.pad(array, extra)

    ep = jnp.concatenate([widen(edge_pair[0, :, :DE], EP), widen(edge_pair[0, :, DE:], EP)], axis=1)
    C = lax.axis_size("dp")
    dims = (S, B, N, K, Q, D, DE, EP, FF, C)
    act, ig, g_fwd, g_bwd, g_dpq, g_small, g_edge = run_relay(
        dims,
        (
            ecat0, oht, mix, clean_nodes.reshape(B * N, D), noise_nodes.reshape(B * N, D),
            cotangent.reshape(B * N, D), pair_weight[0], message_out[0], ffn_in[0], ffn_out[0], ep,
            by_rows(norm_gain), by_rows(norm_shift), by_rows(node_bias), ffn_bias, edge_bias[0],
            message_edge[0], edge_self[0], edge_out[0],
        ),
    )
    grads = run_gradients(
        dims,
        (
            g_fwd.reshape(C * B * N, -1), g_bwd.reshape(C * B * N, -1), g_dpq.reshape(C * B * N, -1),
            g_small, g_edge, ffn_in[0], ffn_out[0], ffn_bias, act.reshape(1, B, N, D), ig.reshape(1, B, N, D),
        ),
    )
    grads, outs = list(grads[:-2]), tuple(grads[-2:])
    grads[8:11] = [by_rows(array) for array in grads[8:11]]
    return outs + tuple(grads)


def solution(mesh):
    sections, copies = mesh.shape["section"], mesh.shape["dp"]

    def body(*args):
        B, N = args[0].shape[:2]
        fits = sections == 4 * B and copies % 2 == 0 and N % 64 == 0
        return stationary(*args) if fits else on_device(*args)

    placed = (
        P("dp", None, None),
        P("dp", None, None),
        P("dp", None, None, None),
        P("dp", None, None),
        P("dp"),
        P("dp", None, None),
        P("section", None, None),
        P("section", None, None),
        P("section", None, None),
        P("section", None, None),
        P("section", None, None),
        P("section", None, None),
        P("section", None, None),
        P("section", None, None),
        P("section", None, None),
        P("section", None, None),
        P("section", None, None),
        P("section", None),
        P("section", None, None),
    )
    return jax.shard_map(
        body,
        mesh=mesh,
        in_specs=placed,
        out_specs=(
            P("section", "dp", None, None),
            P("section", "dp", None, None),
            P("section", None, None),
            P("section", None, None),
            P("section", None, None),
            P("section", None, None),
            P("section", None, None),
            P("section", None, None),
            P("section", None, None),
            P("section", None, None),
            P("section", None, None),
            P("section", None, None),
            P("section", None, None),
            P("section", None),
            P("section", None, None),
        ),
        check_vma=False,
    )
```

```python
import functools
import math

import jax
import jax.numpy as jnp
from jax import lax
from jax.experimental import pallas as pl
from jax.experimental.pallas import tpu as pltpu
from jax.sharding import PartitionSpec as P

TBINS = 100


def from_behind(block, axis, distance):
    devices = range(lax.axis_size(axis))
    route = [(i - distance, i) for i in devices if i - distance in devices]
    return lax.ppermute(block, axis, route)


def for_sending(value):
    return jax.tree.map(lambda a: a.astype(jnp.bfloat16) if a.dtype == jnp.float32 else a, value)


def layer_norm(value, gain, shift):
    centre = jnp.mean(value, axis=-1, keepdims=True)
    centred = value - centre
    spread = jnp.mean(centred * centred, axis=-1, keepdims=True)
    return centred * lax.rsqrt(spread + 1e-05) * gain + shift


def forward_layer(weights, hidden, edge_state, nearest):
    (
        pair_w,
        msg_edge,
        msg_out,
        ffn_w_in,
        ffn_w_out,
        edge_pair_w,
        edge_self_w,
        edge_out_w,
        gains,
        shifts,
        node_b,
        ffn_b,
        edge_b,
    ) = weights
    width = msg_out.shape[0]
    edge_width = edge_self_w.shape[0]
    normed_one = layer_norm(hidden, gains[0], shifts[0]).astype(jnp.bfloat16)
    pair_out = jnp.dot(normed_one, pair_w, preferred_element_type=jnp.float32)
    before_act = (
        pair_out[:, None, :width]
        + jnp.take(pair_out[:, width:], nearest, axis=0)
        + jnp.einsum("nkc,cd->nkd", edge_state, msg_edge, preferred_element_type=jnp.float32)
        + node_b[0]
    )
    message_act = jax.nn.gelu(before_act).astype(jnp.bfloat16)
    message_all = jnp.einsum(
        "nkc,cd->nkd", message_act, msg_out, preferred_element_type=jnp.float32
    )
    after_msg = hidden + jnp.mean(message_all, axis=1) + node_b[1]
    normed_two = layer_norm(after_msg, gains[1], shifts[1]).astype(jnp.bfloat16)
    ffn_pre = jnp.dot(normed_two, ffn_w_in, preferred_element_type=jnp.float32) + ffn_b
    ffn_act = jax.nn.gelu(ffn_pre).astype(jnp.bfloat16)
    after_ffn = (
        after_msg + jnp.dot(ffn_act, ffn_w_out, preferred_element_type=jnp.float32) + node_b[2]
    )
    normed_three = layer_norm(after_ffn, gains[2], shifts[2]).astype(jnp.bfloat16)
    edge_pairs = jnp.dot(normed_three, edge_pair_w, preferred_element_type=jnp.float32)
    edge_pre = (
        edge_pairs[:, None, :edge_width]
        + jnp.take(edge_pairs[:, edge_width:], nearest, axis=0)
        + jnp.einsum("nkc,cd->nkd", edge_state, edge_self_w, preferred_element_type=jnp.float32)
        + edge_b[0]
    )
    edge_act = jax.nn.gelu(edge_pre).astype(jnp.bfloat16)
    edge_next = (
        edge_state.astype(jnp.float32)
        + jnp.einsum("nkc,cd->nkd", edge_act, edge_out_w, preferred_element_type=jnp.float32)
        + edge_b[1]
    )
    saved = (
        normed_one,
        before_act,
        message_act,
        after_msg,
        normed_two,
        ffn_pre,
        ffn_act,
        after_ffn,
        normed_three,
        edge_pre,
        edge_act,
    )
    return (after_ffn, edge_next, saved)


def backward_layer(weights, hidden, edge_state, nearest, grad_nodes_out, grad_edges_out):
    (
        pair_w,
        msg_edge,
        msg_out,
        ffn_w_in,
        ffn_w_out,
        edge_pair_w,
        edge_self_w,
        edge_out_w,
        gains,
        shifts,
        node_b,
        ffn_b,
        edge_b,
    ) = weights
    unused_nodes, unused_edges, saved = forward_layer(weights, hidden, edge_state, nearest)
    (
        normed_one,
        before_act,
        message_act,
        after_msg,
        normed_two,
        ffn_pre,
        ffn_act,
        after_ffn,
        normed_three,
        edge_pre,
        edge_act,
    ) = saved
    width = msg_out.shape[0]
    edge_width = edge_self_w.shape[0]
    count = nearest.shape[1]
    node_count = hidden.shape[0]
    one_hot = (
        nearest.reshape(-1)[None, :] == jnp.arange(node_count, dtype=jnp.int32)[:, None]
    ).astype(jnp.bfloat16)
    edge_grad_low = grad_edges_out.astype(jnp.bfloat16)
    grad_edge_b1 = jnp.sum(grad_edges_out, axis=(0, 1))
    grad_edge_out_w = jnp.einsum(
        "nkc,nkd->cd", edge_act, edge_grad_low, preferred_element_type=jnp.float32
    )
    edge_act_grad = jnp.einsum(
        "nkd,cd->nkc", edge_grad_low, edge_out_w, preferred_element_type=jnp.float32
    )
    unused_value, gelu_edge = jax.vjp(jax.nn.gelu, edge_pre)
    edge_pre_grad = gelu_edge(edge_act_grad)[0].astype(jnp.bfloat16)
    grad_edge_b0 = jnp.sum(edge_pre_grad, axis=(0, 1), dtype=jnp.float32)
    grad_edge_self_w = jnp.einsum(
        "nkc,nkd->cd", edge_state, edge_pre_grad, preferred_element_type=jnp.float32
    )
    edge_total = grad_edges_out + jnp.einsum(
        "nkd,cd->nkc", edge_pre_grad, edge_self_w, preferred_element_type=jnp.float32
    )
    own_edge = jnp.sum(edge_pre_grad, axis=1, dtype=jnp.float32)
    other_edge = jnp.dot(
        one_hot, edge_pre_grad.reshape(-1, edge_width), preferred_element_type=jnp.float32
    )
    pairs_grad = jnp.concatenate([own_edge, other_edge], axis=-1).astype(jnp.bfloat16)
    grad_edge_pair_w = jnp.einsum(
        "nc,nd->cd", normed_three, pairs_grad, preferred_element_type=jnp.float32
    )
    normed_three_grad = jnp.einsum(
        "nd,cd->nc", pairs_grad, edge_pair_w, preferred_element_type=jnp.float32
    )
    unused_value, norm_three_back = jax.vjp(layer_norm, after_ffn, gains[2], shifts[2])
    ffn_side, gain_three, shift_three = norm_three_back(normed_three_grad)
    after_ffn_grad = grad_nodes_out + ffn_side
    grad_node_b2 = jnp.sum(after_ffn_grad, axis=0)
    ffn_out_grad = after_ffn_grad.astype(jnp.bfloat16)
    grad_ffn_w_out = jnp.einsum(
        "nc,nd->cd", ffn_act, ffn_out_grad, preferred_element_type=jnp.float32
    )
    ffn_act_grad = jnp.einsum(
        "nd,cd->nc", ffn_out_grad, ffn_w_out, preferred_element_type=jnp.float32
    )
    unused_value, gelu_ffn = jax.vjp(jax.nn.gelu, ffn_pre)
    ffn_pre_grad = gelu_ffn(ffn_act_grad)[0].astype(jnp.bfloat16)
    grad_ffn_b = jnp.sum(ffn_pre_grad, axis=0, dtype=jnp.float32)
    grad_ffn_w_in = jnp.einsum(
        "nc,nd->cd", normed_two, ffn_pre_grad, preferred_element_type=jnp.float32
    )
    normed_two_grad = jnp.einsum(
        "nd,cd->nc", ffn_pre_grad, ffn_w_in, preferred_element_type=jnp.float32
    )
    unused_value, norm_two_back = jax.vjp(layer_norm, after_msg, gains[1], shifts[1])
    msg_side, gain_two, shift_two = norm_two_back(normed_two_grad)
    after_msg_grad = after_ffn_grad + msg_side
    grad_node_b1 = jnp.sum(after_msg_grad, axis=0)
    message_grad = (after_msg_grad / count).astype(jnp.bfloat16)
    grad_msg_out = jnp.einsum(
        "nkc,nd->cd", message_act, message_grad, preferred_element_type=jnp.float32
    )
    message_act_grad = jnp.einsum(
        "nd,cd->nc", message_grad, msg_out, preferred_element_type=jnp.float32
    )
    unused_value, gelu_msg = jax.vjp(jax.nn.gelu, before_act)
    before_grad = gelu_msg(jnp.broadcast_to(message_act_grad[:, None, :], before_act.shape))[
        0
    ].astype(jnp.bfloat16)
    grad_node_b0 = jnp.sum(before_grad, axis=(0, 1), dtype=jnp.float32)
    grad_msg_edge = jnp.einsum(
        "nkc,nkd->cd", edge_state, before_grad, preferred_element_type=jnp.float32
    )
    edge_total = edge_total + jnp.einsum(
        "nkd,cd->nkc", before_grad, msg_edge, preferred_element_type=jnp.float32
    )
    own_node = jnp.sum(before_grad, axis=1, dtype=jnp.float32)
    other_node = jnp.dot(
        one_hot, before_grad.reshape(-1, width), preferred_element_type=jnp.float32
    )
    pair_grad = jnp.concatenate([own_node, other_node], axis=-1).astype(jnp.bfloat16)
    grad_pair_w = jnp.einsum("nc,nd->cd", normed_one, pair_grad, preferred_element_type=jnp.float32)
    normed_one_grad = jnp.einsum("nd,cd->nc", pair_grad, pair_w, preferred_element_type=jnp.float32)
    unused_value, norm_one_back = jax.vjp(layer_norm, hidden, gains[0], shifts[0])
    input_side, gain_one, shift_one = norm_one_back(normed_one_grad)
    hidden_grad = after_msg_grad + input_side
    grads = (
        grad_pair_w,
        grad_msg_edge,
        grad_msg_out,
        grad_ffn_w_in,
        grad_ffn_w_out,
        grad_edge_pair_w,
        grad_edge_self_w,
        grad_edge_out_w,
        jnp.stack([gain_one, gain_two, gain_three]),
        jnp.stack([shift_one, shift_two, shift_three]),
        jnp.stack([grad_node_b0, grad_node_b1, grad_node_b2]),
        grad_ffn_b,
        jnp.stack([grad_edge_b0, grad_edge_b1]),
    )
    return (hidden_grad.astype(jnp.bfloat16), edge_total.astype(jnp.bfloat16), grads)


def on_device(
    clean_nodes,
    noise_nodes,
    edge_feats,
    neighbours,
    time_bins,
    cotangent,
    pair_weight,
    message_edge,
    message_out,
    ffn_in,
    ffn_out,
    edge_pair,
    edge_self,
    edge_out,
    norm_gain,
    norm_shift,
    node_bias,
    ffn_bias,
    edge_bias,
):
    sections = lax.axis_size("section")
    place = lax.axis_index("section")
    weights = tuple(
        (
            item[0]
            for item in (
                pair_weight,
                message_edge,
                message_out,
                ffn_in,
                ffn_out,
                edge_pair,
                edge_self,
                edge_out,
                norm_gain,
                norm_shift,
                node_bias,
                ffn_bias,
                edge_bias,
            )
        )
    )
    batches, node_count, width = clean_nodes.shape
    phase = (time_bins.astype(jnp.float32) + 0.5) * (math.pi * 0.5 / TBINS)
    start = jnp.cos(phase)[:, None, None] * clean_nodes.astype(jnp.float32) + jnp.sin(phase)[
        :, None, None
    ] * noise_nodes.astype(jnp.float32)
    zero_nodes = jnp.zeros((node_count, width), jnp.bfloat16)
    zero_edges = jnp.zeros(edge_feats.shape[1:], jnp.bfloat16)
    is_first = place == 0
    is_last = place == sections - 1

    def forward_step(step_index, carry):
        recv_nodes, recv_edges, back_nodes, kept_nodes, kept_edges, section_outs = carry
        item = step_index - place
        first_pass = (item >= 0) & (item < batches)
        second_pass = (item >= sections) & (item < sections + batches)
        index = jnp.clip(jnp.where(second_pass, item - sections, item), 0, batches - 1)
        predicted = back_nodes
        own_start = lax.dynamic_index_in_dim(start, index, 0, keepdims=False)
        lead_nodes = own_start + jnp.where(second_pass, predicted.astype(jnp.float32), 0.0)
        nodes_in = jnp.where(is_first, lead_nodes, recv_nodes.astype(jnp.float32))
        edges_in = jnp.where(
            is_first, lax.dynamic_index_in_dim(edge_feats, index, 0, keepdims=False), recv_edges
        )
        nearest = lax.dynamic_index_in_dim(neighbours, index, 0, keepdims=False)

        def run_layer(operand):
            after, edge_next, saved = forward_layer(weights, operand[0], operand[1], operand[2])
            return (after.astype(jnp.bfloat16), edge_next.astype(jnp.bfloat16))

        def skip_layer(operand):
            return (zero_nodes, zero_edges)

        out_nodes, out_edges = lax.cond(
            first_pass | second_pass, run_layer, skip_layer, (nodes_in, edges_in, nearest)
        )
        kept_nodes = lax.dynamic_update_index_in_dim(
            kept_nodes, jnp.where(second_pass, nodes_in, kept_nodes[index]), index, 0
        )
        kept_edges = lax.dynamic_update_index_in_dim(
            kept_edges, jnp.where(second_pass, edges_in, kept_edges[index]), index, 0
        )
        section_outs = lax.dynamic_update_index_in_dim(
            section_outs, jnp.where(second_pass, out_nodes, section_outs[index]), index, 0
        )
        recv_nodes, recv_edges = from_behind((out_nodes, out_edges), "section", 1)
        back_nodes = from_behind(out_nodes, "section", 1 - sections)
        return (recv_nodes, recv_edges, back_nodes, kept_nodes, kept_edges, section_outs)

    forward_init = (
        zero_nodes,
        zero_edges,
        zero_nodes,
        jnp.zeros((batches, node_count, width), jnp.float32),
        jnp.zeros_like(edge_feats),
        jnp.zeros((batches, node_count, width), jnp.bfloat16),
    )
    unused_nodes, unused_edges, unused_back, kept_nodes, kept_edges, section_outs = lax.fori_loop(
        0, 2 * sections + batches - 1, forward_step, forward_init
    )
    grads_zero = tuple((jnp.zeros(item.shape, jnp.float32) for item in weights))

    def backward_step(step_index, carry):
        recv_grad_nodes, recv_grad_edges, grads, input_grads = carry
        item = step_index - (sections - 1 - place)
        live = (item >= 0) & (item < batches)
        index = jnp.clip(item, 0, batches - 1)
        nodes_grad_out = jnp.where(
            is_last,
            lax.dynamic_index_in_dim(cotangent, index, 0, keepdims=False).astype(jnp.float32),
            recv_grad_nodes.astype(jnp.float32),
        )
        edges_grad_out = jnp.where(is_last, 0.0, recv_grad_edges.astype(jnp.float32))
        nearest = lax.dynamic_index_in_dim(neighbours, index, 0, keepdims=False)

        def run_back(operand):
            return backward_layer(
                weights, operand[0], operand[1], operand[2], operand[3], operand[4]
            )

        def skip_back(operand):
            return (zero_nodes, zero_edges, grads_zero)

        nodes_grad, edges_grad, terms = lax.cond(
            live,
            run_back,
            skip_back,
            (kept_nodes[index], kept_edges[index], nearest, nodes_grad_out, edges_grad_out),
        )
        grads = tuple((total + term for total, term in zip(grads, terms)))
        input_grads = lax.dynamic_update_index_in_dim(
            input_grads, jnp.where(live, nodes_grad, input_grads[index]), index, 0
        )
        recv_grad_nodes, recv_grad_edges = from_behind((nodes_grad, edges_grad), "section", -1)
        return (recv_grad_nodes, recv_grad_edges, grads, input_grads)

    backward_init = (
        zero_nodes,
        zero_edges,
        grads_zero,
        jnp.zeros((batches, node_count, width), jnp.bfloat16),
    )
    unused_grad_nodes, unused_grad_edges, grads, input_grads = lax.fori_loop(
        0, sections + batches - 1, backward_step, backward_init
    )
    totals = jax.tree.map(lambda part: part.astype(jnp.float32), lax.psum(for_sending(grads), "dp"))
    return (
        section_outs[None],
        input_grads[None],
        totals[0][None],
        totals[1][None],
        totals[2][None],
        totals[3][None],
        totals[4][None],
        totals[5][None],
        totals[6][None],
        totals[7][None],
        totals[8][None],
        totals[9][None],
        totals[10][None],
        totals[11][None],
        totals[12][None],
    )


BF16 = jnp.bfloat16
F32 = jnp.float32
MESH = pl.DeviceIdType.MESH
GELU_A = 0.7978845608028654
GELU_B = 0.044715


def gelu(x):
    return 0.5 * x * (1.0 + jnp.tanh(x * (GELU_A + (GELU_A * GELU_B) * (x * x))))


def gelu_both(x):
    square = x * x
    t = jnp.tanh(x * (GELU_A + (GELU_A * GELU_B) * square))
    half = 0.5 * (1.0 + t)
    slope = half + (0.5 * x) * (1.0 - t * t) * (GELU_A + (3.0 * GELU_A * GELU_B) * square)
    return x * half, slope


def mm(a, b):
    return jnp.dot(a, b, preferred_element_type=F32)


def mm_bt(a, b):
    return lax.dot_general(a, b, (((1,), (1,)), ((), ())), preferred_element_type=F32)


def mm_at(a, b):
    return lax.dot_general(a, b, (((0,), (0,)), ((), ())), preferred_element_type=F32)


def stacked(blocks):
    return jnp.concatenate(blocks, axis=0)


def row_mean(x):
    return jnp.mean(x, axis=-1, keepdims=True)


def normed(x):
    centred = x - row_mean(x)
    scale = lax.rsqrt(row_mean(centred * centred) + 1e-05)
    return centred * scale, scale


def norm_back(grad, unit, scale, gain):
    t = grad * gain
    return scale * (t - row_mean(t) - unit * row_mean(t * unit))


def col_sum(x):
    return jnp.sum(x, axis=0, keepdims=True)


def relay_kernel(
    dims,
    ecat0, oht, mix, clean, noise, cot, pw, mo, fi, fo, ep, gains, shifts, node_b, fb, edge_b, we_own, ws_own, wo_own,
    act, ig, g_fwd, g_bwd, g_dpq, g_small, g_msg, g_upd,
    start, par, eb0, wall_msg, wall_upd, fwd, bwd, sg,
    msg_g, msg_r, msg_b, msg_o, msg_f, upd_g, upd_r, upd_b, upd_o, upd_f, wo, eb1,
    ecat, wcat, scat, pwn, parn, hin_r, hst, mb_s, mb_r, pq_s, pq_r, rq_s, rq_r,
    un0, un1, un2, hi_s, sc0, sc1, sc2, sci, u_s, slope_s, de, dacc, gp, gpe, dcat, act_t, edge_t,
    x_s, x_r, row_s, row_r, dpqo_r, dmb_s, dmb_r, dh1_s, dh1_r, dh1_f, dh2_s, dn3_s, da2_s, h1_s, a1_s,
    ld_sem, nx_ss, nx_rs, hop_ss, hop_rs,
    pq_ss, pq_rs, ag_ss, ag_rs, rq_ss, rq_rs, ag2_ss, ag2_rs,
    mb_ss, mb_rs, x_ss, x_rs, row_ss, row_rs, dpqo_rs, fw_ss, dmb_ss, dmb_rs, dh_ss, dh_rs,
    e1_ss, e1_rs, e2_ss, e2_rs, g_ss, g_rs, relay_ss, ring_ss, ring_rs, sib_ss, sib_rs,
):
    S, B, N, K, Q, D, DE, EP, FF, C = dims
    BN = B * N
    RB = 16
    top = DE + N
    me_s = lax.axis_index("section")
    me_d = lax.axis_index("dp")
    core = lax.rem(me_d, 2)
    pair = me_d - core
    w = lax.div(me_s, 2)
    q = 2 * lax.rem(me_s, 2) + core
    owner_d = pair + lax.div(w, B)
    slot = lax.rem(w, B)
    my_row = pl.multiple_of(slot * N + q * Q, Q)
    own_rows = pl.ds(top, Q)

    def quarter(j):
        return pl.ds(pl.multiple_of(DE + j * Q, Q), Q)

    def is_me(sec, dpi):
        return (sec == me_s) & (dpi == me_d)

    def far(src, dst, ssem, rsem, sec, dpi):
        return pltpu.make_async_remote_copy(
            src_ref=src, dst_ref=dst, send_sem=ssem, recv_sem=rsem,
            device_id={"section": sec, "dp": dpi}, device_id_type=MESH,
        )

    def push(src, dst, ssem, rsem, sec, dpi):
        lax.cond(
            is_me(sec, dpi),
            lambda: pltpu.make_async_copy(src, dst, rsem).start(),
            lambda: far(src, dst, ssem, rsem, sec, dpi).start(),
        )

    def arrive(ref, sem):
        pltpu.make_async_copy(ref, ref, sem).wait()

    def drain(ref, sem, sec, dpi):
        @pl.when(jnp.logical_not(is_me(sec, dpi)))
        def _():
            arrive(ref, sem)

    def worker_of(p, j):
        return 2 * (core * B + p) + j // 2, pair + j % 2

    def peer(k):
        j = lax.rem(q + k, 4)
        return j, 2 * w + lax.div(j, 2), pair + lax.rem(j, 2)

    works_here = lax.div(w, B) == core

    def at(p, first=0, size=16):
        return pl.ds(pl.multiple_of(p * N + first, size), size)

    near = jnp.clip(w - core * B, 0, B - 1)

    load = pltpu.make_async_copy(ecat0, ecat.at[0], ld_sem)
    load.start()
    barrier = pltpu.get_barrier_semaphore()
    for sec in range(S):
        for c in range(C):
            greeted = (c == pair) | (c == pair + 1) | (w == sec // 2)

            @pl.when(greeted & jnp.logical_not(is_me(sec, c)))
            def _():
                pl.semaphore_signal(
                    barrier, inc=1, device_id={"section": sec, "dp": c}, device_id_type=MESH
                )
    wall_msg[me_s] = we_own[...]
    wall_upd[me_s] = jnp.zeros(wall_upd.shape[1:], BF16)
    wall_upd[me_s, pl.ds(0, DE), pl.ds(0, DE)] = ws_own[...]
    wall_upd[me_s, pl.ds(0, DE), pl.ds(EP, DE)] = wo_own[...]
    bias = edge_b[pl.ds(1, 1), :]
    high = bias.astype(BF16).astype(F32)
    row = lax.broadcasted_iota(jnp.int32, (16, DE), 0)
    wall_upd[me_s, pl.ds(DE, 16), pl.ds(0, DE)] = jnp.where(
        row == 0, high, jnp.where(row == 1, bias - high, 0.0)
    ).astype(BF16)
    eb0[...] = jnp.zeros_like(eb0)
    eb0[:, pl.ds(0, DE)] = edge_b[pl.ds(0, 1), :]
    par[pl.ds(0, 1), :] = gains[0]
    par[pl.ds(1, 1), :] = shifts[0]
    par[pl.ds(2, 1), :] = node_b[0]
    par[pl.ds(3, 5), :] = jnp.zeros((5, D), F32)
    pl.semaphore_wait(barrier, 2 * S - 1 + 2 * (C - 2))

    def section_at(i):
        i = lax.rem(i + S, S)
        return jnp.where(i < S // 2, 2 * i, 2 * (S - i) - 1)

    place = jnp.where(lax.rem(me_s, 2) == 0, w, S - 1 - w)
    sides = ((section_at(place + 1), S // 2), (section_at(place - 1), S // 2 - 1))
    walls = (wall_msg, wall_upd)

    def half_of(which, layer, c):
        size = walls[which].shape[1] // 2
        return walls[which].at[layer, pl.ds(pl.multiple_of(c * size, size), size)]

    def ring_send(which, layer, side, hop):
        sec, reach = sides[side]
        if hop < reach:
            half = half_of(which, layer, core)
            far(half, half, ring_ss.at[which, side, hop], ring_rs.at[which, layer], sec, me_d).start()

    def ring_hop(which, side, hop):
        layer = section_at(place - hop if side == 0 else place + hop)
        half = half_of(which, layer, core)
        arrive(half, ring_rs.at[which, layer])
        ring_send(which, layer, side, hop)
        far(half, half, sib_ss.at[which, layer], sib_rs.at[which, layer], me_s, pair + 1 - core).start()

    hops = [(hop, side) for hop in range(1, S // 2 + 1) for side in range(2) if hop <= sides[side][1]]

    def ring_later(second):
        for hop, side in hops:
            early = (place > 0) & ((place >= hop) if side == 0 else (place + hop <= S))

            @pl.when(early != second)
            def _():
                ring_hop(1, side, hop)

    for side in range(2):
        ring_send(0, me_s, side, 0)
    before = lax.rem(me_s + S - 1, S)
    far(pw, pwn, nx_ss.at[0], nx_rs.at[0], before, me_d).start()
    far(par, parn, nx_ss.at[1], nx_rs.at[1], before, me_d).start()

    for p in range(B):
        rows = pl.ds(p * N, N)
        start[rows, :] = mix[0, p] * clean[rows, :].astype(F32) + mix[1, p] * noise[rows, :].astype(F32)

    def ring_drain():
        for which in range(2):
            for side in range(2):
                for hop in range(sides[side][1]):
                    arrive(half_of(which, me_s, core), ring_ss.at[which, side, hop])
            for layer in range(S):
                @pl.when(layer != me_s)
                def _():
                    arrive(half_of(which, layer, core), sib_ss.at[which, layer])

    def unpack_messages(t):
        @pl.when(t != me_s)
        def _():
            arrive(half_of(0, t, 1 - core), sib_rs.at[0, t])

        wcat[t, pl.ds(0, DE), :] = wall_msg[t]

    def unpack_updates(t):
        @pl.when(t != me_s)
        def _():
            arrive(half_of(1, t, 1 - core), sib_rs.at[1, t])

        scat[t, pl.ds(0, DE), :] = wall_upd[t, pl.ds(0, DE), pl.ds(0, EP)]
        wo[t, pl.ds(0, DE), :] = wall_upd[t, pl.ds(0, DE), pl.ds(EP, EP)]
        wo[t, pl.ds(DE, N), :] = jnp.zeros((N, EP), BF16)
        eb1[t] = wall_upd[t, pl.ds(DE, 16), pl.ds(0, EP)]

    def rows_out(p, src, dst, ssem, rsem):
        for j in range(4):
            sec, dpi = worker_of(p, j)
            push(src.at[at(p, j * Q, Q)], dst, ssem, rsem, sec, dpi)

    def rows_drain(src, ssem):
        lax.cond(
            works_here,
            lambda: arrive(src.at[pl.ds(0, B * N - Q)], ssem),
            lambda: arrive(src, ssem),
        )

    def spread(rows, half, ref, layer, ssem, rsem, rows_sem):
        arrive(rows, rows_sem)
        for k in range(1, 4):
            _, sec, dpi = peer(k)
            far(rows.at[:, pl.ds(half, half)], ref.at[layer, quarter(q)], ssem, rsem, sec, dpi).start()
        ref[layer, own_rows, :] = rows[:, pl.ds(0, half)]
        ref[layer, quarter(q), :] = rows[:, pl.ds(half, half)]

    def spread_wait(ref, layer, sem):
        arrive(ref.at[layer, pl.ds(DE, 3 * Q)], sem)

    def share(group, src, dst):
        for c in range(C):
            push(src, dst.at[me_d], g_ss.at[group, c], g_rs.at[group, me_d], me_s, c)

    def share_wait(group, src, dst):
        for c in range(C):
            arrive(dst.at[c], g_rs.at[group, c])
            drain(src, g_ss.at[group, c], me_s, c)

    def share_near(group, src, dst):
        for c in range(C):
            @pl.when((c == pair) | (c == pair + 1) | (core == c % 2))
            def _():
                push(src, dst(me_d), g_ss.at[group, c], g_rs.at[group, me_d], me_s, c)

    def share_relay(group, src, dst):
        for c in range(C):
            @pl.when((c != me_d) & (core == c % 2))
            def _():
                arrive(dst(c), g_rs.at[group, c])
                far(dst(c), dst(c), relay_ss.at[group - 2, c // 2], g_rs.at[group, c], me_s, pair + 1 - core).start()

    def share_near_wait(group, src, dst):
        for c in range(C):
            @pl.when((c == me_d) | (core != c % 2))
            def _():
                arrive(dst(c), g_rs.at[group, c])

            @pl.when((c != me_d) & ((c == pair) | (c == pair + 1) | (core == c % 2)))
            def _():
                arrive(src, g_ss.at[group, c])

            @pl.when((c != me_d) & (core == c % 2))
            def _():
                arrive(dst(c), relay_ss.at[group - 2, c // 2])

    steps = 4
    KC = K // steps
    RC = KC * Q

    def messages(t):
        own = wcat[t, own_rows, :].astype(F32)
        total = jnp.zeros((Q, D), F32)
        for i in range(steps):
            pre = mm(ecat[t, pl.ds(i * RC, RC), :], wcat[t, pl.ds(0, top), :])
            for k in range(KC):
                total = total + gelu(pre[k * Q : (k + 1) * Q] + own)
        mb_s[...] = (total * (1.0 / K)).astype(BF16)

    def edge_update(t):
        own = scat[t, own_rows, :].astype(F32)
        bias = eb1[t, pl.ds(0, 1), :].astype(F32) + eb1[t, pl.ds(1, 1), :].astype(F32)
        for i in range(steps):
            pe = mm(ecat[t, pl.ds(i * RC, RC), :], scat[t, pl.ds(0, top), :])
            act_e = stacked([gelu(pe[k * Q : (k + 1) * Q] + own).astype(BF16) for k in range(KC)])
            z = mm(act_e, wo[t])
            for k in range(KC):
                rows = pl.ds(i * RC + k * Q, Q)
                ecat[t + 1, rows, :] = (ecat[t, rows, :].astype(F32) + z[k * Q : (k + 1) * Q] + bias).astype(BF16)

    chunks = 4
    FC = FF // chunks

    def node_forward(step):
        @pl.when(step < S)
        def _():
            arrive(pwn, nx_rs.at[0])
            arrive(parn, nx_rs.at[1])
            arrive(pw, nx_ss.at[0])
            arrive(par, nx_ss.at[1])

        @pl.when(step == 0)
        def _():
            hi_s[...] = start[...]

        @pl.when(step > 0)
        def _():
            arrive(hin_r, hop_rs)
            first = jnp.where(me_s == 0, 1.0, 0.0)
            for i in range(0, BN, RB):
                rows = pl.ds(i, RB)
                hi_s[rows, :] = hin_r[rows, :].astype(F32) + first * start[rows, :]

        later = lax.rem(me_s + 1, S)

        def turn(n, carry):
            p = lax.rem(near + n, B)
            whole = at(p, 0, N)
            arrive(mb_r.at[whole], mb_rs.at[p])
            mean = mm(mb_r[whole, :], mo[...])
            for i in range(0, N, RB):
                rows = at(p, i)
                h1 = hi_s[rows, :] + mean[i : i + RB] + node_b[1]
                h1_s[rows, :] = h1
                unit, scale = normed(h1)
                un1[rows, :] = unit
                sc1[rows, :] = scale
                fwd[rows, pl.ds(2 * D, D)] = (unit * gains[1] + shifts[1]).astype(BF16)
                fwd[rows, pl.ds(D, D)] = mb_r[rows, :]
            a2 = fwd[whole, pl.ds(2 * D, D)]
            y = jnp.zeros((N, D), F32)
            for c in range(chunks):
                cols = pl.ds(c * FC, FC)
                u = mm(a2, fi[:, cols])
                v = []
                for i in range(0, N, RB):
                    block = u[i : i + RB] + fb[:, cols]
                    u_s[at(p, i), cols] = block
                    v.append(gelu(block).astype(BF16))
                y = y + mm(stacked(v), fo[cols, :])
            last = jnp.where(me_s == S - 1, 1.0, 0.0)
            for i in range(0, N, RB):
                rows = at(p, i)
                h2 = h1_s[rows, :] + y[i : i + RB] + node_b[2]
                rounded = h2.astype(BF16)
                hst[rows, :] = rounded
                unit, scale = normed(h2)
                un2[rows, :] = unit
                sc2[rows, :] = scale
                fwd[rows, pl.ds(3 * D, D)] = (unit * gains[2] + shifts[2]).astype(BF16)
                pair_norm(rows, rounded.astype(F32) + last * start[rows, :], parn)
            rq = mm(fwd[whole, pl.ds(3 * D, D)], ep[...])
            for i in range(0, N, RB):
                rows = at(p, i)
                rq_s[rows, pl.ds(0, EP)] = (rq[i : i + RB, :EP] + eb0[...]).astype(BF16)
                rq_s[rows, pl.ds(EP, EP)] = rq[i : i + RB, EP:].astype(BF16)
            pair_rows(p, pwn, parn)

            @pl.when(me_s < S - 1)
            def _():
                rows_out(p, rq_s, rq_r, rq_ss, rq_rs)

            @pl.when(step < 2 * S - 1)
            def _():
                rows_out(p, pq_s, pq_r, pq_ss, pq_rs)

            @pl.when((n == 0) & works_here)
            def _():
                pass_on(step)

            return carry

        lax.fori_loop(0, B, turn, 0)

        @pl.when(step < 2 * S - 1)
        def _():
            far(hst, hin_r, hop_ss, hop_rs, later, me_d).start()

        @pl.when(step >= S)
        def _():
            act[...] = hst[...]
            for i in range(0, BN, RB):
                rows = pl.ds(i, RB)
                unit, scale = normed(hi_s[rows, :])
                hi_s[rows, :] = unit
                sci[rows, :] = scale
                fwd[rows, pl.ds(0, D)] = (unit * gains[0] + shifts[0]).astype(BF16)
                for c in range(chunks):
                    cols = pl.ds(c * FC, FC)
                    slope_s[rows, cols] = gelu_both(u_s[rows, cols])[1].astype(BF16)
            share(0, fwd, g_fwd)

    def pair_norm(rows, hidden, first):
        unit, scale = normed(hidden)
        un0[rows, :] = unit
        sc0[rows, :] = scale
        a1_s[rows, :] = (unit * first[pl.ds(0, 1), :] + first[pl.ds(1, 1), :]).astype(BF16)

    def pair_rows(p, weight, first):
        whole = at(p, 0, N)
        for half in range(2):
            cols = pl.ds(half * D, D)
            value = mm(a1_s[whole, :], weight[:, cols])
            if half == 0:
                value = value + first[pl.ds(2, 1), :]
            pq_s[whole, cols] = value.astype(BF16)

    def pass_on(step):
        t = lax.rem(step, S)

        @pl.when(t < S - 1)
        def _():
            spread(rq_r, EP, scat, t, ag2_ss, ag2_rs, rq_rs)

        @pl.when(step < 2 * S - 1)
        def _():
            spread(pq_r, D, wcat, lax.rem(step + 1, S), ag_ss, ag_rs, pq_rs)

    def node_forward_drain():
        arrive(hst, hop_ss)
        rows_drain(pq_s, pq_ss)

        @pl.when(me_s < S - 1)
        def _():
            rows_drain(rq_s, rq_ss)

    @pl.when(me_s == 0)
    def _():
        for i in range(0, BN, RB):
            rows = pl.ds(i, RB)
            pair_norm(rows, start[rows, :], par)
        for p in range(B):
            pair_rows(p, pw, par)
            rows_out(p, pq_s, pq_r, pq_ss, pq_rs)

    def message_slope(t):
        own = wcat[t, own_rows, :].astype(F32)
        for i in range(steps):
            pre = mm(ecat[t, pl.ds(i * RC, RC), :], wcat[t, pl.ds(0, top), :])
            for k in range(KC):
                gp[t, pl.ds(i * RC + k * Q, Q), :] = gelu_both(pre[k * Q : (k + 1) * Q] + own)[1].astype(BF16)

    def edge_slope(t):
        own = scat[t, own_rows, :].astype(F32)
        values = []
        for i in range(steps):
            pe = mm(ecat[t, pl.ds(i * RC, RC), :], scat[t, pl.ds(0, top), :])
            for k in range(KC):
                value, slope = gelu_both(pe[k * Q : (k + 1) * Q] + own)
                values.append(value.astype(BF16))
                gpe[t, pl.ds(i * RC + k * Q, Q), :] = slope.astype(BF16)
        act_t[t] = stacked(values).T

    def prepare(t):
        message_slope(t)
        edge_t[t] = ecat[t].T

        @pl.when(t > 0)
        def _():
            edge_slope(t - 1)

    def forward_step(step, carry):
        t = lax.rem(step, S)

        @pl.when(step < S)
        def _():
            unpack_messages(t)

        spread_wait(wcat, t, ag_rs)
        messages(t)
        spread_wait(wcat, t, ag_ss)
        push(mb_s, mb_r.at[pl.ds(my_row, Q)], mb_ss, mb_rs.at[slot], t, owner_d)

        for second in range(2):
            @pl.when(step == second)
            def _():
                ring_later(second == 1)

        @pl.when((step == 0) & (me_s == 0))
        def _():
            rows_drain(pq_s, pq_ss)

        @pl.when((step > 0) & (me_s == lax.rem(step + S - 1, S)))
        def _():
            node_forward_drain()

        @pl.when(me_s == t)
        def _():
            node_forward(step)

        @pl.when((me_s != t) & (step >= S))
        def _():
            prepare(t)

        @pl.when(jnp.logical_not((me_s == t) & works_here))
        def _():
            pass_on(step)

        @pl.when(t < S - 1)
        def _():
            @pl.when(step < S)
            def _():
                unpack_updates(t)

            spread_wait(scat, t, ag2_rs)
            edge_update(t)
            spread_wait(scat, t, ag2_ss)

        drain(mb_s, mb_ss, t, owner_d)
        return carry

    for hop, side in hops:
        ring_hop(0, side, hop)
    for side in range(2):
        ring_send(1, me_s, side, 0)
    load.wait()
    spread(pq_r, D, wcat, 0, ag_ss, ag_rs, pq_rs)
    lax.fori_loop(0, 2 * S, forward_step, 0)
    ring_drain()

    @pl.when(me_s != S - 1)
    def _():
        arrive(half_of(1, S - 1, 1 - core), sib_rs.at[1, S - 1])

    def edge_back(t):
        b2, n2 = lax.rem(t, 2), lax.rem(t + 1, 2)
        total = jnp.zeros((Q, EP), F32)
        for i in range(steps):
            chunk = pl.ds(i * RC, RC)
            carry = mm_bt(dcat[b2, chunk, pl.ds(0, D)], wcat[t, pl.ds(0, top), :])
            low = []
            for k in range(KC):
                rows = pl.ds(i * RC + k * Q, Q)
                low.append((dacc[rows, :] + carry[k * Q : (k + 1) * Q]).astype(BF16))
                de[n2, rows, :] = low[-1]
            dw = mm_bt(stacked(low), wo[t - 1])
            for k in range(KC):
                rows = pl.ds(i * RC + k * Q, Q)
                d = (gpe[t - 1, rows, :].astype(F32) * dw[k * Q : (k + 1) * Q]).astype(BF16)
                total = total + d.astype(F32)
                dcat[n2, rows, pl.ds(D, EP)] = d
        row_s[:, pl.ds(2 * D, EP)] = total.astype(BF16)
        x_s[:, pl.ds(D, EP)] = mm(oht[...], dcat[n2, :, pl.ds(D, EP)]).astype(BF16)

    def edge_pass(t):
        b3 = lax.rem(t, 2)
        for i in range(steps):
            rows = pl.ds(i * RC, RC)
            d = dcat[b3, rows, pl.ds(D, EP)]
            dacc[rows, :] = de[b3, rows, :].astype(F32) + mm_bt(d, scat[t, pl.ds(0, top), :])

    blocks = 2 * C
    my_block = lax.rem(me_s, 2) * C + me_d
    kinds = ((msg_g, msg_r, msg_b, msg_o, msg_f, g_msg), (upd_g, upd_r, upd_b, upd_o, upd_f, g_upd))
    BW = msg_r.shape[3]

    def block_of(kind, t, half, c):
        array, size = kinds[kind][0], kinds[kind][1].shape[2]
        return array.at[t, pl.ds(pl.multiple_of(half * size, size), size), pl.ds(pl.multiple_of(c * BW, BW), BW)]

    def blocks_out(kind, t):
        for k in range(blocks):
            @pl.when(k != my_block)
            def _():
                far(
                    block_of(kind, t, k // C, k % C), kinds[kind][1].at[t, my_block],
                    e1_ss.at[kind, t, k], e1_rs.at[kind, t, my_block], 2 * w + k // C, k % C,
                ).start()

    def update_grads(t):
        b2 = lax.rem(t, 2)

        @pl.when(t < S - 1)
        def _():
            edges = mm(edge_t[t, pl.ds(0, DE), :], dcat[b2, :, pl.ds(D, EP)])
            upd_g[t, pl.ds(0, DE), pl.ds(0, EP)] = edges.astype(BF16)
            upd_g[t, pl.ds(0, DE), pl.ds(EP, EP)] = mm(act_t[t, pl.ds(0, DE), :], de[b2]).astype(BF16)
            bias = jnp.sum(de[b2].astype(F32), axis=0, keepdims=True)
            upd_g[t, pl.ds(DE, 16), pl.ds(0, EP)] = jnp.broadcast_to(bias, (16, EP)).astype(BF16)

        @pl.when(t == S - 1)
        def _():
            upd_g[t, pl.ds(0, DE + 16), :] = jnp.zeros((DE + 16, 2 * EP), BF16)

        upd_g[t, pl.ds(DE, 16), pl.ds(EP, EP)] = jnp.zeros((16, EP), BF16)
        upd_g[t, pl.ds(DE + 16, 16), :] = jnp.zeros((16, 2 * EP), BF16)
        blocks_out(1, t)

    def message_grads(t):
        msg_g[t] = mm(edge_t[t, pl.ds(0, DE), :], dcat[lax.rem(t, 2), :, pl.ds(0, D)]).astype(BF16)
        blocks_out(0, t)

    def blocks_sum(kind, t):
        _, ref, low, dst, _, _ = kinds[kind]
        ref[t, my_block] = block_of(kind, t, lax.rem(me_s, 2), me_d)[...]
        for k in range(blocks):
            @pl.when(k != my_block)
            def _():
                arrive(ref.at[t, k], e1_rs.at[kind, t, k])
                arrive(block_of(kind, t, k // C, k % C), e1_ss.at[kind, t, k])
        total = ref[t, 0].astype(F32)
        for k in range(1, blocks):
            total = total + ref[t, k].astype(F32)
        low[t] = total.astype(BF16)
        push(low.at[t], dst.at[me_s], e2_ss.at[kind, t], e2_rs.at[kind, me_s], t, me_d)

    def gather_blocks():
        for k in range(1, 4):
            j, sec, dpi = peer(k)
            rows = pl.ds(pl.multiple_of(j * Q, Q), Q)
            far(x_s.at[rows], x_r.at[q], x_ss, x_rs, sec, dpi).start()
        x_r[q] = x_s[pl.ds(pl.multiple_of(q * Q, Q), Q), :]

    def gather_wait():
        arrive(x_r.at[pl.ds(0, 3)], x_rs)
        arrive(x_s.at[pl.ds(0, 3 * Q)], x_ss)
        total = x_r[0].astype(F32)
        for j in range(1, 4):
            total = total + x_r[j].astype(F32)
        return total

    def message_back(t):
        b2 = lax.rem(t, 2)
        dm = dmb_r[...].astype(F32)
        total = jnp.zeros((Q, D), F32)
        for k in range(K):
            rows = pl.ds(k * Q, Q)
            d = (gp[t, rows, :].astype(F32) * dm).astype(BF16)
            total = total + d.astype(F32)
            dcat[b2, rows, pl.ds(0, D)] = d
        row_s[:, pl.ds(0, D)] = total.astype(BF16)
        x_s[:, pl.ds(0, D)] = mm(oht[...], dcat[b2, :, pl.ds(0, D)]).astype(BF16)

    def node_backward():
        @pl.when(me_s < S - 1)
        def _():
            arrive(dh1_r, dh_rs)

        def turn(n, carry):
            p = lax.rem(near + n, B)
            whole = at(p, 0, N)

            @pl.when(me_s < S - 1)
            def _():
                arrive(row_r.at[whole], row_rs.at[p])
                dn0 = mm_bt(row_r[whole, pl.ds(0, 2 * D)], pwn[...])
                dn3 = mm_bt(row_r[whole, pl.ds(2 * D, 2 * EP)], ep[...])
                for i in range(0, N, RB):
                    rows = at(p, i)
                    dn = dn3[i : i + RB]
                    dn3_s[rows, :] = dn
                    first = norm_back(dn0[i : i + RB], un0[rows, :], sc0[rows, :], parn[pl.ds(0, 1), :])
                    dh = (dh1_r[rows, :].astype(F32) + first).astype(BF16).astype(F32)
                    dh2_s[rows, :] = dh + norm_back(dn, un2[rows, :], sc2[rows, :], gains[2])

            @pl.when(me_s == S - 1)
            def _():
                dh2_s[whole, :] = cot[whole, :].astype(F32)

            dy = dh2_s[whole, :].astype(BF16)
            bwd[whole, pl.ds(D, D)] = dy
            da2 = jnp.zeros((N, D), F32)
            for c in range(chunks):
                cols = pl.ds(c * FC, FC)
                dv = mm_bt(dy, fo[cols, :])
                du = stacked(
                    [(slope_s[at(p, i), cols].astype(F32) * dv[i : i + RB]).astype(BF16) for i in range(0, N, RB)]
                )
                da2 = da2 + mm_bt(du, fi[:, cols])
            for i in range(0, N, RB):
                rows = at(p, i)
                block = da2[i : i + RB]
                da2_s[rows, :] = block
                dh1 = dh2_s[rows, :] + norm_back(block, un1[rows, :], sc1[rows, :], gains[1])
                dh1_f[rows, :] = dh1
                bwd[rows, pl.ds(0, D)] = (dh1 * (1.0 / K)).astype(BF16)
            dmb_s[whole, :] = mm_bt(bwd[whole, pl.ds(0, D)], mo[...]).astype(BF16)
            rows_out(p, dmb_s, dmb_r, dmb_ss, dmb_rs)
            return carry

        lax.fori_loop(0, B, turn, 0)

        @pl.when(me_s > 0)
        def _():
            dh1_s[...] = dh1_f[...].astype(BF16)
            far(dh1_s, dh1_r, dh_ss, dh_rs, me_s - 1, me_d).start()

        @pl.when(me_s < S - 1)
        def _():
            far(row_r.at[:, pl.ds(0, 2 * D)], dpqo_r, fw_ss, dpqo_rs, me_s + 1, me_d).start()
            drs = row_r[:, pl.ds(2 * D, 2 * EP)]
            bwd[:, pl.ds(2 * D, 2 * EP)] = drs
            dn = dn3_s[...]
            sg[pl.ds(11, 1), :] = col_sum(dn * un2[...])
            sg[pl.ds(12, 1), :] = col_sum(dn)
            sg[pl.ds(16, 1), pl.ds(0, EP)] = col_sum(drs[:, :EP].astype(F32))

        @pl.when(me_s == S - 1)
        def _():
            bwd[:, pl.ds(2 * D, 2 * EP)] = jnp.zeros((B * N, 2 * EP), BF16)
            sg[pl.ds(11, 1), :] = jnp.zeros((1, D), F32)
            sg[pl.ds(12, 1), :] = jnp.zeros((1, D), F32)
            sg[pl.ds(16, 1), pl.ds(0, EP)] = jnp.zeros((1, EP), F32)

        share(1, bwd, g_bwd)
        sg[pl.ds(13, 1), :] = col_sum(dh2_s[...])
        sg[pl.ds(8, 1), :] = col_sum(da2_s[...] * un1[...])
        sg[pl.ds(9, 1), :] = col_sum(da2_s[...])
        sg[pl.ds(10, 1), :] = col_sum(dh1_f[...])

    def node_backward_drain():
        rows_drain(dmb_s, dmb_ss)

        @pl.when(me_s > 0)
        def _():
            arrive(dh1_s, dh_ss)

        @pl.when(me_s < S - 1)
        def _():
            arrive(row_r.at[:, pl.ds(0, 2 * D)], fw_ss)

    dacc[...] = jnp.zeros_like(dacc)

    def backward_step(step, carry):
        t = S - 1 - step

        @pl.when(me_s == t)
        def _():
            node_backward()

        @pl.when(((t == S - 1) & (me_s >= S - 2)) | (me_s == t - 2))
        def _():
            prepare(me_s)

        @pl.when(t < S - 1)
        def _():
            edge_pass(t)

        update_grads(t)

        @pl.when(t + 2 < S)
        def _():
            for kind in range(2):
                blocks_sum(kind, t + 2)

        @pl.when(t == 0)
        def _():
            for kind in range(2):
                blocks_sum(kind, 1)

        arrive(dmb_r, dmb_rs)
        message_back(t)

        @pl.when(t > 0)
        def _():
            edge_back(t)

        @pl.when(t == 0)
        def _():
            x_s[:, pl.ds(D, EP)] = jnp.zeros((N, EP), BF16)

        gather_blocks()
        other = gather_wait().astype(BF16)
        row_s[:, pl.ds(D, D)] = other[:, :D]
        row_s[:, pl.ds(2 * D + EP, EP)] = other[:, D:]
        dpq = row_s.at[:, pl.ds(0, 2 * D)]

        @pl.when(t > 0)
        def _():
            push(row_s, row_r.at[pl.ds(my_row, Q)], row_ss, row_rs.at[slot], t - 1, owner_d)

        @pl.when(t == 0)
        def _():
            push(dpq, dpqo_r.at[pl.ds(my_row, Q)], row_ss, dpqo_rs, t, owner_d)

        message_grads(t)

        @pl.when(t > 0)
        def _():
            drain(row_s, row_ss, t - 1, owner_d)

        @pl.when(t == 0)
        def _():
            drain(dpq, row_ss, t, owner_d)

        @pl.when(me_s == t)
        def _():
            node_backward_drain()

        return carry

    lax.fori_loop(0, S, backward_step, 0)

    arrive(dpqo_r, dpqo_rs)
    across = [pl.ds(p * N, N) for p in range(B)]
    for p in range(B):
        share_near(2 + p, dpqo_r.at[across[p]], lambda c, p=p: g_dpq.at[c, across[p]])
    dpq = dpqo_r[...]
    sg[pl.ds(2, 1), :] = col_sum(dpq[:, :D].astype(F32))
    dn = mm_bt(dpq, pw[...])
    unit = hi_s[...]
    sg[pl.ds(0, 1), :] = col_sum(dn * unit)
    sg[pl.ds(1, 1), :] = col_sum(dn)
    share(2 + B, sg, g_small)
    ig[...] = (dh1_f[...] + norm_back(dn, unit, sci[...], gains[0])).astype(BF16)
    blocks_sum(1, 0)
    blocks_sum(0, 0)
    for p in range(B):
        share_relay(2 + p, dpqo_r.at[across[p]], lambda c, p=p: g_dpq.at[c, across[p]])
    for kind in range(1, -1, -1):
        _, _, low, src, final, dst = kinds[kind]
        for sec in range(S):
            arrive(src.at[sec], e2_rs.at[kind, sec])
        for half in range(2):
            total = src[half].astype(F32)
            for sec in range(half + 2, S, 2):
                total = total + src[sec].astype(F32)
            final[half] = total.astype(BF16)
        share(3 + B + kind, final, dst)
        for t in range(S):
            drain(low.at[t], e2_ss.at[kind, t], t, me_d)
    share_wait(0, fwd, g_fwd)
    share_wait(1, bwd, g_bwd)
    for p in range(B):
        share_near_wait(2 + p, dpqo_r.at[across[p]], lambda c, p=p: g_dpq.at[c, across[p]])
    share_wait(2 + B, sg, g_small)
    for kind in range(2):
        share_wait(3 + B + kind, kinds[kind][4], kinds[kind][5])


def run_relay(dims, operands):
    S, B, N, K, Q, D, DE, EP, FF, C = dims
    R = K * Q
    BN = B * N
    tall = DE + N + Q
    vm = pl.BlockSpec(memory_space=pltpu.VMEM)
    hbm = pl.BlockSpec(memory_space=pl.ANY)
    dma = pltpu.SemaphoreType.DMA
    sds = jax.ShapeDtypeStruct
    BW = D // C
    tile = 32
    held = -(-(DE + 16) // tile) * tile
    scratch = [
        pltpu.VMEM((BN, D), F32),
        pltpu.VMEM((8, D), F32),
        pltpu.VMEM((1, EP), F32),
        pltpu.VMEM((S, DE, D), BF16),
        pltpu.VMEM((S, held, 2 * EP), BF16),
        pltpu.VMEM((BN, 4 * D), BF16),
        pltpu.VMEM((BN, 2 * D + 2 * EP), BF16),
        pltpu.VMEM((24, D), F32),
        pltpu.VMEM((S, DE, D), BF16),
        pltpu.VMEM((S, 2 * C, DE // 2, BW), BF16),
        pltpu.VMEM((S, DE // 2, BW), BF16),
        pltpu.VMEM((S, DE // 2, BW), BF16),
        pltpu.VMEM((2, DE // 2, BW), BF16),
        pltpu.VMEM((S, held, 2 * EP), BF16),
        pltpu.VMEM((S, 2 * C, held // 2, BW), BF16),
        pltpu.VMEM((S, held // 2, BW), BF16),
        pltpu.VMEM((S, held // 2, BW), BF16),
        pltpu.VMEM((2, held // 2, BW), BF16),
        pltpu.VMEM((S, EP, EP), BF16),
        pltpu.VMEM((S, 16, EP), BF16),
        pltpu.VMEM((S, R, EP), BF16),
        pltpu.VMEM((S, tall, D), BF16),
        pltpu.VMEM((S, tall, EP), BF16),
        pltpu.VMEM((D, 2 * D), BF16),
        pltpu.VMEM((8, D), F32),
        pltpu.VMEM((BN, D), BF16),
        pltpu.VMEM((BN, D), BF16),
        pltpu.VMEM((Q, D), BF16),
        pltpu.VMEM((BN, D), BF16),
        pltpu.VMEM((BN, 2 * D), BF16),
        pltpu.VMEM((Q, 2 * D), BF16),
        pltpu.VMEM((BN, 2 * EP), BF16),
        pltpu.VMEM((Q, 2 * EP), BF16),
        pltpu.VMEM((BN, D), F32),
        pltpu.VMEM((BN, D), F32),
        pltpu.VMEM((BN, D), F32),
        pltpu.VMEM((BN, D), F32),
        pltpu.VMEM((BN, 1), F32),
        pltpu.VMEM((BN, 1), F32),
        pltpu.VMEM((BN, 1), F32),
        pltpu.VMEM((BN, 1), F32),
        pltpu.VMEM((BN, FF), F32),
        pltpu.VMEM((BN, FF), BF16),
        pltpu.VMEM((2, R, EP), BF16),
        pltpu.VMEM((R, EP), F32),
        pltpu.VMEM((S, R, D), BF16),
        pltpu.VMEM((S, R, EP), BF16),
        pltpu.VMEM((2, R, D + EP), BF16),
        pltpu.VMEM((S, EP, R), BF16),
        pltpu.VMEM((S, EP, R), BF16),
        pltpu.VMEM((N, D + EP), BF16),
        pltpu.VMEM((4, Q, D + EP), BF16),
        pltpu.VMEM((Q, 2 * D + 2 * EP), BF16),
        pltpu.VMEM((BN, 2 * D + 2 * EP), BF16),
        pltpu.VMEM((BN, 2 * D), BF16),
        pltpu.VMEM((BN, D), BF16),
        pltpu.VMEM((Q, D), BF16),
        pltpu.VMEM((BN, D), BF16),
        pltpu.VMEM((BN, D), BF16),
        pltpu.VMEM((BN, D), F32),
        pltpu.VMEM((BN, D), F32),
        pltpu.VMEM((BN, D), F32),
        pltpu.VMEM((BN, D), F32),
        pltpu.VMEM((BN, D), F32),
        pltpu.VMEM((BN, D), BF16),
        dma, dma((2,)), dma((2,)), dma, dma,
        dma, dma, dma, dma, dma, dma, dma, dma,
        dma, dma((B,)), dma, dma, dma, dma((B,)), dma,
        dma, dma, dma, dma, dma,
        dma((2, S, 2 * C)), dma((2, S, 2 * C)), dma((2, S)), dma((2, S)), dma((5 + B, C)), dma((5 + B, C)),
        dma((B, C // 2)), dma((2, 2, S // 2)), dma((2, S)), dma((2, S)), dma((2, S)),
    ]
    return pl.pallas_call(
        functools.partial(relay_kernel, dims),
        out_shape=(
            sds((BN, D), BF16),
            sds((BN, D), BF16),
            sds((C, BN, 4 * D), BF16),
            sds((C, BN, 2 * D + 2 * EP), BF16),
            sds((C, BN, 2 * D), BF16),
            sds((C, 24, D), F32),
            sds((C, 2, DE // 2, BW), BF16),
            sds((C, 2, held // 2, BW), BF16),
        ),
        in_specs=[hbm, vm, pl.BlockSpec(memory_space=pltpu.SMEM)] + [vm] * 16,
        out_specs=(vm,) * 2 + (hbm,) * 6,
        scratch_shapes=scratch,
        compiler_params=pltpu.CompilerParams(
            collective_id=0, has_side_effects=True, vmem_limit_bytes=62 * 1024 * 1024
        ),
    )(*operands)


def gradient_kernel(
    dims,
    fwd, bwd, dpq, small, edge, upd, fi, fo, fb, act, ig,
    g_pair, g_edge, g_out, g_fi, g_fo, g_ep, g_self, g_eout, g_gain, g_shift, g_nb, g_fb, g_eb, act_out, ig_out,
    fwd_v, bwd_v, dpq_v, fi_v, fo_v, gfi_v, gfo_v, pair_v, out_v, edge_v, upd_v, in_sems, sems,
):
    S, B, N, K, Q, D, DE, EP, FF, C = dims
    chunks = 4
    FC = FF // chunks

    def part(c, size=D):
        return pl.ds(c * size, size)

    loads = {}

    def load(name, src, dst):
        loads[name] = pltpu.make_async_copy(src, dst, in_sems.at[len(loads)])
        loads[name].start()

    load("a2", fwd.at[:, part(2)], fwd_v.at[2])
    load("dy", bwd.at[:, part(1)], bwd_v.at[1])
    for c in range(chunks):
        load(("fi", c), fi.at[:, part(c, FC)], fi_v.at[c])
        load(("fo", c), fo.at[part(c, FC)], fo_v.at[c])
    load("a1", fwd.at[:, part(0)], fwd_v.at[0])
    load("dpq0", dpq.at[:, part(0)], dpq_v.at[0])
    load("dpq1", dpq.at[:, part(1)], dpq_v.at[1])
    load("mbar", fwd.at[:, part(1)], fwd_v.at[1])
    load("dmsg", bwd.at[:, part(0)], bwd_v.at[0])
    load("a3", fwd.at[:, part(3)], fwd_v.at[3])
    load("drs", bwd.at[:, part(2)], bwd_v.at[2])
    load("edge", edge, edge_v)
    load("upd", upd, upd_v)
    stores = []

    def out(src, dst):
        copy = pltpu.make_async_copy(src, dst, sems.at[len(stores)])
        copy.start()
        stores.append(copy)

    out(act, act_out)
    out(ig, ig_out)
    loads["a2"].wait()
    loads["dy"].wait()
    a2 = fwd_v[2]
    dy = bwd_v[1]
    for c in range(chunks):
        cols = part(c, FC)
        loads["fi", c].wait()
        loads["fo", c].wait()
        value, slope = gelu_both(mm(a2, fi_v[c]) + fb[:, cols])
        du = (slope * mm_bt(dy, fo_v[c])).astype(BF16)
        g_fb[:, cols] = col_sum(du.astype(F32))
        gfi_v[c] = mm_at(a2, du)
        out(gfi_v.at[c], g_fi.at[0, :, cols])
        gfo_v[c] = mm_at(value.astype(BF16), dy)
        out(gfo_v.at[c], g_fo.at[0, cols])
    loads["a1"].wait()
    for c in range(2):
        loads["dpq%d" % c].wait()
        pair_v[c] = mm_at(fwd_v[0], dpq_v[c])
        out(pair_v.at[c], g_pair.at[0, :, part(c)])
    loads["mbar"].wait()
    loads["dmsg"].wait()
    out_v[...] = mm_at(fwd_v[1], bwd_v[0]) * float(K)
    out(out_v, g_out.at[0])
    loads["a3"].wait()
    loads["drs"].wait()
    ends = mm_at(fwd_v[3], bwd_v[2])
    g_ep[0] = jnp.concatenate([ends[:, :DE], ends[:, EP : EP + DE]], axis=1)
    total = small[0]
    for c in range(1, C):
        total = total + small[c]
    for i, rows in enumerate(((0, 1, 2), (8, 9, 10), (11, 12, 13))):
        g_gain[i] = total[rows[0] : rows[0] + 1]
        g_shift[i] = total[rows[1] : rows[1] + 1]
        g_nb[i] = total[rows[2] : rows[2] + 1]
    g_eb[0, pl.ds(0, 1), :] = total[16:17, :DE]
    loads["edge"].wait()
    loads["upd"].wait()
    BW = edge_v.shape[3]
    for c in range(C):
        for half in range(2):
            block = edge_v[c, half].astype(F32)
            g_edge[0, pl.ds(half * (DE // 2), DE // 2), pl.ds(c * BW, BW)] = block
        block = stacked([upd_v[c, 0], upd_v[c, 1]]).astype(F32)
        first = c * BW
        for array, begin in ((g_self, 0), (g_eout, EP)):
            low, high = max(first, begin), min(first + BW, begin + DE)
            if low < high:
                array[0, :, pl.ds(low - begin, high - low)] = block[:DE, low - first : high - first]
        low, high = first, min(first + BW, DE)
        if low < high:
            g_eb[0, pl.ds(1, 1), pl.ds(low, high - low)] = block[DE : DE + 1, low - first : high - first]
    for copy in stores:
        copy.wait()


def run_gradients(dims, operands):
    S, B, N, K, Q, D, DE, EP, FF, C = dims
    rows = C * B * N
    BW = D // C
    held = operands[5].shape[2]
    vm = pl.BlockSpec(memory_space=pltpu.VMEM)
    hbm = pl.BlockSpec(memory_space=pl.ANY)
    sds = jax.ShapeDtypeStruct
    shapes = (
        (1, D, 2 * D), (1, DE, D), (1, D, D), (1, D, FF), (1, FF, D), (1, D, 2 * DE), (1, DE, DE), (1, DE, DE),
        (3, 1, D), (3, 1, D), (3, 1, D), (1, FF), (1, 2, DE),
    )
    return pl.pallas_call(
        functools.partial(gradient_kernel, dims),
        out_shape=tuple(sds(shape, F32) for shape in shapes) + (sds((1, B, N, D), BF16),) * 2,
        in_specs=[hbm, hbm, hbm, vm, hbm, hbm, hbm, hbm, vm, hbm, hbm],
        out_specs=(hbm, vm, hbm, hbm, hbm) + (vm,) * 8 + (hbm,) * 2,
        scratch_shapes=[
            pltpu.VMEM((4, rows, D), BF16),
            pltpu.VMEM((3, rows, D), BF16),
            pltpu.VMEM((2, rows, D), BF16),
            pltpu.VMEM((4, D, FF // 4), BF16),
            pltpu.VMEM((4, FF // 4, D), BF16),
            pltpu.VMEM((4, D, FF // 4), F32),
            pltpu.VMEM((4, FF // 4, D), F32),
            pltpu.VMEM((2, D, D), F32),
            pltpu.VMEM((D, D), F32),
            pltpu.VMEM((C, 2, DE // 2, BW), BF16),
            pltpu.VMEM((C, 2, held, BW), BF16),
            pltpu.SemaphoreType.DMA((19,)),
            pltpu.SemaphoreType.DMA((13,)),
        ],
        compiler_params=pltpu.CompilerParams(vmem_limit_bytes=56 * 1024 * 1024),
    )(*operands)


def stationary(
    clean_nodes, noise_nodes, edge_feats, neighbours, time_bins, cotangent,
    pair_weight, message_edge, message_out, ffn_in, ffn_out, edge_pair, edge_self, edge_out,
    norm_gain, norm_shift, node_bias, ffn_bias, edge_bias,
):
    S = lax.axis_size("section")
    place = lax.axis_index("section")
    column = lax.axis_index("dp")
    B, N, D = clean_nodes.shape
    K, DE = edge_feats.shape[2:]
    FF = ffn_in.shape[2]
    Q = N // 4
    EP = DE + N
    core = column % 2
    w = place // 2
    slab = (place % 2) * 2 * Q

    node_ids = jnp.arange(N, dtype=jnp.int32)
    both = [
        lax.dynamic_slice(array, (w % B, slab) + (0,) * (array.ndim - 2), (1, 2 * Q) + array.shape[2:])[0]
        for array in (edge_feats, neighbours)
    ]
    chosen = (both[1][:, :, None] == node_ids).astype(BF16)
    both = jnp.concatenate([both[0], chosen], axis=2)
    mine = lax.dynamic_slice_in_dim(both, core * Q, Q, 0)
    theirs = lax.dynamic_slice_in_dim(both, (1 - core) * Q, Q, 0)
    got = lax.ppermute(theirs, "dp", [(i, i ^ 1) for i in range(lax.axis_size("dp"))])
    ecat0 = jnp.swapaxes(jnp.where(w // B == core, mine, got), 0, 1).reshape(K * Q, EP)
    oht = jnp.transpose(ecat0[:, DE:])
    phase = (time_bins.astype(F32) + 0.5) * (math.pi * 0.5 / TBINS)
    mix = jnp.cos(phase[None] - jnp.array([[0.0], [math.pi * 0.5]], F32))

    def by_rows(array):
        return jnp.transpose(array, (1, 0, 2))

    def widen(array, size, axis=-1):
        extra = [(0, 0)] * array.ndim
        extra[axis] = (0, size - array.shape[axis])
        return jnp.pad(array, extra)

    ep = jnp.concatenate([widen(edge_pair[0, :, :DE], EP), widen(edge_pair[0, :, DE:], EP)], axis=1)
    C = lax.axis_size("dp")
    dims = (S, B, N, K, Q, D, DE, EP, FF, C)
    act, ig, g_fwd, g_bwd, g_dpq, g_small, g_msg, g_upd = run_relay(
        dims,
        (
            ecat0, oht, mix, clean_nodes.reshape(B * N, D), noise_nodes.reshape(B * N, D),
            cotangent.reshape(B * N, D), pair_weight[0], message_out[0], ffn_in[0], ffn_out[0], ep,
            by_rows(norm_gain), by_rows(norm_shift), by_rows(node_bias), ffn_bias, edge_bias[0],
            message_edge[0], edge_self[0], edge_out[0],
        ),
    )
    grads = run_gradients(
        dims,
        (
            g_fwd.reshape(C * B * N, -1), g_bwd.reshape(C * B * N, -1), g_dpq.reshape(C * B * N, -1),
            g_small, g_msg, g_upd, ffn_in[0], ffn_out[0], ffn_bias, act.reshape(1, B, N, D), ig.reshape(1, B, N, D),
        ),
    )
    grads, outs = list(grads[:-2]), tuple(grads[-2:])
    grads[8:11] = [by_rows(array) for array in grads[8:11]]
    return outs + tuple(grads)


def solution(mesh):
    sections, copies = mesh.shape["section"], mesh.shape["dp"]

    def body(*args):
        B, N = args[0].shape[:2]
        fits = sections == 4 * B and copies % 2 == 0 and N % 64 == 0
        return stationary(*args) if fits else on_device(*args)

    placed = (
        P("dp", None, None),
        P("dp", None, None),
        P("dp", None, None, None),
        P("dp", None, None),
        P("dp"),
        P("dp", None, None),
        P("section", None, None),
        P("section", None, None),
        P("section", None, None),
        P("section", None, None),
        P("section", None, None),
        P("section", None, None),
        P("section", None, None),
        P("section", None, None),
        P("section", None, None),
        P("section", None, None),
        P("section", None, None),
        P("section", None),
        P("section", None, None),
    )
    return jax.shard_map(
        body,
        mesh=mesh,
        in_specs=placed,
        out_specs=(
            P("section", "dp", None, None),
            P("section", "dp", None, None),
            P("section", None, None),
            P("section", None, None),
            P("section", None, None),
            P("section", None, None),
            P("section", None, None),
            P("section", None, None),
            P("section", None, None),
            P("section", None, None),
            P("section", None, None),
            P("section", None, None),
            P("section", None, None),
            P("section", None),
            P("section", None, None),
        ),
        check_vma=False,
    )
```

```python
import functools
import math

import jax
import jax.numpy as jnp
from jax import lax
from jax.experimental import pallas as pl
from jax.experimental.pallas import tpu as pltpu
from jax.sharding import PartitionSpec as P

TBINS = 100


def from_behind(block, axis, distance):
    devices = range(lax.axis_size(axis))
    route = [(i - distance, i) for i in devices if i - distance in devices]
    return lax.ppermute(block, axis, route)


def for_sending(value):
    return jax.tree.map(lambda a: a.astype(jnp.bfloat16) if a.dtype == jnp.float32 else a, value)


def layer_norm(value, gain, shift):
    centre = jnp.mean(value, axis=-1, keepdims=True)
    centred = value - centre
    spread = jnp.mean(centred * centred, axis=-1, keepdims=True)
    return centred * lax.rsqrt(spread + 1e-05) * gain + shift


def forward_layer(weights, hidden, edge_state, nearest):
    (
        pair_w,
        msg_edge,
        msg_out,
        ffn_w_in,
        ffn_w_out,
        edge_pair_w,
        edge_self_w,
        edge_out_w,
        gains,
        shifts,
        node_b,
        ffn_b,
        edge_b,
    ) = weights
    width = msg_out.shape[0]
    edge_width = edge_self_w.shape[0]
    normed_one = layer_norm(hidden, gains[0], shifts[0]).astype(jnp.bfloat16)
    pair_out = jnp.dot(normed_one, pair_w, preferred_element_type=jnp.float32)
    before_act = (
        pair_out[:, None, :width]
        + jnp.take(pair_out[:, width:], nearest, axis=0)
        + jnp.einsum("nkc,cd->nkd", edge_state, msg_edge, preferred_element_type=jnp.float32)
        + node_b[0]
    )
    message_act = jax.nn.gelu(before_act).astype(jnp.bfloat16)
    message_all = jnp.einsum(
        "nkc,cd->nkd", message_act, msg_out, preferred_element_type=jnp.float32
    )
    after_msg = hidden + jnp.mean(message_all, axis=1) + node_b[1]
    normed_two = layer_norm(after_msg, gains[1], shifts[1]).astype(jnp.bfloat16)
    ffn_pre = jnp.dot(normed_two, ffn_w_in, preferred_element_type=jnp.float32) + ffn_b
    ffn_act = jax.nn.gelu(ffn_pre).astype(jnp.bfloat16)
    after_ffn = (
        after_msg + jnp.dot(ffn_act, ffn_w_out, preferred_element_type=jnp.float32) + node_b[2]
    )
    normed_three = layer_norm(after_ffn, gains[2], shifts[2]).astype(jnp.bfloat16)
    edge_pairs = jnp.dot(normed_three, edge_pair_w, preferred_element_type=jnp.float32)
    edge_pre = (
        edge_pairs[:, None, :edge_width]
        + jnp.take(edge_pairs[:, edge_width:], nearest, axis=0)
        + jnp.einsum("nkc,cd->nkd", edge_state, edge_self_w, preferred_element_type=jnp.float32)
        + edge_b[0]
    )
    edge_act = jax.nn.gelu(edge_pre).astype(jnp.bfloat16)
    edge_next = (
        edge_state.astype(jnp.float32)
        + jnp.einsum("nkc,cd->nkd", edge_act, edge_out_w, preferred_element_type=jnp.float32)
        + edge_b[1]
    )
    saved = (
        normed_one,
        before_act,
        message_act,
        after_msg,
        normed_two,
        ffn_pre,
        ffn_act,
        after_ffn,
        normed_three,
        edge_pre,
        edge_act,
    )
    return (after_ffn, edge_next, saved)


def backward_layer(weights, hidden, edge_state, nearest, grad_nodes_out, grad_edges_out):
    (
        pair_w,
        msg_edge,
        msg_out,
        ffn_w_in,
        ffn_w_out,
        edge_pair_w,
        edge_self_w,
        edge_out_w,
        gains,
        shifts,
        node_b,
        ffn_b,
        edge_b,
    ) = weights
    unused_nodes, unused_edges, saved = forward_layer(weights, hidden, edge_state, nearest)
    (
        normed_one,
        before_act,
        message_act,
        after_msg,
        normed_two,
        ffn_pre,
        ffn_act,
        after_ffn,
        normed_three,
        edge_pre,
        edge_act,
    ) = saved
    width = msg_out.shape[0]
    edge_width = edge_self_w.shape[0]
    count = nearest.shape[1]
    node_count = hidden.shape[0]
    one_hot = (
        nearest.reshape(-1)[None, :] == jnp.arange(node_count, dtype=jnp.int32)[:, None]
    ).astype(jnp.bfloat16)
    edge_grad_low = grad_edges_out.astype(jnp.bfloat16)
    grad_edge_b1 = jnp.sum(grad_edges_out, axis=(0, 1))
    grad_edge_out_w = jnp.einsum(
        "nkc,nkd->cd", edge_act, edge_grad_low, preferred_element_type=jnp.float32
    )
    edge_act_grad = jnp.einsum(
        "nkd,cd->nkc", edge_grad_low, edge_out_w, preferred_element_type=jnp.float32
    )
    unused_value, gelu_edge = jax.vjp(jax.nn.gelu, edge_pre)
    edge_pre_grad = gelu_edge(edge_act_grad)[0].astype(jnp.bfloat16)
    grad_edge_b0 = jnp.sum(edge_pre_grad, axis=(0, 1), dtype=jnp.float32)
    grad_edge_self_w = jnp.einsum(
        "nkc,nkd->cd", edge_state, edge_pre_grad, preferred_element_type=jnp.float32
    )
    edge_total = grad_edges_out + jnp.einsum(
        "nkd,cd->nkc", edge_pre_grad, edge_self_w, preferred_element_type=jnp.float32
    )
    own_edge = jnp.sum(edge_pre_grad, axis=1, dtype=jnp.float32)
    other_edge = jnp.dot(
        one_hot, edge_pre_grad.reshape(-1, edge_width), preferred_element_type=jnp.float32
    )
    pairs_grad = jnp.concatenate([own_edge, other_edge], axis=-1).astype(jnp.bfloat16)
    grad_edge_pair_w = jnp.einsum(
        "nc,nd->cd", normed_three, pairs_grad, preferred_element_type=jnp.float32
    )
    normed_three_grad = jnp.einsum(
        "nd,cd->nc", pairs_grad, edge_pair_w, preferred_element_type=jnp.float32
    )
    unused_value, norm_three_back = jax.vjp(layer_norm, after_ffn, gains[2], shifts[2])
    ffn_side, gain_three, shift_three = norm_three_back(normed_three_grad)
    after_ffn_grad = grad_nodes_out + ffn_side
    grad_node_b2 = jnp.sum(after_ffn_grad, axis=0)
    ffn_out_grad = after_ffn_grad.astype(jnp.bfloat16)
    grad_ffn_w_out = jnp.einsum(
        "nc,nd->cd", ffn_act, ffn_out_grad, preferred_element_type=jnp.float32
    )
    ffn_act_grad = jnp.einsum(
        "nd,cd->nc", ffn_out_grad, ffn_w_out, preferred_element_type=jnp.float32
    )
    unused_value, gelu_ffn = jax.vjp(jax.nn.gelu, ffn_pre)
    ffn_pre_grad = gelu_ffn(ffn_act_grad)[0].astype(jnp.bfloat16)
    grad_ffn_b = jnp.sum(ffn_pre_grad, axis=0, dtype=jnp.float32)
    grad_ffn_w_in = jnp.einsum(
        "nc,nd->cd", normed_two, ffn_pre_grad, preferred_element_type=jnp.float32
    )
    normed_two_grad = jnp.einsum(
        "nd,cd->nc", ffn_pre_grad, ffn_w_in, preferred_element_type=jnp.float32
    )
    unused_value, norm_two_back = jax.vjp(layer_norm, after_msg, gains[1], shifts[1])
    msg_side, gain_two, shift_two = norm_two_back(normed_two_grad)
    after_msg_grad = after_ffn_grad + msg_side
    grad_node_b1 = jnp.sum(after_msg_grad, axis=0)
    message_grad = (after_msg_grad / count).astype(jnp.bfloat16)
    grad_msg_out = jnp.einsum(
        "nkc,nd->cd", message_act, message_grad, preferred_element_type=jnp.float32
    )
    message_act_grad = jnp.einsum(
        "nd,cd->nc", message_grad, msg_out, preferred_element_type=jnp.float32
    )
    unused_value, gelu_msg = jax.vjp(jax.nn.gelu, before_act)
    before_grad = gelu_msg(jnp.broadcast_to(message_act_grad[:, None, :], before_act.shape))[
        0
    ].astype(jnp.bfloat16)
    grad_node_b0 = jnp.sum(before_grad, axis=(0, 1), dtype=jnp.float32)
    grad_msg_edge = jnp.einsum(
        "nkc,nkd->cd", edge_state, before_grad, preferred_element_type=jnp.float32
    )
    edge_total = edge_total + jnp.einsum(
        "nkd,cd->nkc", before_grad, msg_edge, preferred_element_type=jnp.float32
    )
    own_node = jnp.sum(before_grad, axis=1, dtype=jnp.float32)
    other_node = jnp.dot(
        one_hot, before_grad.reshape(-1, width), preferred_element_type=jnp.float32
    )
    pair_grad = jnp.concatenate([own_node, other_node], axis=-1).astype(jnp.bfloat16)
    grad_pair_w = jnp.einsum("nc,nd->cd", normed_one, pair_grad, preferred_element_type=jnp.float32)
    normed_one_grad = jnp.einsum("nd,cd->nc", pair_grad, pair_w, preferred_element_type=jnp.float32)
    unused_value, norm_one_back = jax.vjp(layer_norm, hidden, gains[0], shifts[0])
    input_side, gain_one, shift_one = norm_one_back(normed_one_grad)
    hidden_grad = after_msg_grad + input_side
    grads = (
        grad_pair_w,
        grad_msg_edge,
        grad_msg_out,
        grad_ffn_w_in,
        grad_ffn_w_out,
        grad_edge_pair_w,
        grad_edge_self_w,
        grad_edge_out_w,
        jnp.stack([gain_one, gain_two, gain_three]),
        jnp.stack([shift_one, shift_two, shift_three]),
        jnp.stack([grad_node_b0, grad_node_b1, grad_node_b2]),
        grad_ffn_b,
        jnp.stack([grad_edge_b0, grad_edge_b1]),
    )
    return (hidden_grad.astype(jnp.bfloat16), edge_total.astype(jnp.bfloat16), grads)


def on_device(
    clean_nodes,
    noise_nodes,
    edge_feats,
    neighbours,
    time_bins,
    cotangent,
    pair_weight,
    message_edge,
    message_out,
    ffn_in,
    ffn_out,
    edge_pair,
    edge_self,
    edge_out,
    norm_gain,
    norm_shift,
    node_bias,
    ffn_bias,
    edge_bias,
):
    sections = lax.axis_size("section")
    place = lax.axis_index("section")
    weights = tuple(
        (
            item[0]
            for item in (
                pair_weight,
                message_edge,
                message_out,
                ffn_in,
                ffn_out,
                edge_pair,
                edge_self,
                edge_out,
                norm_gain,
                norm_shift,
                node_bias,
                ffn_bias,
                edge_bias,
            )
        )
    )
    batches, node_count, width = clean_nodes.shape
    phase = (time_bins.astype(jnp.float32) + 0.5) * (math.pi * 0.5 / TBINS)
    start = jnp.cos(phase)[:, None, None] * clean_nodes.astype(jnp.float32) + jnp.sin(phase)[
        :, None, None
    ] * noise_nodes.astype(jnp.float32)
    zero_nodes = jnp.zeros((node_count, width), jnp.bfloat16)
    zero_edges = jnp.zeros(edge_feats.shape[1:], jnp.bfloat16)
    is_first = place == 0
    is_last = place == sections - 1

    def forward_step(step_index, carry):
        recv_nodes, recv_edges, back_nodes, kept_nodes, kept_edges, section_outs = carry
        item = step_index - place
        first_pass = (item >= 0) & (item < batches)
        second_pass = (item >= sections) & (item < sections + batches)
        index = jnp.clip(jnp.where(second_pass, item - sections, item), 0, batches - 1)
        predicted = back_nodes
        own_start = lax.dynamic_index_in_dim(start, index, 0, keepdims=False)
        lead_nodes = own_start + jnp.where(second_pass, predicted.astype(jnp.float32), 0.0)
        nodes_in = jnp.where(is_first, lead_nodes, recv_nodes.astype(jnp.float32))
        edges_in = jnp.where(
            is_first, lax.dynamic_index_in_dim(edge_feats, index, 0, keepdims=False), recv_edges
        )
        nearest = lax.dynamic_index_in_dim(neighbours, index, 0, keepdims=False)

        def run_layer(operand):
            after, edge_next, saved = forward_layer(weights, operand[0], operand[1], operand[2])
            return (after.astype(jnp.bfloat16), edge_next.astype(jnp.bfloat16))

        def skip_layer(operand):
            return (zero_nodes, zero_edges)

        out_nodes, out_edges = lax.cond(
            first_pass | second_pass, run_layer, skip_layer, (nodes_in, edges_in, nearest)
        )
        kept_nodes = lax.dynamic_update_index_in_dim(
            kept_nodes, jnp.where(second_pass, nodes_in, kept_nodes[index]), index, 0
        )
        kept_edges = lax.dynamic_update_index_in_dim(
            kept_edges, jnp.where(second_pass, edges_in, kept_edges[index]), index, 0
        )
        section_outs = lax.dynamic_update_index_in_dim(
            section_outs, jnp.where(second_pass, out_nodes, section_outs[index]), index, 0
        )
        recv_nodes, recv_edges = from_behind((out_nodes, out_edges), "section", 1)
        back_nodes = from_behind(out_nodes, "section", 1 - sections)
        return (recv_nodes, recv_edges, back_nodes, kept_nodes, kept_edges, section_outs)

    forward_init = (
        zero_nodes,
        zero_edges,
        zero_nodes,
        jnp.zeros((batches, node_count, width), jnp.float32),
        jnp.zeros_like(edge_feats),
        jnp.zeros((batches, node_count, width), jnp.bfloat16),
    )
    unused_nodes, unused_edges, unused_back, kept_nodes, kept_edges, section_outs = lax.fori_loop(
        0, 2 * sections + batches - 1, forward_step, forward_init
    )
    grads_zero = tuple((jnp.zeros(item.shape, jnp.float32) for item in weights))

    def backward_step(step_index, carry):
        recv_grad_nodes, recv_grad_edges, grads, input_grads = carry
        item = step_index - (sections - 1 - place)
        live = (item >= 0) & (item < batches)
        index = jnp.clip(item, 0, batches - 1)
        nodes_grad_out = jnp.where(
            is_last,
            lax.dynamic_index_in_dim(cotangent, index, 0, keepdims=False).astype(jnp.float32),
            recv_grad_nodes.astype(jnp.float32),
        )
        edges_grad_out = jnp.where(is_last, 0.0, recv_grad_edges.astype(jnp.float32))
        nearest = lax.dynamic_index_in_dim(neighbours, index, 0, keepdims=False)

        def run_back(operand):
            return backward_layer(
                weights, operand[0], operand[1], operand[2], operand[3], operand[4]
            )

        def skip_back(operand):
            return (zero_nodes, zero_edges, grads_zero)

        nodes_grad, edges_grad, terms = lax.cond(
            live,
            run_back,
            skip_back,
            (kept_nodes[index], kept_edges[index], nearest, nodes_grad_out, edges_grad_out),
        )
        grads = tuple((total + term for total, term in zip(grads, terms)))
        input_grads = lax.dynamic_update_index_in_dim(
            input_grads, jnp.where(live, nodes_grad, input_grads[index]), index, 0
        )
        recv_grad_nodes, recv_grad_edges = from_behind((nodes_grad, edges_grad), "section", -1)
        return (recv_grad_nodes, recv_grad_edges, grads, input_grads)

    backward_init = (
        zero_nodes,
        zero_edges,
        grads_zero,
        jnp.zeros((batches, node_count, width), jnp.bfloat16),
    )
    unused_grad_nodes, unused_grad_edges, grads, input_grads = lax.fori_loop(
        0, sections + batches - 1, backward_step, backward_init
    )
    totals = jax.tree.map(lambda part: part.astype(jnp.float32), lax.psum(for_sending(grads), "dp"))
    return (
        section_outs[None],
        input_grads[None],
        totals[0][None],
        totals[1][None],
        totals[2][None],
        totals[3][None],
        totals[4][None],
        totals[5][None],
        totals[6][None],
        totals[7][None],
        totals[8][None],
        totals[9][None],
        totals[10][None],
        totals[11][None],
        totals[12][None],
    )


BF16 = jnp.bfloat16
F32 = jnp.float32
MESH = pl.DeviceIdType.MESH
GELU_A = 0.7978845608028654
GELU_B = 0.044715


def gelu(x):
    return 0.5 * x * (1.0 + jnp.tanh(x * (GELU_A + (GELU_A * GELU_B) * (x * x))))


def gelu_both(x):
    square = x * x
    t = jnp.tanh(x * (GELU_A + (GELU_A * GELU_B) * square))
    half = 0.5 * (1.0 + t)
    slope = half + (0.5 * x) * (1.0 - t * t) * (GELU_A + (3.0 * GELU_A * GELU_B) * square)
    return x * half, slope


def mm(a, b):
    return jnp.dot(a, b, preferred_element_type=F32)


def mm_bt(a, b):
    return lax.dot_general(a, b, (((1,), (1,)), ((), ())), preferred_element_type=F32)


def mm_at(a, b):
    return lax.dot_general(a, b, (((0,), (0,)), ((), ())), preferred_element_type=F32)


def stacked(blocks):
    return jnp.concatenate(blocks, axis=0)


def row_mean(x):
    return jnp.mean(x, axis=-1, keepdims=True)


def normed(x):
    centred = x - row_mean(x)
    scale = lax.rsqrt(row_mean(centred * centred) + 1e-05)
    return centred * scale, scale


def norm_back(grad, unit, scale, gain):
    t = grad * gain
    return scale * (t - row_mean(t) - unit * row_mean(t * unit))


def col_sum(x):
    return jnp.sum(x, axis=0, keepdims=True)


def relay_kernel(
    dims,
    ecat0, oht, mix, clean, noise, cot, pw, mo, fi, fo, ep, gains, shifts, node_b, fb, edge_b, we_own, ws_own, wo_own,
    act, ig, g_fwd, g_bwd, g_dpq, g_small, g_msg, g_upd,
    start, par, eb0, wall_msg, wall_upd, fwd, bwd, sg,
    eg, eg_r, eg_b, msg_o, msg_f, upd_o, upd_f, wo, eb1,
    ecat, wcat, scat, pwn, parn, hin_r, hst, mb_s, mb_r, pq_s, pq_r, rq_s, rq_r,
    un0, un1, un2, hi_s, sc0, sc1, sc2, sci, u_s, slope_s, de, dacc, gp, gpe, dcat, act_t, edge_t,
    x_s, x_r, row_s, row_r, dpqo_r, dmb_s, dmb_r, dh1_s, dh1_r, dh1_f, dh2_s, dn3_s, da2_s, h1_s, a1_s,
    ld_sem, nx_ss, nx_rs, hop_ss, hop_rs,
    pq_ss, pq_rs, ag_ss, ag_rs, rq_ss, rq_rs, ag2_ss, ag2_rs,
    mb_ss, mb_rs, x_ss, x_rs, row_ss, row_rs, dpqo_rs, fw_ss, dmb_ss, dmb_rs, dh_ss, dh_rs,
    e1_ss, e1_rs, e2_ss, e2_rs, g_ss, g_rs, relay_ss, ring_ss, ring_rs, sib_ss, sib_rs,
):
    S, B, N, K, Q, D, DE, EP, FF, C = dims
    BN = B * N
    RB = 16
    top = DE + N
    me_s = lax.axis_index("section")
    me_d = lax.axis_index("dp")
    core = lax.rem(me_d, 2)
    pair = me_d - core
    w = lax.div(me_s, 2)
    q = 2 * lax.rem(me_s, 2) + core
    owner_d = pair + lax.div(w, B)
    slot = lax.rem(w, B)
    my_row = pl.multiple_of(slot * N + q * Q, Q)
    own_rows = pl.ds(top, Q)

    def quarter(j):
        return pl.ds(pl.multiple_of(DE + j * Q, Q), Q)

    def is_me(sec, dpi):
        return (sec == me_s) & (dpi == me_d)

    def far(src, dst, ssem, rsem, sec, dpi):
        return pltpu.make_async_remote_copy(
            src_ref=src, dst_ref=dst, send_sem=ssem, recv_sem=rsem,
            device_id={"section": sec, "dp": dpi}, device_id_type=MESH,
        )

    def push(src, dst, ssem, rsem, sec, dpi):
        lax.cond(
            is_me(sec, dpi),
            lambda: pltpu.make_async_copy(src, dst, rsem).start(),
            lambda: far(src, dst, ssem, rsem, sec, dpi).start(),
        )

    def arrive(ref, sem):
        pltpu.make_async_copy(ref, ref, sem).wait()

    def drain(ref, sem, sec, dpi):
        @pl.when(jnp.logical_not(is_me(sec, dpi)))
        def _():
            arrive(ref, sem)

    def worker_of(p, j):
        return 2 * (core * B + p) + j // 2, pair + j % 2

    def peer(k):
        j = lax.rem(q + k, 4)
        return j, 2 * w + lax.div(j, 2), pair + lax.rem(j, 2)

    works_here = lax.div(w, B) == core

    def at(p, first=0, size=16):
        return pl.ds(pl.multiple_of(p * N + first, size), size)

    near = jnp.clip(w - core * B, 0, B - 1)

    load = pltpu.make_async_copy(ecat0, ecat.at[0], ld_sem)
    load.start()
    barrier = pltpu.get_barrier_semaphore()
    for sec in range(S):
        for c in range(C):
            greeted = (c == pair) | (c == pair + 1) | (w == sec // 2)

            @pl.when(greeted & jnp.logical_not(is_me(sec, c)))
            def _():
                pl.semaphore_signal(
                    barrier, inc=1, device_id={"section": sec, "dp": c}, device_id_type=MESH
                )
    wall_msg[me_s] = we_own[...]
    wall_upd[me_s] = jnp.zeros(wall_upd.shape[1:], BF16)
    wall_upd[me_s, pl.ds(0, DE), pl.ds(0, DE)] = ws_own[...]
    wall_upd[me_s, pl.ds(0, DE), pl.ds(EP, DE)] = wo_own[...]
    bias = edge_b[pl.ds(1, 1), :]
    high = bias.astype(BF16).astype(F32)
    row = lax.broadcasted_iota(jnp.int32, (16, DE), 0)
    wall_upd[me_s, pl.ds(DE, 16), pl.ds(0, DE)] = jnp.where(
        row == 0, high, jnp.where(row == 1, bias - high, 0.0)
    ).astype(BF16)
    eb0[...] = jnp.zeros_like(eb0)
    eb0[:, pl.ds(0, DE)] = edge_b[pl.ds(0, 1), :]
    par[pl.ds(0, 1), :] = gains[0]
    par[pl.ds(1, 1), :] = shifts[0]
    par[pl.ds(2, 1), :] = node_b[0]
    par[pl.ds(3, 5), :] = jnp.zeros((5, D), F32)
    pl.semaphore_wait(barrier, 2 * S - 1 + 2 * (C - 2))

    def section_at(i):
        i = lax.rem(i + S, S)
        return jnp.where(i < S // 2, 2 * i, 2 * (S - i) - 1)

    place = jnp.where(lax.rem(me_s, 2) == 0, w, S - 1 - w)
    sides = ((section_at(place + 1), S // 2), (section_at(place - 1), S // 2 - 1))
    walls = (wall_msg, wall_upd)

    def half_of(which, layer, c):
        size = walls[which].shape[1] // 2
        return walls[which].at[layer, pl.ds(pl.multiple_of(c * size, size), size)]

    def ring_send(which, layer, side, hop):
        sec, reach = sides[side]
        if hop < reach:
            half = half_of(which, layer, core)
            far(half, half, ring_ss.at[which, side, hop], ring_rs.at[which, layer], sec, me_d).start()

    def ring_hop(which, side, hop):
        layer = section_at(place - hop if side == 0 else place + hop)
        half = half_of(which, layer, core)
        arrive(half, ring_rs.at[which, layer])
        ring_send(which, layer, side, hop)
        far(half, half, sib_ss.at[which, layer], sib_rs.at[which, layer], me_s, pair + 1 - core).start()

    hops = [(hop, side) for hop in range(1, S // 2 + 1) for side in range(2) if hop <= sides[side][1]]

    def ring_later(second):
        for hop, side in hops:
            early = (place > 0) & ((place >= hop) if side == 0 else (place + hop <= S))

            @pl.when(early != second)
            def _():
                ring_hop(1, side, hop)

    for side in range(2):
        ring_send(0, me_s, side, 0)
    before = lax.rem(me_s + S - 1, S)
    far(pw, pwn, nx_ss.at[0], nx_rs.at[0], before, me_d).start()
    far(par, parn, nx_ss.at[1], nx_rs.at[1], before, me_d).start()

    for p in range(B):
        rows = pl.ds(p * N, N)
        start[rows, :] = mix[0, p] * clean[rows, :].astype(F32) + mix[1, p] * noise[rows, :].astype(F32)

    def ring_drain():
        for which in range(2):
            for side in range(2):
                for hop in range(sides[side][1]):
                    arrive(half_of(which, me_s, core), ring_ss.at[which, side, hop])
            for layer in range(S):
                @pl.when(layer != me_s)
                def _():
                    arrive(half_of(which, layer, core), sib_ss.at[which, layer])

    def unpack_messages(t):
        @pl.when(t != me_s)
        def _():
            arrive(half_of(0, t, 1 - core), sib_rs.at[0, t])

        wcat[t, pl.ds(0, DE), :] = wall_msg[t]

    def unpack_updates(t):
        @pl.when(t != me_s)
        def _():
            arrive(half_of(1, t, 1 - core), sib_rs.at[1, t])

        scat[t, pl.ds(0, DE), :] = wall_upd[t, pl.ds(0, DE), pl.ds(0, EP)]
        wo[t, pl.ds(0, DE), :] = wall_upd[t, pl.ds(0, DE), pl.ds(EP, EP)]
        wo[t, pl.ds(DE, N), :] = jnp.zeros((N, EP), BF16)
        eb1[t] = wall_upd[t, pl.ds(DE, 16), pl.ds(0, EP)]

    def rows_out(p, src, dst, ssem, rsem):
        for j in range(4):
            sec, dpi = worker_of(p, j)
            push(src.at[at(p, j * Q, Q)], dst, ssem, rsem, sec, dpi)

    def rows_drain(src, ssem):
        lax.cond(
            works_here,
            lambda: arrive(src.at[pl.ds(0, B * N - Q)], ssem),
            lambda: arrive(src, ssem),
        )

    def spread(rows, half, ref, layer, ssem, rsem, rows_sem):
        arrive(rows, rows_sem)
        for k in range(1, 4):
            _, sec, dpi = peer(k)
            far(rows.at[:, pl.ds(half, half)], ref.at[layer, quarter(q)], ssem, rsem, sec, dpi).start()
        ref[layer, own_rows, :] = rows[:, pl.ds(0, half)]
        ref[layer, quarter(q), :] = rows[:, pl.ds(half, half)]

    def spread_wait(ref, layer, sem):
        arrive(ref.at[layer, pl.ds(DE, 3 * Q)], sem)

    def share(group, src, dst):
        for c in range(C):
            push(src, dst.at[me_d], g_ss.at[group, c], g_rs.at[group, me_d], me_s, c)

    def share_wait(group, src, dst):
        for c in range(C):
            arrive(dst.at[c], g_rs.at[group, c])
            drain(src, g_ss.at[group, c], me_s, c)

    def share_near(group, src, dst):
        for c in range(C):
            @pl.when((c == pair) | (c == pair + 1) | (core == c % 2))
            def _():
                push(src, dst(me_d), g_ss.at[group, c], g_rs.at[group, me_d], me_s, c)

    def share_relay(group, src, dst):
        for c in range(C):
            @pl.when((c != me_d) & (core == c % 2))
            def _():
                arrive(dst(c), g_rs.at[group, c])
                far(dst(c), dst(c), relay_ss.at[group - 2, c // 2], g_rs.at[group, c], me_s, pair + 1 - core).start()

    def share_near_wait(group, src, dst):
        for c in range(C):
            @pl.when((c == me_d) | (core != c % 2))
            def _():
                arrive(dst(c), g_rs.at[group, c])

            @pl.when((c != me_d) & ((c == pair) | (c == pair + 1) | (core == c % 2)))
            def _():
                arrive(src, g_ss.at[group, c])

            @pl.when((c != me_d) & (core == c % 2))
            def _():
                arrive(dst(c), relay_ss.at[group - 2, c // 2])

    steps = 4
    KC = K // steps
    RC = KC * Q

    def messages(t):
        own = wcat[t, own_rows, :].astype(F32)
        total = jnp.zeros((Q, D), F32)
        for i in range(steps):
            pre = mm(ecat[t, pl.ds(i * RC, RC), :], wcat[t, pl.ds(0, top), :])
            for k in range(KC):
                total = total + gelu(pre[k * Q : (k + 1) * Q] + own)
        mb_s[...] = (total * (1.0 / K)).astype(BF16)

    def edge_update(t):
        own = scat[t, own_rows, :].astype(F32)
        bias = eb1[t, pl.ds(0, 1), :].astype(F32) + eb1[t, pl.ds(1, 1), :].astype(F32)
        for i in range(steps):
            pe = mm(ecat[t, pl.ds(i * RC, RC), :], scat[t, pl.ds(0, top), :])
            act_e = stacked([gelu(pe[k * Q : (k + 1) * Q] + own).astype(BF16) for k in range(KC)])
            z = mm(act_e, wo[t])
            for k in range(KC):
                rows = pl.ds(i * RC + k * Q, Q)
                ecat[t + 1, rows, :] = (ecat[t, rows, :].astype(F32) + z[k * Q : (k + 1) * Q] + bias).astype(BF16)

    chunks = 4
    FC = FF // chunks

    def node_forward(step):
        @pl.when(step < S)
        def _():
            arrive(pwn, nx_rs.at[0])
            arrive(parn, nx_rs.at[1])
            arrive(pw, nx_ss.at[0])
            arrive(par, nx_ss.at[1])

        @pl.when(step == 0)
        def _():
            hi_s[...] = start[...]

        @pl.when(step > 0)
        def _():
            arrive(hin_r, hop_rs)
            first = jnp.where(me_s == 0, 1.0, 0.0)
            for i in range(0, BN, RB):
                rows = pl.ds(i, RB)
                hi_s[rows, :] = hin_r[rows, :].astype(F32) + first * start[rows, :]

        later = lax.rem(me_s + 1, S)

        def turn(n, carry):
            p = lax.rem(near + n, B)
            whole = at(p, 0, N)
            arrive(mb_r.at[whole], mb_rs.at[p])
            mean = mm(mb_r[whole, :], mo[...])
            for i in range(0, N, RB):
                rows = at(p, i)
                h1 = hi_s[rows, :] + mean[i : i + RB] + node_b[1]
                h1_s[rows, :] = h1
                unit, scale = normed(h1)
                un1[rows, :] = unit
                sc1[rows, :] = scale
                fwd[rows, pl.ds(2 * D, D)] = (unit * gains[1] + shifts[1]).astype(BF16)
                fwd[rows, pl.ds(D, D)] = mb_r[rows, :]
            a2 = fwd[whole, pl.ds(2 * D, D)]
            y = jnp.zeros((N, D), F32)
            for c in range(chunks):
                cols = pl.ds(c * FC, FC)
                u = mm(a2, fi[:, cols])
                v = []
                for i in range(0, N, RB):
                    block = u[i : i + RB] + fb[:, cols]
                    u_s[at(p, i), cols] = block
                    v.append(gelu(block).astype(BF16))
                y = y + mm(stacked(v), fo[cols, :])
            last = jnp.where(me_s == S - 1, 1.0, 0.0)
            for i in range(0, N, RB):
                rows = at(p, i)
                h2 = h1_s[rows, :] + y[i : i + RB] + node_b[2]
                rounded = h2.astype(BF16)
                hst[rows, :] = rounded
                unit, scale = normed(h2)
                un2[rows, :] = unit
                sc2[rows, :] = scale
                fwd[rows, pl.ds(3 * D, D)] = (unit * gains[2] + shifts[2]).astype(BF16)
                pair_norm(rows, rounded.astype(F32) + last * start[rows, :], parn)
            rq = mm(fwd[whole, pl.ds(3 * D, D)], ep[...])
            for i in range(0, N, RB):
                rows = at(p, i)
                rq_s[rows, pl.ds(0, EP)] = (rq[i : i + RB, :EP] + eb0[...]).astype(BF16)
                rq_s[rows, pl.ds(EP, EP)] = rq[i : i + RB, EP:].astype(BF16)
            pair_rows(p, pwn, parn)

            @pl.when(me_s < S - 1)
            def _():
                rows_out(p, rq_s, rq_r, rq_ss, rq_rs)

            @pl.when(step < 2 * S - 1)
            def _():
                rows_out(p, pq_s, pq_r, pq_ss, pq_rs)

            @pl.when((n == 0) & works_here)
            def _():
                pass_on(step)

            return carry

        lax.fori_loop(0, B, turn, 0)

        @pl.when(step < 2 * S - 1)
        def _():
            far(hst, hin_r, hop_ss, hop_rs, later, me_d).start()

        @pl.when(step >= S)
        def _():
            act[...] = hst[...]
            for i in range(0, BN, RB):
                rows = pl.ds(i, RB)
                unit, scale = normed(hi_s[rows, :])
                hi_s[rows, :] = unit
                sci[rows, :] = scale
                fwd[rows, pl.ds(0, D)] = (unit * gains[0] + shifts[0]).astype(BF16)
                for c in range(chunks):
                    cols = pl.ds(c * FC, FC)
                    slope_s[rows, cols] = gelu_both(u_s[rows, cols])[1].astype(BF16)
            share(0, fwd, g_fwd)

    def pair_norm(rows, hidden, first):
        unit, scale = normed(hidden)
        un0[rows, :] = unit
        sc0[rows, :] = scale
        a1_s[rows, :] = (unit * first[pl.ds(0, 1), :] + first[pl.ds(1, 1), :]).astype(BF16)

    def pair_rows(p, weight, first):
        whole = at(p, 0, N)
        for half in range(2):
            cols = pl.ds(half * D, D)
            value = mm(a1_s[whole, :], weight[:, cols])
            if half == 0:
                value = value + first[pl.ds(2, 1), :]
            pq_s[whole, cols] = value.astype(BF16)

    def pass_on(step):
        t = lax.rem(step, S)

        @pl.when(t < S - 1)
        def _():
            spread(rq_r, EP, scat, t, ag2_ss, ag2_rs, rq_rs)

        @pl.when(step < 2 * S - 1)
        def _():
            spread(pq_r, D, wcat, lax.rem(step + 1, S), ag_ss, ag_rs, pq_rs)

    def node_forward_drain():
        arrive(hst, hop_ss)
        rows_drain(pq_s, pq_ss)

        @pl.when(me_s < S - 1)
        def _():
            rows_drain(rq_s, rq_ss)

    @pl.when(me_s == 0)
    def _():
        for i in range(0, BN, RB):
            rows = pl.ds(i, RB)
            pair_norm(rows, start[rows, :], par)
        for p in range(B):
            pair_rows(p, pw, par)
            rows_out(p, pq_s, pq_r, pq_ss, pq_rs)

    def message_slope(t):
        own = wcat[t, own_rows, :].astype(F32)
        for i in range(steps):
            pre = mm(ecat[t, pl.ds(i * RC, RC), :], wcat[t, pl.ds(0, top), :])
            for k in range(KC):
                gp[t, pl.ds(i * RC + k * Q, Q), :] = gelu_both(pre[k * Q : (k + 1) * Q] + own)[1].astype(BF16)

    def edge_slope(t):
        own = scat[t, own_rows, :].astype(F32)
        values = []
        for i in range(steps):
            pe = mm(ecat[t, pl.ds(i * RC, RC), :], scat[t, pl.ds(0, top), :])
            for k in range(KC):
                value, slope = gelu_both(pe[k * Q : (k + 1) * Q] + own)
                values.append(value.astype(BF16))
                gpe[t, pl.ds(i * RC + k * Q, Q), :] = slope.astype(BF16)
        act_t[t] = stacked(values).T

    def prepare(t):
        message_slope(t)
        edge_t[t] = ecat[t].T

        @pl.when(t > 0)
        def _():
            edge_slope(t - 1)

    def forward_step(step, carry):
        t = lax.rem(step, S)

        @pl.when(step < S)
        def _():
            unpack_messages(t)

        spread_wait(wcat, t, ag_rs)
        messages(t)
        spread_wait(wcat, t, ag_ss)
        push(mb_s, mb_r.at[pl.ds(my_row, Q)], mb_ss, mb_rs.at[slot], t, owner_d)

        for second in range(2):
            @pl.when(step == second)
            def _():
                ring_later(second == 1)

        @pl.when((step == 0) & (me_s == 0))
        def _():
            rows_drain(pq_s, pq_ss)

        @pl.when((step > 0) & (me_s == lax.rem(step + S - 1, S)))
        def _():
            node_forward_drain()

        @pl.when(me_s == t)
        def _():
            node_forward(step)

        @pl.when((me_s != t) & (step >= S))
        def _():
            prepare(t)

        @pl.when(jnp.logical_not((me_s == t) & works_here))
        def _():
            pass_on(step)

        @pl.when(t < S - 1)
        def _():
            @pl.when(step < S)
            def _():
                unpack_updates(t)

            spread_wait(scat, t, ag2_rs)
            edge_update(t)
            spread_wait(scat, t, ag2_ss)

        drain(mb_s, mb_ss, t, owner_d)
        return carry

    for hop, side in hops:
        ring_hop(0, side, hop)
    for side in range(2):
        ring_send(1, me_s, side, 0)
    load.wait()
    spread(pq_r, D, wcat, 0, ag_ss, ag_rs, pq_rs)
    lax.fori_loop(0, 2 * S, forward_step, 0)
    ring_drain()

    @pl.when(me_s != S - 1)
    def _():
        arrive(half_of(1, S - 1, 1 - core), sib_rs.at[1, S - 1])

    def edge_back(t):
        b2, n2 = lax.rem(t, 2), lax.rem(t + 1, 2)
        total = jnp.zeros((Q, EP), F32)
        for i in range(steps):
            chunk = pl.ds(i * RC, RC)
            carry = mm_bt(dcat[b2, chunk, pl.ds(0, D)], wcat[t, pl.ds(0, top), :])
            low = []
            for k in range(KC):
                rows = pl.ds(i * RC + k * Q, Q)
                low.append((dacc[rows, :] + carry[k * Q : (k + 1) * Q]).astype(BF16))
                de[n2, rows, :] = low[-1]
            dw = mm_bt(stacked(low), wo[t - 1])
            for k in range(KC):
                rows = pl.ds(i * RC + k * Q, Q)
                d = (gpe[t - 1, rows, :].astype(F32) * dw[k * Q : (k + 1) * Q]).astype(BF16)
                total = total + d.astype(F32)
                dcat[n2, rows, pl.ds(D, EP)] = d
        row_s[:, pl.ds(2 * D, EP)] = total.astype(BF16)
        x_s[:, pl.ds(D, EP)] = mm(oht[...], dcat[n2, :, pl.ds(D, EP)]).astype(BF16)

    def edge_pass(t):
        b3 = lax.rem(t, 2)
        for i in range(steps):
            rows = pl.ds(i * RC, RC)
            d = dcat[b3, rows, pl.ds(D, EP)]
            dacc[rows, :] = de[b3, rows, :].astype(F32) + mm_bt(d, scat[t, pl.ds(0, top), :])

    blocks = 2 * C
    my_block = lax.rem(me_s, 2) * C + me_d
    BW, HM, HU = msg_o.shape[2], msg_o.shape[1], upd_o.shape[1]

    def block_of(t, half, c, size):
        return eg.at[t, half, pl.ds(0, size), pl.ds(pl.multiple_of(c * BW, BW), BW)]

    def blocks_out(t, size):
        for k in range(blocks):
            @pl.when(k != my_block)
            def _():
                far(
                    block_of(t, k // C, k % C, size), eg_r.at[t, my_block, pl.ds(0, size)],
                    e1_ss.at[t, k], e1_rs.at[t, my_block], 2 * w + k // C, k % C,
                ).start()

    def edge_grads(t):
        grad = mm(edge_t[t, pl.ds(0, DE), :], dcat[lax.rem(t, 2), :, pl.ds(0, D)]).astype(BF16)
        for half in range(2):
            eg[t, half, pl.ds(0, HM), :] = grad[half * HM : (half + 1) * HM]

        @pl.when(t > 0)
        def _():
            n2 = lax.rem(t + 1, 2)
            edges = mm(edge_t[t - 1, pl.ds(0, DE), :], dcat[n2, :, pl.ds(D, EP)])
            outs = mm(act_t[t - 1, pl.ds(0, DE), :], de[n2])
            bias = jnp.sum(de[n2].astype(F32), axis=0, keepdims=True)
            grad = jnp.concatenate([edges, outs], axis=1).astype(BF16)
            eg[t, 0, pl.ds(HM, HU), :] = grad[:HU]
            eg[t, 1, pl.ds(HM, DE - HU), :] = grad[HU:]
            eg[t, 1, pl.ds(HM + DE - HU, 16), pl.ds(0, EP)] = jnp.broadcast_to(bias, (16, EP)).astype(BF16)
            eg[t, 1, pl.ds(HM + DE - HU, 16), pl.ds(EP, EP)] = jnp.zeros((16, EP), BF16)
            eg[t, 1, pl.ds(HM + DE - HU + 16, 2 * HU - DE - 16), :] = jnp.zeros((2 * HU - DE - 16, 2 * EP), BF16)
            blocks_out(t, HM + HU)

        @pl.when(t == 0)
        def _():
            blocks_out(t, HM)

    def blocks_sum(t, size):
        eg_r[t, my_block, pl.ds(0, size), :] = block_of(t, lax.rem(me_s, 2), me_d, size)[...]
        for k in range(blocks):
            @pl.when(k != my_block)
            def _():
                arrive(eg_r.at[t, k, pl.ds(0, size)], e1_rs.at[t, k])
                arrive(block_of(t, k // C, k % C, size), e1_ss.at[t, k])
        total = eg_r[t, 0, pl.ds(0, size), :].astype(F32)
        for k in range(1, blocks):
            total = total + eg_r[t, k, pl.ds(0, size), :].astype(F32)
        eg_b[t, pl.ds(0, size), :] = total.astype(BF16)
        push(eg_b.at[t, pl.ds(0, HM)], msg_o.at[me_s], e2_ss.at[0, t], e2_rs.at[0, me_s], t, me_d)
        if size > HM:
            push(eg_b.at[t, pl.ds(HM, HU)], upd_o.at[me_s], e2_ss.at[1, t], e2_rs.at[1, me_s], t - 1, me_d)

    def gather_blocks():
        for k in range(1, 4):
            j, sec, dpi = peer(k)
            rows = pl.ds(pl.multiple_of(j * Q, Q), Q)
            far(x_s.at[rows], x_r.at[q], x_ss, x_rs, sec, dpi).start()
        x_r[q] = x_s[pl.ds(pl.multiple_of(q * Q, Q), Q), :]

    def gather_wait():
        arrive(x_r.at[pl.ds(0, 3)], x_rs)
        arrive(x_s.at[pl.ds(0, 3 * Q)], x_ss)
        total = x_r[0].astype(F32)
        for j in range(1, 4):
            total = total + x_r[j].astype(F32)
        return total

    def message_back(t):
        b2 = lax.rem(t, 2)
        dm = dmb_r[...].astype(F32)
        total = jnp.zeros((Q, D), F32)
        for k in range(K):
            rows = pl.ds(k * Q, Q)
            d = (gp[t, rows, :].astype(F32) * dm).astype(BF16)
            total = total + d.astype(F32)
            dcat[b2, rows, pl.ds(0, D)] = d
        row_s[:, pl.ds(0, D)] = total.astype(BF16)
        x_s[:, pl.ds(0, D)] = mm(oht[...], dcat[b2, :, pl.ds(0, D)]).astype(BF16)

    def node_backward():
        @pl.when(me_s < S - 1)
        def _():
            arrive(dh1_r, dh_rs)

        def turn(n, carry):
            p = lax.rem(near + n, B)
            whole = at(p, 0, N)

            @pl.when(me_s < S - 1)
            def _():
                arrive(row_r.at[whole], row_rs.at[p])
                dn0 = mm_bt(row_r[whole, pl.ds(0, 2 * D)], pwn[...])
                dn3 = mm_bt(row_r[whole, pl.ds(2 * D, 2 * EP)], ep[...])
                for i in range(0, N, RB):
                    rows = at(p, i)
                    dn = dn3[i : i + RB]
                    dn3_s[rows, :] = dn
                    first = norm_back(dn0[i : i + RB], un0[rows, :], sc0[rows, :], parn[pl.ds(0, 1), :])
                    dh = (dh1_r[rows, :].astype(F32) + first).astype(BF16).astype(F32)
                    dh2_s[rows, :] = dh + norm_back(dn, un2[rows, :], sc2[rows, :], gains[2])

            @pl.when(me_s == S - 1)
            def _():
                dh2_s[whole, :] = cot[whole, :].astype(F32)

            dy = dh2_s[whole, :].astype(BF16)
            bwd[whole, pl.ds(D, D)] = dy
            da2 = jnp.zeros((N, D), F32)
            for c in range(chunks):
                cols = pl.ds(c * FC, FC)
                dv = mm_bt(dy, fo[cols, :])
                du = stacked(
                    [(slope_s[at(p, i), cols].astype(F32) * dv[i : i + RB]).astype(BF16) for i in range(0, N, RB)]
                )
                da2 = da2 + mm_bt(du, fi[:, cols])
            for i in range(0, N, RB):
                rows = at(p, i)
                block = da2[i : i + RB]
                da2_s[rows, :] = block
                dh1 = dh2_s[rows, :] + norm_back(block, un1[rows, :], sc1[rows, :], gains[1])
                dh1_f[rows, :] = dh1
                bwd[rows, pl.ds(0, D)] = (dh1 * (1.0 / K)).astype(BF16)
            dmb_s[whole, :] = mm_bt(bwd[whole, pl.ds(0, D)], mo[...]).astype(BF16)
            rows_out(p, dmb_s, dmb_r, dmb_ss, dmb_rs)
            return carry

        lax.fori_loop(0, B, turn, 0)

        @pl.when(me_s > 0)
        def _():
            dh1_s[...] = dh1_f[...].astype(BF16)
            far(dh1_s, dh1_r, dh_ss, dh_rs, me_s - 1, me_d).start()

        @pl.when(me_s < S - 1)
        def _():
            far(row_r.at[:, pl.ds(0, 2 * D)], dpqo_r, fw_ss, dpqo_rs, me_s + 1, me_d).start()
            drs = row_r[:, pl.ds(2 * D, 2 * EP)]
            bwd[:, pl.ds(2 * D, 2 * EP)] = drs
            dn = dn3_s[...]
            sg[pl.ds(11, 1), :] = col_sum(dn * un2[...])
            sg[pl.ds(12, 1), :] = col_sum(dn)
            sg[pl.ds(16, 1), pl.ds(0, EP)] = col_sum(drs[:, :EP].astype(F32))

        @pl.when(me_s == S - 1)
        def _():
            bwd[:, pl.ds(2 * D, 2 * EP)] = jnp.zeros((B * N, 2 * EP), BF16)
            sg[pl.ds(11, 1), :] = jnp.zeros((1, D), F32)
            sg[pl.ds(12, 1), :] = jnp.zeros((1, D), F32)
            sg[pl.ds(16, 1), pl.ds(0, EP)] = jnp.zeros((1, EP), F32)

        share(1, bwd, g_bwd)
        sg[pl.ds(13, 1), :] = col_sum(dh2_s[...])
        sg[pl.ds(8, 1), :] = col_sum(da2_s[...] * un1[...])
        sg[pl.ds(9, 1), :] = col_sum(da2_s[...])
        sg[pl.ds(10, 1), :] = col_sum(dh1_f[...])

    def node_backward_drain():
        rows_drain(dmb_s, dmb_ss)

        @pl.when(me_s > 0)
        def _():
            arrive(dh1_s, dh_ss)

        @pl.when(me_s < S - 1)
        def _():
            arrive(row_r.at[:, pl.ds(0, 2 * D)], fw_ss)

    dacc[...] = jnp.zeros_like(dacc)

    def backward_step(step, carry):
        t = S - 1 - step

        @pl.when(me_s == t)
        def _():
            node_backward()

        @pl.when(((t == S - 1) & (me_s >= S - 2)) | (me_s == t - 2))
        def _():
            prepare(me_s)

        @pl.when(t < S - 1)
        def _():
            edge_pass(t)

        @pl.when(t + 2 < S)
        def _():
            blocks_sum(t + 2, HM + HU)

        @pl.when(t == 0)
        def _():
            blocks_sum(1, HM + HU)

        arrive(dmb_r, dmb_rs)
        message_back(t)

        @pl.when(t > 0)
        def _():
            edge_back(t)

        @pl.when(t == 0)
        def _():
            x_s[:, pl.ds(D, EP)] = jnp.zeros((N, EP), BF16)

        gather_blocks()
        other = gather_wait().astype(BF16)
        row_s[:, pl.ds(D, D)] = other[:, :D]
        row_s[:, pl.ds(2 * D + EP, EP)] = other[:, D:]
        dpq = row_s.at[:, pl.ds(0, 2 * D)]

        @pl.when(t > 0)
        def _():
            push(row_s, row_r.at[pl.ds(my_row, Q)], row_ss, row_rs.at[slot], t - 1, owner_d)

        @pl.when(t == 0)
        def _():
            push(dpq, dpqo_r.at[pl.ds(my_row, Q)], row_ss, dpqo_rs, t, owner_d)

        edge_grads(t)

        @pl.when(t > 0)
        def _():
            drain(row_s, row_ss, t - 1, owner_d)

        @pl.when(t == 0)
        def _():
            drain(dpq, row_ss, t, owner_d)

        @pl.when(me_s == t)
        def _():
            node_backward_drain()

        return carry

    lax.fori_loop(0, S, backward_step, 0)

    arrive(dpqo_r, dpqo_rs)
    across = [pl.ds(p * N, N) for p in range(B)]
    for p in range(B):
        share_near(2 + p, dpqo_r.at[across[p]], lambda c, p=p: g_dpq.at[c, across[p]])
    dpq = dpqo_r[...]
    sg[pl.ds(2, 1), :] = col_sum(dpq[:, :D].astype(F32))
    dn = mm_bt(dpq, pw[...])
    unit = hi_s[...]
    sg[pl.ds(0, 1), :] = col_sum(dn * unit)
    sg[pl.ds(1, 1), :] = col_sum(dn)
    share(2 + B, sg, g_small)
    ig[...] = (dh1_f[...] + norm_back(dn, unit, sci[...], gains[0])).astype(BF16)
    blocks_sum(0, HM)
    for p in range(B):
        share_relay(2 + p, dpqo_r.at[across[p]], lambda c, p=p: g_dpq.at[c, across[p]])
    def combine(kind, src, final):
        for sec in range(S):
            arrive(src.at[sec], e2_rs.at[kind, sec])
        for half in range(2):
            total = src[half].astype(F32)
            for sec in range(half + 2, S, 2):
                total = total + src[sec].astype(F32)
            final[half] = total.astype(BF16)

    @pl.when(me_s < S - 1)
    def _():
        combine(1, upd_o, upd_f)

    @pl.when(me_s == S - 1)
    def _():
        upd_f[...] = jnp.zeros_like(upd_f)

    share(4 + B, upd_f, g_upd)
    combine(0, msg_o, msg_f)
    share(3 + B, msg_f, g_msg)
    for t in range(S):
        drain(eg_b.at[t, pl.ds(0, HM)], e2_ss.at[0, t], t, me_d)
        if t > 0:
            drain(eg_b.at[t, pl.ds(HM, HU)], e2_ss.at[1, t], t - 1, me_d)
    share_wait(0, fwd, g_fwd)
    share_wait(1, bwd, g_bwd)
    for p in range(B):
        share_near_wait(2 + p, dpqo_r.at[across[p]], lambda c, p=p: g_dpq.at[c, across[p]])
    share_wait(2 + B, sg, g_small)
    share_wait(3 + B, msg_f, g_msg)
    share_wait(4 + B, upd_f, g_upd)


def run_relay(dims, operands):
    S, B, N, K, Q, D, DE, EP, FF, C = dims
    R = K * Q
    BN = B * N
    tall = DE + N + Q
    vm = pl.BlockSpec(memory_space=pltpu.VMEM)
    hbm = pl.BlockSpec(memory_space=pl.ANY)
    dma = pltpu.SemaphoreType.DMA
    sds = jax.ShapeDtypeStruct
    BW = D // C
    tile = 32
    held = -(-(DE + 16) // tile) * tile
    scratch = [
        pltpu.VMEM((BN, D), F32),
        pltpu.VMEM((8, D), F32),
        pltpu.VMEM((1, EP), F32),
        pltpu.VMEM((S, DE, D), BF16),
        pltpu.VMEM((S, held, 2 * EP), BF16),
        pltpu.VMEM((BN, 4 * D), BF16),
        pltpu.VMEM((BN, 2 * D + 2 * EP), BF16),
        pltpu.VMEM((24, D), F32),
        pltpu.VMEM((S, 2, (DE + held) // 2, D), BF16),
        pltpu.VMEM((S, 2 * C, (DE + held) // 2, BW), BF16),
        pltpu.VMEM((S, (DE + held) // 2, BW), BF16),
        pltpu.VMEM((S, DE // 2, BW), BF16),
        pltpu.VMEM((2, DE // 2, BW), BF16),
        pltpu.VMEM((S, held // 2, BW), BF16),
        pltpu.VMEM((2, held // 2, BW), BF16),
        pltpu.VMEM((S, EP, EP), BF16),
        pltpu.VMEM((S, 16, EP), BF16),
        pltpu.VMEM((S, R, EP), BF16),
        pltpu.VMEM((S, tall, D), BF16),
        pltpu.VMEM((S, tall, EP), BF16),
        pltpu.VMEM((D, 2 * D), BF16),
        pltpu.VMEM((8, D), F32),
        pltpu.VMEM((BN, D), BF16),
        pltpu.VMEM((BN, D), BF16),
        pltpu.VMEM((Q, D), BF16),
        pltpu.VMEM((BN, D), BF16),
        pltpu.VMEM((BN, 2 * D), BF16),
        pltpu.VMEM((Q, 2 * D), BF16),
        pltpu.VMEM((BN, 2 * EP), BF16),
        pltpu.VMEM((Q, 2 * EP), BF16),
        pltpu.VMEM((BN, D), F32),
        pltpu.VMEM((BN, D), F32),
        pltpu.VMEM((BN, D), F32),
        pltpu.VMEM((BN, D), F32),
        pltpu.VMEM((BN, 1), F32),
        pltpu.VMEM((BN, 1), F32),
        pltpu.VMEM((BN, 1), F32),
        pltpu.VMEM((BN, 1), F32),
        pltpu.VMEM((BN, FF), F32),
        pltpu.VMEM((BN, FF), BF16),
        pltpu.VMEM((2, R, EP), BF16),
        pltpu.VMEM((R, EP), F32),
        pltpu.VMEM((S, R, D), BF16),
        pltpu.VMEM((S, R, EP), BF16),
        pltpu.VMEM((2, R, D + EP), BF16),
        pltpu.VMEM((S, EP, R), BF16),
        pltpu.VMEM((S, EP, R), BF16),
        pltpu.VMEM((N, D + EP), BF16),
        pltpu.VMEM((4, Q, D + EP), BF16),
        pltpu.VMEM((Q, 2 * D + 2 * EP), BF16),
        pltpu.VMEM((BN, 2 * D + 2 * EP), BF16),
        pltpu.VMEM((BN, 2 * D), BF16),
        pltpu.VMEM((BN, D), BF16),
        pltpu.VMEM((Q, D), BF16),
        pltpu.VMEM((BN, D), BF16),
        pltpu.VMEM((BN, D), BF16),
        pltpu.VMEM((BN, D), F32),
        pltpu.VMEM((BN, D), F32),
        pltpu.VMEM((BN, D), F32),
        pltpu.VMEM((BN, D), F32),
        pltpu.VMEM((BN, D), F32),
        pltpu.VMEM((BN, D), BF16),
        dma, dma((2,)), dma((2,)), dma, dma,
        dma, dma, dma, dma, dma, dma, dma, dma,
        dma, dma((B,)), dma, dma, dma, dma((B,)), dma,
        dma, dma, dma, dma, dma,
        dma((S, 2 * C)), dma((S, 2 * C)), dma((2, S)), dma((2, S)), dma((5 + B, C)), dma((5 + B, C)),
        dma((B, C // 2)), dma((2, 2, S // 2)), dma((2, S)), dma((2, S)), dma((2, S)),
    ]
    return pl.pallas_call(
        functools.partial(relay_kernel, dims),
        out_shape=(
            sds((BN, D), BF16),
            sds((BN, D), BF16),
            sds((C, BN, 4 * D), BF16),
            sds((C, BN, 2 * D + 2 * EP), BF16),
            sds((C, BN, 2 * D), BF16),
            sds((C, 24, D), F32),
            sds((C, 2, DE // 2, BW), BF16),
            sds((C, 2, held // 2, BW), BF16),
        ),
        in_specs=[hbm, vm, pl.BlockSpec(memory_space=pltpu.SMEM)] + [vm] * 16,
        out_specs=(vm,) * 2 + (hbm,) * 6,
        scratch_shapes=scratch,
        compiler_params=pltpu.CompilerParams(
            collective_id=0, has_side_effects=True, vmem_limit_bytes=62 * 1024 * 1024
        ),
    )(*operands)


def gradient_kernel(
    dims,
    fwd, bwd, dpq, small, edge, upd, fi, fo, fb, act, ig,
    g_pair, g_edge, g_out, g_fi, g_fo, g_ep, g_self, g_eout, g_gain, g_shift, g_nb, g_fb, g_eb, act_out, ig_out,
    fwd_v, bwd_v, dpq_v, fi_v, fo_v, gfi_v, gfo_v, pair_v, out_v, edge_v, upd_v, in_sems, sems,
):
    S, B, N, K, Q, D, DE, EP, FF, C = dims
    chunks = 4
    FC = FF // chunks

    def part(c, size=D):
        return pl.ds(c * size, size)

    loads = {}

    def load(name, src, dst):
        loads[name] = pltpu.make_async_copy(src, dst, in_sems.at[len(loads)])
        loads[name].start()

    load("a2", fwd.at[:, part(2)], fwd_v.at[2])
    load("dy", bwd.at[:, part(1)], bwd_v.at[1])
    for c in range(chunks):
        load(("fi", c), fi.at[:, part(c, FC)], fi_v.at[c])
        load(("fo", c), fo.at[part(c, FC)], fo_v.at[c])
    load("a1", fwd.at[:, part(0)], fwd_v.at[0])
    load("dpq0", dpq.at[:, part(0)], dpq_v.at[0])
    load("dpq1", dpq.at[:, part(1)], dpq_v.at[1])
    load("mbar", fwd.at[:, part(1)], fwd_v.at[1])
    load("dmsg", bwd.at[:, part(0)], bwd_v.at[0])
    load("a3", fwd.at[:, part(3)], fwd_v.at[3])
    load("drs", bwd.at[:, part(2)], bwd_v.at[2])
    load("edge", edge, edge_v)
    load("upd", upd, upd_v)
    stores = []

    def out(src, dst):
        copy = pltpu.make_async_copy(src, dst, sems.at[len(stores)])
        copy.start()
        stores.append(copy)

    out(act, act_out)
    out(ig, ig_out)
    loads["a2"].wait()
    loads["dy"].wait()
    a2 = fwd_v[2]
    dy = bwd_v[1]
    for c in range(chunks):
        cols = part(c, FC)
        loads["fi", c].wait()
        loads["fo", c].wait()
        value, slope = gelu_both(mm(a2, fi_v[c]) + fb[:, cols])
        du = (slope * mm_bt(dy, fo_v[c])).astype(BF16)
        g_fb[:, cols] = col_sum(du.astype(F32))
        gfi_v[c] = mm_at(a2, du)
        out(gfi_v.at[c], g_fi.at[0, :, cols])
        gfo_v[c] = mm_at(value.astype(BF16), dy)
        out(gfo_v.at[c], g_fo.at[0, cols])
    loads["a1"].wait()
    for c in range(2):
        loads["dpq%d" % c].wait()
        pair_v[c] = mm_at(fwd_v[0], dpq_v[c])
        out(pair_v.at[c], g_pair.at[0, :, part(c)])
    loads["mbar"].wait()
    loads["dmsg"].wait()
    out_v[...] = mm_at(fwd_v[1], bwd_v[0]) * float(K)
    out(out_v, g_out.at[0])
    loads["a3"].wait()
    loads["drs"].wait()
    ends = mm_at(fwd_v[3], bwd_v[2])
    g_ep[0] = jnp.concatenate([ends[:, :DE], ends[:, EP : EP + DE]], axis=1)
    total = small[0]
    for c in range(1, C):
        total = total + small[c]
    for i, rows in enumerate(((0, 1, 2), (8, 9, 10), (11, 12, 13))):
        g_gain[i] = total[rows[0] : rows[0] + 1]
        g_shift[i] = total[rows[1] : rows[1] + 1]
        g_nb[i] = total[rows[2] : rows[2] + 1]
    g_eb[0, pl.ds(0, 1), :] = total[16:17, :DE]
    loads["edge"].wait()
    loads["upd"].wait()
    BW = edge_v.shape[3]
    for c in range(C):
        for half in range(2):
            block = edge_v[c, half].astype(F32)
            g_edge[0, pl.ds(half * (DE // 2), DE // 2), pl.ds(c * BW, BW)] = block
        block = stacked([upd_v[c, 0], upd_v[c, 1]]).astype(F32)
        first = c * BW
        for array, begin in ((g_self, 0), (g_eout, EP)):
            low, high = max(first, begin), min(first + BW, begin + DE)
            if low < high:
                array[0, :, pl.ds(low - begin, high - low)] = block[:DE, low - first : high - first]
        low, high = first, min(first + BW, DE)
        if low < high:
            g_eb[0, pl.ds(1, 1), pl.ds(low, high - low)] = block[DE : DE + 1, low - first : high - first]
    for copy in stores:
        copy.wait()


def run_gradients(dims, operands):
    S, B, N, K, Q, D, DE, EP, FF, C = dims
    rows = C * B * N
    BW = D // C
    held = operands[5].shape[2]
    vm = pl.BlockSpec(memory_space=pltpu.VMEM)
    hbm = pl.BlockSpec(memory_space=pl.ANY)
    sds = jax.ShapeDtypeStruct
    shapes = (
        (1, D, 2 * D), (1, DE, D), (1, D, D), (1, D, FF), (1, FF, D), (1, D, 2 * DE), (1, DE, DE), (1, DE, DE),
        (3, 1, D), (3, 1, D), (3, 1, D), (1, FF), (1, 2, DE),
    )
    return pl.pallas_call(
        functools.partial(gradient_kernel, dims),
        out_shape=tuple(sds(shape, F32) for shape in shapes) + (sds((1, B, N, D), BF16),) * 2,
        in_specs=[hbm, hbm, hbm, vm, hbm, hbm, hbm, hbm, vm, hbm, hbm],
        out_specs=(hbm, vm, hbm, hbm, hbm) + (vm,) * 8 + (hbm,) * 2,
        scratch_shapes=[
            pltpu.VMEM((4, rows, D), BF16),
            pltpu.VMEM((3, rows, D), BF16),
            pltpu.VMEM((2, rows, D), BF16),
            pltpu.VMEM((4, D, FF // 4), BF16),
            pltpu.VMEM((4, FF // 4, D), BF16),
            pltpu.VMEM((4, D, FF // 4), F32),
            pltpu.VMEM((4, FF // 4, D), F32),
            pltpu.VMEM((2, D, D), F32),
            pltpu.VMEM((D, D), F32),
            pltpu.VMEM((C, 2, DE // 2, BW), BF16),
            pltpu.VMEM((C, 2, held, BW), BF16),
            pltpu.SemaphoreType.DMA((19,)),
            pltpu.SemaphoreType.DMA((13,)),
        ],
        compiler_params=pltpu.CompilerParams(vmem_limit_bytes=56 * 1024 * 1024),
    )(*operands)


def stationary(
    clean_nodes, noise_nodes, edge_feats, neighbours, time_bins, cotangent,
    pair_weight, message_edge, message_out, ffn_in, ffn_out, edge_pair, edge_self, edge_out,
    norm_gain, norm_shift, node_bias, ffn_bias, edge_bias,
):
    S = lax.axis_size("section")
    place = lax.axis_index("section")
    column = lax.axis_index("dp")
    B, N, D = clean_nodes.shape
    K, DE = edge_feats.shape[2:]
    FF = ffn_in.shape[2]
    Q = N // 4
    EP = DE + N
    core = column % 2
    w = place // 2
    slab = (place % 2) * 2 * Q

    node_ids = jnp.arange(N, dtype=jnp.int32)
    both = [
        lax.dynamic_slice(array, (w % B, slab) + (0,) * (array.ndim - 2), (1, 2 * Q) + array.shape[2:])[0]
        for array in (edge_feats, neighbours)
    ]
    chosen = (both[1][:, :, None] == node_ids).astype(BF16)
    both = jnp.concatenate([both[0], chosen], axis=2)
    mine = lax.dynamic_slice_in_dim(both, core * Q, Q, 0)
    theirs = lax.dynamic_slice_in_dim(both, (1 - core) * Q, Q, 0)
    got = lax.ppermute(theirs, "dp", [(i, i ^ 1) for i in range(lax.axis_size("dp"))])
    ecat0 = jnp.swapaxes(jnp.where(w // B == core, mine, got), 0, 1).reshape(K * Q, EP)
    oht = jnp.transpose(ecat0[:, DE:])
    phase = (time_bins.astype(F32) + 0.5) * (math.pi * 0.5 / TBINS)
    mix = jnp.cos(phase[None] - jnp.array([[0.0], [math.pi * 0.5]], F32))

    def by_rows(array):
        return jnp.transpose(array, (1, 0, 2))

    def widen(array, size, axis=-1):
        extra = [(0, 0)] * array.ndim
        extra[axis] = (0, size - array.shape[axis])
        return jnp.pad(array, extra)

    ep = jnp.concatenate([widen(edge_pair[0, :, :DE], EP), widen(edge_pair[0, :, DE:], EP)], axis=1)
    C = lax.axis_size("dp")
    dims = (S, B, N, K, Q, D, DE, EP, FF, C)
    act, ig, g_fwd, g_bwd, g_dpq, g_small, g_msg, g_upd = run_relay(
        dims,
        (
            ecat0, oht, mix, clean_nodes.reshape(B * N, D), noise_nodes.reshape(B * N, D),
            cotangent.reshape(B * N, D), pair_weight[0], message_out[0], ffn_in[0], ffn_out[0], ep,
            by_rows(norm_gain), by_rows(norm_shift), by_rows(node_bias), ffn_bias, edge_bias[0],
            message_edge[0], edge_self[0], edge_out[0],
        ),
    )
    grads = run_gradients(
        dims,
        (
            g_fwd.reshape(C * B * N, -1), g_bwd.reshape(C * B * N, -1), g_dpq.reshape(C * B * N, -1),
            g_small, g_msg, g_upd, ffn_in[0], ffn_out[0], ffn_bias, act.reshape(1, B, N, D), ig.reshape(1, B, N, D),
        ),
    )
    grads, outs = list(grads[:-2]), tuple(grads[-2:])
    grads[8:11] = [by_rows(array) for array in grads[8:11]]
    return outs + tuple(grads)


def solution(mesh):
    sections, copies = mesh.shape["section"], mesh.shape["dp"]

    def body(*args):
        B, N = args[0].shape[:2]
        fits = sections == 4 * B and copies % 2 == 0 and N % 64 == 0
        return stationary(*args) if fits else on_device(*args)

    placed = (
        P("dp", None, None),
        P("dp", None, None),
        P("dp", None, None, None),
        P("dp", None, None),
        P("dp"),
        P("dp", None, None),
        P("section", None, None),
        P("section", None, None),
        P("section", None, None),
        P("section", None, None),
        P("section", None, None),
        P("section", None, None),
        P("section", None, None),
        P("section", None, None),
        P("section", None, None),
        P("section", None, None),
        P("section", None, None),
        P("section", None),
        P("section", None, None),
    )
    return jax.shard_map(
        body,
        mesh=mesh,
        in_specs=placed,
        out_specs=(
            P("section", "dp", None, None),
            P("section", "dp", None, None),
            P("section", None, None),
            P("section", None, None),
            P("section", None, None),
            P("section", None, None),
            P("section", None, None),
            P("section", None, None),
            P("section", None, None),
            P("section", None, None),
            P("section", None, None),
            P("section", None, None),
            P("section", None, None),
            P("section", None),
            P("section", None, None),
        ),
        check_vma=False,
    )
```

```python
import functools
import math

import jax
import jax.numpy as jnp
from jax import lax
from jax.experimental import pallas as pl
from jax.experimental.pallas import tpu as pltpu
from jax.sharding import PartitionSpec as P

TBINS = 100


def from_behind(block, axis, distance):
    devices = range(lax.axis_size(axis))
    route = [(i - distance, i) for i in devices if i - distance in devices]
    return lax.ppermute(block, axis, route)


def for_sending(value):
    return jax.tree.map(lambda a: a.astype(jnp.bfloat16) if a.dtype == jnp.float32 else a, value)


def layer_norm(value, gain, shift):
    centre = jnp.mean(value, axis=-1, keepdims=True)
    centred = value - centre
    spread = jnp.mean(centred * centred, axis=-1, keepdims=True)
    return centred * lax.rsqrt(spread + 1e-05) * gain + shift


def forward_layer(weights, hidden, edge_state, nearest):
    (
        pair_w,
        msg_edge,
        msg_out,
        ffn_w_in,
        ffn_w_out,
        edge_pair_w,
        edge_self_w,
        edge_out_w,
        gains,
        shifts,
        node_b,
        ffn_b,
        edge_b,
    ) = weights
    width = msg_out.shape[0]
    edge_width = edge_self_w.shape[0]
    normed_one = layer_norm(hidden, gains[0], shifts[0]).astype(jnp.bfloat16)
    pair_out = jnp.dot(normed_one, pair_w, preferred_element_type=jnp.float32)
    before_act = (
        pair_out[:, None, :width]
        + jnp.take(pair_out[:, width:], nearest, axis=0)
        + jnp.einsum("nkc,cd->nkd", edge_state, msg_edge, preferred_element_type=jnp.float32)
        + node_b[0]
    )
    message_act = jax.nn.gelu(before_act).astype(jnp.bfloat16)
    message_all = jnp.einsum(
        "nkc,cd->nkd", message_act, msg_out, preferred_element_type=jnp.float32
    )
    after_msg = hidden + jnp.mean(message_all, axis=1) + node_b[1]
    normed_two = layer_norm(after_msg, gains[1], shifts[1]).astype(jnp.bfloat16)
    ffn_pre = jnp.dot(normed_two, ffn_w_in, preferred_element_type=jnp.float32) + ffn_b
    ffn_act = jax.nn.gelu(ffn_pre).astype(jnp.bfloat16)
    after_ffn = (
        after_msg + jnp.dot(ffn_act, ffn_w_out, preferred_element_type=jnp.float32) + node_b[2]
    )
    normed_three = layer_norm(after_ffn, gains[2], shifts[2]).astype(jnp.bfloat16)
    edge_pairs = jnp.dot(normed_three, edge_pair_w, preferred_element_type=jnp.float32)
    edge_pre = (
        edge_pairs[:, None, :edge_width]
        + jnp.take(edge_pairs[:, edge_width:], nearest, axis=0)
        + jnp.einsum("nkc,cd->nkd", edge_state, edge_self_w, preferred_element_type=jnp.float32)
        + edge_b[0]
    )
    edge_act = jax.nn.gelu(edge_pre).astype(jnp.bfloat16)
    edge_next = (
        edge_state.astype(jnp.float32)
        + jnp.einsum("nkc,cd->nkd", edge_act, edge_out_w, preferred_element_type=jnp.float32)
        + edge_b[1]
    )
    saved = (
        normed_one,
        before_act,
        message_act,
        after_msg,
        normed_two,
        ffn_pre,
        ffn_act,
        after_ffn,
        normed_three,
        edge_pre,
        edge_act,
    )
    return (after_ffn, edge_next, saved)


def backward_layer(weights, hidden, edge_state, nearest, grad_nodes_out, grad_edges_out):
    (
        pair_w,
        msg_edge,
        msg_out,
        ffn_w_in,
        ffn_w_out,
        edge_pair_w,
        edge_self_w,
        edge_out_w,
        gains,
        shifts,
        node_b,
        ffn_b,
        edge_b,
    ) = weights
    unused_nodes, unused_edges, saved = forward_layer(weights, hidden, edge_state, nearest)
    (
        normed_one,
        before_act,
        message_act,
        after_msg,
        normed_two,
        ffn_pre,
        ffn_act,
        after_ffn,
        normed_three,
        edge_pre,
        edge_act,
    ) = saved
    width = msg_out.shape[0]
    edge_width = edge_self_w.shape[0]
    count = nearest.shape[1]
    node_count = hidden.shape[0]
    one_hot = (
        nearest.reshape(-1)[None, :] == jnp.arange(node_count, dtype=jnp.int32)[:, None]
    ).astype(jnp.bfloat16)
    edge_grad_low = grad_edges_out.astype(jnp.bfloat16)
    grad_edge_b1 = jnp.sum(grad_edges_out, axis=(0, 1))
    grad_edge_out_w = jnp.einsum(
        "nkc,nkd->cd", edge_act, edge_grad_low, preferred_element_type=jnp.float32
    )
    edge_act_grad = jnp.einsum(
        "nkd,cd->nkc", edge_grad_low, edge_out_w, preferred_element_type=jnp.float32
    )
    unused_value, gelu_edge = jax.vjp(jax.nn.gelu, edge_pre)
    edge_pre_grad = gelu_edge(edge_act_grad)[0].astype(jnp.bfloat16)
    grad_edge_b0 = jnp.sum(edge_pre_grad, axis=(0, 1), dtype=jnp.float32)
    grad_edge_self_w = jnp.einsum(
        "nkc,nkd->cd", edge_state, edge_pre_grad, preferred_element_type=jnp.float32
    )
    edge_total = grad_edges_out + jnp.einsum(
        "nkd,cd->nkc", edge_pre_grad, edge_self_w, preferred_element_type=jnp.float32
    )
    own_edge = jnp.sum(edge_pre_grad, axis=1, dtype=jnp.float32)
    other_edge = jnp.dot(
        one_hot, edge_pre_grad.reshape(-1, edge_width), preferred_element_type=jnp.float32
    )
    pairs_grad = jnp.concatenate([own_edge, other_edge], axis=-1).astype(jnp.bfloat16)
    grad_edge_pair_w = jnp.einsum(
        "nc,nd->cd", normed_three, pairs_grad, preferred_element_type=jnp.float32
    )
    normed_three_grad = jnp.einsum(
        "nd,cd->nc", pairs_grad, edge_pair_w, preferred_element_type=jnp.float32
    )
    unused_value, norm_three_back = jax.vjp(layer_norm, after_ffn, gains[2], shifts[2])
    ffn_side, gain_three, shift_three = norm_three_back(normed_three_grad)
    after_ffn_grad = grad_nodes_out + ffn_side
    grad_node_b2 = jnp.sum(after_ffn_grad, axis=0)
    ffn_out_grad = after_ffn_grad.astype(jnp.bfloat16)
    grad_ffn_w_out = jnp.einsum(
        "nc,nd->cd", ffn_act, ffn_out_grad, preferred_element_type=jnp.float32
    )
    ffn_act_grad = jnp.einsum(
        "nd,cd->nc", ffn_out_grad, ffn_w_out, preferred_element_type=jnp.float32
    )
    unused_value, gelu_ffn = jax.vjp(jax.nn.gelu, ffn_pre)
    ffn_pre_grad = gelu_ffn(ffn_act_grad)[0].astype(jnp.bfloat16)
    grad_ffn_b = jnp.sum(ffn_pre_grad, axis=0, dtype=jnp.float32)
    grad_ffn_w_in = jnp.einsum(
        "nc,nd->cd", normed_two, ffn_pre_grad, preferred_element_type=jnp.float32
    )
    normed_two_grad = jnp.einsum(
        "nd,cd->nc", ffn_pre_grad, ffn_w_in, preferred_element_type=jnp.float32
    )
    unused_value, norm_two_back = jax.vjp(layer_norm, after_msg, gains[1], shifts[1])
    msg_side, gain_two, shift_two = norm_two_back(normed_two_grad)
    after_msg_grad = after_ffn_grad + msg_side
    grad_node_b1 = jnp.sum(after_msg_grad, axis=0)
    message_grad = (after_msg_grad / count).astype(jnp.bfloat16)
    grad_msg_out = jnp.einsum(
        "nkc,nd->cd", message_act, message_grad, preferred_element_type=jnp.float32
    )
    message_act_grad = jnp.einsum(
        "nd,cd->nc", message_grad, msg_out, preferred_element_type=jnp.float32
    )
    unused_value, gelu_msg = jax.vjp(jax.nn.gelu, before_act)
    before_grad = gelu_msg(jnp.broadcast_to(message_act_grad[:, None, :], before_act.shape))[
        0
    ].astype(jnp.bfloat16)
    grad_node_b0 = jnp.sum(before_grad, axis=(0, 1), dtype=jnp.float32)
    grad_msg_edge = jnp.einsum(
        "nkc,nkd->cd", edge_state, before_grad, preferred_element_type=jnp.float32
    )
    edge_total = edge_total + jnp.einsum(
        "nkd,cd->nkc", before_grad, msg_edge, preferred_element_type=jnp.float32
    )
    own_node = jnp.sum(before_grad, axis=1, dtype=jnp.float32)
    other_node = jnp.dot(
        one_hot, before_grad.reshape(-1, width), preferred_element_type=jnp.float32
    )
    pair_grad = jnp.concatenate([own_node, other_node], axis=-1).astype(jnp.bfloat16)
    grad_pair_w = jnp.einsum("nc,nd->cd", normed_one, pair_grad, preferred_element_type=jnp.float32)
    normed_one_grad = jnp.einsum("nd,cd->nc", pair_grad, pair_w, preferred_element_type=jnp.float32)
    unused_value, norm_one_back = jax.vjp(layer_norm, hidden, gains[0], shifts[0])
    input_side, gain_one, shift_one = norm_one_back(normed_one_grad)
    hidden_grad = after_msg_grad + input_side
    grads = (
        grad_pair_w,
        grad_msg_edge,
        grad_msg_out,
        grad_ffn_w_in,
        grad_ffn_w_out,
        grad_edge_pair_w,
        grad_edge_self_w,
        grad_edge_out_w,
        jnp.stack([gain_one, gain_two, gain_three]),
        jnp.stack([shift_one, shift_two, shift_three]),
        jnp.stack([grad_node_b0, grad_node_b1, grad_node_b2]),
        grad_ffn_b,
        jnp.stack([grad_edge_b0, grad_edge_b1]),
    )
    return (hidden_grad.astype(jnp.bfloat16), edge_total.astype(jnp.bfloat16), grads)


def on_device(
    clean_nodes,
    noise_nodes,
    edge_feats,
    neighbours,
    time_bins,
    cotangent,
    pair_weight,
    message_edge,
    message_out,
    ffn_in,
    ffn_out,
    edge_pair,
    edge_self,
    edge_out,
    norm_gain,
    norm_shift,
    node_bias,
    ffn_bias,
    edge_bias,
):
    sections = lax.axis_size("section")
    place = lax.axis_index("section")
    weights = tuple(
        (
            item[0]
            for item in (
                pair_weight,
                message_edge,
                message_out,
                ffn_in,
                ffn_out,
                edge_pair,
                edge_self,
                edge_out,
                norm_gain,
                norm_shift,
                node_bias,
                ffn_bias,
                edge_bias,
            )
        )
    )
    batches, node_count, width = clean_nodes.shape
    phase = (time_bins.astype(jnp.float32) + 0.5) * (math.pi * 0.5 / TBINS)
    start = jnp.cos(phase)[:, None, None] * clean_nodes.astype(jnp.float32) + jnp.sin(phase)[
        :, None, None
    ] * noise_nodes.astype(jnp.float32)
    zero_nodes = jnp.zeros((node_count, width), jnp.bfloat16)
    zero_edges = jnp.zeros(edge_feats.shape[1:], jnp.bfloat16)
    is_first = place == 0
    is_last = place == sections - 1

    def forward_step(step_index, carry):
        recv_nodes, recv_edges, back_nodes, kept_nodes, kept_edges, section_outs = carry
        item = step_index - place
        first_pass = (item >= 0) & (item < batches)
        second_pass = (item >= sections) & (item < sections + batches)
        index = jnp.clip(jnp.where(second_pass, item - sections, item), 0, batches - 1)
        predicted = back_nodes
        own_start = lax.dynamic_index_in_dim(start, index, 0, keepdims=False)
        lead_nodes = own_start + jnp.where(second_pass, predicted.astype(jnp.float32), 0.0)
        nodes_in = jnp.where(is_first, lead_nodes, recv_nodes.astype(jnp.float32))
        edges_in = jnp.where(
            is_first, lax.dynamic_index_in_dim(edge_feats, index, 0, keepdims=False), recv_edges
        )
        nearest = lax.dynamic_index_in_dim(neighbours, index, 0, keepdims=False)

        def run_layer(operand):
            after, edge_next, saved = forward_layer(weights, operand[0], operand[1], operand[2])
            return (after.astype(jnp.bfloat16), edge_next.astype(jnp.bfloat16))

        def skip_layer(operand):
            return (zero_nodes, zero_edges)

        out_nodes, out_edges = lax.cond(
            first_pass | second_pass, run_layer, skip_layer, (nodes_in, edges_in, nearest)
        )
        kept_nodes = lax.dynamic_update_index_in_dim(
            kept_nodes, jnp.where(second_pass, nodes_in, kept_nodes[index]), index, 0
        )
        kept_edges = lax.dynamic_update_index_in_dim(
            kept_edges, jnp.where(second_pass, edges_in, kept_edges[index]), index, 0
        )
        section_outs = lax.dynamic_update_index_in_dim(
            section_outs, jnp.where(second_pass, out_nodes, section_outs[index]), index, 0
        )
        recv_nodes, recv_edges = from_behind((out_nodes, out_edges), "section", 1)
        back_nodes = from_behind(out_nodes, "section", 1 - sections)
        return (recv_nodes, recv_edges, back_nodes, kept_nodes, kept_edges, section_outs)

    forward_init = (
        zero_nodes,
        zero_edges,
        zero_nodes,
        jnp.zeros((batches, node_count, width), jnp.float32),
        jnp.zeros_like(edge_feats),
        jnp.zeros((batches, node_count, width), jnp.bfloat16),
    )
    unused_nodes, unused_edges, unused_back, kept_nodes, kept_edges, section_outs = lax.fori_loop(
        0, 2 * sections + batches - 1, forward_step, forward_init
    )
    grads_zero = tuple((jnp.zeros(item.shape, jnp.float32) for item in weights))

    def backward_step(step_index, carry):
        recv_grad_nodes, recv_grad_edges, grads, input_grads = carry
        item = step_index - (sections - 1 - place)
        live = (item >= 0) & (item < batches)
        index = jnp.clip(item, 0, batches - 1)
        nodes_grad_out = jnp.where(
            is_last,
            lax.dynamic_index_in_dim(cotangent, index, 0, keepdims=False).astype(jnp.float32),
            recv_grad_nodes.astype(jnp.float32),
        )
        edges_grad_out = jnp.where(is_last, 0.0, recv_grad_edges.astype(jnp.float32))
        nearest = lax.dynamic_index_in_dim(neighbours, index, 0, keepdims=False)

        def run_back(operand):
            return backward_layer(
                weights, operand[0], operand[1], operand[2], operand[3], operand[4]
            )

        def skip_back(operand):
            return (zero_nodes, zero_edges, grads_zero)

        nodes_grad, edges_grad, terms = lax.cond(
            live,
            run_back,
            skip_back,
            (kept_nodes[index], kept_edges[index], nearest, nodes_grad_out, edges_grad_out),
        )
        grads = tuple((total + term for total, term in zip(grads, terms)))
        input_grads = lax.dynamic_update_index_in_dim(
            input_grads, jnp.where(live, nodes_grad, input_grads[index]), index, 0
        )
        recv_grad_nodes, recv_grad_edges = from_behind((nodes_grad, edges_grad), "section", -1)
        return (recv_grad_nodes, recv_grad_edges, grads, input_grads)

    backward_init = (
        zero_nodes,
        zero_edges,
        grads_zero,
        jnp.zeros((batches, node_count, width), jnp.bfloat16),
    )
    unused_grad_nodes, unused_grad_edges, grads, input_grads = lax.fori_loop(
        0, sections + batches - 1, backward_step, backward_init
    )
    totals = jax.tree.map(lambda part: part.astype(jnp.float32), lax.psum(for_sending(grads), "dp"))
    return (
        section_outs[None],
        input_grads[None],
        totals[0][None],
        totals[1][None],
        totals[2][None],
        totals[3][None],
        totals[4][None],
        totals[5][None],
        totals[6][None],
        totals[7][None],
        totals[8][None],
        totals[9][None],
        totals[10][None],
        totals[11][None],
        totals[12][None],
    )


BF16 = jnp.bfloat16
F32 = jnp.float32
MESH = pl.DeviceIdType.MESH
GELU_A = 0.7978845608028654
GELU_B = 0.044715


def gelu(x):
    return 0.5 * x * (1.0 + jnp.tanh(x * (GELU_A + (GELU_A * GELU_B) * (x * x))))


def gelu_both(x):
    square = x * x
    t = jnp.tanh(x * (GELU_A + (GELU_A * GELU_B) * square))
    half = 0.5 * (1.0 + t)
    slope = half + (0.5 * x) * (1.0 - t * t) * (GELU_A + (3.0 * GELU_A * GELU_B) * square)
    return x * half, slope


def mm(a, b):
    return jnp.dot(a, b, preferred_element_type=F32)


def mm_bt(a, b):
    return lax.dot_general(a, b, (((1,), (1,)), ((), ())), preferred_element_type=F32)


def mm_at(a, b):
    return lax.dot_general(a, b, (((0,), (0,)), ((), ())), preferred_element_type=F32)


def stacked(blocks):
    return jnp.concatenate(blocks, axis=0)


def row_mean(x):
    return jnp.mean(x, axis=-1, keepdims=True)


def normed(x):
    centred = x - row_mean(x)
    scale = lax.rsqrt(row_mean(centred * centred) + 1e-05)
    return centred * scale, scale


def norm_back(grad, unit, scale, gain):
    t = grad * gain
    return scale * (t - row_mean(t) - unit * row_mean(t * unit))


def col_sum(x):
    return jnp.sum(x, axis=0, keepdims=True)


def protein_on(plane, B):
    if B != 2:
        return plane
    return jnp.where(plane == 0, 0, jnp.where(plane == 3, 1, plane + 1))


def plane_of(protein, B):
    if B != 2:
        return protein
    return jnp.where(protein == 0, 0, jnp.where(protein == 1, 3, protein - 1))


def relay_kernel(
    dims,
    ecat0, oht, mix, clean, noise, cot, pw, mo, fi, fo, ep, gains, shifts, node_b, fb, edge_b, we_own, ws_own, wo_own,
    act, ig, g_fwd, g_bwd, g_dpq, g_small, g_msg, g_upd,
    start, par, eb0, wall_msg, wall_upd, fwd, bwd, sg,
    eg, eg_r, eg_b, msg_o, msg_f, upd_o, upd_f, wo, eb1,
    ecat, wcat, scat, pwn, parn, hin_r, hst, mb_s, mb_r, pq_s, pq_r, rq_s, rq_r,
    un0, un1, un2, hi_s, sc0, sc1, sc2, sci, u_s, slope_s, de, dacc, gp, gpe, dcat, act_t, edge_t,
    x_s, x_r, row_s, row_r, dpqo_r, dmb_s, dmb_r, dh1_s, dh1_r, dh1_f, dh2_s, dn3_s, da2_s, h1_s, a1_s,
    ld_sem, nx_ss, nx_rs, hop_ss, hop_rs,
    pq_ss, pq_rs, ag_ss, ag_rs, rq_ss, rq_rs, ag2_ss, ag2_rs,
    mb_ss, mb_rs, x_ss, x_rs, row_ss, row_rs, dpqo_rs, fw_ss, dmb_ss, dmb_rs, dh_ss, dh_rs,
    e1_ss, e1_rs, e2_ss, e2_rs, g_ss, g_rs, relay_ss, ring_ss, ring_rs, sib_ss, sib_rs,
):
    S, B, N, K, Q, D, DE, EP, FF, C = dims
    BN = B * N
    RB = 16
    top = DE + N
    me_s = lax.axis_index("section")
    me_d = lax.axis_index("dp")
    core = lax.rem(me_d, 2)
    pair = me_d - core
    w = lax.div(me_s, 2)
    q = 2 * lax.rem(me_s, 2) + core
    protein = protein_on(w, B)
    owner_d = pair + lax.div(protein, B)
    slot = lax.rem(protein, B)
    my_row = pl.multiple_of(slot * N + q * Q, Q)
    own_rows = pl.ds(top, Q)

    def quarter(j):
        return pl.ds(pl.multiple_of(DE + j * Q, Q), Q)

    def is_me(sec, dpi):
        return (sec == me_s) & (dpi == me_d)

    def far(src, dst, ssem, rsem, sec, dpi):
        return pltpu.make_async_remote_copy(
            src_ref=src, dst_ref=dst, send_sem=ssem, recv_sem=rsem,
            device_id={"section": sec, "dp": dpi}, device_id_type=MESH,
        )

    def push(src, dst, ssem, rsem, sec, dpi):
        lax.cond(
            is_me(sec, dpi),
            lambda: pltpu.make_async_copy(src, dst, rsem).start(),
            lambda: far(src, dst, ssem, rsem, sec, dpi).start(),
        )

    def arrive(ref, sem):
        pltpu.make_async_copy(ref, ref, sem).wait()

    def drain(ref, sem, sec, dpi):
        @pl.when(jnp.logical_not(is_me(sec, dpi)))
        def _():
            arrive(ref, sem)

    def worker_of(p, j):
        return 2 * plane_of(core * B + p, B) + j // 2, pair + j % 2

    def peer(k):
        j = lax.rem(q + k, 4)
        return j, 2 * w + lax.div(j, 2), pair + lax.rem(j, 2)

    works_here = lax.div(protein, B) == core

    def at(p, first=0, size=16):
        return pl.ds(pl.multiple_of(p * N + first, size), size)

    away = [jnp.abs(plane_of(core * B + p, B) - w) for p in range(B)]
    near = 0
    for p in range(1, B):
        near = jnp.where(away[p] < functools.reduce(jnp.minimum, away[:p]), p, near)

    load = pltpu.make_async_copy(ecat0, ecat.at[0], ld_sem)
    load.start()
    barrier = pltpu.get_barrier_semaphore()
    for sec in range(S):
        for c in range(C):
            greeted = (c == pair) | (c == pair + 1) | (w == sec // 2)

            @pl.when(greeted & jnp.logical_not(is_me(sec, c)))
            def _():
                pl.semaphore_signal(
                    barrier, inc=1, device_id={"section": sec, "dp": c}, device_id_type=MESH
                )
    wall_msg[me_s] = we_own[...]
    wall_upd[me_s] = jnp.zeros(wall_upd.shape[1:], BF16)
    wall_upd[me_s, pl.ds(0, DE), pl.ds(0, DE)] = ws_own[...]
    wall_upd[me_s, pl.ds(0, DE), pl.ds(EP, DE)] = wo_own[...]
    bias = edge_b[pl.ds(1, 1), :]
    high = bias.astype(BF16).astype(F32)
    row = lax.broadcasted_iota(jnp.int32, (16, DE), 0)
    wall_upd[me_s, pl.ds(DE, 16), pl.ds(0, DE)] = jnp.where(
        row == 0, high, jnp.where(row == 1, bias - high, 0.0)
    ).astype(BF16)
    eb0[...] = jnp.zeros_like(eb0)
    eb0[:, pl.ds(0, DE)] = edge_b[pl.ds(0, 1), :]
    par[pl.ds(0, 1), :] = gains[0]
    par[pl.ds(1, 1), :] = shifts[0]
    par[pl.ds(2, 1), :] = node_b[0]
    par[pl.ds(3, 5), :] = jnp.zeros((5, D), F32)
    pl.semaphore_wait(barrier, 2 * S - 1 + 2 * (C - 2))

    def section_at(i):
        i = lax.rem(i + S, S)
        return jnp.where(i < S // 2, 2 * i, 2 * (S - i) - 1)

    place = jnp.where(lax.rem(me_s, 2) == 0, w, S - 1 - w)
    sides = ((section_at(place + 1), S // 2), (section_at(place - 1), S // 2 - 1))
    walls = (wall_msg, wall_upd)

    def half_of(which, layer, c):
        size = walls[which].shape[1] // 2
        return walls[which].at[layer, pl.ds(pl.multiple_of(c * size, size), size)]

    def ring_send(which, layer, side, hop):
        sec, reach = sides[side]
        if hop < reach:
            half = half_of(which, layer, core)
            far(half, half, ring_ss.at[which, side, hop], ring_rs.at[which, layer], sec, me_d).start()

    def ring_hop(which, side, hop):
        layer = section_at(place - hop if side == 0 else place + hop)
        half = half_of(which, layer, core)
        arrive(half, ring_rs.at[which, layer])
        ring_send(which, layer, side, hop)
        far(half, half, sib_ss.at[which, layer], sib_rs.at[which, layer], me_s, pair + 1 - core).start()

    hops = [(hop, side) for hop in range(1, S // 2 + 1) for side in range(2) if hop <= sides[side][1]]

    def ring_later(second):
        for hop, side in hops:
            early = (place > 0) & ((place >= hop) if side == 0 else (place + hop <= S))

            @pl.when(early != second)
            def _():
                ring_hop(1, side, hop)

    for side in range(2):
        ring_send(0, me_s, side, 0)
    before = lax.rem(me_s + S - 1, S)
    far(pw, pwn, nx_ss.at[0], nx_rs.at[0], before, me_d).start()
    far(par, parn, nx_ss.at[1], nx_rs.at[1], before, me_d).start()

    for p in range(B):
        rows = pl.ds(p * N, N)
        start[rows, :] = mix[0, p] * clean[rows, :].astype(F32) + mix[1, p] * noise[rows, :].astype(F32)

    def ring_drain():
        for which in range(2):
            for side in range(2):
                for hop in range(sides[side][1]):
                    arrive(half_of(which, me_s, core), ring_ss.at[which, side, hop])
            for layer in range(S):
                @pl.when(layer != me_s)
                def _():
                    arrive(half_of(which, layer, core), sib_ss.at[which, layer])

    def unpack_messages(t):
        @pl.when(t != me_s)
        def _():
            arrive(half_of(0, t, 1 - core), sib_rs.at[0, t])

        wcat[t, pl.ds(0, DE), :] = wall_msg[t]

    def unpack_updates(t):
        @pl.when(t != me_s)
        def _():
            arrive(half_of(1, t, 1 - core), sib_rs.at[1, t])

        scat[t, pl.ds(0, DE), :] = wall_upd[t, pl.ds(0, DE), pl.ds(0, EP)]
        wo[t, pl.ds(0, DE), :] = wall_upd[t, pl.ds(0, DE), pl.ds(EP, EP)]
        wo[t, pl.ds(DE, N), :] = jnp.zeros((N, EP), BF16)
        eb1[t] = wall_upd[t, pl.ds(DE, 16), pl.ds(0, EP)]

    def rows_out(p, src, dst, ssem, rsem):
        for j in range(4):
            sec, dpi = worker_of(p, j)
            push(src.at[at(p, j * Q, Q)], dst, ssem, rsem, sec, dpi)

    def rows_drain(src, ssem):
        lax.cond(
            works_here,
            lambda: arrive(src.at[pl.ds(0, B * N - Q)], ssem),
            lambda: arrive(src, ssem),
        )

    def spread(rows, half, ref, layer, ssem, rsem, rows_sem):
        arrive(rows, rows_sem)
        for k in range(1, 4):
            _, sec, dpi = peer(k)
            far(rows.at[:, pl.ds(half, half)], ref.at[layer, quarter(q)], ssem, rsem, sec, dpi).start()
        ref[layer, own_rows, :] = rows[:, pl.ds(0, half)]
        ref[layer, quarter(q), :] = rows[:, pl.ds(half, half)]

    def spread_wait(ref, layer, sem):
        arrive(ref.at[layer, pl.ds(DE, 3 * Q)], sem)

    def share(group, src, dst):
        for c in range(C):
            push(src, dst.at[me_d], g_ss.at[group, c], g_rs.at[group, me_d], me_s, c)

    def share_wait(group, src, dst):
        for c in range(C):
            arrive(dst.at[c], g_rs.at[group, c])
            drain(src, g_ss.at[group, c], me_s, c)

    def share_near(group, src, dst):
        for c in range(C):
            @pl.when((c == pair) | (c == pair + 1) | (core == c % 2))
            def _():
                push(src, dst(me_d), g_ss.at[group, c], g_rs.at[group, me_d], me_s, c)

    def share_relay(group, src, dst):
        for c in range(C):
            @pl.when((c != me_d) & (core == c % 2))
            def _():
                arrive(dst(c), g_rs.at[group, c])
                far(dst(c), dst(c), relay_ss.at[group - 2, c // 2], g_rs.at[group, c], me_s, pair + 1 - core).start()

    def share_near_wait(group, src, dst):
        for c in range(C):
            @pl.when((c == me_d) | (core != c % 2))
            def _():
                arrive(dst(c), g_rs.at[group, c])

            @pl.when((c != me_d) & ((c == pair) | (c == pair + 1) | (core == c % 2)))
            def _():
                arrive(src, g_ss.at[group, c])

            @pl.when((c != me_d) & (core == c % 2))
            def _():
                arrive(dst(c), relay_ss.at[group - 2, c // 2])

    steps = 4
    KC = K // steps
    RC = KC * Q

    def messages(t):
        own = wcat[t, own_rows, :].astype(F32)
        total = jnp.zeros((Q, D), F32)
        for i in range(steps):
            pre = mm(ecat[t, pl.ds(i * RC, RC), :], wcat[t, pl.ds(0, top), :])
            for k in range(KC):
                total = total + gelu(pre[k * Q : (k + 1) * Q] + own)
        mb_s[...] = (total * (1.0 / K)).astype(BF16)

    def edge_update(t):
        own = scat[t, own_rows, :].astype(F32)
        bias = eb1[t, pl.ds(0, 1), :].astype(F32) + eb1[t, pl.ds(1, 1), :].astype(F32)
        for i in range(steps):
            pe = mm(ecat[t, pl.ds(i * RC, RC), :], scat[t, pl.ds(0, top), :])
            act_e = stacked([gelu(pe[k * Q : (k + 1) * Q] + own).astype(BF16) for k in range(KC)])
            z = mm(act_e, wo[t])
            for k in range(KC):
                rows = pl.ds(i * RC + k * Q, Q)
                ecat[t + 1, rows, :] = (ecat[t, rows, :].astype(F32) + z[k * Q : (k + 1) * Q] + bias).astype(BF16)

    chunks = 4
    FC = FF // chunks

    def node_forward(step):
        @pl.when(step < S)
        def _():
            arrive(pwn, nx_rs.at[0])
            arrive(parn, nx_rs.at[1])
            arrive(pw, nx_ss.at[0])
            arrive(par, nx_ss.at[1])

        @pl.when(step == 0)
        def _():
            hi_s[...] = start[...]

        @pl.when(step > 0)
        def _():
            arrive(hin_r, hop_rs)
            first = jnp.where(me_s == 0, 1.0, 0.0)
            for i in range(0, BN, RB):
                rows = pl.ds(i, RB)
                hi_s[rows, :] = hin_r[rows, :].astype(F32) + first * start[rows, :]

        later = lax.rem(me_s + 1, S)

        def turn(n, carry):
            p = lax.rem(near + n, B)
            whole = at(p, 0, N)
            arrive(mb_r.at[whole], mb_rs.at[p])
            mean = mm(mb_r[whole, :], mo[...])
            for i in range(0, N, RB):
                rows = at(p, i)
                h1 = hi_s[rows, :] + mean[i : i + RB] + node_b[1]
                h1_s[rows, :] = h1
                unit, scale = normed(h1)
                un1[rows, :] = unit
                sc1[rows, :] = scale
                fwd[rows, pl.ds(2 * D, D)] = (unit * gains[1] + shifts[1]).astype(BF16)
                fwd[rows, pl.ds(D, D)] = mb_r[rows, :]
            a2 = fwd[whole, pl.ds(2 * D, D)]
            y = jnp.zeros((N, D), F32)
            for c in range(chunks):
                cols = pl.ds(c * FC, FC)
                u = mm(a2, fi[:, cols])
                v = []
                for i in range(0, N, RB):
                    block = u[i : i + RB] + fb[:, cols]
                    u_s[at(p, i), cols] = block
                    v.append(gelu(block).astype(BF16))
                y = y + mm(stacked(v), fo[cols, :])
            last = jnp.where(me_s == S - 1, 1.0, 0.0)
            for i in range(0, N, RB):
                rows = at(p, i)
                h2 = h1_s[rows, :] + y[i : i + RB] + node_b[2]
                rounded = h2.astype(BF16)
                hst[rows, :] = rounded
                unit, scale = normed(h2)
                un2[rows, :] = unit
                sc2[rows, :] = scale
                fwd[rows, pl.ds(3 * D, D)] = (unit * gains[2] + shifts[2]).astype(BF16)
                pair_norm(rows, rounded.astype(F32) + last * start[rows, :], parn)
            rq = mm(fwd[whole, pl.ds(3 * D, D)], ep[...])
            for i in range(0, N, RB):
                rows = at(p, i)
                rq_s[rows, pl.ds(0, EP)] = (rq[i : i + RB, :EP] + eb0[...]).astype(BF16)
                rq_s[rows, pl.ds(EP, EP)] = rq[i : i + RB, EP:].astype(BF16)
            pair_rows(p, pwn, parn)

            @pl.when(me_s < S - 1)
            def _():
                rows_out(p, rq_s, rq_r, rq_ss, rq_rs)

            @pl.when(step < 2 * S - 1)
            def _():
                rows_out(p, pq_s, pq_r, pq_ss, pq_rs)

            @pl.when((n == 0) & works_here)
            def _():
                pass_on(step)

            return carry

        lax.fori_loop(0, B, turn, 0)

        @pl.when(step < 2 * S - 1)
        def _():
            far(hst, hin_r, hop_ss, hop_rs, later, me_d).start()

        @pl.when(step >= S)
        def _():
            act[...] = hst[...]
            for i in range(0, BN, RB):
                rows = pl.ds(i, RB)
                unit, scale = normed(hi_s[rows, :])
                hi_s[rows, :] = unit
                sci[rows, :] = scale
                fwd[rows, pl.ds(0, D)] = (unit * gains[0] + shifts[0]).astype(BF16)
                for c in range(chunks):
                    cols = pl.ds(c * FC, FC)
                    slope_s[rows, cols] = gelu_both(u_s[rows, cols])[1].astype(BF16)
            share(0, fwd, g_fwd)

    def pair_norm(rows, hidden, first):
        unit, scale = normed(hidden)
        un0[rows, :] = unit
        sc0[rows, :] = scale
        a1_s[rows, :] = (unit * first[pl.ds(0, 1), :] + first[pl.ds(1, 1), :]).astype(BF16)

    def pair_rows(p, weight, first):
        whole = at(p, 0, N)
        for half in range(2):
            cols = pl.ds(half * D, D)
            value = mm(a1_s[whole, :], weight[:, cols])
            if half == 0:
                value = value + first[pl.ds(2, 1), :]
            pq_s[whole, cols] = value.astype(BF16)

    def pass_on(step):
        t = lax.rem(step, S)

        @pl.when(t < S - 1)
        def _():
            spread(rq_r, EP, scat, t, ag2_ss, ag2_rs, rq_rs)

        @pl.when(step < 2 * S - 1)
        def _():
            spread(pq_r, D, wcat, lax.rem(step + 1, S), ag_ss, ag_rs, pq_rs)

    def node_forward_drain():
        arrive(hst, hop_ss)
        rows_drain(pq_s, pq_ss)

        @pl.when(me_s < S - 1)
        def _():
            rows_drain(rq_s, rq_ss)

    @pl.when(me_s == 0)
    def _():
        for i in range(0, BN, RB):
            rows = pl.ds(i, RB)
            pair_norm(rows, start[rows, :], par)
        for p in range(B):
            pair_rows(p, pw, par)
            rows_out(p, pq_s, pq_r, pq_ss, pq_rs)

    def message_slope(t):
        own = wcat[t, own_rows, :].astype(F32)
        for i in range(steps):
            pre = mm(ecat[t, pl.ds(i * RC, RC), :], wcat[t, pl.ds(0, top), :])
            for k in range(KC):
                gp[t, pl.ds(i * RC + k * Q, Q), :] = gelu_both(pre[k * Q : (k + 1) * Q] + own)[1].astype(BF16)

    def edge_slope(t):
        own = scat[t, own_rows, :].astype(F32)
        values = []
        for i in range(steps):
            pe = mm(ecat[t, pl.ds(i * RC, RC), :], scat[t, pl.ds(0, top), :])
            for k in range(KC):
                value, slope = gelu_both(pe[k * Q : (k + 1) * Q] + own)
                values.append(value.astype(BF16))
                gpe[t, pl.ds(i * RC + k * Q, Q), :] = slope.astype(BF16)
        act_t[t] = stacked(values).T

    def prepare(t):
        message_slope(t)
        edge_t[t] = ecat[t].T

        @pl.when(t > 0)
        def _():
            edge_slope(t - 1)

    def forward_step(step, carry):
        t = lax.rem(step, S)

        @pl.when(step < S)
        def _():
            unpack_messages(t)

        spread_wait(wcat, t, ag_rs)
        messages(t)
        spread_wait(wcat, t, ag_ss)
        push(mb_s, mb_r.at[pl.ds(my_row, Q)], mb_ss, mb_rs.at[slot], t, owner_d)

        for second in range(2):
            @pl.when(step == second)
            def _():
                ring_later(second == 1)

        @pl.when((step == 0) & (me_s == 0))
        def _():
            rows_drain(pq_s, pq_ss)

        @pl.when((step > 0) & (me_s == lax.rem(step + S - 1, S)))
        def _():
            node_forward_drain()

        @pl.when(me_s == t)
        def _():
            node_forward(step)

        @pl.when((me_s != t) & (step >= S))
        def _():
            prepare(t)

        @pl.when(jnp.logical_not((me_s == t) & works_here))
        def _():
            pass_on(step)

        @pl.when(t < S - 1)
        def _():
            @pl.when(step < S)
            def _():
                unpack_updates(t)

            spread_wait(scat, t, ag2_rs)
            edge_update(t)
            spread_wait(scat, t, ag2_ss)

        drain(mb_s, mb_ss, t, owner_d)
        return carry

    for hop, side in hops:
        ring_hop(0, side, hop)
    for side in range(2):
        ring_send(1, me_s, side, 0)
    load.wait()
    spread(pq_r, D, wcat, 0, ag_ss, ag_rs, pq_rs)
    lax.fori_loop(0, 2 * S, forward_step, 0)
    ring_drain()

    @pl.when(me_s != S - 1)
    def _():
        arrive(half_of(1, S - 1, 1 - core), sib_rs.at[1, S - 1])

    def edge_back(t):
        b2, n2 = lax.rem(t, 2), lax.rem(t + 1, 2)
        total = jnp.zeros((Q, EP), F32)
        for i in range(steps):
            chunk = pl.ds(i * RC, RC)
            carry = mm_bt(dcat[b2, chunk, pl.ds(0, D)], wcat[t, pl.ds(0, top), :])
            low = []
            for k in range(KC):
                rows = pl.ds(i * RC + k * Q, Q)
                low.append((dacc[rows, :] + carry[k * Q : (k + 1) * Q]).astype(BF16))
                de[n2, rows, :] = low[-1]
            dw = mm_bt(stacked(low), wo[t - 1])
            for k in range(KC):
                rows = pl.ds(i * RC + k * Q, Q)
                d = (gpe[t - 1, rows, :].astype(F32) * dw[k * Q : (k + 1) * Q]).astype(BF16)
                total = total + d.astype(F32)
                dcat[n2, rows, pl.ds(D, EP)] = d
        row_s[:, pl.ds(2 * D, EP)] = total.astype(BF16)
        x_s[:, pl.ds(D, EP)] = mm(oht[...], dcat[n2, :, pl.ds(D, EP)]).astype(BF16)

    def edge_pass(t):
        b3 = lax.rem(t, 2)
        for i in range(steps):
            rows = pl.ds(i * RC, RC)
            d = dcat[b3, rows, pl.ds(D, EP)]
            dacc[rows, :] = de[b3, rows, :].astype(F32) + mm_bt(d, scat[t, pl.ds(0, top), :])

    blocks = 2 * C
    my_block = lax.rem(me_s, 2) * C + me_d
    BW, HM, HU = msg_o.shape[2], msg_o.shape[1], upd_o.shape[1]

    def block_of(t, half, c, size):
        return eg.at[t, half, pl.ds(0, size), pl.ds(pl.multiple_of(c * BW, BW), BW)]

    def blocks_out(t, size):
        for k in range(blocks):
            @pl.when(k != my_block)
            def _():
                far(
                    block_of(t, k // C, k % C, size), eg_r.at[t, my_block, pl.ds(0, size)],
                    e1_ss.at[t, k], e1_rs.at[t, my_block], 2 * w + k // C, k % C,
                ).start()

    def edge_grads(t):
        grad = mm(edge_t[t, pl.ds(0, DE), :], dcat[lax.rem(t, 2), :, pl.ds(0, D)]).astype(BF16)
        for half in range(2):
            eg[t, half, pl.ds(0, HM), :] = grad[half * HM : (half + 1) * HM]

        @pl.when(t > 0)
        def _():
            n2 = lax.rem(t + 1, 2)
            edges = mm(edge_t[t - 1, pl.ds(0, DE), :], dcat[n2, :, pl.ds(D, EP)])
            outs = mm(act_t[t - 1, pl.ds(0, DE), :], de[n2])
            bias = jnp.sum(de[n2].astype(F32), axis=0, keepdims=True)
            grad = jnp.concatenate([edges, outs], axis=1).astype(BF16)
            eg[t, 0, pl.ds(HM, HU), :] = grad[:HU]
            eg[t, 1, pl.ds(HM, DE - HU), :] = grad[HU:]
            eg[t, 1, pl.ds(HM + DE - HU, 16), pl.ds(0, EP)] = jnp.broadcast_to(bias, (16, EP)).astype(BF16)
            eg[t, 1, pl.ds(HM + DE - HU, 16), pl.ds(EP, EP)] = jnp.zeros((16, EP), BF16)
            eg[t, 1, pl.ds(HM + DE - HU + 16, 2 * HU - DE - 16), :] = jnp.zeros((2 * HU - DE - 16, 2 * EP), BF16)
            blocks_out(t, HM + HU)

        @pl.when(t == 0)
        def _():
            blocks_out(t, HM)

    def blocks_sum(t, size):
        eg_r[t, my_block, pl.ds(0, size), :] = block_of(t, lax.rem(me_s, 2), me_d, size)[...]
        for k in range(blocks):
            @pl.when(k != my_block)
            def _():
                arrive(eg_r.at[t, k, pl.ds(0, size)], e1_rs.at[t, k])
                arrive(block_of(t, k // C, k % C, size), e1_ss.at[t, k])
        total = eg_r[t, 0, pl.ds(0, size), :].astype(F32)
        for k in range(1, blocks):
            total = total + eg_r[t, k, pl.ds(0, size), :].astype(F32)
        eg_b[t, pl.ds(0, size), :] = total.astype(BF16)
        push(eg_b.at[t, pl.ds(0, HM)], msg_o.at[me_s], e2_ss.at[0, t], e2_rs.at[0, me_s], t, me_d)
        if size > HM:
            push(eg_b.at[t, pl.ds(HM, HU)], upd_o.at[me_s], e2_ss.at[1, t], e2_rs.at[1, me_s], t - 1, me_d)

    def gather_blocks():
        for k in range(1, 4):
            j, sec, dpi = peer(k)
            rows = pl.ds(pl.multiple_of(j * Q, Q), Q)
            far(x_s.at[rows], x_r.at[q], x_ss, x_rs, sec, dpi).start()
        x_r[q] = x_s[pl.ds(pl.multiple_of(q * Q, Q), Q), :]

    def gather_wait():
        arrive(x_r.at[pl.ds(0, 3)], x_rs)
        arrive(x_s.at[pl.ds(0, 3 * Q)], x_ss)
        total = x_r[0].astype(F32)
        for j in range(1, 4):
            total = total + x_r[j].astype(F32)
        return total

    def message_back(t):
        b2 = lax.rem(t, 2)
        dm = dmb_r[...].astype(F32)
        total = jnp.zeros((Q, D), F32)
        for k in range(K):
            rows = pl.ds(k * Q, Q)
            d = (gp[t, rows, :].astype(F32) * dm).astype(BF16)
            total = total + d.astype(F32)
            dcat[b2, rows, pl.ds(0, D)] = d
        row_s[:, pl.ds(0, D)] = total.astype(BF16)
        x_s[:, pl.ds(0, D)] = mm(oht[...], dcat[b2, :, pl.ds(0, D)]).astype(BF16)

    def node_backward():
        @pl.when(me_s < S - 1)
        def _():
            arrive(dh1_r, dh_rs)

        def turn(n, carry):
            p = lax.rem(near + n, B)
            whole = at(p, 0, N)

            @pl.when(me_s < S - 1)
            def _():
                arrive(row_r.at[whole], row_rs.at[p])
                dn0 = mm_bt(row_r[whole, pl.ds(0, 2 * D)], pwn[...])
                dn3 = mm_bt(row_r[whole, pl.ds(2 * D, 2 * EP)], ep[...])
                for i in range(0, N, RB):
                    rows = at(p, i)
                    dn = dn3[i : i + RB]
                    dn3_s[rows, :] = dn
                    first = norm_back(dn0[i : i + RB], un0[rows, :], sc0[rows, :], parn[pl.ds(0, 1), :])
                    dh = (dh1_r[rows, :].astype(F32) + first).astype(BF16).astype(F32)
                    dh2_s[rows, :] = dh + norm_back(dn, un2[rows, :], sc2[rows, :], gains[2])

            @pl.when(me_s == S - 1)
            def _():
                dh2_s[whole, :] = cot[whole, :].astype(F32)

            dy = dh2_s[whole, :].astype(BF16)
            bwd[whole, pl.ds(D, D)] = dy
            da2 = jnp.zeros((N, D), F32)
            for c in range(chunks):
                cols = pl.ds(c * FC, FC)
                dv = mm_bt(dy, fo[cols, :])
                du = stacked(
                    [(slope_s[at(p, i), cols].astype(F32) * dv[i : i + RB]).astype(BF16) for i in range(0, N, RB)]
                )
                da2 = da2 + mm_bt(du, fi[:, cols])
            for i in range(0, N, RB):
                rows = at(p, i)
                block = da2[i : i + RB]
                da2_s[rows, :] = block
                dh1 = dh2_s[rows, :] + norm_back(block, un1[rows, :], sc1[rows, :], gains[1])
                dh1_f[rows, :] = dh1
                bwd[rows, pl.ds(0, D)] = (dh1 * (1.0 / K)).astype(BF16)
            dmb_s[whole, :] = mm_bt(bwd[whole, pl.ds(0, D)], mo[...]).astype(BF16)
            rows_out(p, dmb_s, dmb_r, dmb_ss, dmb_rs)
            return carry

        lax.fori_loop(0, B, turn, 0)

        @pl.when(me_s > 0)
        def _():
            dh1_s[...] = dh1_f[...].astype(BF16)
            far(dh1_s, dh1_r, dh_ss, dh_rs, me_s - 1, me_d).start()

        @pl.when(me_s < S - 1)
        def _():
            far(row_r.at[:, pl.ds(0, 2 * D)], dpqo_r, fw_ss, dpqo_rs, me_s + 1, me_d).start()
            drs = row_r[:, pl.ds(2 * D, 2 * EP)]
            bwd[:, pl.ds(2 * D, 2 * EP)] = drs
            dn = dn3_s[...]
            sg[pl.ds(11, 1), :] = col_sum(dn * un2[...])
            sg[pl.ds(12, 1), :] = col_sum(dn)
            sg[pl.ds(16, 1), pl.ds(0, EP)] = col_sum(drs[:, :EP].astype(F32))

        @pl.when(me_s == S - 1)
        def _():
            bwd[:, pl.ds(2 * D, 2 * EP)] = jnp.zeros((B * N, 2 * EP), BF16)
            sg[pl.ds(11, 1), :] = jnp.zeros((1, D), F32)
            sg[pl.ds(12, 1), :] = jnp.zeros((1, D), F32)
            sg[pl.ds(16, 1), pl.ds(0, EP)] = jnp.zeros((1, EP), F32)

        share(1, bwd, g_bwd)
        sg[pl.ds(13, 1), :] = col_sum(dh2_s[...])
        sg[pl.ds(8, 1), :] = col_sum(da2_s[...] * un1[...])
        sg[pl.ds(9, 1), :] = col_sum(da2_s[...])
        sg[pl.ds(10, 1), :] = col_sum(dh1_f[...])

    def node_backward_drain():
        rows_drain(dmb_s, dmb_ss)

        @pl.when(me_s > 0)
        def _():
            arrive(dh1_s, dh_ss)

        @pl.when(me_s < S - 1)
        def _():
            arrive(row_r.at[:, pl.ds(0, 2 * D)], fw_ss)

    dacc[...] = jnp.zeros_like(dacc)

    def backward_step(step, carry):
        t = S - 1 - step

        @pl.when(me_s == t)
        def _():
            node_backward()

        @pl.when(((t == S - 1) & (me_s >= S - 2)) | (me_s == t - 2))
        def _():
            prepare(me_s)

        @pl.when(t < S - 1)
        def _():
            edge_pass(t)

        @pl.when(t + 2 < S)
        def _():
            blocks_sum(t + 2, HM + HU)

        @pl.when(t == 0)
        def _():
            blocks_sum(1, HM + HU)

        arrive(dmb_r, dmb_rs)
        message_back(t)

        @pl.when(t > 0)
        def _():
            edge_back(t)

        @pl.when(t == 0)
        def _():
            x_s[:, pl.ds(D, EP)] = jnp.zeros((N, EP), BF16)

        gather_blocks()
        other = gather_wait().astype(BF16)
        row_s[:, pl.ds(D, D)] = other[:, :D]
        row_s[:, pl.ds(2 * D + EP, EP)] = other[:, D:]
        dpq = row_s.at[:, pl.ds(0, 2 * D)]

        @pl.when(t > 0)
        def _():
            push(row_s, row_r.at[pl.ds(my_row, Q)], row_ss, row_rs.at[slot], t - 1, owner_d)

        @pl.when(t == 0)
        def _():
            push(dpq, dpqo_r.at[pl.ds(my_row, Q)], row_ss, dpqo_rs, t, owner_d)

        edge_grads(t)

        @pl.when(t > 0)
        def _():
            drain(row_s, row_ss, t - 1, owner_d)

        @pl.when(t == 0)
        def _():
            drain(dpq, row_ss, t, owner_d)

        @pl.when(me_s == t)
        def _():
            node_backward_drain()

        return carry

    lax.fori_loop(0, S, backward_step, 0)

    arrive(dpqo_r, dpqo_rs)
    across = [pl.ds(p * N, N) for p in range(B)]
    for p in range(B):
        share_near(2 + p, dpqo_r.at[across[p]], lambda c, p=p: g_dpq.at[c, across[p]])
    dpq = dpqo_r[...]
    sg[pl.ds(2, 1), :] = col_sum(dpq[:, :D].astype(F32))
    dn = mm_bt(dpq, pw[...])
    unit = hi_s[...]
    sg[pl.ds(0, 1), :] = col_sum(dn * unit)
    sg[pl.ds(1, 1), :] = col_sum(dn)
    share(2 + B, sg, g_small)
    ig[...] = (dh1_f[...] + norm_back(dn, unit, sci[...], gains[0])).astype(BF16)
    blocks_sum(0, HM)
    for p in range(B):
        share_relay(2 + p, dpqo_r.at[across[p]], lambda c, p=p: g_dpq.at[c, across[p]])
    def combine(kind, src, final):
        for sec in range(S):
            arrive(src.at[sec], e2_rs.at[kind, sec])
        for half in range(2):
            total = src[half].astype(F32)
            for sec in range(half + 2, S, 2):
                total = total + src[sec].astype(F32)
            final[half] = total.astype(BF16)

    @pl.when(me_s < S - 1)
    def _():
        combine(1, upd_o, upd_f)

    @pl.when(me_s == S - 1)
    def _():
        upd_f[...] = jnp.zeros_like(upd_f)

    share(4 + B, upd_f, g_upd)
    combine(0, msg_o, msg_f)
    share(3 + B, msg_f, g_msg)
    for t in range(S):
        drain(eg_b.at[t, pl.ds(0, HM)], e2_ss.at[0, t], t, me_d)
        if t > 0:
            drain(eg_b.at[t, pl.ds(HM, HU)], e2_ss.at[1, t], t - 1, me_d)
    share_wait(0, fwd, g_fwd)
    share_wait(1, bwd, g_bwd)
    for p in range(B):
        share_near_wait(2 + p, dpqo_r.at[across[p]], lambda c, p=p: g_dpq.at[c, across[p]])
    share_wait(2 + B, sg, g_small)
    share_wait(3 + B, msg_f, g_msg)
    share_wait(4 + B, upd_f, g_upd)


def run_relay(dims, operands):
    S, B, N, K, Q, D, DE, EP, FF, C = dims
    R = K * Q
    BN = B * N
    tall = DE + N + Q
    vm = pl.BlockSpec(memory_space=pltpu.VMEM)
    hbm = pl.BlockSpec(memory_space=pl.ANY)
    dma = pltpu.SemaphoreType.DMA
    sds = jax.ShapeDtypeStruct
    BW = D // C
    tile = 32
    held = -(-(DE + 16) // tile) * tile
    scratch = [
        pltpu.VMEM((BN, D), F32),
        pltpu.VMEM((8, D), F32),
        pltpu.VMEM((1, EP), F32),
        pltpu.VMEM((S, DE, D), BF16),
        pltpu.VMEM((S, held, 2 * EP), BF16),
        pltpu.VMEM((BN, 4 * D), BF16),
        pltpu.VMEM((BN, 2 * D + 2 * EP), BF16),
        pltpu.VMEM((24, D), F32),
        pltpu.VMEM((S, 2, (DE + held) // 2, D), BF16),
        pltpu.VMEM((S, 2 * C, (DE + held) // 2, BW), BF16),
        pltpu.VMEM((S, (DE + held) // 2, BW), BF16),
        pltpu.VMEM((S, DE // 2, BW), BF16),
        pltpu.VMEM((2, DE // 2, BW), BF16),
        pltpu.VMEM((S, held // 2, BW), BF16),
        pltpu.VMEM((2, held // 2, BW), BF16),
        pltpu.VMEM((S, EP, EP), BF16),
        pltpu.VMEM((S, 16, EP), BF16),
        pltpu.VMEM((S, R, EP), BF16),
        pltpu.VMEM((S, tall, D), BF16),
        pltpu.VMEM((S, tall, EP), BF16),
        pltpu.VMEM((D, 2 * D), BF16),
        pltpu.VMEM((8, D), F32),
        pltpu.VMEM((BN, D), BF16),
        pltpu.VMEM((BN, D), BF16),
        pltpu.VMEM((Q, D), BF16),
        pltpu.VMEM((BN, D), BF16),
        pltpu.VMEM((BN, 2 * D), BF16),
        pltpu.VMEM((Q, 2 * D), BF16),
        pltpu.VMEM((BN, 2 * EP), BF16),
        pltpu.VMEM((Q, 2 * EP), BF16),
        pltpu.VMEM((BN, D), F32),
        pltpu.VMEM((BN, D), F32),
        pltpu.VMEM((BN, D), F32),
        pltpu.VMEM((BN, D), F32),
        pltpu.VMEM((BN, 1), F32),
        pltpu.VMEM((BN, 1), F32),
        pltpu.VMEM((BN, 1), F32),
        pltpu.VMEM((BN, 1), F32),
        pltpu.VMEM((BN, FF), F32),
        pltpu.VMEM((BN, FF), BF16),
        pltpu.VMEM((2, R, EP), BF16),
        pltpu.VMEM((R, EP), F32),
        pltpu.VMEM((S, R, D), BF16),
        pltpu.VMEM((S, R, EP), BF16),
        pltpu.VMEM((2, R, D + EP), BF16),
        pltpu.VMEM((S, EP, R), BF16),
        pltpu.VMEM((S, EP, R), BF16),
        pltpu.VMEM((N, D + EP), BF16),
        pltpu.VMEM((4, Q, D + EP), BF16),
        pltpu.VMEM((Q, 2 * D + 2 * EP), BF16),
        pltpu.VMEM((BN, 2 * D + 2 * EP), BF16),
        pltpu.VMEM((BN, 2 * D), BF16),
        pltpu.VMEM((BN, D), BF16),
        pltpu.VMEM((Q, D), BF16),
        pltpu.VMEM((BN, D), BF16),
        pltpu.VMEM((BN, D), BF16),
        pltpu.VMEM((BN, D), F32),
        pltpu.VMEM((BN, D), F32),
        pltpu.VMEM((BN, D), F32),
        pltpu.VMEM((BN, D), F32),
        pltpu.VMEM((BN, D), F32),
        pltpu.VMEM((BN, D), BF16),
        dma, dma((2,)), dma((2,)), dma, dma,
        dma, dma, dma, dma, dma, dma, dma, dma,
        dma, dma((B,)), dma, dma, dma, dma((B,)), dma,
        dma, dma, dma, dma, dma,
        dma((S, 2 * C)), dma((S, 2 * C)), dma((2, S)), dma((2, S)), dma((5 + B, C)), dma((5 + B, C)),
        dma((B, C // 2)), dma((2, 2, S // 2)), dma((2, S)), dma((2, S)), dma((2, S)),
    ]
    return pl.pallas_call(
        functools.partial(relay_kernel, dims),
        out_shape=(
            sds((BN, D), BF16),
            sds((BN, D), BF16),
            sds((C, BN, 4 * D), BF16),
            sds((C, BN, 2 * D + 2 * EP), BF16),
            sds((C, BN, 2 * D), BF16),
            sds((C, 24, D), F32),
            sds((C, 2, DE // 2, BW), BF16),
            sds((C, 2, held // 2, BW), BF16),
        ),
        in_specs=[hbm, vm, pl.BlockSpec(memory_space=pltpu.SMEM)] + [vm] * 16,
        out_specs=(vm,) * 2 + (hbm,) * 6,
        scratch_shapes=scratch,
        compiler_params=pltpu.CompilerParams(
            collective_id=0, has_side_effects=True, vmem_limit_bytes=62 * 1024 * 1024
        ),
    )(*operands)


def gradient_kernel(
    dims,
    fwd, bwd, dpq, small, edge, upd, fi, fo, fb, act, ig,
    g_pair, g_edge, g_out, g_fi, g_fo, g_ep, g_self, g_eout, g_gain, g_shift, g_nb, g_fb, g_eb, act_out, ig_out,
    fwd_v, bwd_v, dpq_v, fi_v, fo_v, gfi_v, gfo_v, pair_v, out_v, edge_v, upd_v, in_sems, sems,
):
    S, B, N, K, Q, D, DE, EP, FF, C = dims
    chunks = 4
    FC = FF // chunks

    def part(c, size=D):
        return pl.ds(c * size, size)

    loads = {}

    def load(name, src, dst):
        loads[name] = pltpu.make_async_copy(src, dst, in_sems.at[len(loads)])
        loads[name].start()

    load("a2", fwd.at[:, part(2)], fwd_v.at[2])
    load("dy", bwd.at[:, part(1)], bwd_v.at[1])
    for c in range(chunks):
        load(("fi", c), fi.at[:, part(c, FC)], fi_v.at[c])
        load(("fo", c), fo.at[part(c, FC)], fo_v.at[c])
    load("a1", fwd.at[:, part(0)], fwd_v.at[0])
    load("dpq0", dpq.at[:, part(0)], dpq_v.at[0])
    load("dpq1", dpq.at[:, part(1)], dpq_v.at[1])
    load("mbar", fwd.at[:, part(1)], fwd_v.at[1])
    load("dmsg", bwd.at[:, part(0)], bwd_v.at[0])
    load("a3", fwd.at[:, part(3)], fwd_v.at[3])
    load("drs", bwd.at[:, part(2)], bwd_v.at[2])
    load("edge", edge, edge_v)
    load("upd", upd, upd_v)
    stores = []

    def out(src, dst):
        copy = pltpu.make_async_copy(src, dst, sems.at[len(stores)])
        copy.start()
        stores.append(copy)

    out(act, act_out)
    out(ig, ig_out)
    loads["a2"].wait()
    loads["dy"].wait()
    a2 = fwd_v[2]
    dy = bwd_v[1]
    for c in range(chunks):
        cols = part(c, FC)
        loads["fi", c].wait()
        loads["fo", c].wait()
        value, slope = gelu_both(mm(a2, fi_v[c]) + fb[:, cols])
        du = (slope * mm_bt(dy, fo_v[c])).astype(BF16)
        g_fb[:, cols] = col_sum(du.astype(F32))
        gfi_v[c] = mm_at(a2, du)
        out(gfi_v.at[c], g_fi.at[0, :, cols])
        gfo_v[c] = mm_at(value.astype(BF16), dy)
        out(gfo_v.at[c], g_fo.at[0, cols])
    loads["a1"].wait()
    for c in range(2):
        loads["dpq%d" % c].wait()
        pair_v[c] = mm_at(fwd_v[0], dpq_v[c])
        out(pair_v.at[c], g_pair.at[0, :, part(c)])
    loads["mbar"].wait()
    loads["dmsg"].wait()
    out_v[...] = mm_at(fwd_v[1], bwd_v[0]) * float(K)
    out(out_v, g_out.at[0])
    loads["a3"].wait()
    loads["drs"].wait()
    ends = mm_at(fwd_v[3], bwd_v[2])
    g_ep[0] = jnp.concatenate([ends[:, :DE], ends[:, EP : EP + DE]], axis=1)
    total = small[0]
    for c in range(1, C):
        total = total + small[c]
    for i, rows in enumerate(((0, 1, 2), (8, 9, 10), (11, 12, 13))):
        g_gain[i] = total[rows[0] : rows[0] + 1]
        g_shift[i] = total[rows[1] : rows[1] + 1]
        g_nb[i] = total[rows[2] : rows[2] + 1]
    g_eb[0, pl.ds(0, 1), :] = total[16:17, :DE]
    loads["edge"].wait()
    loads["upd"].wait()
    BW = edge_v.shape[3]
    for c in range(C):
        for half in range(2):
            block = edge_v[c, half].astype(F32)
            g_edge[0, pl.ds(half * (DE // 2), DE // 2), pl.ds(c * BW, BW)] = block
        block = stacked([upd_v[c, 0], upd_v[c, 1]]).astype(F32)
        first = c * BW
        for array, begin in ((g_self, 0), (g_eout, EP)):
            low, high = max(first, begin), min(first + BW, begin + DE)
            if low < high:
                array[0, :, pl.ds(low - begin, high - low)] = block[:DE, low - first : high - first]
        low, high = first, min(first + BW, DE)
        if low < high:
            g_eb[0, pl.ds(1, 1), pl.ds(low, high - low)] = block[DE : DE + 1, low - first : high - first]
    for copy in stores:
        copy.wait()


def run_gradients(dims, operands):
    S, B, N, K, Q, D, DE, EP, FF, C = dims
    rows = C * B * N
    BW = D // C
    held = operands[5].shape[2]
    vm = pl.BlockSpec(memory_space=pltpu.VMEM)
    hbm = pl.BlockSpec(memory_space=pl.ANY)
    sds = jax.ShapeDtypeStruct
    shapes = (
        (1, D, 2 * D), (1, DE, D), (1, D, D), (1, D, FF), (1, FF, D), (1, D, 2 * DE), (1, DE, DE), (1, DE, DE),
        (3, 1, D), (3, 1, D), (3, 1, D), (1, FF), (1, 2, DE),
    )
    return pl.pallas_call(
        functools.partial(gradient_kernel, dims),
        out_shape=tuple(sds(shape, F32) for shape in shapes) + (sds((1, B, N, D), BF16),) * 2,
        in_specs=[hbm, hbm, hbm, vm, hbm, hbm, hbm, hbm, vm, hbm, hbm],
        out_specs=(hbm, vm, hbm, hbm, hbm) + (vm,) * 8 + (hbm,) * 2,
        scratch_shapes=[
            pltpu.VMEM((4, rows, D), BF16),
            pltpu.VMEM((3, rows, D), BF16),
            pltpu.VMEM((2, rows, D), BF16),
            pltpu.VMEM((4, D, FF // 4), BF16),
            pltpu.VMEM((4, FF // 4, D), BF16),
            pltpu.VMEM((4, D, FF // 4), F32),
            pltpu.VMEM((4, FF // 4, D), F32),
            pltpu.VMEM((2, D, D), F32),
            pltpu.VMEM((D, D), F32),
            pltpu.VMEM((C, 2, DE // 2, BW), BF16),
            pltpu.VMEM((C, 2, held, BW), BF16),
            pltpu.SemaphoreType.DMA((19,)),
            pltpu.SemaphoreType.DMA((13,)),
        ],
        compiler_params=pltpu.CompilerParams(vmem_limit_bytes=56 * 1024 * 1024),
    )(*operands)


def stationary(
    clean_nodes, noise_nodes, edge_feats, neighbours, time_bins, cotangent,
    pair_weight, message_edge, message_out, ffn_in, ffn_out, edge_pair, edge_self, edge_out,
    norm_gain, norm_shift, node_bias, ffn_bias, edge_bias,
):
    S = lax.axis_size("section")
    place = lax.axis_index("section")
    column = lax.axis_index("dp")
    B, N, D = clean_nodes.shape
    K, DE = edge_feats.shape[2:]
    FF = ffn_in.shape[2]
    Q = N // 4
    EP = DE + N
    core = column % 2
    w = protein_on(place // 2, B)
    slab = (place % 2) * 2 * Q

    node_ids = jnp.arange(N, dtype=jnp.int32)
    both = [
        lax.dynamic_slice(array, (w % B, slab) + (0,) * (array.ndim - 2), (1, 2 * Q) + array.shape[2:])[0]
        for array in (edge_feats, neighbours)
    ]
    chosen = (both[1][:, :, None] == node_ids).astype(BF16)
    both = jnp.concatenate([both[0], chosen], axis=2)
    mine = lax.dynamic_slice_in_dim(both, core * Q, Q, 0)
    theirs = lax.dynamic_slice_in_dim(both, (1 - core) * Q, Q, 0)
    got = lax.ppermute(theirs, "dp", [(i, i ^ 1) for i in range(lax.axis_size("dp"))])
    ecat0 = jnp.swapaxes(jnp.where(w // B == core, mine, got), 0, 1).reshape(K * Q, EP)
    oht = jnp.transpose(ecat0[:, DE:])
    phase = (time_bins.astype(F32) + 0.5) * (math.pi * 0.5 / TBINS)
    mix = jnp.cos(phase[None] - jnp.array([[0.0], [math.pi * 0.5]], F32))

    def by_rows(array):
        return jnp.transpose(array, (1, 0, 2))

    def widen(array, size, axis=-1):
        extra = [(0, 0)] * array.ndim
        extra[axis] = (0, size - array.shape[axis])
        return jnp.pad(array, extra)

    ep = jnp.concatenate([widen(edge_pair[0, :, :DE], EP), widen(edge_pair[0, :, DE:], EP)], axis=1)
    C = lax.axis_size("dp")
    dims = (S, B, N, K, Q, D, DE, EP, FF, C)
    act, ig, g_fwd, g_bwd, g_dpq, g_small, g_msg, g_upd = run_relay(
        dims,
        (
            ecat0, oht, mix, clean_nodes.reshape(B * N, D), noise_nodes.reshape(B * N, D),
            cotangent.reshape(B * N, D), pair_weight[0], message_out[0], ffn_in[0], ffn_out[0], ep,
            by_rows(norm_gain), by_rows(norm_shift), by_rows(node_bias), ffn_bias, edge_bias[0],
            message_edge[0], edge_self[0], edge_out[0],
        ),
    )
    grads = run_gradients(
        dims,
        (
            g_fwd.reshape(C * B * N, -1), g_bwd.reshape(C * B * N, -1), g_dpq.reshape(C * B * N, -1),
            g_small, g_msg, g_upd, ffn_in[0], ffn_out[0], ffn_bias, act.reshape(1, B, N, D), ig.reshape(1, B, N, D),
        ),
    )
    grads, outs = list(grads[:-2]), tuple(grads[-2:])
    grads[8:11] = [by_rows(array) for array in grads[8:11]]
    return outs + tuple(grads)


def solution(mesh):
    sections, copies = mesh.shape["section"], mesh.shape["dp"]

    def body(*args):
        B, N = args[0].shape[:2]
        fits = sections == 4 * B and copies % 2 == 0 and N % 64 == 0
        return stationary(*args) if fits else on_device(*args)

    placed = (
        P("dp", None, None),
        P("dp", None, None),
        P("dp", None, None, None),
        P("dp", None, None),
        P("dp"),
        P("dp", None, None),
        P("section", None, None),
        P("section", None, None),
        P("section", None, None),
        P("section", None, None),
        P("section", None, None),
        P("section", None, None),
        P("section", None, None),
        P("section", None, None),
        P("section", None, None),
        P("section", None, None),
        P("section", None, None),
        P("section", None),
        P("section", None, None),
    )
    return jax.shard_map(
        body,
        mesh=mesh,
        in_specs=placed,
        out_specs=(
            P("section", "dp", None, None),
            P("section", "dp", None, None),
            P("section", None, None),
            P("section", None, None),
            P("section", None, None),
            P("section", None, None),
            P("section", None, None),
            P("section", None, None),
            P("section", None, None),
            P("section", None, None),
            P("section", None, None),
            P("section", None, None),
            P("section", None, None),
            P("section", None),
            P("section", None, None),
        ),
        check_vma=False,
    )
```

```python
import functools
import math

import jax
import jax.numpy as jnp
from jax import lax
from jax.experimental import pallas as pl
from jax.experimental.pallas import tpu as pltpu
from jax.sharding import PartitionSpec as P

TBINS = 100


def from_behind(block, axis, distance):
    devices = range(lax.axis_size(axis))
    route = [(i - distance, i) for i in devices if i - distance in devices]
    return lax.ppermute(block, axis, route)


def for_sending(value):
    return jax.tree.map(lambda a: a.astype(jnp.bfloat16) if a.dtype == jnp.float32 else a, value)


def layer_norm(value, gain, shift):
    centre = jnp.mean(value, axis=-1, keepdims=True)
    centred = value - centre
    spread = jnp.mean(centred * centred, axis=-1, keepdims=True)
    return centred * lax.rsqrt(spread + 1e-05) * gain + shift


def forward_layer(weights, hidden, edge_state, nearest):
    (
        pair_w,
        msg_edge,
        msg_out,
        ffn_w_in,
        ffn_w_out,
        edge_pair_w,
        edge_self_w,
        edge_out_w,
        gains,
        shifts,
        node_b,
        ffn_b,
        edge_b,
    ) = weights
    width = msg_out.shape[0]
    edge_width = edge_self_w.shape[0]
    normed_one = layer_norm(hidden, gains[0], shifts[0]).astype(jnp.bfloat16)
    pair_out = jnp.dot(normed_one, pair_w, preferred_element_type=jnp.float32)
    before_act = (
        pair_out[:, None, :width]
        + jnp.take(pair_out[:, width:], nearest, axis=0)
        + jnp.einsum("nkc,cd->nkd", edge_state, msg_edge, preferred_element_type=jnp.float32)
        + node_b[0]
    )
    message_act = jax.nn.gelu(before_act).astype(jnp.bfloat16)
    message_all = jnp.einsum(
        "nkc,cd->nkd", message_act, msg_out, preferred_element_type=jnp.float32
    )
    after_msg = hidden + jnp.mean(message_all, axis=1) + node_b[1]
    normed_two = layer_norm(after_msg, gains[1], shifts[1]).astype(jnp.bfloat16)
    ffn_pre = jnp.dot(normed_two, ffn_w_in, preferred_element_type=jnp.float32) + ffn_b
    ffn_act = jax.nn.gelu(ffn_pre).astype(jnp.bfloat16)
    after_ffn = (
        after_msg + jnp.dot(ffn_act, ffn_w_out, preferred_element_type=jnp.float32) + node_b[2]
    )
    normed_three = layer_norm(after_ffn, gains[2], shifts[2]).astype(jnp.bfloat16)
    edge_pairs = jnp.dot(normed_three, edge_pair_w, preferred_element_type=jnp.float32)
    edge_pre = (
        edge_pairs[:, None, :edge_width]
        + jnp.take(edge_pairs[:, edge_width:], nearest, axis=0)
        + jnp.einsum("nkc,cd->nkd", edge_state, edge_self_w, preferred_element_type=jnp.float32)
        + edge_b[0]
    )
    edge_act = jax.nn.gelu(edge_pre).astype(jnp.bfloat16)
    edge_next = (
        edge_state.astype(jnp.float32)
        + jnp.einsum("nkc,cd->nkd", edge_act, edge_out_w, preferred_element_type=jnp.float32)
        + edge_b[1]
    )
    saved = (
        normed_one,
        before_act,
        message_act,
        after_msg,
        normed_two,
        ffn_pre,
        ffn_act,
        after_ffn,
        normed_three,
        edge_pre,
        edge_act,
    )
    return (after_ffn, edge_next, saved)


def backward_layer(weights, hidden, edge_state, nearest, grad_nodes_out, grad_edges_out):
    (
        pair_w,
        msg_edge,
        msg_out,
        ffn_w_in,
        ffn_w_out,
        edge_pair_w,
        edge_self_w,
        edge_out_w,
        gains,
        shifts,
        node_b,
        ffn_b,
        edge_b,
    ) = weights
    unused_nodes, unused_edges, saved = forward_layer(weights, hidden, edge_state, nearest)
    (
        normed_one,
        before_act,
        message_act,
        after_msg,
        normed_two,
        ffn_pre,
        ffn_act,
        after_ffn,
        normed_three,
        edge_pre,
        edge_act,
    ) = saved
    width = msg_out.shape[0]
    edge_width = edge_self_w.shape[0]
    count = nearest.shape[1]
    node_count = hidden.shape[0]
    one_hot = (
        nearest.reshape(-1)[None, :] == jnp.arange(node_count, dtype=jnp.int32)[:, None]
    ).astype(jnp.bfloat16)
    edge_grad_low = grad_edges_out.astype(jnp.bfloat16)
    grad_edge_b1 = jnp.sum(grad_edges_out, axis=(0, 1))
    grad_edge_out_w = jnp.einsum(
        "nkc,nkd->cd", edge_act, edge_grad_low, preferred_element_type=jnp.float32
    )
    edge_act_grad = jnp.einsum(
        "nkd,cd->nkc", edge_grad_low, edge_out_w, preferred_element_type=jnp.float32
    )
    unused_value, gelu_edge = jax.vjp(jax.nn.gelu, edge_pre)
    edge_pre_grad = gelu_edge(edge_act_grad)[0].astype(jnp.bfloat16)
    grad_edge_b0 = jnp.sum(edge_pre_grad, axis=(0, 1), dtype=jnp.float32)
    grad_edge_self_w = jnp.einsum(
        "nkc,nkd->cd", edge_state, edge_pre_grad, preferred_element_type=jnp.float32
    )
    edge_total = grad_edges_out + jnp.einsum(
        "nkd,cd->nkc", edge_pre_grad, edge_self_w, preferred_element_type=jnp.float32
    )
    own_edge = jnp.sum(edge_pre_grad, axis=1, dtype=jnp.float32)
    other_edge = jnp.dot(
        one_hot, edge_pre_grad.reshape(-1, edge_width), preferred_element_type=jnp.float32
    )
    pairs_grad = jnp.concatenate([own_edge, other_edge], axis=-1).astype(jnp.bfloat16)
    grad_edge_pair_w = jnp.einsum(
        "nc,nd->cd", normed_three, pairs_grad, preferred_element_type=jnp.float32
    )
    normed_three_grad = jnp.einsum(
        "nd,cd->nc", pairs_grad, edge_pair_w, preferred_element_type=jnp.float32
    )
    unused_value, norm_three_back = jax.vjp(layer_norm, after_ffn, gains[2], shifts[2])
    ffn_side, gain_three, shift_three = norm_three_back(normed_three_grad)
    after_ffn_grad = grad_nodes_out + ffn_side
    grad_node_b2 = jnp.sum(after_ffn_grad, axis=0)
    ffn_out_grad = after_ffn_grad.astype(jnp.bfloat16)
    grad_ffn_w_out = jnp.einsum(
        "nc,nd->cd", ffn_act, ffn_out_grad, preferred_element_type=jnp.float32
    )
    ffn_act_grad = jnp.einsum(
        "nd,cd->nc", ffn_out_grad, ffn_w_out, preferred_element_type=jnp.float32
    )
    unused_value, gelu_ffn = jax.vjp(jax.nn.gelu, ffn_pre)
    ffn_pre_grad = gelu_ffn(ffn_act_grad)[0].astype(jnp.bfloat16)
    grad_ffn_b = jnp.sum(ffn_pre_grad, axis=0, dtype=jnp.float32)
    grad_ffn_w_in = jnp.einsum(
        "nc,nd->cd", normed_two, ffn_pre_grad, preferred_element_type=jnp.float32
    )
    normed_two_grad = jnp.einsum(
        "nd,cd->nc", ffn_pre_grad, ffn_w_in, preferred_element_type=jnp.float32
    )
    unused_value, norm_two_back = jax.vjp(layer_norm, after_msg, gains[1], shifts[1])
    msg_side, gain_two, shift_two = norm_two_back(normed_two_grad)
    after_msg_grad = after_ffn_grad + msg_side
    grad_node_b1 = jnp.sum(after_msg_grad, axis=0)
    message_grad = (after_msg_grad / count).astype(jnp.bfloat16)
    grad_msg_out = jnp.einsum(
        "nkc,nd->cd", message_act, message_grad, preferred_element_type=jnp.float32
    )
    message_act_grad = jnp.einsum(
        "nd,cd->nc", message_grad, msg_out, preferred_element_type=jnp.float32
    )
    unused_value, gelu_msg = jax.vjp(jax.nn.gelu, before_act)
    before_grad = gelu_msg(jnp.broadcast_to(message_act_grad[:, None, :], before_act.shape))[
        0
    ].astype(jnp.bfloat16)
    grad_node_b0 = jnp.sum(before_grad, axis=(0, 1), dtype=jnp.float32)
    grad_msg_edge = jnp.einsum(
        "nkc,nkd->cd", edge_state, before_grad, preferred_element_type=jnp.float32
    )
    edge_total = edge_total + jnp.einsum(
        "nkd,cd->nkc", before_grad, msg_edge, preferred_element_type=jnp.float32
    )
    own_node = jnp.sum(before_grad, axis=1, dtype=jnp.float32)
    other_node = jnp.dot(
        one_hot, before_grad.reshape(-1, width), preferred_element_type=jnp.float32
    )
    pair_grad = jnp.concatenate([own_node, other_node], axis=-1).astype(jnp.bfloat16)
    grad_pair_w = jnp.einsum("nc,nd->cd", normed_one, pair_grad, preferred_element_type=jnp.float32)
    normed_one_grad = jnp.einsum("nd,cd->nc", pair_grad, pair_w, preferred_element_type=jnp.float32)
    unused_value, norm_one_back = jax.vjp(layer_norm, hidden, gains[0], shifts[0])
    input_side, gain_one, shift_one = norm_one_back(normed_one_grad)
    hidden_grad = after_msg_grad + input_side
    grads = (
        grad_pair_w,
        grad_msg_edge,
        grad_msg_out,
        grad_ffn_w_in,
        grad_ffn_w_out,
        grad_edge_pair_w,
        grad_edge_self_w,
        grad_edge_out_w,
        jnp.stack([gain_one, gain_two, gain_three]),
        jnp.stack([shift_one, shift_two, shift_three]),
        jnp.stack([grad_node_b0, grad_node_b1, grad_node_b2]),
        grad_ffn_b,
        jnp.stack([grad_edge_b0, grad_edge_b1]),
    )
    return (hidden_grad.astype(jnp.bfloat16), edge_total.astype(jnp.bfloat16), grads)


def on_device(
    clean_nodes,
    noise_nodes,
    edge_feats,
    neighbours,
    time_bins,
    cotangent,
    pair_weight,
    message_edge,
    message_out,
    ffn_in,
    ffn_out,
    edge_pair,
    edge_self,
    edge_out,
    norm_gain,
    norm_shift,
    node_bias,
    ffn_bias,
    edge_bias,
):
    sections = lax.axis_size("section")
    place = lax.axis_index("section")
    weights = tuple(
        (
            item[0]
            for item in (
                pair_weight,
                message_edge,
                message_out,
                ffn_in,
                ffn_out,
                edge_pair,
                edge_self,
                edge_out,
                norm_gain,
                norm_shift,
                node_bias,
                ffn_bias,
                edge_bias,
            )
        )
    )
    batches, node_count, width = clean_nodes.shape
    phase = (time_bins.astype(jnp.float32) + 0.5) * (math.pi * 0.5 / TBINS)
    start = jnp.cos(phase)[:, None, None] * clean_nodes.astype(jnp.float32) + jnp.sin(phase)[
        :, None, None
    ] * noise_nodes.astype(jnp.float32)
    zero_nodes = jnp.zeros((node_count, width), jnp.bfloat16)
    zero_edges = jnp.zeros(edge_feats.shape[1:], jnp.bfloat16)
    is_first = place == 0
    is_last = place == sections - 1

    def forward_step(step_index, carry):
        recv_nodes, recv_edges, back_nodes, kept_nodes, kept_edges, section_outs = carry
        item = step_index - place
        first_pass = (item >= 0) & (item < batches)
        second_pass = (item >= sections) & (item < sections + batches)
        index = jnp.clip(jnp.where(second_pass, item - sections, item), 0, batches - 1)
        predicted = back_nodes
        own_start = lax.dynamic_index_in_dim(start, index, 0, keepdims=False)
        lead_nodes = own_start + jnp.where(second_pass, predicted.astype(jnp.float32), 0.0)
        nodes_in = jnp.where(is_first, lead_nodes, recv_nodes.astype(jnp.float32))
        edges_in = jnp.where(
            is_first, lax.dynamic_index_in_dim(edge_feats, index, 0, keepdims=False), recv_edges
        )
        nearest = lax.dynamic_index_in_dim(neighbours, index, 0, keepdims=False)

        def run_layer(operand):
            after, edge_next, saved = forward_layer(weights, operand[0], operand[1], operand[2])
            return (after.astype(jnp.bfloat16), edge_next.astype(jnp.bfloat16))

        def skip_layer(operand):
            return (zero_nodes, zero_edges)

        out_nodes, out_edges = lax.cond(
            first_pass | second_pass, run_layer, skip_layer, (nodes_in, edges_in, nearest)
        )
        kept_nodes = lax.dynamic_update_index_in_dim(
            kept_nodes, jnp.where(second_pass, nodes_in, kept_nodes[index]), index, 0
        )
        kept_edges = lax.dynamic_update_index_in_dim(
            kept_edges, jnp.where(second_pass, edges_in, kept_edges[index]), index, 0
        )
        section_outs = lax.dynamic_update_index_in_dim(
            section_outs, jnp.where(second_pass, out_nodes, section_outs[index]), index, 0
        )
        recv_nodes, recv_edges = from_behind((out_nodes, out_edges), "section", 1)
        back_nodes = from_behind(out_nodes, "section", 1 - sections)
        return (recv_nodes, recv_edges, back_nodes, kept_nodes, kept_edges, section_outs)

    forward_init = (
        zero_nodes,
        zero_edges,
        zero_nodes,
        jnp.zeros((batches, node_count, width), jnp.float32),
        jnp.zeros_like(edge_feats),
        jnp.zeros((batches, node_count, width), jnp.bfloat16),
    )
    unused_nodes, unused_edges, unused_back, kept_nodes, kept_edges, section_outs = lax.fori_loop(
        0, 2 * sections + batches - 1, forward_step, forward_init
    )
    grads_zero = tuple((jnp.zeros(item.shape, jnp.float32) for item in weights))

    def backward_step(step_index, carry):
        recv_grad_nodes, recv_grad_edges, grads, input_grads = carry
        item = step_index - (sections - 1 - place)
        live = (item >= 0) & (item < batches)
        index = jnp.clip(item, 0, batches - 1)
        nodes_grad_out = jnp.where(
            is_last,
            lax.dynamic_index_in_dim(cotangent, index, 0, keepdims=False).astype(jnp.float32),
            recv_grad_nodes.astype(jnp.float32),
        )
        edges_grad_out = jnp.where(is_last, 0.0, recv_grad_edges.astype(jnp.float32))
        nearest = lax.dynamic_index_in_dim(neighbours, index, 0, keepdims=False)

        def run_back(operand):
            return backward_layer(
                weights, operand[0], operand[1], operand[2], operand[3], operand[4]
            )

        def skip_back(operand):
            return (zero_nodes, zero_edges, grads_zero)

        nodes_grad, edges_grad, terms = lax.cond(
            live,
            run_back,
            skip_back,
            (kept_nodes[index], kept_edges[index], nearest, nodes_grad_out, edges_grad_out),
        )
        grads = tuple((total + term for total, term in zip(grads, terms)))
        input_grads = lax.dynamic_update_index_in_dim(
            input_grads, jnp.where(live, nodes_grad, input_grads[index]), index, 0
        )
        recv_grad_nodes, recv_grad_edges = from_behind((nodes_grad, edges_grad), "section", -1)
        return (recv_grad_nodes, recv_grad_edges, grads, input_grads)

    backward_init = (
        zero_nodes,
        zero_edges,
        grads_zero,
        jnp.zeros((batches, node_count, width), jnp.bfloat16),
    )
    unused_grad_nodes, unused_grad_edges, grads, input_grads = lax.fori_loop(
        0, sections + batches - 1, backward_step, backward_init
    )
    totals = jax.tree.map(lambda part: part.astype(jnp.float32), lax.psum(for_sending(grads), "dp"))
    return (
        section_outs[None],
        input_grads[None],
        totals[0][None],
        totals[1][None],
        totals[2][None],
        totals[3][None],
        totals[4][None],
        totals[5][None],
        totals[6][None],
        totals[7][None],
        totals[8][None],
        totals[9][None],
        totals[10][None],
        totals[11][None],
        totals[12][None],
    )


BF16 = jnp.bfloat16
F32 = jnp.float32
MESH = pl.DeviceIdType.MESH
GELU_A = 0.7978845608028654
GELU_B = 0.044715


def gelu(x):
    return 0.5 * x * (1.0 + jnp.tanh(x * (GELU_A + (GELU_A * GELU_B) * (x * x))))


def gelu_both(x):
    square = x * x
    t = jnp.tanh(x * (GELU_A + (GELU_A * GELU_B) * square))
    half = 0.5 * (1.0 + t)
    slope = half + (0.5 * x) * (1.0 - t * t) * (GELU_A + (3.0 * GELU_A * GELU_B) * square)
    return x * half, slope


def mm(a, b):
    return jnp.dot(a, b, preferred_element_type=F32)


def mm_bt(a, b):
    return lax.dot_general(a, b, (((1,), (1,)), ((), ())), preferred_element_type=F32)


def mm_at(a, b):
    return lax.dot_general(a, b, (((0,), (0,)), ((), ())), preferred_element_type=F32)


def stacked(blocks):
    return jnp.concatenate(blocks, axis=0)


def row_mean(x):
    return jnp.mean(x, axis=-1, keepdims=True)


def normed(x):
    centred = x - row_mean(x)
    scale = lax.rsqrt(row_mean(centred * centred) + 1e-05)
    return centred * scale, scale


def norm_back(grad, unit, scale, gain):
    t = grad * gain
    return scale * (t - row_mean(t) - unit * row_mean(t * unit))


def col_sum(x):
    return jnp.sum(x, axis=0, keepdims=True)


def relay_kernel(
    dims,
    ecat0, oht, mix, clean, noise, cot, pw, mo, fi, fo, ep, gains, shifts, node_b, fb, edge_b, we_own, ws_own, wo_own,
    act, ig, g_fwd, g_bwd, g_dpq, g_small, g_msg, g_upd,
    start, par, eb0, wall_msg, wall_upd, fwd, bwd, sg,
    eg, eg_r, eg_b, msg_o, msg_f, upd_o, upd_f, wo, eb1,
    ecat, wcat, scat, pwn, parn, hin_r, hst, mb_s, mb_r, pq_s, pq_r, rq_s, rq_r,
    un0, un1, un2, hi_s, sc0, sc1, sc2, sci, u_s, slope_s, de, dacc, gp, gpe, dcat, act_t, edge_t,
    x_s, x_r, row_s, row_r, dpqo_r, dmb_s, dmb_r, dh1_s, dh1_r, dh1_f, dh2_s, dn3_s, da2_s, h1_s, a1_s,
    ld_sem, nx_ss, nx_rs, hop_ss, hop_rs,
    pq_ss, pq_rs, ag_ss, ag_rs, rq_ss, rq_rs, ag2_ss, ag2_rs,
    mb_ss, mb_rs, x_ss, x_rs, row_ss, row_rs, dpqo_rs, fw_ss, dmb_ss, dmb_rs, dh_ss, dh_rs,
    e1_ss, e1_rs, e2_ss, e2_rs, g_ss, g_rs, relay_ss, ring_ss, ring_rs, sib_ss, sib_rs,
):
    S, B, N, K, Q, D, DE, EP, FF, C = dims
    BN = B * N
    RB = 16
    top = DE + N
    me_s = lax.axis_index("section")
    me_d = lax.axis_index("dp")
    core = lax.rem(me_d, 2)
    pair = me_d - core
    w = lax.div(me_s, 2)
    q = 2 * lax.rem(me_s, 2) + core
    owner_d = pair + lax.div(w, B)
    slot = lax.rem(w, B)
    my_row = pl.multiple_of(slot * N + q * Q, Q)
    own_rows = pl.ds(top, Q)

    def quarter(j):
        return pl.ds(pl.multiple_of(DE + j * Q, Q), Q)

    def is_me(sec, dpi):
        return (sec == me_s) & (dpi == me_d)

    def far(src, dst, ssem, rsem, sec, dpi):
        return pltpu.make_async_remote_copy(
            src_ref=src, dst_ref=dst, send_sem=ssem, recv_sem=rsem,
            device_id={"section": sec, "dp": dpi}, device_id_type=MESH,
        )

    def push(src, dst, ssem, rsem, sec, dpi):
        lax.cond(
            is_me(sec, dpi),
            lambda: pltpu.make_async_copy(src, dst, rsem).start(),
            lambda: far(src, dst, ssem, rsem, sec, dpi).start(),
        )

    def arrive(ref, sem):
        pltpu.make_async_copy(ref, ref, sem).wait()

    def drain(ref, sem, sec, dpi):
        @pl.when(jnp.logical_not(is_me(sec, dpi)))
        def _():
            arrive(ref, sem)

    def worker_of(p, j):
        return 2 * (core * B + p) + j // 2, pair + j % 2

    def peer(k):
        j = lax.rem(q + k, 4)
        return j, 2 * w + lax.div(j, 2), pair + lax.rem(j, 2)

    works_here = lax.div(w, B) == core

    def at(p, first=0, size=16):
        return pl.ds(pl.multiple_of(p * N + first, size), size)

    near = jnp.clip(w - core * B, 0, B - 1)

    load = pltpu.make_async_copy(ecat0, ecat.at[0], ld_sem)
    load.start()
    barrier = pltpu.get_barrier_semaphore()
    for sec in range(S):
        for c in range(C):
            greeted = (c == pair) | (c == pair + 1) | (w == sec // 2)

            @pl.when(greeted & jnp.logical_not(is_me(sec, c)))
            def _():
                pl.semaphore_signal(
                    barrier, inc=1, device_id={"section": sec, "dp": c}, device_id_type=MESH
                )
    wall_msg[me_s] = we_own[...]
    wall_upd[me_s] = jnp.zeros(wall_upd.shape[1:], BF16)
    wall_upd[me_s, pl.ds(0, DE), pl.ds(0, DE)] = ws_own[...]
    wall_upd[me_s, pl.ds(0, DE), pl.ds(EP, DE)] = wo_own[...]
    bias = edge_b[pl.ds(1, 1), :]
    high = bias.astype(BF16).astype(F32)
    row = lax.broadcasted_iota(jnp.int32, (16, DE), 0)
    wall_upd[me_s, pl.ds(DE, 16), pl.ds(0, DE)] = jnp.where(
        row == 0, high, jnp.where(row == 1, bias - high, 0.0)
    ).astype(BF16)
    eb0[...] = jnp.zeros_like(eb0)
    eb0[:, pl.ds(0, DE)] = edge_b[pl.ds(0, 1), :]
    par[pl.ds(0, 1), :] = gains[0]
    par[pl.ds(1, 1), :] = shifts[0]
    par[pl.ds(2, 1), :] = node_b[0]
    par[pl.ds(3, 5), :] = jnp.zeros((5, D), F32)
    pl.semaphore_wait(barrier, 2 * S - 1 + 2 * (C - 2))

    def section_at(i):
        i = lax.rem(i + S, S)
        return jnp.where(i < S // 2, 2 * i, 2 * (S - i) - 1)

    place = jnp.where(lax.rem(me_s, 2) == 0, w, S - 1 - w)
    sides = ((section_at(place + 1), S // 2), (section_at(place - 1), S // 2 - 1))
    walls = (wall_msg, wall_upd)

    def half_of(which, layer, c):
        size = walls[which].shape[1] // 2
        return walls[which].at[layer, pl.ds(pl.multiple_of(c * size, size), size)]

    def ring_send(which, layer, side, hop):
        sec, reach = sides[side]
        if hop < reach:
            half = half_of(which, layer, core)
            far(half, half, ring_ss.at[which, side, hop], ring_rs.at[which, layer], sec, me_d).start()

    def ring_hop(which, side, hop):
        layer = section_at(place - hop if side == 0 else place + hop)
        half = half_of(which, layer, core)
        arrive(half, ring_rs.at[which, layer])
        ring_send(which, layer, side, hop)
        far(half, half, sib_ss.at[which, layer], sib_rs.at[which, layer], me_s, pair + 1 - core).start()

    hops = [(hop, side) for hop in range(1, S // 2 + 1) for side in range(2) if hop <= sides[side][1]]

    def ring_later(second):
        for hop, side in hops:
            early = (place > 0) & ((place >= hop) if side == 0 else (place + hop <= S))

            @pl.when(early != second)
            def _():
                ring_hop(1, side, hop)

    for side in range(2):
        ring_send(0, me_s, side, 0)
    before = lax.rem(me_s + S - 1, S)
    far(pw, pwn, nx_ss.at[0], nx_rs.at[0], before, me_d).start()
    far(par, parn, nx_ss.at[1], nx_rs.at[1], before, me_d).start()

    for p in range(B):
        rows = pl.ds(p * N, N)
        start[rows, :] = mix[0, p] * clean[rows, :].astype(F32) + mix[1, p] * noise[rows, :].astype(F32)

    def ring_drain():
        for which in range(2):
            for side in range(2):
                for hop in range(sides[side][1]):
                    arrive(half_of(which, me_s, core), ring_ss.at[which, side, hop])
            for layer in range(S):
                @pl.when(layer != me_s)
                def _():
                    arrive(half_of(which, layer, core), sib_ss.at[which, layer])

    def unpack_messages(t):
        @pl.when(t != me_s)
        def _():
            arrive(half_of(0, t, 1 - core), sib_rs.at[0, t])

        wcat[t, pl.ds(0, DE), :] = wall_msg[t]

    def unpack_updates(t):
        @pl.when(t != me_s)
        def _():
            arrive(half_of(1, t, 1 - core), sib_rs.at[1, t])

        scat[t, pl.ds(0, DE), :] = wall_upd[t, pl.ds(0, DE), pl.ds(0, EP)]
        wo[t, pl.ds(0, DE), :] = wall_upd[t, pl.ds(0, DE), pl.ds(EP, EP)]
        wo[t, pl.ds(DE, N), :] = jnp.zeros((N, EP), BF16)
        eb1[t] = wall_upd[t, pl.ds(DE, 16), pl.ds(0, EP)]

    def rows_out(p, src, dst, ssem, rsem):
        for j in range(4):
            sec, dpi = worker_of(p, j)
            push(src.at[at(p, j * Q, Q)], dst, ssem, rsem, sec, dpi)

    def rows_drain(src, ssem):
        lax.cond(
            works_here,
            lambda: arrive(src.at[pl.ds(0, B * N - Q)], ssem),
            lambda: arrive(src, ssem),
        )

    def spread(rows, half, ref, layer, ssem, rsem, rows_sem):
        arrive(rows, rows_sem)
        for k in range(1, 4):
            _, sec, dpi = peer(k)
            far(rows.at[:, pl.ds(half, half)], ref.at[layer, quarter(q)], ssem, rsem, sec, dpi).start()
        ref[layer, own_rows, :] = rows[:, pl.ds(0, half)]
        ref[layer, quarter(q), :] = rows[:, pl.ds(half, half)]

    def spread_wait(ref, layer, sem):
        arrive(ref.at[layer, pl.ds(DE, 3 * Q)], sem)

    def share(group, src, dst):
        for c in range(C):
            push(src, dst.at[me_d], g_ss.at[group, c], g_rs.at[group, me_d], me_s, c)

    def share_wait(group, src, dst):
        for c in range(C):
            arrive(dst.at[c], g_rs.at[group, c])
            drain(src, g_ss.at[group, c], me_s, c)

    def share_near(group, src, dst):
        for c in range(C):
            @pl.when((c == pair) | (c == pair + 1) | (core == c % 2))
            def _():
                push(src, dst(me_d), g_ss.at[group, c], g_rs.at[group, me_d], me_s, c)

    def share_relay(group, src, dst):
        for c in range(C):
            @pl.when((c != me_d) & (core == c % 2))
            def _():
                arrive(dst(c), g_rs.at[group, c])
                far(dst(c), dst(c), relay_ss.at[group - 2, c // 2], g_rs.at[group, c], me_s, pair + 1 - core).start()

    def share_near_wait(group, src, dst):
        for c in range(C):
            @pl.when((c == me_d) | (core != c % 2))
            def _():
                arrive(dst(c), g_rs.at[group, c])

            @pl.when((c != me_d) & ((c == pair) | (c == pair + 1) | (core == c % 2)))
            def _():
                arrive(src, g_ss.at[group, c])

            @pl.when((c != me_d) & (core == c % 2))
            def _():
                arrive(dst(c), relay_ss.at[group - 2, c // 2])

    steps = 4
    KC = K // steps
    RC = KC * Q

    def messages(t):
        own = wcat[t, own_rows, :].astype(F32)
        total = jnp.zeros((Q, D), F32)
        for i in range(steps):
            pre = mm(ecat[t, pl.ds(i * RC, RC), :], wcat[t, pl.ds(0, top), :])
            for k in range(KC):
                total = total + gelu(pre[k * Q : (k + 1) * Q] + own)
        mb_s[...] = (total * (1.0 / K)).astype(BF16)

    def edge_update(t):
        own = scat[t, own_rows, :].astype(F32)
        bias = eb1[t, pl.ds(0, 1), :].astype(F32) + eb1[t, pl.ds(1, 1), :].astype(F32)
        for i in range(steps):
            pe = mm(ecat[t, pl.ds(i * RC, RC), :], scat[t, pl.ds(0, top), :])
            act_e = stacked([gelu(pe[k * Q : (k + 1) * Q] + own).astype(BF16) for k in range(KC)])
            z = mm(act_e, wo[t])
            for k in range(KC):
                rows = pl.ds(i * RC + k * Q, Q)
                ecat[t + 1, rows, :] = (ecat[t, rows, :].astype(F32) + z[k * Q : (k + 1) * Q] + bias).astype(BF16)

    chunks = 4
    FC = FF // chunks

    def node_forward(step):
        @pl.when(step < S)
        def _():
            arrive(pwn, nx_rs.at[0])
            arrive(parn, nx_rs.at[1])
            arrive(pw, nx_ss.at[0])
            arrive(par, nx_ss.at[1])

        @pl.when(step == 0)
        def _():
            hi_s[...] = start[...]

        @pl.when(step > 0)
        def _():
            arrive(hin_r, hop_rs)
            first = jnp.where(me_s == 0, 1.0, 0.0)
            for i in range(0, BN, RB):
                rows = pl.ds(i, RB)
                hi_s[rows, :] = hin_r[rows, :].astype(F32) + first * start[rows, :]

        later = lax.rem(me_s + 1, S)

        def turn(n, carry):
            p = lax.rem(near + n, B)
            whole = at(p, 0, N)
            arrive(mb_r.at[whole], mb_rs.at[p])
            mean = mm(mb_r[whole, :], mo[...])
            for i in range(0, N, RB):
                rows = at(p, i)
                h1 = hi_s[rows, :] + mean[i : i + RB] + node_b[1]
                h1_s[rows, :] = h1
                unit, scale = normed(h1)
                un1[rows, :] = unit
                sc1[rows, :] = scale
                fwd[rows, pl.ds(2 * D, D)] = (unit * gains[1] + shifts[1]).astype(BF16)
                fwd[rows, pl.ds(D, D)] = mb_r[rows, :]
            a2 = fwd[whole, pl.ds(2 * D, D)]
            y = jnp.zeros((N, D), F32)
            for c in range(chunks):
                cols = pl.ds(c * FC, FC)
                u = mm(a2, fi[:, cols])
                v = []
                for i in range(0, N, RB):
                    block = u[i : i + RB] + fb[:, cols]
                    u_s[at(p, i), cols] = block
                    v.append(gelu(block).astype(BF16))
                y = y + mm(stacked(v), fo[cols, :])
            last = jnp.where(me_s == S - 1, 1.0, 0.0)
            for i in range(0, N, RB):
                rows = at(p, i)
                h2 = h1_s[rows, :] + y[i : i + RB] + node_b[2]
                rounded = h2.astype(BF16)
                hst[rows, :] = rounded
                unit, scale = normed(h2)
                un2[rows, :] = unit
                sc2[rows, :] = scale
                fwd[rows, pl.ds(3 * D, D)] = (unit * gains[2] + shifts[2]).astype(BF16)
                pair_norm(rows, rounded.astype(F32) + last * start[rows, :], parn)
            rq = mm(fwd[whole, pl.ds(3 * D, D)], ep[...])
            for i in range(0, N, RB):
                rows = at(p, i)
                rq_s[rows, pl.ds(0, EP)] = (rq[i : i + RB, :EP] + eb0[...]).astype(BF16)
                rq_s[rows, pl.ds(EP, EP)] = rq[i : i + RB, EP:].astype(BF16)
            pair_rows(p, pwn, parn)

            @pl.when(me_s < S - 1)
            def _():
                rows_out(p, rq_s, rq_r, rq_ss, rq_rs)

            @pl.when(step < 2 * S - 1)
            def _():
                rows_out(p, pq_s, pq_r, pq_ss, pq_rs)

            @pl.when(n == 0)
            def _():
                pass_on(step)

            return carry

        lax.fori_loop(0, B, turn, 0)

        @pl.when(step < 2 * S - 1)
        def _():
            far(hst, hin_r, hop_ss, hop_rs, later, me_d).start()

        @pl.when(step >= S)
        def _():
            act[...] = hst[...]
            for i in range(0, BN, RB):
                rows = pl.ds(i, RB)
                unit, scale = normed(hi_s[rows, :])
                hi_s[rows, :] = unit
                sci[rows, :] = scale
                fwd[rows, pl.ds(0, D)] = (unit * gains[0] + shifts[0]).astype(BF16)
                for c in range(chunks):
                    cols = pl.ds(c * FC, FC)
                    slope_s[rows, cols] = gelu_both(u_s[rows, cols])[1].astype(BF16)
            share(0, fwd, g_fwd)

    def pair_norm(rows, hidden, first):
        unit, scale = normed(hidden)
        un0[rows, :] = unit
        sc0[rows, :] = scale
        a1_s[rows, :] = (unit * first[pl.ds(0, 1), :] + first[pl.ds(1, 1), :]).astype(BF16)

    def pair_rows(p, weight, first):
        whole = at(p, 0, N)
        for half in range(2):
            cols = pl.ds(half * D, D)
            value = mm(a1_s[whole, :], weight[:, cols])
            if half == 0:
                value = value + first[pl.ds(2, 1), :]
            pq_s[whole, cols] = value.astype(BF16)

    def pass_on(step):
        t = lax.rem(step, S)

        @pl.when(t < S - 1)
        def _():
            spread(rq_r, EP, scat, t, ag2_ss, ag2_rs, rq_rs)

        @pl.when(step < 2 * S - 1)
        def _():
            spread(pq_r, D, wcat, lax.rem(step + 1, S), ag_ss, ag_rs, pq_rs)

    def node_forward_drain():
        arrive(hst, hop_ss)
        rows_drain(pq_s, pq_ss)

        @pl.when(me_s < S - 1)
        def _():
            rows_drain(rq_s, rq_ss)

    @pl.when(me_s == 0)
    def _():
        for i in range(0, BN, RB):
            rows = pl.ds(i, RB)
            pair_norm(rows, start[rows, :], par)
        for p in range(B):
            pair_rows(p, pw, par)
            rows_out(p, pq_s, pq_r, pq_ss, pq_rs)

    def message_slope(t):
        own = wcat[t, own_rows, :].astype(F32)
        for i in range(steps):
            pre = mm(ecat[t, pl.ds(i * RC, RC), :], wcat[t, pl.ds(0, top), :])
            for k in range(KC):
                gp[t, pl.ds(i * RC + k * Q, Q), :] = gelu_both(pre[k * Q : (k + 1) * Q] + own)[1].astype(BF16)

    def edge_slope(t):
        own = scat[t, own_rows, :].astype(F32)
        values = []
        for i in range(steps):
            pe = mm(ecat[t, pl.ds(i * RC, RC), :], scat[t, pl.ds(0, top), :])
            for k in range(KC):
                value, slope = gelu_both(pe[k * Q : (k + 1) * Q] + own)
                values.append(value.astype(BF16))
                gpe[t, pl.ds(i * RC + k * Q, Q), :] = slope.astype(BF16)
        act_t[t] = stacked(values).T

    def prepare(t):
        message_slope(t)
        edge_t[t] = ecat[t].T

        @pl.when(t > 0)
        def _():
            edge_slope(t - 1)

    def forward_step(step, carry):
        t = lax.rem(step, S)

        @pl.when(step < S)
        def _():
            unpack_messages(t)

        spread_wait(wcat, t, ag_rs)
        messages(t)
        spread_wait(wcat, t, ag_ss)
        push(mb_s, mb_r.at[pl.ds(my_row, Q)], mb_ss, mb_rs.at[slot], t, owner_d)

        for second in range(2):
            @pl.when(step == second)
            def _():
                ring_later(second == 1)

        @pl.when((step == 0) & (me_s == 0))
        def _():
            rows_drain(pq_s, pq_ss)

        @pl.when((step > 0) & (me_s == lax.rem(step + S - 1, S)))
        def _():
            node_forward_drain()

        @pl.when(me_s == t)
        def _():
            node_forward(step)

        @pl.when((me_s != t) & (step >= S))
        def _():
            prepare(t)

        @pl.when(me_s != t)
        def _():
            pass_on(step)

        @pl.when(t < S - 1)
        def _():
            @pl.when(step < S)
            def _():
                unpack_updates(t)

            spread_wait(scat, t, ag2_rs)
            edge_update(t)
            spread_wait(scat, t, ag2_ss)

        drain(mb_s, mb_ss, t, owner_d)
        return carry

    for hop, side in hops:
        ring_hop(0, side, hop)
    for side in range(2):
        ring_send(1, me_s, side, 0)
    load.wait()
    spread(pq_r, D, wcat, 0, ag_ss, ag_rs, pq_rs)
    lax.fori_loop(0, 2 * S, forward_step, 0)
    ring_drain()

    @pl.when(me_s != S - 1)
    def _():
        arrive(half_of(1, S - 1, 1 - core), sib_rs.at[1, S - 1])

    def edge_back(t):
        b2, n2 = lax.rem(t, 2), lax.rem(t + 1, 2)
        total = jnp.zeros((Q, EP), F32)
        for i in range(steps):
            chunk = pl.ds(i * RC, RC)
            carry = mm_bt(dcat[b2, chunk, pl.ds(0, D)], wcat[t, pl.ds(0, top), :])
            low = []
            for k in range(KC):
                rows = pl.ds(i * RC + k * Q, Q)
                low.append((dacc[rows, :] + carry[k * Q : (k + 1) * Q]).astype(BF16))
                de[n2, rows, :] = low[-1]
            dw = mm_bt(stacked(low), wo[t - 1])
            for k in range(KC):
                rows = pl.ds(i * RC + k * Q, Q)
                d = (gpe[t - 1, rows, :].astype(F32) * dw[k * Q : (k + 1) * Q]).astype(BF16)
                total = total + d.astype(F32)
                dcat[n2, rows, pl.ds(D, EP)] = d
        row_s[:, pl.ds(2 * D, EP)] = total.astype(BF16)
        x_s[:, pl.ds(D, EP)] = mm(oht[...], dcat[n2, :, pl.ds(D, EP)]).astype(BF16)

    def edge_pass(t):
        b3 = lax.rem(t, 2)
        for i in range(steps):
            rows = pl.ds(i * RC, RC)
            d = dcat[b3, rows, pl.ds(D, EP)]
            dacc[rows, :] = de[b3, rows, :].astype(F32) + mm_bt(d, scat[t, pl.ds(0, top), :])

    blocks = 2 * C
    my_block = lax.rem(me_s, 2) * C + me_d
    BW, HM, HU = msg_o.shape[2], msg_o.shape[1], upd_o.shape[1]

    def block_of(t, half, c, size):
        return eg.at[t, half, pl.ds(0, size), pl.ds(pl.multiple_of(c * BW, BW), BW)]

    def blocks_out(t, size):
        for k in range(blocks):
            @pl.when(k != my_block)
            def _():
                far(
                    block_of(t, k // C, k % C, size), eg_r.at[t, my_block, pl.ds(0, size)],
                    e1_ss.at[t, k], e1_rs.at[t, my_block], 2 * w + k // C, k % C,
                ).start()

    def edge_grads(t):
        grad = mm(edge_t[t, pl.ds(0, DE), :], dcat[lax.rem(t, 2), :, pl.ds(0, D)]).astype(BF16)
        for half in range(2):
            eg[t, half, pl.ds(0, HM), :] = grad[half * HM : (half + 1) * HM]

        @pl.when(t > 0)
        def _():
            n2 = lax.rem(t + 1, 2)
            edges = mm(edge_t[t - 1, pl.ds(0, DE), :], dcat[n2, :, pl.ds(D, EP)])
            outs = mm(act_t[t - 1, pl.ds(0, DE), :], de[n2])
            bias = jnp.sum(de[n2].astype(F32), axis=0, keepdims=True)
            grad = jnp.concatenate([edges, outs], axis=1).astype(BF16)
            eg[t, 0, pl.ds(HM, HU), :] = grad[:HU]
            eg[t, 1, pl.ds(HM, DE - HU), :] = grad[HU:]
            eg[t, 1, pl.ds(HM + DE - HU, 16), pl.ds(0, EP)] = jnp.broadcast_to(bias, (16, EP)).astype(BF16)
            eg[t, 1, pl.ds(HM + DE - HU, 16), pl.ds(EP, EP)] = jnp.zeros((16, EP), BF16)
            eg[t, 1, pl.ds(HM + DE - HU + 16, 2 * HU - DE - 16), :] = jnp.zeros((2 * HU - DE - 16, 2 * EP), BF16)
            blocks_out(t, HM + HU)

        @pl.when(t == 0)
        def _():
            blocks_out(t, HM)

    def blocks_sum(t, size):
        eg_r[t, my_block, pl.ds(0, size), :] = block_of(t, lax.rem(me_s, 2), me_d, size)[...]
        for k in range(blocks):
            @pl.when(k != my_block)
            def _():
                arrive(eg_r.at[t, k, pl.ds(0, size)], e1_rs.at[t, k])
                arrive(block_of(t, k // C, k % C, size), e1_ss.at[t, k])
        total = eg_r[t, 0, pl.ds(0, size), :].astype(F32)
        for k in range(1, blocks):
            total = total + eg_r[t, k, pl.ds(0, size), :].astype(F32)
        eg_b[t, pl.ds(0, size), :] = total.astype(BF16)
        push(eg_b.at[t, pl.ds(0, HM)], msg_o.at[me_s], e2_ss.at[0, t], e2_rs.at[0, me_s], t, me_d)
        if size > HM:
            push(eg_b.at[t, pl.ds(HM, HU)], upd_o.at[me_s], e2_ss.at[1, t], e2_rs.at[1, me_s], t - 1, me_d)

    def gather_blocks():
        for k in range(1, 4):
            j, sec, dpi = peer(k)
            rows = pl.ds(pl.multiple_of(j * Q, Q), Q)
            far(x_s.at[rows], x_r.at[q], x_ss, x_rs, sec, dpi).start()
        x_r[q] = x_s[pl.ds(pl.multiple_of(q * Q, Q), Q), :]

    def gather_wait():
        arrive(x_r.at[pl.ds(0, 3)], x_rs)
        arrive(x_s.at[pl.ds(0, 3 * Q)], x_ss)
        total = x_r[0].astype(F32)
        for j in range(1, 4):
            total = total + x_r[j].astype(F32)
        return total

    def message_back(t):
        b2 = lax.rem(t, 2)
        dm = dmb_r[...].astype(F32)
        total = jnp.zeros((Q, D), F32)
        for k in range(K):
            rows = pl.ds(k * Q, Q)
            d = (gp[t, rows, :].astype(F32) * dm).astype(BF16)
            total = total + d.astype(F32)
            dcat[b2, rows, pl.ds(0, D)] = d
        row_s[:, pl.ds(0, D)] = total.astype(BF16)
        x_s[:, pl.ds(0, D)] = mm(oht[...], dcat[b2, :, pl.ds(0, D)]).astype(BF16)

    def node_backward():
        @pl.when(me_s < S - 1)
        def _():
            arrive(dh1_r, dh_rs)

        def turn(n, carry):
            p = lax.rem(near + n, B)
            whole = at(p, 0, N)

            @pl.when(me_s < S - 1)
            def _():
                arrive(row_r.at[whole], row_rs.at[p])
                dn0 = mm_bt(row_r[whole, pl.ds(0, 2 * D)], pwn[...])
                dn3 = mm_bt(row_r[whole, pl.ds(2 * D, 2 * EP)], ep[...])
                for i in range(0, N, RB):
                    rows = at(p, i)
                    dn = dn3[i : i + RB]
                    dn3_s[rows, :] = dn
                    first = norm_back(dn0[i : i + RB], un0[rows, :], sc0[rows, :], parn[pl.ds(0, 1), :])
                    dh = (dh1_r[rows, :].astype(F32) + first).astype(BF16).astype(F32)
                    dh2_s[rows, :] = dh + norm_back(dn, un2[rows, :], sc2[rows, :], gains[2])

            @pl.when(me_s == S - 1)
            def _():
                dh2_s[whole, :] = cot[whole, :].astype(F32)

            dy = dh2_s[whole, :].astype(BF16)
            bwd[whole, pl.ds(D, D)] = dy
            da2 = jnp.zeros((N, D), F32)
            for c in range(chunks):
                cols = pl.ds(c * FC, FC)
                dv = mm_bt(dy, fo[cols, :])
                du = stacked(
                    [(slope_s[at(p, i), cols].astype(F32) * dv[i : i + RB]).astype(BF16) for i in range(0, N, RB)]
                )
                da2 = da2 + mm_bt(du, fi[:, cols])
            for i in range(0, N, RB):
                rows = at(p, i)
                block = da2[i : i + RB]
                da2_s[rows, :] = block
                dh1 = dh2_s[rows, :] + norm_back(block, un1[rows, :], sc1[rows, :], gains[1])
                dh1_f[rows, :] = dh1
                bwd[rows, pl.ds(0, D)] = (dh1 * (1.0 / K)).astype(BF16)
            dmb_s[whole, :] = mm_bt(bwd[whole, pl.ds(0, D)], mo[...]).astype(BF16)
            rows_out(p, dmb_s, dmb_r, dmb_ss, dmb_rs)
            return carry

        lax.fori_loop(0, B, turn, 0)

        @pl.when(me_s > 0)
        def _():
            dh1_s[...] = dh1_f[...].astype(BF16)
            far(dh1_s, dh1_r, dh_ss, dh_rs, me_s - 1, me_d).start()

        @pl.when(me_s < S - 1)
        def _():
            far(row_r.at[:, pl.ds(0, 2 * D)], dpqo_r, fw_ss, dpqo_rs, me_s + 1, me_d).start()
            drs = row_r[:, pl.ds(2 * D, 2 * EP)]
            bwd[:, pl.ds(2 * D, 2 * EP)] = drs
            dn = dn3_s[...]
            sg[pl.ds(11, 1), :] = col_sum(dn * un2[...])
            sg[pl.ds(12, 1), :] = col_sum(dn)
            sg[pl.ds(16, 1), pl.ds(0, EP)] = col_sum(drs[:, :EP].astype(F32))

        @pl.when(me_s == S - 1)
        def _():
            bwd[:, pl.ds(2 * D, 2 * EP)] = jnp.zeros((B * N, 2 * EP), BF16)
            sg[pl.ds(11, 1), :] = jnp.zeros((1, D), F32)
            sg[pl.ds(12, 1), :] = jnp.zeros((1, D), F32)
            sg[pl.ds(16, 1), pl.ds(0, EP)] = jnp.zeros((1, EP), F32)

        share(1, bwd, g_bwd)
        sg[pl.ds(13, 1), :] = col_sum(dh2_s[...])
        sg[pl.ds(8, 1), :] = col_sum(da2_s[...] * un1[...])
        sg[pl.ds(9, 1), :] = col_sum(da2_s[...])
        sg[pl.ds(10, 1), :] = col_sum(dh1_f[...])

    def node_backward_drain():
        rows_drain(dmb_s, dmb_ss)

        @pl.when(me_s > 0)
        def _():
            arrive(dh1_s, dh_ss)

        @pl.when(me_s < S - 1)
        def _():
            arrive(row_r.at[:, pl.ds(0, 2 * D)], fw_ss)

    dacc[...] = jnp.zeros_like(dacc)

    def backward_step(step, carry):
        t = S - 1 - step

        @pl.when(me_s == t)
        def _():
            node_backward()

        @pl.when(((t == S - 1) & (me_s >= S - 2)) | (me_s == t - 2))
        def _():
            prepare(me_s)

        @pl.when(t < S - 1)
        def _():
            edge_pass(t)

        @pl.when(t + 2 < S)
        def _():
            blocks_sum(t + 2, HM + HU)

        @pl.when(t == 0)
        def _():
            blocks_sum(1, HM + HU)

        arrive(dmb_r, dmb_rs)
        message_back(t)

        @pl.when(t > 0)
        def _():
            edge_back(t)

        @pl.when(t == 0)
        def _():
            x_s[:, pl.ds(D, EP)] = jnp.zeros((N, EP), BF16)

        gather_blocks()
        other = gather_wait().astype(BF16)
        row_s[:, pl.ds(D, D)] = other[:, :D]
        row_s[:, pl.ds(2 * D + EP, EP)] = other[:, D:]
        dpq = row_s.at[:, pl.ds(0, 2 * D)]

        @pl.when(t > 0)
        def _():
            push(row_s, row_r.at[pl.ds(my_row, Q)], row_ss, row_rs.at[slot], t - 1, owner_d)

        @pl.when(t == 0)
        def _():
            push(dpq, dpqo_r.at[pl.ds(my_row, Q)], row_ss, dpqo_rs, t, owner_d)

        edge_grads(t)

        @pl.when(t > 0)
        def _():
            drain(row_s, row_ss, t - 1, owner_d)

        @pl.when(t == 0)
        def _():
            drain(dpq, row_ss, t, owner_d)

        @pl.when(me_s == t)
        def _():
            node_backward_drain()

        return carry

    lax.fori_loop(0, S, backward_step, 0)

    arrive(dpqo_r, dpqo_rs)
    across = [pl.ds(p * N, N) for p in range(B)]
    for p in range(B):
        share_near(2 + p, dpqo_r.at[across[p]], lambda c, p=p: g_dpq.at[c, across[p]])
    dpq = dpqo_r[...]
    sg[pl.ds(2, 1), :] = col_sum(dpq[:, :D].astype(F32))
    dn = mm_bt(dpq, pw[...])
    unit = hi_s[...]
    sg[pl.ds(0, 1), :] = col_sum(dn * unit)
    sg[pl.ds(1, 1), :] = col_sum(dn)
    share(2 + B, sg, g_small)
    ig[...] = (dh1_f[...] + norm_back(dn, unit, sci[...], gains[0])).astype(BF16)
    blocks_sum(0, HM)
    for p in range(B):
        share_relay(2 + p, dpqo_r.at[across[p]], lambda c, p=p: g_dpq.at[c, across[p]])
    def combine(kind, src, final):
        for sec in range(S):
            arrive(src.at[sec], e2_rs.at[kind, sec])
        for half in range(2):
            total = src[half].astype(F32)
            for sec in range(half + 2, S, 2):
                total = total + src[sec].astype(F32)
            final[half] = total.astype(BF16)

    @pl.when(me_s < S - 1)
    def _():
        combine(1, upd_o, upd_f)

    @pl.when(me_s == S - 1)
    def _():
        upd_f[...] = jnp.zeros_like(upd_f)

    share(4 + B, upd_f, g_upd)
    combine(0, msg_o, msg_f)
    share(3 + B, msg_f, g_msg)
    for t in range(S):
        drain(eg_b.at[t, pl.ds(0, HM)], e2_ss.at[0, t], t, me_d)
        if t > 0:
            drain(eg_b.at[t, pl.ds(HM, HU)], e2_ss.at[1, t], t - 1, me_d)
    share_wait(0, fwd, g_fwd)
    share_wait(1, bwd, g_bwd)
    for p in range(B):
        share_near_wait(2 + p, dpqo_r.at[across[p]], lambda c, p=p: g_dpq.at[c, across[p]])
    share_wait(2 + B, sg, g_small)
    share_wait(3 + B, msg_f, g_msg)
    share_wait(4 + B, upd_f, g_upd)


def run_relay(dims, operands):
    S, B, N, K, Q, D, DE, EP, FF, C = dims
    R = K * Q
    BN = B * N
    tall = DE + N + Q
    vm = pl.BlockSpec(memory_space=pltpu.VMEM)
    hbm = pl.BlockSpec(memory_space=pl.ANY)
    dma = pltpu.SemaphoreType.DMA
    sds = jax.ShapeDtypeStruct
    BW = D // C
    tile = 32
    held = -(-(DE + 16) // tile) * tile
    scratch = [
        pltpu.VMEM((BN, D), F32),
        pltpu.VMEM((8, D), F32),
        pltpu.VMEM((1, EP), F32),
        pltpu.VMEM((S, DE, D), BF16),
        pltpu.VMEM((S, held, 2 * EP), BF16),
        pltpu.VMEM((BN, 4 * D), BF16),
        pltpu.VMEM((BN, 2 * D + 2 * EP), BF16),
        pltpu.VMEM((24, D), F32),
        pltpu.VMEM((S, 2, (DE + held) // 2, D), BF16),
        pltpu.VMEM((S, 2 * C, (DE + held) // 2, BW), BF16),
        pltpu.VMEM((S, (DE + held) // 2, BW), BF16),
        pltpu.VMEM((S, DE // 2, BW), BF16),
        pltpu.VMEM((2, DE // 2, BW), BF16),
        pltpu.VMEM((S, held // 2, BW), BF16),
        pltpu.VMEM((2, held // 2, BW), BF16),
        pltpu.VMEM((S, EP, EP), BF16),
        pltpu.VMEM((S, 16, EP), BF16),
        pltpu.VMEM((S, R, EP), BF16),
        pltpu.VMEM((S, tall, D), BF16),
        pltpu.VMEM((S, tall, EP), BF16),
        pltpu.VMEM((D, 2 * D), BF16),
        pltpu.VMEM((8, D), F32),
        pltpu.VMEM((BN, D), BF16),
        pltpu.VMEM((BN, D), BF16),
        pltpu.VMEM((Q, D), BF16),
        pltpu.VMEM((BN, D), BF16),
        pltpu.VMEM((BN, 2 * D), BF16),
        pltpu.VMEM((Q, 2 * D), BF16),
        pltpu.VMEM((BN, 2 * EP), BF16),
        pltpu.VMEM((Q, 2 * EP), BF16),
        pltpu.VMEM((BN, D), F32),
        pltpu.VMEM((BN, D), F32),
        pltpu.VMEM((BN, D), F32),
        pltpu.VMEM((BN, D), F32),
        pltpu.VMEM((BN, 1), F32),
        pltpu.VMEM((BN, 1), F32),
        pltpu.VMEM((BN, 1), F32),
        pltpu.VMEM((BN, 1), F32),
        pltpu.VMEM((BN, FF), F32),
        pltpu.VMEM((BN, FF), BF16),
        pltpu.VMEM((2, R, EP), BF16),
        pltpu.VMEM((R, EP), F32),
        pltpu.VMEM((S, R, D), BF16),
        pltpu.VMEM((S, R, EP), BF16),
        pltpu.VMEM((2, R, D + EP), BF16),
        pltpu.VMEM((S, EP, R), BF16),
        pltpu.VMEM((S, EP, R), BF16),
        pltpu.VMEM((N, D + EP), BF16),
        pltpu.VMEM((4, Q, D + EP), BF16),
        pltpu.VMEM((Q, 2 * D + 2 * EP), BF16),
        pltpu.VMEM((BN, 2 * D + 2 * EP), BF16),
        pltpu.VMEM((BN, 2 * D), BF16),
        pltpu.VMEM((BN, D), BF16),
        pltpu.VMEM((Q, D), BF16),
        pltpu.VMEM((BN, D), BF16),
        pltpu.VMEM((BN, D), BF16),
        pltpu.VMEM((BN, D), F32),
        pltpu.VMEM((BN, D), F32),
        pltpu.VMEM((BN, D), F32),
        pltpu.VMEM((BN, D), F32),
        pltpu.VMEM((BN, D), F32),
        pltpu.VMEM((BN, D), BF16),
        dma, dma((2,)), dma((2,)), dma, dma,
        dma, dma, dma, dma, dma, dma, dma, dma,
        dma, dma((B,)), dma, dma, dma, dma((B,)), dma,
        dma, dma, dma, dma, dma,
        dma((S, 2 * C)), dma((S, 2 * C)), dma((2, S)), dma((2, S)), dma((5 + B, C)), dma((5 + B, C)),
        dma((B, C // 2)), dma((2, 2, S // 2)), dma((2, S)), dma((2, S)), dma((2, S)),
    ]
    return pl.pallas_call(
        functools.partial(relay_kernel, dims),
        out_shape=(
            sds((BN, D), BF16),
            sds((BN, D), BF16),
            sds((C, BN, 4 * D), BF16),
            sds((C, BN, 2 * D + 2 * EP), BF16),
            sds((C, BN, 2 * D), BF16),
            sds((C, 24, D), F32),
            sds((C, 2, DE // 2, BW), BF16),
            sds((C, 2, held // 2, BW), BF16),
        ),
        in_specs=[hbm, vm, pl.BlockSpec(memory_space=pltpu.SMEM)] + [vm] * 16,
        out_specs=(vm,) * 2 + (hbm,) * 6,
        scratch_shapes=scratch,
        compiler_params=pltpu.CompilerParams(
            collective_id=0, has_side_effects=True, vmem_limit_bytes=62 * 1024 * 1024
        ),
    )(*operands)


def gradient_kernel(
    dims,
    fwd, bwd, dpq, small, edge, upd, fi, fo, fb, act, ig,
    g_pair, g_edge, g_out, g_fi, g_fo, g_ep, g_self, g_eout, g_gain, g_shift, g_nb, g_fb, g_eb, act_out, ig_out,
    fwd_v, bwd_v, dpq_v, fi_v, fo_v, gfi_v, gfo_v, pair_v, out_v, edge_v, upd_v, in_sems, sems,
):
    S, B, N, K, Q, D, DE, EP, FF, C = dims
    chunks = 4
    FC = FF // chunks

    def part(c, size=D):
        return pl.ds(c * size, size)

    loads = {}

    def load(name, src, dst):
        loads[name] = pltpu.make_async_copy(src, dst, in_sems.at[len(loads)])
        loads[name].start()

    load("a2", fwd.at[:, part(2)], fwd_v.at[2])
    load("dy", bwd.at[:, part(1)], bwd_v.at[1])
    for c in range(chunks):
        load(("fi", c), fi.at[:, part(c, FC)], fi_v.at[c])
        load(("fo", c), fo.at[part(c, FC)], fo_v.at[c])
    load("a1", fwd.at[:, part(0)], fwd_v.at[0])
    load("dpq0", dpq.at[:, part(0)], dpq_v.at[0])
    load("dpq1", dpq.at[:, part(1)], dpq_v.at[1])
    load("mbar", fwd.at[:, part(1)], fwd_v.at[1])
    load("dmsg", bwd.at[:, part(0)], bwd_v.at[0])
    load("a3", fwd.at[:, part(3)], fwd_v.at[3])
    load("drs", bwd.at[:, part(2)], bwd_v.at[2])
    load("edge", edge, edge_v)
    load("upd", upd, upd_v)
    stores = []

    def out(src, dst):
        copy = pltpu.make_async_copy(src, dst, sems.at[len(stores)])
        copy.start()
        stores.append(copy)

    out(act, act_out)
    out(ig, ig_out)
    loads["a2"].wait()
    loads["dy"].wait()
    a2 = fwd_v[2]
    dy = bwd_v[1]
    for c in range(chunks):
        cols = part(c, FC)
        loads["fi", c].wait()
        loads["fo", c].wait()
        value, slope = gelu_both(mm(a2, fi_v[c]) + fb[:, cols])
        du = (slope * mm_bt(dy, fo_v[c])).astype(BF16)
        g_fb[:, cols] = col_sum(du.astype(F32))
        gfi_v[c] = mm_at(a2, du)
        out(gfi_v.at[c], g_fi.at[0, :, cols])
        gfo_v[c] = mm_at(value.astype(BF16), dy)
        out(gfo_v.at[c], g_fo.at[0, cols])
    loads["a1"].wait()
    for c in range(2):
        loads["dpq%d" % c].wait()
        pair_v[c] = mm_at(fwd_v[0], dpq_v[c])
        out(pair_v.at[c], g_pair.at[0, :, part(c)])
    loads["mbar"].wait()
    loads["dmsg"].wait()
    out_v[...] = mm_at(fwd_v[1], bwd_v[0]) * float(K)
    out(out_v, g_out.at[0])
    loads["a3"].wait()
    loads["drs"].wait()
    ends = mm_at(fwd_v[3], bwd_v[2])
    g_ep[0] = jnp.concatenate([ends[:, :DE], ends[:, EP : EP + DE]], axis=1)
    total = small[0]
    for c in range(1, C):
        total = total + small[c]
    for i, rows in enumerate(((0, 1, 2), (8, 9, 10), (11, 12, 13))):
        g_gain[i] = total[rows[0] : rows[0] + 1]
        g_shift[i] = total[rows[1] : rows[1] + 1]
        g_nb[i] = total[rows[2] : rows[2] + 1]
    g_eb[0, pl.ds(0, 1), :] = total[16:17, :DE]
    loads["edge"].wait()
    loads["upd"].wait()
    BW = edge_v.shape[3]
    for c in range(C):
        for half in range(2):
            block = edge_v[c, half].astype(F32)
            g_edge[0, pl.ds(half * (DE // 2), DE // 2), pl.ds(c * BW, BW)] = block
        block = stacked([upd_v[c, 0], upd_v[c, 1]]).astype(F32)
        first = c * BW
        for array, begin in ((g_self, 0), (g_eout, EP)):
            low, high = max(first, begin), min(first + BW, begin + DE)
            if low < high:
                array[0, :, pl.ds(low - begin, high - low)] = block[:DE, low - first : high - first]
        low, high = first, min(first + BW, DE)
        if low < high:
            g_eb[0, pl.ds(1, 1), pl.ds(low, high - low)] = block[DE : DE + 1, low - first : high - first]
    for copy in stores:
        copy.wait()


def run_gradients(dims, operands):
    S, B, N, K, Q, D, DE, EP, FF, C = dims
    rows = C * B * N
    BW = D // C
    held = operands[5].shape[2]
    vm = pl.BlockSpec(memory_space=pltpu.VMEM)
    hbm = pl.BlockSpec(memory_space=pl.ANY)
    sds = jax.ShapeDtypeStruct
    shapes = (
        (1, D, 2 * D), (1, DE, D), (1, D, D), (1, D, FF), (1, FF, D), (1, D, 2 * DE), (1, DE, DE), (1, DE, DE),
        (3, 1, D), (3, 1, D), (3, 1, D), (1, FF), (1, 2, DE),
    )
    return pl.pallas_call(
        functools.partial(gradient_kernel, dims),
        out_shape=tuple(sds(shape, F32) for shape in shapes) + (sds((1, B, N, D), BF16),) * 2,
        in_specs=[hbm, hbm, hbm, vm, hbm, hbm, hbm, hbm, vm, hbm, hbm],
        out_specs=(hbm, vm, hbm, hbm, hbm) + (vm,) * 8 + (hbm,) * 2,
        scratch_shapes=[
            pltpu.VMEM((4, rows, D), BF16),
            pltpu.VMEM((3, rows, D), BF16),
            pltpu.VMEM((2, rows, D), BF16),
            pltpu.VMEM((4, D, FF // 4), BF16),
            pltpu.VMEM((4, FF // 4, D), BF16),
            pltpu.VMEM((4, D, FF // 4), F32),
            pltpu.VMEM((4, FF // 4, D), F32),
            pltpu.VMEM((2, D, D), F32),
            pltpu.VMEM((D, D), F32),
            pltpu.VMEM((C, 2, DE // 2, BW), BF16),
            pltpu.VMEM((C, 2, held, BW), BF16),
            pltpu.SemaphoreType.DMA((19,)),
            pltpu.SemaphoreType.DMA((13,)),
        ],
        compiler_params=pltpu.CompilerParams(vmem_limit_bytes=56 * 1024 * 1024),
    )(*operands)


def stationary(
    clean_nodes, noise_nodes, edge_feats, neighbours, time_bins, cotangent,
    pair_weight, message_edge, message_out, ffn_in, ffn_out, edge_pair, edge_self, edge_out,
    norm_gain, norm_shift, node_bias, ffn_bias, edge_bias,
):
    S = lax.axis_size("section")
    place = lax.axis_index("section")
    column = lax.axis_index("dp")
    B, N, D = clean_nodes.shape
    K, DE = edge_feats.shape[2:]
    FF = ffn_in.shape[2]
    Q = N // 4
    EP = DE + N
    core = column % 2
    w = place // 2
    slab = (place % 2) * 2 * Q

    node_ids = jnp.arange(N, dtype=jnp.int32)
    both = [
        lax.dynamic_slice(array, (w % B, slab) + (0,) * (array.ndim - 2), (1, 2 * Q) + array.shape[2:])[0]
        for array in (edge_feats, neighbours)
    ]
    chosen = (both[1][:, :, None] == node_ids).astype(BF16)
    both = jnp.concatenate([both[0], chosen], axis=2)
    mine = lax.dynamic_slice_in_dim(both, core * Q, Q, 0)
    theirs = lax.dynamic_slice_in_dim(both, (1 - core) * Q, Q, 0)
    got = lax.ppermute(theirs, "dp", [(i, i ^ 1) for i in range(lax.axis_size("dp"))])
    ecat0 = jnp.swapaxes(jnp.where(w // B == core, mine, got), 0, 1).reshape(K * Q, EP)
    oht = jnp.transpose(ecat0[:, DE:])
    phase = (time_bins.astype(F32) + 0.5) * (math.pi * 0.5 / TBINS)
    mix = jnp.cos(phase[None] - jnp.array([[0.0], [math.pi * 0.5]], F32))

    def by_rows(array):
        return jnp.transpose(array, (1, 0, 2))

    def widen(array, size, axis=-1):
        extra = [(0, 0)] * array.ndim
        extra[axis] = (0, size - array.shape[axis])
        return jnp.pad(array, extra)

    ep = jnp.concatenate([widen(edge_pair[0, :, :DE], EP), widen(edge_pair[0, :, DE:], EP)], axis=1)
    C = lax.axis_size("dp")
    dims = (S, B, N, K, Q, D, DE, EP, FF, C)
    act, ig, g_fwd, g_bwd, g_dpq, g_small, g_msg, g_upd = run_relay(
        dims,
        (
            ecat0, oht, mix, clean_nodes.reshape(B * N, D), noise_nodes.reshape(B * N, D),
            cotangent.reshape(B * N, D), pair_weight[0], message_out[0], ffn_in[0], ffn_out[0], ep,
            by_rows(norm_gain), by_rows(norm_shift), by_rows(node_bias), ffn_bias, edge_bias[0],
            message_edge[0], edge_self[0], edge_out[0],
        ),
    )
    grads = run_gradients(
        dims,
        (
            g_fwd.reshape(C * B * N, -1), g_bwd.reshape(C * B * N, -1), g_dpq.reshape(C * B * N, -1),
            g_small, g_msg, g_upd, ffn_in[0], ffn_out[0], ffn_bias, act.reshape(1, B, N, D), ig.reshape(1, B, N, D),
        ),
    )
    grads, outs = list(grads[:-2]), tuple(grads[-2:])
    grads[8:11] = [by_rows(array) for array in grads[8:11]]
    return outs + tuple(grads)


def solution(mesh):
    sections, copies = mesh.shape["section"], mesh.shape["dp"]

    def body(*args):
        B, N = args[0].shape[:2]
        fits = sections == 4 * B and copies % 2 == 0 and N % 64 == 0
        return stationary(*args) if fits else on_device(*args)

    placed = (
        P("dp", None, None),
        P("dp", None, None),
        P("dp", None, None, None),
        P("dp", None, None),
        P("dp"),
        P("dp", None, None),
        P("section", None, None),
        P("section", None, None),
        P("section", None, None),
        P("section", None, None),
        P("section", None, None),
        P("section", None, None),
        P("section", None, None),
        P("section", None, None),
        P("section", None, None),
        P("section", None, None),
        P("section", None, None),
        P("section", None),
        P("section", None, None),
    )
    return jax.shard_map(
        body,
        mesh=mesh,
        in_specs=placed,
        out_specs=(
            P("section", "dp", None, None),
            P("section", "dp", None, None),
            P("section", None, None),
            P("section", None, None),
            P("section", None, None),
            P("section", None, None),
            P("section", None, None),
            P("section", None, None),
            P("section", None, None),
            P("section", None, None),
            P("section", None, None),
            P("section", None, None),
            P("section", None, None),
            P("section", None),
            P("section", None, None),
        ),
        check_vma=False,
    )
```

```python
import functools
import math

import jax
import jax.numpy as jnp
from jax import lax
from jax.experimental import pallas as pl
from jax.experimental.pallas import tpu as pltpu
from jax.sharding import PartitionSpec as P

TBINS = 100


def from_behind(block, axis, distance):
    devices = range(lax.axis_size(axis))
    route = [(i - distance, i) for i in devices if i - distance in devices]
    return lax.ppermute(block, axis, route)


def for_sending(value):
    return jax.tree.map(lambda a: a.astype(jnp.bfloat16) if a.dtype == jnp.float32 else a, value)


def layer_norm(value, gain, shift):
    centre = jnp.mean(value, axis=-1, keepdims=True)
    centred = value - centre
    spread = jnp.mean(centred * centred, axis=-1, keepdims=True)
    return centred * lax.rsqrt(spread + 1e-05) * gain + shift


def forward_layer(weights, hidden, edge_state, nearest):
    (
        pair_w,
        msg_edge,
        msg_out,
        ffn_w_in,
        ffn_w_out,
        edge_pair_w,
        edge_self_w,
        edge_out_w,
        gains,
        shifts,
        node_b,
        ffn_b,
        edge_b,
    ) = weights
    width = msg_out.shape[0]
    edge_width = edge_self_w.shape[0]
    normed_one = layer_norm(hidden, gains[0], shifts[0]).astype(jnp.bfloat16)
    pair_out = jnp.dot(normed_one, pair_w, preferred_element_type=jnp.float32)
    before_act = (
        pair_out[:, None, :width]
        + jnp.take(pair_out[:, width:], nearest, axis=0)
        + jnp.einsum("nkc,cd->nkd", edge_state, msg_edge, preferred_element_type=jnp.float32)
        + node_b[0]
    )
    message_act = jax.nn.gelu(before_act).astype(jnp.bfloat16)
    message_all = jnp.einsum(
        "nkc,cd->nkd", message_act, msg_out, preferred_element_type=jnp.float32
    )
    after_msg = hidden + jnp.mean(message_all, axis=1) + node_b[1]
    normed_two = layer_norm(after_msg, gains[1], shifts[1]).astype(jnp.bfloat16)
    ffn_pre = jnp.dot(normed_two, ffn_w_in, preferred_element_type=jnp.float32) + ffn_b
    ffn_act = jax.nn.gelu(ffn_pre).astype(jnp.bfloat16)
    after_ffn = (
        after_msg + jnp.dot(ffn_act, ffn_w_out, preferred_element_type=jnp.float32) + node_b[2]
    )
    normed_three = layer_norm(after_ffn, gains[2], shifts[2]).astype(jnp.bfloat16)
    edge_pairs = jnp.dot(normed_three, edge_pair_w, preferred_element_type=jnp.float32)
    edge_pre = (
        edge_pairs[:, None, :edge_width]
        + jnp.take(edge_pairs[:, edge_width:], nearest, axis=0)
        + jnp.einsum("nkc,cd->nkd", edge_state, edge_self_w, preferred_element_type=jnp.float32)
        + edge_b[0]
    )
    edge_act = jax.nn.gelu(edge_pre).astype(jnp.bfloat16)
    edge_next = (
        edge_state.astype(jnp.float32)
        + jnp.einsum("nkc,cd->nkd", edge_act, edge_out_w, preferred_element_type=jnp.float32)
        + edge_b[1]
    )
    saved = (
        normed_one,
        before_act,
        message_act,
        after_msg,
        normed_two,
        ffn_pre,
        ffn_act,
        after_ffn,
        normed_three,
        edge_pre,
        edge_act,
    )
    return (after_ffn, edge_next, saved)


def backward_layer(weights, hidden, edge_state, nearest, grad_nodes_out, grad_edges_out):
    (
        pair_w,
        msg_edge,
        msg_out,
        ffn_w_in,
        ffn_w_out,
        edge_pair_w,
        edge_self_w,
        edge_out_w,
        gains,
        shifts,
        node_b,
        ffn_b,
        edge_b,
    ) = weights
    unused_nodes, unused_edges, saved = forward_layer(weights, hidden, edge_state, nearest)
    (
        normed_one,
        before_act,
        message_act,
        after_msg,
        normed_two,
        ffn_pre,
        ffn_act,
        after_ffn,
        normed_three,
        edge_pre,
        edge_act,
    ) = saved
    width = msg_out.shape[0]
    edge_width = edge_self_w.shape[0]
    count = nearest.shape[1]
    node_count = hidden.shape[0]
    one_hot = (
        nearest.reshape(-1)[None, :] == jnp.arange(node_count, dtype=jnp.int32)[:, None]
    ).astype(jnp.bfloat16)
    edge_grad_low = grad_edges_out.astype(jnp.bfloat16)
    grad_edge_b1 = jnp.sum(grad_edges_out, axis=(0, 1))
    grad_edge_out_w = jnp.einsum(
        "nkc,nkd->cd", edge_act, edge_grad_low, preferred_element_type=jnp.float32
    )
    edge_act_grad = jnp.einsum(
        "nkd,cd->nkc", edge_grad_low, edge_out_w, preferred_element_type=jnp.float32
    )
    unused_value, gelu_edge = jax.vjp(jax.nn.gelu, edge_pre)
    edge_pre_grad = gelu_edge(edge_act_grad)[0].astype(jnp.bfloat16)
    grad_edge_b0 = jnp.sum(edge_pre_grad, axis=(0, 1), dtype=jnp.float32)
    grad_edge_self_w = jnp.einsum(
        "nkc,nkd->cd", edge_state, edge_pre_grad, preferred_element_type=jnp.float32
    )
    edge_total = grad_edges_out + jnp.einsum(
        "nkd,cd->nkc", edge_pre_grad, edge_self_w, preferred_element_type=jnp.float32
    )
    own_edge = jnp.sum(edge_pre_grad, axis=1, dtype=jnp.float32)
    other_edge = jnp.dot(
        one_hot, edge_pre_grad.reshape(-1, edge_width), preferred_element_type=jnp.float32
    )
    pairs_grad = jnp.concatenate([own_edge, other_edge], axis=-1).astype(jnp.bfloat16)
    grad_edge_pair_w = jnp.einsum(
        "nc,nd->cd", normed_three, pairs_grad, preferred_element_type=jnp.float32
    )
    normed_three_grad = jnp.einsum(
        "nd,cd->nc", pairs_grad, edge_pair_w, preferred_element_type=jnp.float32
    )
    unused_value, norm_three_back = jax.vjp(layer_norm, after_ffn, gains[2], shifts[2])
    ffn_side, gain_three, shift_three = norm_three_back(normed_three_grad)
    after_ffn_grad = grad_nodes_out + ffn_side
    grad_node_b2 = jnp.sum(after_ffn_grad, axis=0)
    ffn_out_grad = after_ffn_grad.astype(jnp.bfloat16)
    grad_ffn_w_out = jnp.einsum(
        "nc,nd->cd", ffn_act, ffn_out_grad, preferred_element_type=jnp.float32
    )
    ffn_act_grad = jnp.einsum(
        "nd,cd->nc", ffn_out_grad, ffn_w_out, preferred_element_type=jnp.float32
    )
    unused_value, gelu_ffn = jax.vjp(jax.nn.gelu, ffn_pre)
    ffn_pre_grad = gelu_ffn(ffn_act_grad)[0].astype(jnp.bfloat16)
    grad_ffn_b = jnp.sum(ffn_pre_grad, axis=0, dtype=jnp.float32)
    grad_ffn_w_in = jnp.einsum(
        "nc,nd->cd", normed_two, ffn_pre_grad, preferred_element_type=jnp.float32
    )
    normed_two_grad = jnp.einsum(
        "nd,cd->nc", ffn_pre_grad, ffn_w_in, preferred_element_type=jnp.float32
    )
    unused_value, norm_two_back = jax.vjp(layer_norm, after_msg, gains[1], shifts[1])
    msg_side, gain_two, shift_two = norm_two_back(normed_two_grad)
    after_msg_grad = after_ffn_grad + msg_side
    grad_node_b1 = jnp.sum(after_msg_grad, axis=0)
    message_grad = (after_msg_grad / count).astype(jnp.bfloat16)
    grad_msg_out = jnp.einsum(
        "nkc,nd->cd", message_act, message_grad, preferred_element_type=jnp.float32
    )
    message_act_grad = jnp.einsum(
        "nd,cd->nc", message_grad, msg_out, preferred_element_type=jnp.float32
    )
    unused_value, gelu_msg = jax.vjp(jax.nn.gelu, before_act)
    before_grad = gelu_msg(jnp.broadcast_to(message_act_grad[:, None, :], before_act.shape))[
        0
    ].astype(jnp.bfloat16)
    grad_node_b0 = jnp.sum(before_grad, axis=(0, 1), dtype=jnp.float32)
    grad_msg_edge = jnp.einsum(
        "nkc,nkd->cd", edge_state, before_grad, preferred_element_type=jnp.float32
    )
    edge_total = edge_total + jnp.einsum(
        "nkd,cd->nkc", before_grad, msg_edge, preferred_element_type=jnp.float32
    )
    own_node = jnp.sum(before_grad, axis=1, dtype=jnp.float32)
    other_node = jnp.dot(
        one_hot, before_grad.reshape(-1, width), preferred_element_type=jnp.float32
    )
    pair_grad = jnp.concatenate([own_node, other_node], axis=-1).astype(jnp.bfloat16)
    grad_pair_w = jnp.einsum("nc,nd->cd", normed_one, pair_grad, preferred_element_type=jnp.float32)
    normed_one_grad = jnp.einsum("nd,cd->nc", pair_grad, pair_w, preferred_element_type=jnp.float32)
    unused_value, norm_one_back = jax.vjp(layer_norm, hidden, gains[0], shifts[0])
    input_side, gain_one, shift_one = norm_one_back(normed_one_grad)
    hidden_grad = after_msg_grad + input_side
    grads = (
        grad_pair_w,
        grad_msg_edge,
        grad_msg_out,
        grad_ffn_w_in,
        grad_ffn_w_out,
        grad_edge_pair_w,
        grad_edge_self_w,
        grad_edge_out_w,
        jnp.stack([gain_one, gain_two, gain_three]),
        jnp.stack([shift_one, shift_two, shift_three]),
        jnp.stack([grad_node_b0, grad_node_b1, grad_node_b2]),
        grad_ffn_b,
        jnp.stack([grad_edge_b0, grad_edge_b1]),
    )
    return (hidden_grad.astype(jnp.bfloat16), edge_total.astype(jnp.bfloat16), grads)


def on_device(
    clean_nodes,
    noise_nodes,
    edge_feats,
    neighbours,
    time_bins,
    cotangent,
    pair_weight,
    message_edge,
    message_out,
    ffn_in,
    ffn_out,
    edge_pair,
    edge_self,
    edge_out,
    norm_gain,
    norm_shift,
    node_bias,
    ffn_bias,
    edge_bias,
):
    sections = lax.axis_size("section")
    place = lax.axis_index("section")
    weights = tuple(
        (
            item[0]
            for item in (
                pair_weight,
                message_edge,
                message_out,
                ffn_in,
                ffn_out,
                edge_pair,
                edge_self,
                edge_out,
                norm_gain,
                norm_shift,
                node_bias,
                ffn_bias,
                edge_bias,
            )
        )
    )
    batches, node_count, width = clean_nodes.shape
    phase = (time_bins.astype(jnp.float32) + 0.5) * (math.pi * 0.5 / TBINS)
    start = jnp.cos(phase)[:, None, None] * clean_nodes.astype(jnp.float32) + jnp.sin(phase)[
        :, None, None
    ] * noise_nodes.astype(jnp.float32)
    zero_nodes = jnp.zeros((node_count, width), jnp.bfloat16)
    zero_edges = jnp.zeros(edge_feats.shape[1:], jnp.bfloat16)
    is_first = place == 0
    is_last = place == sections - 1

    def forward_step(step_index, carry):
        recv_nodes, recv_edges, back_nodes, kept_nodes, kept_edges, section_outs = carry
        item = step_index - place
        first_pass = (item >= 0) & (item < batches)
        second_pass = (item >= sections) & (item < sections + batches)
        index = jnp.clip(jnp.where(second_pass, item - sections, item), 0, batches - 1)
        predicted = back_nodes
        own_start = lax.dynamic_index_in_dim(start, index, 0, keepdims=False)
        lead_nodes = own_start + jnp.where(second_pass, predicted.astype(jnp.float32), 0.0)
        nodes_in = jnp.where(is_first, lead_nodes, recv_nodes.astype(jnp.float32))
        edges_in = jnp.where(
            is_first, lax.dynamic_index_in_dim(edge_feats, index, 0, keepdims=False), recv_edges
        )
        nearest = lax.dynamic_index_in_dim(neighbours, index, 0, keepdims=False)

        def run_layer(operand):
            after, edge_next, saved = forward_layer(weights, operand[0], operand[1], operand[2])
            return (after.astype(jnp.bfloat16), edge_next.astype(jnp.bfloat16))

        def skip_layer(operand):
            return (zero_nodes, zero_edges)

        out_nodes, out_edges = lax.cond(
            first_pass | second_pass, run_layer, skip_layer, (nodes_in, edges_in, nearest)
        )
        kept_nodes = lax.dynamic_update_index_in_dim(
            kept_nodes, jnp.where(second_pass, nodes_in, kept_nodes[index]), index, 0
        )
        kept_edges = lax.dynamic_update_index_in_dim(
            kept_edges, jnp.where(second_pass, edges_in, kept_edges[index]), index, 0
        )
        section_outs = lax.dynamic_update_index_in_dim(
            section_outs, jnp.where(second_pass, out_nodes, section_outs[index]), index, 0
        )
        recv_nodes, recv_edges = from_behind((out_nodes, out_edges), "section", 1)
        back_nodes = from_behind(out_nodes, "section", 1 - sections)
        return (recv_nodes, recv_edges, back_nodes, kept_nodes, kept_edges, section_outs)

    forward_init = (
        zero_nodes,
        zero_edges,
        zero_nodes,
        jnp.zeros((batches, node_count, width), jnp.float32),
        jnp.zeros_like(edge_feats),
        jnp.zeros((batches, node_count, width), jnp.bfloat16),
    )
    unused_nodes, unused_edges, unused_back, kept_nodes, kept_edges, section_outs = lax.fori_loop(
        0, 2 * sections + batches - 1, forward_step, forward_init
    )
    grads_zero = tuple((jnp.zeros(item.shape, jnp.float32) for item in weights))

    def backward_step(step_index, carry):
        recv_grad_nodes, recv_grad_edges, grads, input_grads = carry
        item = step_index - (sections - 1 - place)
        live = (item >= 0) & (item < batches)
        index = jnp.clip(item, 0, batches - 1)
        nodes_grad_out = jnp.where(
            is_last,
            lax.dynamic_index_in_dim(cotangent, index, 0, keepdims=False).astype(jnp.float32),
            recv_grad_nodes.astype(jnp.float32),
        )
        edges_grad_out = jnp.where(is_last, 0.0, recv_grad_edges.astype(jnp.float32))
        nearest = lax.dynamic_index_in_dim(neighbours, index, 0, keepdims=False)

        def run_back(operand):
            return backward_layer(
                weights, operand[0], operand[1], operand[2], operand[3], operand[4]
            )

        def skip_back(operand):
            return (zero_nodes, zero_edges, grads_zero)

        nodes_grad, edges_grad, terms = lax.cond(
            live,
            run_back,
            skip_back,
            (kept_nodes[index], kept_edges[index], nearest, nodes_grad_out, edges_grad_out),
        )
        grads = tuple((total + term for total, term in zip(grads, terms)))
        input_grads = lax.dynamic_update_index_in_dim(
            input_grads, jnp.where(live, nodes_grad, input_grads[index]), index, 0
        )
        recv_grad_nodes, recv_grad_edges = from_behind((nodes_grad, edges_grad), "section", -1)
        return (recv_grad_nodes, recv_grad_edges, grads, input_grads)

    backward_init = (
        zero_nodes,
        zero_edges,
        grads_zero,
        jnp.zeros((batches, node_count, width), jnp.bfloat16),
    )
    unused_grad_nodes, unused_grad_edges, grads, input_grads = lax.fori_loop(
        0, sections + batches - 1, backward_step, backward_init
    )
    totals = jax.tree.map(lambda part: part.astype(jnp.float32), lax.psum(for_sending(grads), "dp"))
    return (
        section_outs[None],
        input_grads[None],
        totals[0][None],
        totals[1][None],
        totals[2][None],
        totals[3][None],
        totals[4][None],
        totals[5][None],
        totals[6][None],
        totals[7][None],
        totals[8][None],
        totals[9][None],
        totals[10][None],
        totals[11][None],
        totals[12][None],
    )


BF16 = jnp.bfloat16
F32 = jnp.float32
MESH = pl.DeviceIdType.MESH
GELU_A = 0.7978845608028654
GELU_B = 0.044715


def gelu(x):
    return 0.5 * x * (1.0 + jnp.tanh(x * (GELU_A + (GELU_A * GELU_B) * (x * x))))


def gelu_both(x):
    square = x * x
    t = jnp.tanh(x * (GELU_A + (GELU_A * GELU_B) * square))
    half = 0.5 * (1.0 + t)
    slope = half + (0.5 * x) * (1.0 - t * t) * (GELU_A + (3.0 * GELU_A * GELU_B) * square)
    return x * half, slope


def mm(a, b):
    return jnp.dot(a, b, preferred_element_type=F32)


def mm_bt(a, b):
    return lax.dot_general(a, b, (((1,), (1,)), ((), ())), preferred_element_type=F32)


def mm_at(a, b):
    return lax.dot_general(a, b, (((0,), (0,)), ((), ())), preferred_element_type=F32)


def stacked(blocks):
    return jnp.concatenate(blocks, axis=0)


def row_mean(x):
    return jnp.mean(x, axis=-1, keepdims=True)


def normed(x):
    centred = x - row_mean(x)
    scale = lax.rsqrt(row_mean(centred * centred) + 1e-05)
    return centred * scale, scale


def norm_back(grad, unit, scale, gain):
    t = grad * gain
    return scale * (t - row_mean(t) - unit * row_mean(t * unit))


def col_sum(x):
    return jnp.sum(x, axis=0, keepdims=True)


def relay_kernel(
    dims,
    ecat0, oht, mix, clean, noise, cot, pw, mo, fi, fo, ep, gains, shifts, node_b, fb, edge_b, we_own, ws_own, wo_own,
    act, ig, g_fwd, g_bwd, g_dpq, g_small, g_msg, g_upd,
    start, par, eb0, wall_msg, wall_upd, fwd, bwd, sg,
    eg, eg_r, eg_b, msg_o, msg_f, upd_o, upd_f, wo, eb1,
    ecat, wcat, scat, pwn, parn, hin_r, hst, mb_s, mb_r, pq_s, pq_r, rq_s, rq_r,
    un0, un1, un2, hi_s, sc0, sc1, sc2, sci, u_s, slope_s, de, dacc, gp, gpe, dcat, act_t, edge_t,
    x_s, x_r, row_s, row_r, dpqo_r, dmb_s, dmb_r, dh1_s, dh1_r, dh1_f, dh2_s, dn3_s, da2_s, h1_s, a1_s,
    ld_sem, nx_ss, nx_rs, hop_ss, hop_rs,
    pq_ss, pq_rs, ag_ss, ag_rs, rq_ss, rq_rs, ag2_ss, ag2_rs,
    mb_ss, mb_rs, x_ss, x_rs, row_ss, row_rs, dpqo_rs, fw_ss, dmb_ss, dmb_rs, dh_ss, dh_rs,
    e1_ss, e1_rs, e2_ss, e2_rs, g_ss, g_rs, relay_ss, ring_ss, ring_rs, sib_ss, sib_rs,
):
    S, B, N, K, Q, D, DE, EP, FF, C = dims
    BN = B * N
    RB = 16
    top = DE + N
    me_s = lax.axis_index("section")
    me_d = lax.axis_index("dp")
    core = lax.rem(me_d, 2)
    pair = me_d - core
    w = lax.div(me_s, 2)
    q = 2 * lax.rem(me_s, 2) + core
    owner_d = pair + lax.div(w, B)
    slot = lax.rem(w, B)
    my_row = pl.multiple_of(slot * N + q * Q, Q)
    own_rows = pl.ds(top, Q)

    def quarter(j):
        return pl.ds(pl.multiple_of(DE + j * Q, Q), Q)

    def is_me(sec, dpi):
        return (sec == me_s) & (dpi == me_d)

    def far(src, dst, ssem, rsem, sec, dpi):
        return pltpu.make_async_remote_copy(
            src_ref=src, dst_ref=dst, send_sem=ssem, recv_sem=rsem,
            device_id={"section": sec, "dp": dpi}, device_id_type=MESH,
        )

    def push(src, dst, ssem, rsem, sec, dpi):
        lax.cond(
            is_me(sec, dpi),
            lambda: pltpu.make_async_copy(src, dst, rsem).start(),
            lambda: far(src, dst, ssem, rsem, sec, dpi).start(),
        )

    def arrive(ref, sem):
        pltpu.make_async_copy(ref, ref, sem).wait()

    def drain(ref, sem, sec, dpi):
        @pl.when(jnp.logical_not(is_me(sec, dpi)))
        def _():
            arrive(ref, sem)

    def worker_of(p, j):
        return 2 * (core * B + p) + j // 2, pair + j % 2

    def peer(k):
        j = lax.rem(q + k, 4)
        return j, 2 * w + lax.div(j, 2), pair + lax.rem(j, 2)

    works_here = lax.div(w, B) == core

    def at(p, first=0, size=16):
        return pl.ds(pl.multiple_of(p * N + first, size), size)

    near = jnp.clip(w - core * B, 0, B - 1)
    leading = jnp.where(works_here, near, B - 1 - near)

    load = pltpu.make_async_copy(ecat0, ecat.at[0], ld_sem)
    load.start()
    barrier = pltpu.get_barrier_semaphore()
    for sec in range(S):
        for c in range(C):
            greeted = (c == pair) | (c == pair + 1) | (w == sec // 2)

            @pl.when(greeted & jnp.logical_not(is_me(sec, c)))
            def _():
                pl.semaphore_signal(
                    barrier, inc=1, device_id={"section": sec, "dp": c}, device_id_type=MESH
                )
    wall_msg[me_s] = we_own[...]
    wall_upd[me_s] = jnp.zeros(wall_upd.shape[1:], BF16)
    wall_upd[me_s, pl.ds(0, DE), pl.ds(0, DE)] = ws_own[...]
    wall_upd[me_s, pl.ds(0, DE), pl.ds(EP, DE)] = wo_own[...]
    bias = edge_b[pl.ds(1, 1), :]
    high = bias.astype(BF16).astype(F32)
    row = lax.broadcasted_iota(jnp.int32, (16, DE), 0)
    wall_upd[me_s, pl.ds(DE, 16), pl.ds(0, DE)] = jnp.where(
        row == 0, high, jnp.where(row == 1, bias - high, 0.0)
    ).astype(BF16)
    eb0[...] = jnp.zeros_like(eb0)
    eb0[:, pl.ds(0, DE)] = edge_b[pl.ds(0, 1), :]
    par[pl.ds(0, 1), :] = gains[0]
    par[pl.ds(1, 1), :] = shifts[0]
    par[pl.ds(2, 1), :] = node_b[0]
    par[pl.ds(3, 5), :] = jnp.zeros((5, D), F32)
    pl.semaphore_wait(barrier, 2 * S - 1 + 2 * (C - 2))

    def section_at(i):
        i = lax.rem(i + S, S)
        return jnp.where(i < S // 2, 2 * i, 2 * (S - i) - 1)

    place = jnp.where(lax.rem(me_s, 2) == 0, w, S - 1 - w)
    sides = ((section_at(place + 1), S // 2), (section_at(place - 1), S // 2 - 1))
    walls = (wall_msg, wall_upd)

    def half_of(which, layer, c):
        size = walls[which].shape[1] // 2
        return walls[which].at[layer, pl.ds(pl.multiple_of(c * size, size), size)]

    def ring_send(which, layer, side, hop):
        sec, reach = sides[side]
        if hop < reach:
            half = half_of(which, layer, core)
            far(half, half, ring_ss.at[which, side, hop], ring_rs.at[which, layer], sec, me_d).start()

    def ring_hop(which, side, hop):
        layer = section_at(place - hop if side == 0 else place + hop)
        half = half_of(which, layer, core)
        arrive(half, ring_rs.at[which, layer])
        ring_send(which, layer, side, hop)
        far(half, half, sib_ss.at[which, layer], sib_rs.at[which, layer], me_s, pair + 1 - core).start()

    hops = [(hop, side) for hop in range(1, S // 2 + 1) for side in range(2) if hop <= sides[side][1]]

    def ring_later(second):
        for hop, side in hops:
            early = (place > 0) & ((place >= hop) if side == 0 else (place + hop <= S))

            @pl.when(early != second)
            def _():
                ring_hop(1, side, hop)

    for side in range(2):
        ring_send(0, me_s, side, 0)
    before = lax.rem(me_s + S - 1, S)
    far(pw, pwn, nx_ss.at[0], nx_rs.at[0], before, me_d).start()
    far(par, parn, nx_ss.at[1], nx_rs.at[1], before, me_d).start()

    for p in range(B):
        rows = pl.ds(p * N, N)
        start[rows, :] = mix[0, p] * clean[rows, :].astype(F32) + mix[1, p] * noise[rows, :].astype(F32)

    def ring_drain():
        for which in range(2):
            for side in range(2):
                for hop in range(sides[side][1]):
                    arrive(half_of(which, me_s, core), ring_ss.at[which, side, hop])
            for layer in range(S):
                @pl.when(layer != me_s)
                def _():
                    arrive(half_of(which, layer, core), sib_ss.at[which, layer])

    def unpack_messages(t):
        @pl.when(t != me_s)
        def _():
            arrive(half_of(0, t, 1 - core), sib_rs.at[0, t])

        wcat[t, pl.ds(0, DE), :] = wall_msg[t]

    def unpack_updates(t):
        @pl.when(t != me_s)
        def _():
            arrive(half_of(1, t, 1 - core), sib_rs.at[1, t])

        scat[t, pl.ds(0, DE), :] = wall_upd[t, pl.ds(0, DE), pl.ds(0, EP)]
        wo[t, pl.ds(0, DE), :] = wall_upd[t, pl.ds(0, DE), pl.ds(EP, EP)]
        wo[t, pl.ds(DE, N), :] = jnp.zeros((N, EP), BF16)
        eb1[t] = wall_upd[t, pl.ds(DE, 16), pl.ds(0, EP)]

    def rows_out(p, src, dst, ssem, rsem):
        for j in range(4):
            sec, dpi = worker_of(p, j)
            push(src.at[at(p, j * Q, Q)], dst, ssem, rsem, sec, dpi)

    def rows_drain(src, ssem):
        lax.cond(
            works_here,
            lambda: arrive(src.at[pl.ds(0, B * N - Q)], ssem),
            lambda: arrive(src, ssem),
        )

    def spread(rows, half, ref, layer, ssem, rsem, rows_sem):
        arrive(rows, rows_sem)
        for k in range(1, 4):
            _, sec, dpi = peer(k)
            far(rows.at[:, pl.ds(half, half)], ref.at[layer, quarter(q)], ssem, rsem, sec, dpi).start()
        ref[layer, own_rows, :] = rows[:, pl.ds(0, half)]
        ref[layer, quarter(q), :] = rows[:, pl.ds(half, half)]

    def spread_wait(ref, layer, sem):
        arrive(ref.at[layer, pl.ds(DE, 3 * Q)], sem)

    def share(group, src, dst):
        for c in range(C):
            push(src, dst.at[me_d], g_ss.at[group, c], g_rs.at[group, me_d], me_s, c)

    def share_wait(group, src, dst):
        for c in range(C):
            arrive(dst.at[c], g_rs.at[group, c])
            drain(src, g_ss.at[group, c], me_s, c)

    def share_near(group, src, dst):
        for c in range(C):
            @pl.when((c == pair) | (c == pair + 1) | (core == c % 2))
            def _():
                push(src, dst(me_d), g_ss.at[group, c], g_rs.at[group, me_d], me_s, c)

    def share_relay(group, src, dst):
        for c in range(C):
            @pl.when((c != me_d) & (core == c % 2))
            def _():
                arrive(dst(c), g_rs.at[group, c])
                far(dst(c), dst(c), relay_ss.at[group - 2, c // 2], g_rs.at[group, c], me_s, pair + 1 - core).start()

    def share_near_wait(group, src, dst):
        for c in range(C):
            @pl.when((c == me_d) | (core != c % 2))
            def _():
                arrive(dst(c), g_rs.at[group, c])

            @pl.when((c != me_d) & ((c == pair) | (c == pair + 1) | (core == c % 2)))
            def _():
                arrive(src, g_ss.at[group, c])

            @pl.when((c != me_d) & (core == c % 2))
            def _():
                arrive(dst(c), relay_ss.at[group - 2, c // 2])

    steps = 4
    KC = K // steps
    RC = KC * Q

    def messages(t):
        own = wcat[t, own_rows, :].astype(F32)
        total = jnp.zeros((Q, D), F32)
        for i in range(steps):
            pre = mm(ecat[t, pl.ds(i * RC, RC), :], wcat[t, pl.ds(0, top), :])
            for k in range(KC):
                total = total + gelu(pre[k * Q : (k + 1) * Q] + own)
        mb_s[...] = (total * (1.0 / K)).astype(BF16)

    def edge_update(t):
        own = scat[t, own_rows, :].astype(F32)
        bias = eb1[t, pl.ds(0, 1), :].astype(F32) + eb1[t, pl.ds(1, 1), :].astype(F32)
        for i in range(steps):
            pe = mm(ecat[t, pl.ds(i * RC, RC), :], scat[t, pl.ds(0, top), :])
            act_e = stacked([gelu(pe[k * Q : (k + 1) * Q] + own).astype(BF16) for k in range(KC)])
            z = mm(act_e, wo[t])
            for k in range(KC):
                rows = pl.ds(i * RC + k * Q, Q)
                ecat[t + 1, rows, :] = (ecat[t, rows, :].astype(F32) + z[k * Q : (k + 1) * Q] + bias).astype(BF16)

    chunks = 4
    FC = FF // chunks

    def node_forward(step):
        @pl.when(step < S)
        def _():
            arrive(pwn, nx_rs.at[0])
            arrive(parn, nx_rs.at[1])
            arrive(pw, nx_ss.at[0])
            arrive(par, nx_ss.at[1])

        @pl.when(step == 0)
        def _():
            hi_s[...] = start[...]

        @pl.when(step > 0)
        def _():
            arrive(hin_r, hop_rs)
            first = jnp.where(me_s == 0, 1.0, 0.0)
            for i in range(0, BN, RB):
                rows = pl.ds(i, RB)
                hi_s[rows, :] = hin_r[rows, :].astype(F32) + first * start[rows, :]

        later = lax.rem(me_s + 1, S)

        def turn(n, carry):
            p = lax.rem(leading + n, B)
            whole = at(p, 0, N)
            arrive(mb_r.at[whole], mb_rs.at[p])
            mean = mm(mb_r[whole, :], mo[...])
            for i in range(0, N, RB):
                rows = at(p, i)
                h1 = hi_s[rows, :] + mean[i : i + RB] + node_b[1]
                h1_s[rows, :] = h1
                unit, scale = normed(h1)
                un1[rows, :] = unit
                sc1[rows, :] = scale
                fwd[rows, pl.ds(2 * D, D)] = (unit * gains[1] + shifts[1]).astype(BF16)
                fwd[rows, pl.ds(D, D)] = mb_r[rows, :]
            a2 = fwd[whole, pl.ds(2 * D, D)]
            y = jnp.zeros((N, D), F32)
            for c in range(chunks):
                cols = pl.ds(c * FC, FC)
                u = mm(a2, fi[:, cols])
                v = []
                for i in range(0, N, RB):
                    block = u[i : i + RB] + fb[:, cols]
                    u_s[at(p, i), cols] = block
                    v.append(gelu(block).astype(BF16))
                y = y + mm(stacked(v), fo[cols, :])
            last = jnp.where(me_s == S - 1, 1.0, 0.0)
            for i in range(0, N, RB):
                rows = at(p, i)
                h2 = h1_s[rows, :] + y[i : i + RB] + node_b[2]
                rounded = h2.astype(BF16)
                hst[rows, :] = rounded
                unit, scale = normed(h2)
                un2[rows, :] = unit
                sc2[rows, :] = scale
                fwd[rows, pl.ds(3 * D, D)] = (unit * gains[2] + shifts[2]).astype(BF16)
                pair_norm(rows, rounded.astype(F32) + last * start[rows, :], parn)
            rq = mm(fwd[whole, pl.ds(3 * D, D)], ep[...])
            for i in range(0, N, RB):
                rows = at(p, i)
                rq_s[rows, pl.ds(0, EP)] = (rq[i : i + RB, :EP] + eb0[...]).astype(BF16)
                rq_s[rows, pl.ds(EP, EP)] = rq[i : i + RB, EP:].astype(BF16)
            pair_rows(p, pwn, parn)

            @pl.when(me_s < S - 1)
            def _():
                rows_out(p, rq_s, rq_r, rq_ss, rq_rs)

            @pl.when(step < 2 * S - 1)
            def _():
                rows_out(p, pq_s, pq_r, pq_ss, pq_rs)

            @pl.when((n == 0) & works_here)
            def _():
                pass_on(step)

            return carry

        lax.fori_loop(0, B, turn, 0)

        @pl.when(step < 2 * S - 1)
        def _():
            far(hst, hin_r, hop_ss, hop_rs, later, me_d).start()

        @pl.when(step >= S)
        def _():
            act[...] = hst[...]
            for i in range(0, BN, RB):
                rows = pl.ds(i, RB)
                unit, scale = normed(hi_s[rows, :])
                hi_s[rows, :] = unit
                sci[rows, :] = scale
                fwd[rows, pl.ds(0, D)] = (unit * gains[0] + shifts[0]).astype(BF16)
                for c in range(chunks):
                    cols = pl.ds(c * FC, FC)
                    slope_s[rows, cols] = gelu_both(u_s[rows, cols])[1].astype(BF16)
            share(0, fwd, g_fwd)

    def pair_norm(rows, hidden, first):
        unit, scale = normed(hidden)
        un0[rows, :] = unit
        sc0[rows, :] = scale
        a1_s[rows, :] = (unit * first[pl.ds(0, 1), :] + first[pl.ds(1, 1), :]).astype(BF16)

    def pair_rows(p, weight, first):
        whole = at(p, 0, N)
        for half in range(2):
            cols = pl.ds(half * D, D)
            value = mm(a1_s[whole, :], weight[:, cols])
            if half == 0:
                value = value + first[pl.ds(2, 1), :]
            pq_s[whole, cols] = value.astype(BF16)

    def pass_on(step):
        t = lax.rem(step, S)

        @pl.when(t < S - 1)
        def _():
            spread(rq_r, EP, scat, t, ag2_ss, ag2_rs, rq_rs)

        @pl.when(step < 2 * S - 1)
        def _():
            spread(pq_r, D, wcat, lax.rem(step + 1, S), ag_ss, ag_rs, pq_rs)

    def node_forward_drain():
        arrive(hst, hop_ss)
        rows_drain(pq_s, pq_ss)

        @pl.when(me_s < S - 1)
        def _():
            rows_drain(rq_s, rq_ss)

    @pl.when(me_s == 0)
    def _():
        for i in range(0, BN, RB):
            rows = pl.ds(i, RB)
            pair_norm(rows, start[rows, :], par)
        for p in range(B):
            pair_rows(p, pw, par)
            rows_out(p, pq_s, pq_r, pq_ss, pq_rs)

    def message_slope(t):
        own = wcat[t, own_rows, :].astype(F32)
        for i in range(steps):
            pre = mm(ecat[t, pl.ds(i * RC, RC), :], wcat[t, pl.ds(0, top), :])
            for k in range(KC):
                gp[t, pl.ds(i * RC + k * Q, Q), :] = gelu_both(pre[k * Q : (k + 1) * Q] + own)[1].astype(BF16)

    def edge_slope(t):
        own = scat[t, own_rows, :].astype(F32)
        values = []
        for i in range(steps):
            pe = mm(ecat[t, pl.ds(i * RC, RC), :], scat[t, pl.ds(0, top), :])
            for k in range(KC):
                value, slope = gelu_both(pe[k * Q : (k + 1) * Q] + own)
                values.append(value.astype(BF16))
                gpe[t, pl.ds(i * RC + k * Q, Q), :] = slope.astype(BF16)
        act_t[t] = stacked(values).T

    def prepare(t):
        message_slope(t)
        edge_t[t] = ecat[t].T

        @pl.when(t > 0)
        def _():
            edge_slope(t - 1)

    def forward_step(step, carry):
        t = lax.rem(step, S)

        @pl.when(step < S)
        def _():
            unpack_messages(t)

        spread_wait(wcat, t, ag_rs)
        messages(t)
        spread_wait(wcat, t, ag_ss)
        push(mb_s, mb_r.at[pl.ds(my_row, Q)], mb_ss, mb_rs.at[slot], t, owner_d)

        for second in range(2):
            @pl.when(step == second)
            def _():
                ring_later(second == 1)

        @pl.when((step == 0) & (me_s == 0))
        def _():
            rows_drain(pq_s, pq_ss)

        @pl.when((step > 0) & (me_s == lax.rem(step + S - 1, S)))
        def _():
            node_forward_drain()

        @pl.when(me_s == t)
        def _():
            node_forward(step)

        @pl.when((me_s != t) & (step >= S))
        def _():
            prepare(t)

        @pl.when(jnp.logical_not((me_s == t) & works_here))
        def _():
            pass_on(step)

        @pl.when(t < S - 1)
        def _():
            @pl.when(step < S)
            def _():
                unpack_updates(t)

            spread_wait(scat, t, ag2_rs)
            edge_update(t)
            spread_wait(scat, t, ag2_ss)

        drain(mb_s, mb_ss, t, owner_d)
        return carry

    for hop, side in hops:
        ring_hop(0, side, hop)
    for side in range(2):
        ring_send(1, me_s, side, 0)
    load.wait()
    spread(pq_r, D, wcat, 0, ag_ss, ag_rs, pq_rs)
    lax.fori_loop(0, 2 * S, forward_step, 0)
    ring_drain()

    @pl.when(me_s != S - 1)
    def _():
        arrive(half_of(1, S - 1, 1 - core), sib_rs.at[1, S - 1])

    def edge_back(t):
        b2, n2 = lax.rem(t, 2), lax.rem(t + 1, 2)
        total = jnp.zeros((Q, EP), F32)
        for i in range(steps):
            chunk = pl.ds(i * RC, RC)
            carry = mm_bt(dcat[b2, chunk, pl.ds(0, D)], wcat[t, pl.ds(0, top), :])
            low = []
            for k in range(KC):
                rows = pl.ds(i * RC + k * Q, Q)
                low.append((dacc[rows, :] + carry[k * Q : (k + 1) * Q]).astype(BF16))
                de[n2, rows, :] = low[-1]
            dw = mm_bt(stacked(low), wo[t - 1])
            for k in range(KC):
                rows = pl.ds(i * RC + k * Q, Q)
                d = (gpe[t - 1, rows, :].astype(F32) * dw[k * Q : (k + 1) * Q]).astype(BF16)
                total = total + d.astype(F32)
                dcat[n2, rows, pl.ds(D, EP)] = d
        row_s[:, pl.ds(2 * D, EP)] = total.astype(BF16)
        x_s[:, pl.ds(D, EP)] = mm(oht[...], dcat[n2, :, pl.ds(D, EP)]).astype(BF16)

    def edge_pass(t):
        b3 = lax.rem(t, 2)
        for i in range(steps):
            rows = pl.ds(i * RC, RC)
            d = dcat[b3, rows, pl.ds(D, EP)]
            dacc[rows, :] = de[b3, rows, :].astype(F32) + mm_bt(d, scat[t, pl.ds(0, top), :])

    blocks = 2 * C
    my_block = lax.rem(me_s, 2) * C + me_d
    BW, HM, HU = msg_o.shape[2], msg_o.shape[1], upd_o.shape[1]

    def block_of(t, half, c, size):
        return eg.at[t, half, pl.ds(0, size), pl.ds(pl.multiple_of(c * BW, BW), BW)]

    def blocks_out(t, size):
        for k in range(blocks):
            @pl.when(k != my_block)
            def _():
                far(
                    block_of(t, k // C, k % C, size), eg_r.at[t, my_block, pl.ds(0, size)],
                    e1_ss.at[t, k], e1_rs.at[t, my_block], 2 * w + k // C, k % C,
                ).start()

    def edge_grads(t):
        grad = mm(edge_t[t, pl.ds(0, DE), :], dcat[lax.rem(t, 2), :, pl.ds(0, D)]).astype(BF16)
        for half in range(2):
            eg[t, half, pl.ds(0, HM), :] = grad[half * HM : (half + 1) * HM]

        @pl.when(t > 0)
        def _():
            n2 = lax.rem(t + 1, 2)
            edges = mm(edge_t[t - 1, pl.ds(0, DE), :], dcat[n2, :, pl.ds(D, EP)])
            outs = mm(act_t[t - 1, pl.ds(0, DE), :], de[n2])
            bias = jnp.sum(de[n2].astype(F32), axis=0, keepdims=True)
            grad = jnp.concatenate([edges, outs], axis=1).astype(BF16)
            eg[t, 0, pl.ds(HM, HU), :] = grad[:HU]
            eg[t, 1, pl.ds(HM, DE - HU), :] = grad[HU:]
            eg[t, 1, pl.ds(HM + DE - HU, 16), pl.ds(0, EP)] = jnp.broadcast_to(bias, (16, EP)).astype(BF16)
            eg[t, 1, pl.ds(HM + DE - HU, 16), pl.ds(EP, EP)] = jnp.zeros((16, EP), BF16)
            eg[t, 1, pl.ds(HM + DE - HU + 16, 2 * HU - DE - 16), :] = jnp.zeros((2 * HU - DE - 16, 2 * EP), BF16)
            blocks_out(t, HM + HU)

        @pl.when(t == 0)
        def _():
            blocks_out(t, HM)

    def blocks_sum(t, size):
        eg_r[t, my_block, pl.ds(0, size), :] = block_of(t, lax.rem(me_s, 2), me_d, size)[...]
        for k in range(blocks):
            @pl.when(k != my_block)
            def _():
                arrive(eg_r.at[t, k, pl.ds(0, size)], e1_rs.at[t, k])
                arrive(block_of(t, k // C, k % C, size), e1_ss.at[t, k])
        total = eg_r[t, 0, pl.ds(0, size), :].astype(F32)
        for k in range(1, blocks):
            total = total + eg_r[t, k, pl.ds(0, size), :].astype(F32)
        eg_b[t, pl.ds(0, size), :] = total.astype(BF16)
        push(eg_b.at[t, pl.ds(0, HM)], msg_o.at[me_s], e2_ss.at[0, t], e2_rs.at[0, me_s], t, me_d)
        if size > HM:
            push(eg_b.at[t, pl.ds(HM, HU)], upd_o.at[me_s], e2_ss.at[1, t], e2_rs.at[1, me_s], t - 1, me_d)

    def gather_blocks():
        for k in range(1, 4):
            j, sec, dpi = peer(k)
            rows = pl.ds(pl.multiple_of(j * Q, Q), Q)
            far(x_s.at[rows], x_r.at[q], x_ss, x_rs, sec, dpi).start()
        x_r[q] = x_s[pl.ds(pl.multiple_of(q * Q, Q), Q), :]

    def gather_wait():
        arrive(x_r.at[pl.ds(0, 3)], x_rs)
        arrive(x_s.at[pl.ds(0, 3 * Q)], x_ss)
        total = x_r[0].astype(F32)
        for j in range(1, 4):
            total = total + x_r[j].astype(F32)
        return total

    def message_back(t):
        b2 = lax.rem(t, 2)
        dm = dmb_r[...].astype(F32)
        total = jnp.zeros((Q, D), F32)
        for k in range(K):
            rows = pl.ds(k * Q, Q)
            d = (gp[t, rows, :].astype(F32) * dm).astype(BF16)
            total = total + d.astype(F32)
            dcat[b2, rows, pl.ds(0, D)] = d
        row_s[:, pl.ds(0, D)] = total.astype(BF16)
        x_s[:, pl.ds(0, D)] = mm(oht[...], dcat[b2, :, pl.ds(0, D)]).astype(BF16)

    def node_backward():
        @pl.when(me_s < S - 1)
        def _():
            arrive(dh1_r, dh_rs)

        def turn(n, carry):
            p = lax.rem(leading + n, B)
            whole = at(p, 0, N)

            @pl.when(me_s < S - 1)
            def _():
                arrive(row_r.at[whole], row_rs.at[p])
                dn0 = mm_bt(row_r[whole, pl.ds(0, 2 * D)], pwn[...])
                dn3 = mm_bt(row_r[whole, pl.ds(2 * D, 2 * EP)], ep[...])
                for i in range(0, N, RB):
                    rows = at(p, i)
                    dn = dn3[i : i + RB]
                    dn3_s[rows, :] = dn
                    first = norm_back(dn0[i : i + RB], un0[rows, :], sc0[rows, :], parn[pl.ds(0, 1), :])
                    dh = (dh1_r[rows, :].astype(F32) + first).astype(BF16).astype(F32)
                    dh2_s[rows, :] = dh + norm_back(dn, un2[rows, :], sc2[rows, :], gains[2])

            @pl.when(me_s == S - 1)
            def _():
                dh2_s[whole, :] = cot[whole, :].astype(F32)

            dy = dh2_s[whole, :].astype(BF16)
            bwd[whole, pl.ds(D, D)] = dy
            da2 = jnp.zeros((N, D), F32)
            for c in range(chunks):
                cols = pl.ds(c * FC, FC)
                dv = mm_bt(dy, fo[cols, :])
                du = stacked(
                    [(slope_s[at(p, i), cols].astype(F32) * dv[i : i + RB]).astype(BF16) for i in range(0, N, RB)]
                )
                da2 = da2 + mm_bt(du, fi[:, cols])
            for i in range(0, N, RB):
                rows = at(p, i)
                block = da2[i : i + RB]
                da2_s[rows, :] = block
                dh1 = dh2_s[rows, :] + norm_back(block, un1[rows, :], sc1[rows, :], gains[1])
                dh1_f[rows, :] = dh1
                bwd[rows, pl.ds(0, D)] = (dh1 * (1.0 / K)).astype(BF16)
            dmb_s[whole, :] = mm_bt(bwd[whole, pl.ds(0, D)], mo[...]).astype(BF16)
            rows_out(p, dmb_s, dmb_r, dmb_ss, dmb_rs)
            return carry

        lax.fori_loop(0, B, turn, 0)

        @pl.when(me_s > 0)
        def _():
            dh1_s[...] = dh1_f[...].astype(BF16)
            far(dh1_s, dh1_r, dh_ss, dh_rs, me_s - 1, me_d).start()

        @pl.when(me_s < S - 1)
        def _():
            far(row_r.at[:, pl.ds(0, 2 * D)], dpqo_r, fw_ss, dpqo_rs, me_s + 1, me_d).start()
            drs = row_r[:, pl.ds(2 * D, 2 * EP)]
            bwd[:, pl.ds(2 * D, 2 * EP)] = drs
            dn = dn3_s[...]
            sg[pl.ds(11, 1), :] = col_sum(dn * un2[...])
            sg[pl.ds(12, 1), :] = col_sum(dn)
            sg[pl.ds(16, 1), pl.ds(0, EP)] = col_sum(drs[:, :EP].astype(F32))

        @pl.when(me_s == S - 1)
        def _():
            bwd[:, pl.ds(2 * D, 2 * EP)] = jnp.zeros((B * N, 2 * EP), BF16)
            sg[pl.ds(11, 1), :] = jnp.zeros((1, D), F32)
            sg[pl.ds(12, 1), :] = jnp.zeros((1, D), F32)
            sg[pl.ds(16, 1), pl.ds(0, EP)] = jnp.zeros((1, EP), F32)

        share(1, bwd, g_bwd)
        sg[pl.ds(13, 1), :] = col_sum(dh2_s[...])
        sg[pl.ds(8, 1), :] = col_sum(da2_s[...] * un1[...])
        sg[pl.ds(9, 1), :] = col_sum(da2_s[...])
        sg[pl.ds(10, 1), :] = col_sum(dh1_f[...])

    def node_backward_drain():
        rows_drain(dmb_s, dmb_ss)

        @pl.when(me_s > 0)
        def _():
            arrive(dh1_s, dh_ss)

        @pl.when(me_s < S - 1)
        def _():
            arrive(row_r.at[:, pl.ds(0, 2 * D)], fw_ss)

    dacc[...] = jnp.zeros_like(dacc)

    def backward_step(step, carry):
        t = S - 1 - step

        @pl.when(me_s == t)
        def _():
            node_backward()

        @pl.when(((t == S - 1) & (me_s >= S - 2)) | (me_s == t - 2))
        def _():
            prepare(me_s)

        @pl.when(t < S - 1)
        def _():
            edge_pass(t)

        @pl.when(t + 2 < S)
        def _():
            blocks_sum(t + 2, HM + HU)

        @pl.when(t == 0)
        def _():
            blocks_sum(1, HM + HU)

        arrive(dmb_r, dmb_rs)
        message_back(t)

        @pl.when(t > 0)
        def _():
            edge_back(t)

        @pl.when(t == 0)
        def _():
            x_s[:, pl.ds(D, EP)] = jnp.zeros((N, EP), BF16)

        gather_blocks()
        other = gather_wait().astype(BF16)
        row_s[:, pl.ds(D, D)] = other[:, :D]
        row_s[:, pl.ds(2 * D + EP, EP)] = other[:, D:]
        dpq = row_s.at[:, pl.ds(0, 2 * D)]

        @pl.when(t > 0)
        def _():
            push(row_s, row_r.at[pl.ds(my_row, Q)], row_ss, row_rs.at[slot], t - 1, owner_d)

        @pl.when(t == 0)
        def _():
            push(dpq, dpqo_r.at[pl.ds(my_row, Q)], row_ss, dpqo_rs, t, owner_d)

        edge_grads(t)

        @pl.when(t > 0)
        def _():
            drain(row_s, row_ss, t - 1, owner_d)

        @pl.when(t == 0)
        def _():
            drain(dpq, row_ss, t, owner_d)

        @pl.when(me_s == t)
        def _():
            node_backward_drain()

        return carry

    lax.fori_loop(0, S, backward_step, 0)

    arrive(dpqo_r, dpqo_rs)
    across = [pl.ds(p * N, N) for p in range(B)]
    for p in range(B):
        share_near(2 + p, dpqo_r.at[across[p]], lambda c, p=p: g_dpq.at[c, across[p]])
    dpq = dpqo_r[...]
    sg[pl.ds(2, 1), :] = col_sum(dpq[:, :D].astype(F32))
    dn = mm_bt(dpq, pw[...])
    unit = hi_s[...]
    sg[pl.ds(0, 1), :] = col_sum(dn * unit)
    sg[pl.ds(1, 1), :] = col_sum(dn)
    share(2 + B, sg, g_small)
    ig[...] = (dh1_f[...] + norm_back(dn, unit, sci[...], gains[0])).astype(BF16)
    blocks_sum(0, HM)
    for p in range(B):
        share_relay(2 + p, dpqo_r.at[across[p]], lambda c, p=p: g_dpq.at[c, across[p]])
    def combine(kind, src, final):
        for sec in range(S):
            arrive(src.at[sec], e2_rs.at[kind, sec])
        for half in range(2):
            total = src[half].astype(F32)
            for sec in range(half + 2, S, 2):
                total = total + src[sec].astype(F32)
            final[half] = total.astype(BF16)

    @pl.when(me_s < S - 1)
    def _():
        combine(1, upd_o, upd_f)

    @pl.when(me_s == S - 1)
    def _():
        upd_f[...] = jnp.zeros_like(upd_f)

    share(4 + B, upd_f, g_upd)
    combine(0, msg_o, msg_f)
    share(3 + B, msg_f, g_msg)
    for t in range(S):
        drain(eg_b.at[t, pl.ds(0, HM)], e2_ss.at[0, t], t, me_d)
        if t > 0:
            drain(eg_b.at[t, pl.ds(HM, HU)], e2_ss.at[1, t], t - 1, me_d)
    share_wait(0, fwd, g_fwd)
    share_wait(1, bwd, g_bwd)
    for p in range(B):
        share_near_wait(2 + p, dpqo_r.at[across[p]], lambda c, p=p: g_dpq.at[c, across[p]])
    share_wait(2 + B, sg, g_small)
    share_wait(3 + B, msg_f, g_msg)
    share_wait(4 + B, upd_f, g_upd)


def run_relay(dims, operands):
    S, B, N, K, Q, D, DE, EP, FF, C = dims
    R = K * Q
    BN = B * N
    tall = DE + N + Q
    vm = pl.BlockSpec(memory_space=pltpu.VMEM)
    hbm = pl.BlockSpec(memory_space=pl.ANY)
    dma = pltpu.SemaphoreType.DMA
    sds = jax.ShapeDtypeStruct
    BW = D // C
    tile = 32
    held = -(-(DE + 16) // tile) * tile
    scratch = [
        pltpu.VMEM((BN, D), F32),
        pltpu.VMEM((8, D), F32),
        pltpu.VMEM((1, EP), F32),
        pltpu.VMEM((S, DE, D), BF16),
        pltpu.VMEM((S, held, 2 * EP), BF16),
        pltpu.VMEM((BN, 4 * D), BF16),
        pltpu.VMEM((BN, 2 * D + 2 * EP), BF16),
        pltpu.VMEM((24, D), F32),
        pltpu.VMEM((S, 2, (DE + held) // 2, D), BF16),
        pltpu.VMEM((S, 2 * C, (DE + held) // 2, BW), BF16),
        pltpu.VMEM((S, (DE + held) // 2, BW), BF16),
        pltpu.VMEM((S, DE // 2, BW), BF16),
        pltpu.VMEM((2, DE // 2, BW), BF16),
        pltpu.VMEM((S, held // 2, BW), BF16),
        pltpu.VMEM((2, held // 2, BW), BF16),
        pltpu.VMEM((S, EP, EP), BF16),
        pltpu.VMEM((S, 16, EP), BF16),
        pltpu.VMEM((S, R, EP), BF16),
        pltpu.VMEM((S, tall, D), BF16),
        pltpu.VMEM((S, tall, EP), BF16),
        pltpu.VMEM((D, 2 * D), BF16),
        pltpu.VMEM((8, D), F32),
        pltpu.VMEM((BN, D), BF16),
        pltpu.VMEM((BN, D), BF16),
        pltpu.VMEM((Q, D), BF16),
        pltpu.VMEM((BN, D), BF16),
        pltpu.VMEM((BN, 2 * D), BF16),
        pltpu.VMEM((Q, 2 * D), BF16),
        pltpu.VMEM((BN, 2 * EP), BF16),
        pltpu.VMEM((Q, 2 * EP), BF16),
        pltpu.VMEM((BN, D), F32),
        pltpu.VMEM((BN, D), F32),
        pltpu.VMEM((BN, D), F32),
        pltpu.VMEM((BN, D), F32),
        pltpu.VMEM((BN, 1), F32),
        pltpu.VMEM((BN, 1), F32),
        pltpu.VMEM((BN, 1), F32),
        pltpu.VMEM((BN, 1), F32),
        pltpu.VMEM((BN, FF), F32),
        pltpu.VMEM((BN, FF), BF16),
        pltpu.VMEM((2, R, EP), BF16),
        pltpu.VMEM((R, EP), F32),
        pltpu.VMEM((S, R, D), BF16),
        pltpu.VMEM((S, R, EP), BF16),
        pltpu.VMEM((2, R, D + EP), BF16),
        pltpu.VMEM((S, EP, R), BF16),
        pltpu.VMEM((S, EP, R), BF16),
        pltpu.VMEM((N, D + EP), BF16),
        pltpu.VMEM((4, Q, D + EP), BF16),
        pltpu.VMEM((Q, 2 * D + 2 * EP), BF16),
        pltpu.VMEM((BN, 2 * D + 2 * EP), BF16),
        pltpu.VMEM((BN, 2 * D), BF16),
        pltpu.VMEM((BN, D), BF16),
        pltpu.VMEM((Q, D), BF16),
        pltpu.VMEM((BN, D), BF16),
        pltpu.VMEM((BN, D), BF16),
        pltpu.VMEM((BN, D), F32),
        pltpu.VMEM((BN, D), F32),
        pltpu.VMEM((BN, D), F32),
        pltpu.VMEM((BN, D), F32),
        pltpu.VMEM((BN, D), F32),
        pltpu.VMEM((BN, D), BF16),
        dma, dma((2,)), dma((2,)), dma, dma,
        dma, dma, dma, dma, dma, dma, dma, dma,
        dma, dma((B,)), dma, dma, dma, dma((B,)), dma,
        dma, dma, dma, dma, dma,
        dma((S, 2 * C)), dma((S, 2 * C)), dma((2, S)), dma((2, S)), dma((5 + B, C)), dma((5 + B, C)),
        dma((B, C // 2)), dma((2, 2, S // 2)), dma((2, S)), dma((2, S)), dma((2, S)),
    ]
    return pl.pallas_call(
        functools.partial(relay_kernel, dims),
        out_shape=(
            sds((BN, D), BF16),
            sds((BN, D), BF16),
            sds((C, BN, 4 * D), BF16),
            sds((C, BN, 2 * D + 2 * EP), BF16),
            sds((C, BN, 2 * D), BF16),
            sds((C, 24, D), F32),
            sds((C, 2, DE // 2, BW), BF16),
            sds((C, 2, held // 2, BW), BF16),
        ),
        in_specs=[hbm, vm, pl.BlockSpec(memory_space=pltpu.SMEM)] + [vm] * 16,
        out_specs=(vm,) * 2 + (hbm,) * 6,
        scratch_shapes=scratch,
        compiler_params=pltpu.CompilerParams(
            collective_id=0, has_side_effects=True, vmem_limit_bytes=62 * 1024 * 1024
        ),
    )(*operands)


def gradient_kernel(
    dims,
    fwd, bwd, dpq, small, edge, upd, fi, fo, fb, act, ig,
    g_pair, g_edge, g_out, g_fi, g_fo, g_ep, g_self, g_eout, g_gain, g_shift, g_nb, g_fb, g_eb, act_out, ig_out,
    fwd_v, bwd_v, dpq_v, fi_v, fo_v, gfi_v, gfo_v, pair_v, out_v, edge_v, upd_v, in_sems, sems,
):
    S, B, N, K, Q, D, DE, EP, FF, C = dims
    chunks = 4
    FC = FF // chunks

    def part(c, size=D):
        return pl.ds(c * size, size)

    loads = {}

    def load(name, src, dst):
        loads[name] = pltpu.make_async_copy(src, dst, in_sems.at[len(loads)])
        loads[name].start()

    load("a2", fwd.at[:, part(2)], fwd_v.at[2])
    load("dy", bwd.at[:, part(1)], bwd_v.at[1])
    for c in range(chunks):
        load(("fi", c), fi.at[:, part(c, FC)], fi_v.at[c])
        load(("fo", c), fo.at[part(c, FC)], fo_v.at[c])
    load("a1", fwd.at[:, part(0)], fwd_v.at[0])
    load("dpq0", dpq.at[:, part(0)], dpq_v.at[0])
    load("dpq1", dpq.at[:, part(1)], dpq_v.at[1])
    load("mbar", fwd.at[:, part(1)], fwd_v.at[1])
    load("dmsg", bwd.at[:, part(0)], bwd_v.at[0])
    load("a3", fwd.at[:, part(3)], fwd_v.at[3])
    load("drs", bwd.at[:, part(2)], bwd_v.at[2])
    load("edge", edge, edge_v)
    load("upd", upd, upd_v)
    stores = []

    def out(src, dst):
        copy = pltpu.make_async_copy(src, dst, sems.at[len(stores)])
        copy.start()
        stores.append(copy)

    out(act, act_out)
    out(ig, ig_out)
    loads["a2"].wait()
    loads["dy"].wait()
    a2 = fwd_v[2]
    dy = bwd_v[1]
    for c in range(chunks):
        cols = part(c, FC)
        loads["fi", c].wait()
        loads["fo", c].wait()
        value, slope = gelu_both(mm(a2, fi_v[c]) + fb[:, cols])
        du = (slope * mm_bt(dy, fo_v[c])).astype(BF16)
        g_fb[:, cols] = col_sum(du.astype(F32))
        gfi_v[c] = mm_at(a2, du)
        out(gfi_v.at[c], g_fi.at[0, :, cols])
        gfo_v[c] = mm_at(value.astype(BF16), dy)
        out(gfo_v.at[c], g_fo.at[0, cols])
    loads["a1"].wait()
    for c in range(2):
        loads["dpq%d" % c].wait()
        pair_v[c] = mm_at(fwd_v[0], dpq_v[c])
        out(pair_v.at[c], g_pair.at[0, :, part(c)])
    loads["mbar"].wait()
    loads["dmsg"].wait()
    out_v[...] = mm_at(fwd_v[1], bwd_v[0]) * float(K)
    out(out_v, g_out.at[0])
    loads["a3"].wait()
    loads["drs"].wait()
    ends = mm_at(fwd_v[3], bwd_v[2])
    g_ep[0] = jnp.concatenate([ends[:, :DE], ends[:, EP : EP + DE]], axis=1)
    total = small[0]
    for c in range(1, C):
        total = total + small[c]
    for i, rows in enumerate(((0, 1, 2), (8, 9, 10), (11, 12, 13))):
        g_gain[i] = total[rows[0] : rows[0] + 1]
        g_shift[i] = total[rows[1] : rows[1] + 1]
        g_nb[i] = total[rows[2] : rows[2] + 1]
    g_eb[0, pl.ds(0, 1), :] = total[16:17, :DE]
    loads["edge"].wait()
    loads["upd"].wait()
    BW = edge_v.shape[3]
    for c in range(C):
        for half in range(2):
            block = edge_v[c, half].astype(F32)
            g_edge[0, pl.ds(half * (DE // 2), DE // 2), pl.ds(c * BW, BW)] = block
        block = stacked([upd_v[c, 0], upd_v[c, 1]]).astype(F32)
        first = c * BW
        for array, begin in ((g_self, 0), (g_eout, EP)):
            low, high = max(first, begin), min(first + BW, begin + DE)
            if low < high:
                array[0, :, pl.ds(low - begin, high - low)] = block[:DE, low - first : high - first]
        low, high = first, min(first + BW, DE)
        if low < high:
            g_eb[0, pl.ds(1, 1), pl.ds(low, high - low)] = block[DE : DE + 1, low - first : high - first]
    for copy in stores:
        copy.wait()


def run_gradients(dims, operands):
    S, B, N, K, Q, D, DE, EP, FF, C = dims
    rows = C * B * N
    BW = D // C
    held = operands[5].shape[2]
    vm = pl.BlockSpec(memory_space=pltpu.VMEM)
    hbm = pl.BlockSpec(memory_space=pl.ANY)
    sds = jax.ShapeDtypeStruct
    shapes = (
        (1, D, 2 * D), (1, DE, D), (1, D, D), (1, D, FF), (1, FF, D), (1, D, 2 * DE), (1, DE, DE), (1, DE, DE),
        (3, 1, D), (3, 1, D), (3, 1, D), (1, FF), (1, 2, DE),
    )
    return pl.pallas_call(
        functools.partial(gradient_kernel, dims),
        out_shape=tuple(sds(shape, F32) for shape in shapes) + (sds((1, B, N, D), BF16),) * 2,
        in_specs=[hbm, hbm, hbm, vm, hbm, hbm, hbm, hbm, vm, hbm, hbm],
        out_specs=(hbm, vm, hbm, hbm, hbm) + (vm,) * 8 + (hbm,) * 2,
        scratch_shapes=[
            pltpu.VMEM((4, rows, D), BF16),
            pltpu.VMEM((3, rows, D), BF16),
            pltpu.VMEM((2, rows, D), BF16),
            pltpu.VMEM((4, D, FF // 4), BF16),
            pltpu.VMEM((4, FF // 4, D), BF16),
            pltpu.VMEM((4, D, FF // 4), F32),
            pltpu.VMEM((4, FF // 4, D), F32),
            pltpu.VMEM((2, D, D), F32),
            pltpu.VMEM((D, D), F32),
            pltpu.VMEM((C, 2, DE // 2, BW), BF16),
            pltpu.VMEM((C, 2, held, BW), BF16),
            pltpu.SemaphoreType.DMA((19,)),
            pltpu.SemaphoreType.DMA((13,)),
        ],
        compiler_params=pltpu.CompilerParams(vmem_limit_bytes=56 * 1024 * 1024),
    )(*operands)


def stationary(
    clean_nodes, noise_nodes, edge_feats, neighbours, time_bins, cotangent,
    pair_weight, message_edge, message_out, ffn_in, ffn_out, edge_pair, edge_self, edge_out,
    norm_gain, norm_shift, node_bias, ffn_bias, edge_bias,
):
    S = lax.axis_size("section")
    place = lax.axis_index("section")
    column = lax.axis_index("dp")
    B, N, D = clean_nodes.shape
    K, DE = edge_feats.shape[2:]
    FF = ffn_in.shape[2]
    Q = N // 4
    EP = DE + N
    core = column % 2
    w = place // 2
    slab = (place % 2) * 2 * Q

    node_ids = jnp.arange(N, dtype=jnp.int32)
    both = [
        lax.dynamic_slice(array, (w % B, slab) + (0,) * (array.ndim - 2), (1, 2 * Q) + array.shape[2:])[0]
        for array in (edge_feats, neighbours)
    ]
    chosen = (both[1][:, :, None] == node_ids).astype(BF16)
    both = jnp.concatenate([both[0], chosen], axis=2)
    mine = lax.dynamic_slice_in_dim(both, core * Q, Q, 0)
    theirs = lax.dynamic_slice_in_dim(both, (1 - core) * Q, Q, 0)
    got = lax.ppermute(theirs, "dp", [(i, i ^ 1) for i in range(lax.axis_size("dp"))])
    ecat0 = jnp.swapaxes(jnp.where(w // B == core, mine, got), 0, 1).reshape(K * Q, EP)
    oht = jnp.transpose(ecat0[:, DE:])
    phase = (time_bins.astype(F32) + 0.5) * (math.pi * 0.5 / TBINS)
    mix = jnp.cos(phase[None] - jnp.array([[0.0], [math.pi * 0.5]], F32))

    def by_rows(array):
        return jnp.transpose(array, (1, 0, 2))

    def widen(array, size, axis=-1):
        extra = [(0, 0)] * array.ndim
        extra[axis] = (0, size - array.shape[axis])
        return jnp.pad(array, extra)

    ep = jnp.concatenate([widen(edge_pair[0, :, :DE], EP), widen(edge_pair[0, :, DE:], EP)], axis=1)
    C = lax.axis_size("dp")
    dims = (S, B, N, K, Q, D, DE, EP, FF, C)
    act, ig, g_fwd, g_bwd, g_dpq, g_small, g_msg, g_upd = run_relay(
        dims,
        (
            ecat0, oht, mix, clean_nodes.reshape(B * N, D), noise_nodes.reshape(B * N, D),
            cotangent.reshape(B * N, D), pair_weight[0], message_out[0], ffn_in[0], ffn_out[0], ep,
            by_rows(norm_gain), by_rows(norm_shift), by_rows(node_bias), ffn_bias, edge_bias[0],
            message_edge[0], edge_self[0], edge_out[0],
        ),
    )
    grads = run_gradients(
        dims,
        (
            g_fwd.reshape(C * B * N, -1), g_bwd.reshape(C * B * N, -1), g_dpq.reshape(C * B * N, -1),
            g_small, g_msg, g_upd, ffn_in[0], ffn_out[0], ffn_bias, act.reshape(1, B, N, D), ig.reshape(1, B, N, D),
        ),
    )
    grads, outs = list(grads[:-2]), tuple(grads[-2:])
    grads[8:11] = [by_rows(array) for array in grads[8:11]]
    return outs + tuple(grads)


def solution(mesh):
    sections, copies = mesh.shape["section"], mesh.shape["dp"]

    def body(*args):
        B, N = args[0].shape[:2]
        fits = sections == 4 * B and copies % 2 == 0 and N % 64 == 0
        return stationary(*args) if fits else on_device(*args)

    placed = (
        P("dp", None, None),
        P("dp", None, None),
        P("dp", None, None, None),
        P("dp", None, None),
        P("dp"),
        P("dp", None, None),
        P("section", None, None),
        P("section", None, None),
        P("section", None, None),
        P("section", None, None),
        P("section", None, None),
        P("section", None, None),
        P("section", None, None),
        P("section", None, None),
        P("section", None, None),
        P("section", None, None),
        P("section", None, None),
        P("section", None),
        P("section", None, None),
    )
    return jax.shard_map(
        body,
        mesh=mesh,
        in_specs=placed,
        out_specs=(
            P("section", "dp", None, None),
            P("section", "dp", None, None),
            P("section", None, None),
            P("section", None, None),
            P("section", None, None),
            P("section", None, None),
            P("section", None, None),
            P("section", None, None),
            P("section", None, None),
            P("section", None, None),
            P("section", None, None),
            P("section", None, None),
            P("section", None, None),
            P("section", None),
            P("section", None, None),
        ),
        check_vma=False,
    )
```

```python
import functools
import math

import jax
import jax.numpy as jnp
from jax import lax
from jax.experimental import pallas as pl
from jax.experimental.pallas import tpu as pltpu
from jax.sharding import PartitionSpec as P

TBINS = 100


def from_behind(block, axis, distance):
    devices = range(lax.axis_size(axis))
    route = [(i - distance, i) for i in devices if i - distance in devices]
    return lax.ppermute(block, axis, route)


def for_sending(value):
    return jax.tree.map(lambda a: a.astype(jnp.bfloat16) if a.dtype == jnp.float32 else a, value)


def layer_norm(value, gain, shift):
    centre = jnp.mean(value, axis=-1, keepdims=True)
    centred = value - centre
    spread = jnp.mean(centred * centred, axis=-1, keepdims=True)
    return centred * lax.rsqrt(spread + 1e-05) * gain + shift


def forward_layer(weights, hidden, edge_state, nearest):
    (
        pair_w,
        msg_edge,
        msg_out,
        ffn_w_in,
        ffn_w_out,
        edge_pair_w,
        edge_self_w,
        edge_out_w,
        gains,
        shifts,
        node_b,
        ffn_b,
        edge_b,
    ) = weights
    width = msg_out.shape[0]
    edge_width = edge_self_w.shape[0]
    normed_one = layer_norm(hidden, gains[0], shifts[0]).astype(jnp.bfloat16)
    pair_out = jnp.dot(normed_one, pair_w, preferred_element_type=jnp.float32)
    before_act = (
        pair_out[:, None, :width]
        + jnp.take(pair_out[:, width:], nearest, axis=0)
        + jnp.einsum("nkc,cd->nkd", edge_state, msg_edge, preferred_element_type=jnp.float32)
        + node_b[0]
    )
    message_act = jax.nn.gelu(before_act).astype(jnp.bfloat16)
    message_all = jnp.einsum(
        "nkc,cd->nkd", message_act, msg_out, preferred_element_type=jnp.float32
    )
    after_msg = hidden + jnp.mean(message_all, axis=1) + node_b[1]
    normed_two = layer_norm(after_msg, gains[1], shifts[1]).astype(jnp.bfloat16)
    ffn_pre = jnp.dot(normed_two, ffn_w_in, preferred_element_type=jnp.float32) + ffn_b
    ffn_act = jax.nn.gelu(ffn_pre).astype(jnp.bfloat16)
    after_ffn = (
        after_msg + jnp.dot(ffn_act, ffn_w_out, preferred_element_type=jnp.float32) + node_b[2]
    )
    normed_three = layer_norm(after_ffn, gains[2], shifts[2]).astype(jnp.bfloat16)
    edge_pairs = jnp.dot(normed_three, edge_pair_w, preferred_element_type=jnp.float32)
    edge_pre = (
        edge_pairs[:, None, :edge_width]
        + jnp.take(edge_pairs[:, edge_width:], nearest, axis=0)
        + jnp.einsum("nkc,cd->nkd", edge_state, edge_self_w, preferred_element_type=jnp.float32)
        + edge_b[0]
    )
    edge_act = jax.nn.gelu(edge_pre).astype(jnp.bfloat16)
    edge_next = (
        edge_state.astype(jnp.float32)
        + jnp.einsum("nkc,cd->nkd", edge_act, edge_out_w, preferred_element_type=jnp.float32)
        + edge_b[1]
    )
    saved = (
        normed_one,
        before_act,
        message_act,
        after_msg,
        normed_two,
        ffn_pre,
        ffn_act,
        after_ffn,
        normed_three,
        edge_pre,
        edge_act,
    )
    return (after_ffn, edge_next, saved)


def backward_layer(weights, hidden, edge_state, nearest, grad_nodes_out, grad_edges_out):
    (
        pair_w,
        msg_edge,
        msg_out,
        ffn_w_in,
        ffn_w_out,
        edge_pair_w,
        edge_self_w,
        edge_out_w,
        gains,
        shifts,
        node_b,
        ffn_b,
        edge_b,
    ) = weights
    unused_nodes, unused_edges, saved = forward_layer(weights, hidden, edge_state, nearest)
    (
        normed_one,
        before_act,
        message_act,
        after_msg,
        normed_two,
        ffn_pre,
        ffn_act,
        after_ffn,
        normed_three,
        edge_pre,
        edge_act,
    ) = saved
    width = msg_out.shape[0]
    edge_width = edge_self_w.shape[0]
    count = nearest.shape[1]
    node_count = hidden.shape[0]
    one_hot = (
        nearest.reshape(-1)[None, :] == jnp.arange(node_count, dtype=jnp.int32)[:, None]
    ).astype(jnp.bfloat16)
    edge_grad_low = grad_edges_out.astype(jnp.bfloat16)
    grad_edge_b1 = jnp.sum(grad_edges_out, axis=(0, 1))
    grad_edge_out_w = jnp.einsum(
        "nkc,nkd->cd", edge_act, edge_grad_low, preferred_element_type=jnp.float32
    )
    edge_act_grad = jnp.einsum(
        "nkd,cd->nkc", edge_grad_low, edge_out_w, preferred_element_type=jnp.float32
    )
    unused_value, gelu_edge = jax.vjp(jax.nn.gelu, edge_pre)
    edge_pre_grad = gelu_edge(edge_act_grad)[0].astype(jnp.bfloat16)
    grad_edge_b0 = jnp.sum(edge_pre_grad, axis=(0, 1), dtype=jnp.float32)
    grad_edge_self_w = jnp.einsum(
        "nkc,nkd->cd", edge_state, edge_pre_grad, preferred_element_type=jnp.float32
    )
    edge_total = grad_edges_out + jnp.einsum(
        "nkd,cd->nkc", edge_pre_grad, edge_self_w, preferred_element_type=jnp.float32
    )
    own_edge = jnp.sum(edge_pre_grad, axis=1, dtype=jnp.float32)
    other_edge = jnp.dot(
        one_hot, edge_pre_grad.reshape(-1, edge_width), preferred_element_type=jnp.float32
    )
    pairs_grad = jnp.concatenate([own_edge, other_edge], axis=-1).astype(jnp.bfloat16)
    grad_edge_pair_w = jnp.einsum(
        "nc,nd->cd", normed_three, pairs_grad, preferred_element_type=jnp.float32
    )
    normed_three_grad = jnp.einsum(
        "nd,cd->nc", pairs_grad, edge_pair_w, preferred_element_type=jnp.float32
    )
    unused_value, norm_three_back = jax.vjp(layer_norm, after_ffn, gains[2], shifts[2])
    ffn_side, gain_three, shift_three = norm_three_back(normed_three_grad)
    after_ffn_grad = grad_nodes_out + ffn_side
    grad_node_b2 = jnp.sum(after_ffn_grad, axis=0)
    ffn_out_grad = after_ffn_grad.astype(jnp.bfloat16)
    grad_ffn_w_out = jnp.einsum(
        "nc,nd->cd", ffn_act, ffn_out_grad, preferred_element_type=jnp.float32
    )
    ffn_act_grad = jnp.einsum(
        "nd,cd->nc", ffn_out_grad, ffn_w_out, preferred_element_type=jnp.float32
    )
    unused_value, gelu_ffn = jax.vjp(jax.nn.gelu, ffn_pre)
    ffn_pre_grad = gelu_ffn(ffn_act_grad)[0].astype(jnp.bfloat16)
    grad_ffn_b = jnp.sum(ffn_pre_grad, axis=0, dtype=jnp.float32)
    grad_ffn_w_in = jnp.einsum(
        "nc,nd->cd", normed_two, ffn_pre_grad, preferred_element_type=jnp.float32
    )
    normed_two_grad = jnp.einsum(
        "nd,cd->nc", ffn_pre_grad, ffn_w_in, preferred_element_type=jnp.float32
    )
    unused_value, norm_two_back = jax.vjp(layer_norm, after_msg, gains[1], shifts[1])
    msg_side, gain_two, shift_two = norm_two_back(normed_two_grad)
    after_msg_grad = after_ffn_grad + msg_side
    grad_node_b1 = jnp.sum(after_msg_grad, axis=0)
    message_grad = (after_msg_grad / count).astype(jnp.bfloat16)
    grad_msg_out = jnp.einsum(
        "nkc,nd->cd", message_act, message_grad, preferred_element_type=jnp.float32
    )
    message_act_grad = jnp.einsum(
        "nd,cd->nc", message_grad, msg_out, preferred_element_type=jnp.float32
    )
    unused_value, gelu_msg = jax.vjp(jax.nn.gelu, before_act)
    before_grad = gelu_msg(jnp.broadcast_to(message_act_grad[:, None, :], before_act.shape))[
        0
    ].astype(jnp.bfloat16)
    grad_node_b0 = jnp.sum(before_grad, axis=(0, 1), dtype=jnp.float32)
    grad_msg_edge = jnp.einsum(
        "nkc,nkd->cd", edge_state, before_grad, preferred_element_type=jnp.float32
    )
    edge_total = edge_total + jnp.einsum(
        "nkd,cd->nkc", before_grad, msg_edge, preferred_element_type=jnp.float32
    )
    own_node = jnp.sum(before_grad, axis=1, dtype=jnp.float32)
    other_node = jnp.dot(
        one_hot, before_grad.reshape(-1, width), preferred_element_type=jnp.float32
    )
    pair_grad = jnp.concatenate([own_node, other_node], axis=-1).astype(jnp.bfloat16)
    grad_pair_w = jnp.einsum("nc,nd->cd", normed_one, pair_grad, preferred_element_type=jnp.float32)
    normed_one_grad = jnp.einsum("nd,cd->nc", pair_grad, pair_w, preferred_element_type=jnp.float32)
    unused_value, norm_one_back = jax.vjp(layer_norm, hidden, gains[0], shifts[0])
    input_side, gain_one, shift_one = norm_one_back(normed_one_grad)
    hidden_grad = after_msg_grad + input_side
    grads = (
        grad_pair_w,
        grad_msg_edge,
        grad_msg_out,
        grad_ffn_w_in,
        grad_ffn_w_out,
        grad_edge_pair_w,
        grad_edge_self_w,
        grad_edge_out_w,
        jnp.stack([gain_one, gain_two, gain_three]),
        jnp.stack([shift_one, shift_two, shift_three]),
        jnp.stack([grad_node_b0, grad_node_b1, grad_node_b2]),
        grad_ffn_b,
        jnp.stack([grad_edge_b0, grad_edge_b1]),
    )
    return (hidden_grad.astype(jnp.bfloat16), edge_total.astype(jnp.bfloat16), grads)


def on_device(
    clean_nodes,
    noise_nodes,
    edge_feats,
    neighbours,
    time_bins,
    cotangent,
    pair_weight,
    message_edge,
    message_out,
    ffn_in,
    ffn_out,
    edge_pair,
    edge_self,
    edge_out,
    norm_gain,
    norm_shift,
    node_bias,
    ffn_bias,
    edge_bias,
):
    sections = lax.axis_size("section")
    place = lax.axis_index("section")
    weights = tuple(
        (
            item[0]
            for item in (
                pair_weight,
                message_edge,
                message_out,
                ffn_in,
                ffn_out,
                edge_pair,
                edge_self,
                edge_out,
                norm_gain,
                norm_shift,
                node_bias,
                ffn_bias,
                edge_bias,
            )
        )
    )
    batches, node_count, width = clean_nodes.shape
    phase = (time_bins.astype(jnp.float32) + 0.5) * (math.pi * 0.5 / TBINS)
    start = jnp.cos(phase)[:, None, None] * clean_nodes.astype(jnp.float32) + jnp.sin(phase)[
        :, None, None
    ] * noise_nodes.astype(jnp.float32)
    zero_nodes = jnp.zeros((node_count, width), jnp.bfloat16)
    zero_edges = jnp.zeros(edge_feats.shape[1:], jnp.bfloat16)
    is_first = place == 0
    is_last = place == sections - 1

    def forward_step(step_index, carry):
        recv_nodes, recv_edges, back_nodes, kept_nodes, kept_edges, section_outs = carry
        item = step_index - place
        first_pass = (item >= 0) & (item < batches)
        second_pass = (item >= sections) & (item < sections + batches)
        index = jnp.clip(jnp.where(second_pass, item - sections, item), 0, batches - 1)
        predicted = back_nodes
        own_start = lax.dynamic_index_in_dim(start, index, 0, keepdims=False)
        lead_nodes = own_start + jnp.where(second_pass, predicted.astype(jnp.float32), 0.0)
        nodes_in = jnp.where(is_first, lead_nodes, recv_nodes.astype(jnp.float32))
        edges_in = jnp.where(
            is_first, lax.dynamic_index_in_dim(edge_feats, index, 0, keepdims=False), recv_edges
        )
        nearest = lax.dynamic_index_in_dim(neighbours, index, 0, keepdims=False)

        def run_layer(operand):
            after, edge_next, saved = forward_layer(weights, operand[0], operand[1], operand[2])
            return (after.astype(jnp.bfloat16), edge_next.astype(jnp.bfloat16))

        def skip_layer(operand):
            return (zero_nodes, zero_edges)

        out_nodes, out_edges = lax.cond(
            first_pass | second_pass, run_layer, skip_layer, (nodes_in, edges_in, nearest)
        )
        kept_nodes = lax.dynamic_update_index_in_dim(
            kept_nodes, jnp.where(second_pass, nodes_in, kept_nodes[index]), index, 0
        )
        kept_edges = lax.dynamic_update_index_in_dim(
            kept_edges, jnp.where(second_pass, edges_in, kept_edges[index]), index, 0
        )
        section_outs = lax.dynamic_update_index_in_dim(
            section_outs, jnp.where(second_pass, out_nodes, section_outs[index]), index, 0
        )
        recv_nodes, recv_edges = from_behind((out_nodes, out_edges), "section", 1)
        back_nodes = from_behind(out_nodes, "section", 1 - sections)
        return (recv_nodes, recv_edges, back_nodes, kept_nodes, kept_edges, section_outs)

    forward_init = (
        zero_nodes,
        zero_edges,
        zero_nodes,
        jnp.zeros((batches, node_count, width), jnp.float32),
        jnp.zeros_like(edge_feats),
        jnp.zeros((batches, node_count, width), jnp.bfloat16),
    )
    unused_nodes, unused_edges, unused_back, kept_nodes, kept_edges, section_outs = lax.fori_loop(
        0, 2 * sections + batches - 1, forward_step, forward_init
    )
    grads_zero = tuple((jnp.zeros(item.shape, jnp.float32) for item in weights))

    def backward_step(step_index, carry):
        recv_grad_nodes, recv_grad_edges, grads, input_grads = carry
        item = step_index - (sections - 1 - place)
        live = (item >= 0) & (item < batches)
        index = jnp.clip(item, 0, batches - 1)
        nodes_grad_out = jnp.where(
            is_last,
            lax.dynamic_index_in_dim(cotangent, index, 0, keepdims=False).astype(jnp.float32),
            recv_grad_nodes.astype(jnp.float32),
        )
        edges_grad_out = jnp.where(is_last, 0.0, recv_grad_edges.astype(jnp.float32))
        nearest = lax.dynamic_index_in_dim(neighbours, index, 0, keepdims=False)

        def run_back(operand):
            return backward_layer(
                weights, operand[0], operand[1], operand[2], operand[3], operand[4]
            )

        def skip_back(operand):
            return (zero_nodes, zero_edges, grads_zero)

        nodes_grad, edges_grad, terms = lax.cond(
            live,
            run_back,
            skip_back,
            (kept_nodes[index], kept_edges[index], nearest, nodes_grad_out, edges_grad_out),
        )
        grads = tuple((total + term for total, term in zip(grads, terms)))
        input_grads = lax.dynamic_update_index_in_dim(
            input_grads, jnp.where(live, nodes_grad, input_grads[index]), index, 0
        )
        recv_grad_nodes, recv_grad_edges = from_behind((nodes_grad, edges_grad), "section", -1)
        return (recv_grad_nodes, recv_grad_edges, grads, input_grads)

    backward_init = (
        zero_nodes,
        zero_edges,
        grads_zero,
        jnp.zeros((batches, node_count, width), jnp.bfloat16),
    )
    unused_grad_nodes, unused_grad_edges, grads, input_grads = lax.fori_loop(
        0, sections + batches - 1, backward_step, backward_init
    )
    totals = jax.tree.map(lambda part: part.astype(jnp.float32), lax.psum(for_sending(grads), "dp"))
    return (
        section_outs[None],
        input_grads[None],
        totals[0][None],
        totals[1][None],
        totals[2][None],
        totals[3][None],
        totals[4][None],
        totals[5][None],
        totals[6][None],
        totals[7][None],
        totals[8][None],
        totals[9][None],
        totals[10][None],
        totals[11][None],
        totals[12][None],
    )


BF16 = jnp.bfloat16
F32 = jnp.float32
MESH = pl.DeviceIdType.MESH
GELU_A = 0.7978845608028654
GELU_B = 0.044715


def gelu(x):
    return 0.5 * x * (1.0 + jnp.tanh(x * (GELU_A + (GELU_A * GELU_B) * (x * x))))


def gelu_both(x):
    square = x * x
    t = jnp.tanh(x * (GELU_A + (GELU_A * GELU_B) * square))
    half = 0.5 * (1.0 + t)
    slope = half + (0.5 * x) * (1.0 - t * t) * (GELU_A + (3.0 * GELU_A * GELU_B) * square)
    return x * half, slope


def mm(a, b):
    return jnp.dot(a, b, preferred_element_type=F32)


def mm_bt(a, b):
    return lax.dot_general(a, b, (((1,), (1,)), ((), ())), preferred_element_type=F32)


def mm_at(a, b):
    return lax.dot_general(a, b, (((0,), (0,)), ((), ())), preferred_element_type=F32)


def stacked(blocks):
    return jnp.concatenate(blocks, axis=0)


def row_mean(x):
    return jnp.mean(x, axis=-1, keepdims=True)


def normed(x):
    centred = x - row_mean(x)
    scale = lax.rsqrt(row_mean(centred * centred) + 1e-05)
    return centred * scale, scale


def norm_back(grad, unit, scale, gain):
    t = grad * gain
    return scale * (t - row_mean(t) - unit * row_mean(t * unit))


def col_sum(x):
    return jnp.sum(x, axis=0, keepdims=True)


def relay_kernel(
    dims,
    edges_in, near_in, mix, clean, noise, cot, pw, mo, fi, fo, ends, gains, shifts, node_b, fb, edge_b, we_own, ws_own, wo_own,
    act, ig, g_fwd, g_bwd, g_dpq, g_small, g_msg, g_upd,
    ep, e0, nb0, oht, start, par, eb0, wall_msg, wall_upd, fwd, bwd, sg,
    eg, eg_r, eg_b, msg_o, msg_f, upd_o, upd_f, wo, eb1,
    ecat, wcat, scat, pwn, parn, hin_r, hst, mb_s, mb_r, pq_s, pq_r, rq_s, rq_r,
    un0, un1, un2, hi_s, sc0, sc1, sc2, sci, u_s, slope_s, de, dacc, gp, gpe, dcat, act_t, edge_t,
    x_s, x_r, row_s, row_r, dpqo_r, dmb_s, dmb_r, dh1_s, dh1_r, dh1_f, dh2_s, dn3_s, da2_s, h1_s, a1_s,
    ld_sem, ld_ss, nx_ss, nx_rs, hop_ss, hop_rs,
    pq_ss, pq_rs, ag_ss, ag_rs, rq_ss, rq_rs, ag2_ss, ag2_rs,
    mb_ss, mb_rs, x_ss, x_rs, row_ss, row_rs, dpqo_rs, fw_ss, dmb_ss, dmb_rs, dh_ss, dh_rs,
    e1_ss, e1_rs, e2_ss, e2_rs, g_ss, g_rs, relay_ss, ring_ss, ring_rs, sib_ss, sib_rs,
):
    S, B, N, K, Q, D, DE, EP, FF, C = dims
    BN = B * N
    RB = 16
    top = DE + N
    me_s = lax.axis_index("section")
    me_d = lax.axis_index("dp")
    core = lax.rem(me_d, 2)
    pair = me_d - core
    w = lax.div(me_s, 2)
    q = 2 * lax.rem(me_s, 2) + core
    owner_d = pair + lax.div(w, B)
    slot = lax.rem(w, B)
    my_row = pl.multiple_of(slot * N + q * Q, Q)
    own_rows = pl.ds(top, Q)

    def quarter(j):
        return pl.ds(pl.multiple_of(DE + j * Q, Q), Q)

    def is_me(sec, dpi):
        return (sec == me_s) & (dpi == me_d)

    def far(src, dst, ssem, rsem, sec, dpi):
        return pltpu.make_async_remote_copy(
            src_ref=src, dst_ref=dst, send_sem=ssem, recv_sem=rsem,
            device_id={"section": sec, "dp": dpi}, device_id_type=MESH,
        )

    def push(src, dst, ssem, rsem, sec, dpi):
        lax.cond(
            is_me(sec, dpi),
            lambda: pltpu.make_async_copy(src, dst, rsem).start(),
            lambda: far(src, dst, ssem, rsem, sec, dpi).start(),
        )

    def arrive(ref, sem):
        pltpu.make_async_copy(ref, ref, sem).wait()

    def drain(ref, sem, sec, dpi):
        @pl.when(jnp.logical_not(is_me(sec, dpi)))
        def _():
            arrive(ref, sem)

    def worker_of(p, j):
        return 2 * (core * B + p) + j // 2, pair + j % 2

    def peer(k):
        j = lax.rem(q + k, 4)
        return j, 2 * w + lax.div(j, 2), pair + lax.rem(j, 2)

    works_here = lax.div(w, B) == core

    def at(p, first=0, size=16):
        return pl.ds(pl.multiple_of(p * N + first, size), size)

    near = jnp.clip(w - core * B, 0, B - 1)

    barrier = pltpu.get_barrier_semaphore()
    for sec in range(S):
        for c in range(C):
            greeted = (c == pair) | (c == pair + 1) | (w == sec // 2)

            @pl.when(greeted & jnp.logical_not(is_me(sec, c)))
            def _():
                pl.semaphore_signal(
                    barrier, inc=1, device_id={"section": sec, "dp": c}, device_id_type=MESH
                )
    wall_msg[me_s] = we_own[...]
    wall_upd[me_s] = jnp.zeros(wall_upd.shape[1:], BF16)
    wall_upd[me_s, pl.ds(0, DE), pl.ds(0, DE)] = ws_own[...]
    wall_upd[me_s, pl.ds(0, DE), pl.ds(EP, DE)] = wo_own[...]
    bias = edge_b[pl.ds(1, 1), :]
    high = bias.astype(BF16).astype(F32)
    row = lax.broadcasted_iota(jnp.int32, (16, DE), 0)
    wall_upd[me_s, pl.ds(DE, 16), pl.ds(0, DE)] = jnp.where(
        row == 0, high, jnp.where(row == 1, bias - high, 0.0)
    ).astype(BF16)
    eb0[...] = jnp.zeros_like(eb0)
    eb0[:, pl.ds(0, DE)] = edge_b[pl.ds(0, 1), :]
    par[pl.ds(0, 1), :] = gains[0]
    par[pl.ds(1, 1), :] = shifts[0]
    par[pl.ds(2, 1), :] = node_b[0]
    par[pl.ds(3, 5), :] = jnp.zeros((5, D), F32)
    pl.semaphore_wait(barrier, 2 * S - 1 + 2 * (C - 2))

    def section_at(i):
        i = lax.rem(i + S, S)
        return jnp.where(i < S // 2, 2 * i, 2 * (S - i) - 1)

    place = jnp.where(lax.rem(me_s, 2) == 0, w, S - 1 - w)
    sides = ((section_at(place + 1), S // 2), (section_at(place - 1), S // 2 - 1))
    walls = (wall_msg, wall_upd)

    def half_of(which, layer, c):
        size = walls[which].shape[1] // 2
        return walls[which].at[layer, pl.ds(pl.multiple_of(c * size, size), size)]

    def ring_send(which, layer, side, hop):
        sec, reach = sides[side]
        if hop < reach:
            half = half_of(which, layer, core)
            far(half, half, ring_ss.at[which, side, hop], ring_rs.at[which, layer], sec, me_d).start()

    def ring_hop(which, side, hop):
        layer = section_at(place - hop if side == 0 else place + hop)
        half = half_of(which, layer, core)
        arrive(half, ring_rs.at[which, layer])
        ring_send(which, layer, side, hop)
        far(half, half, sib_ss.at[which, layer], sib_rs.at[which, layer], me_s, pair + 1 - core).start()

    hops = [(hop, side) for hop in range(1, S // 2 + 1) for side in range(2) if hop <= sides[side][1]]

    def ring_later(second):
        for hop, side in hops:
            early = (place > 0) & ((place >= hop) if side == 0 else (place + hop <= S))

            @pl.when(early != second)
            def _():
                ring_hop(1, side, hop)

    for side in range(2):
        ring_send(0, me_s, side, 0)

    ep[...] = jnp.zeros_like(ep)
    ep[:, pl.ds(0, DE)] = ends[:, pl.ds(0, DE)]
    ep[:, pl.ds(EP, DE)] = ends[...].astype(F32)[:, DE:].astype(BF16)

    arrays = ((edges_in, e0), (near_in, nb0))

    def quarter_of(n, j):
        rows = pl.ds(pl.multiple_of(j * Q, Q), Q)
        return edges_in.at[slot, :, rows] if n == 0 else near_in.at[slot, rows]

    @pl.when(works_here)
    def _():
        for n, (_, dst) in enumerate(arrays):
            pltpu.make_async_copy(quarter_of(n, q), dst, ld_sem.at[n]).start()
            other = q + 1 - 2 * core
            far(quarter_of(n, other), dst, ld_ss.at[n], ld_sem.at[n], me_s, pair + 1 - core).start()

    def edges_laid_out():
        for n, (_, dst) in enumerate(arrays):
            arrive(dst, ld_sem.at[n])
        nearest = nb0[...]
        lane = lax.broadcasted_iota(jnp.int32, (Q, EP), 1) - DE
        for k in range(K):
            rows = pl.ds(k * Q, Q)
            ecat[0, rows, :] = jnp.where(lane == nearest[:, k : k + 1], 1.0, 0.0).astype(BF16)
            ecat[0, rows, pl.ds(0, DE)] = e0[k]
        node = lax.broadcasted_iota(jnp.int32, (N, EP), 0)
        lane = lax.broadcasted_iota(jnp.int32, (N, EP), 1) - DE
        chosen = jnp.where(lane == node, 1.0, 0.0).astype(BF16)
        oht[...] = mm_bt(chosen, ecat[0]).astype(BF16)

        @pl.when(works_here)
        def _():
            for n, (_, dst) in enumerate(arrays):
                arrive(dst, ld_ss.at[n])

    before = lax.rem(me_s + S - 1, S)
    far(pw, pwn, nx_ss.at[0], nx_rs.at[0], before, me_d).start()
    far(par, parn, nx_ss.at[1], nx_rs.at[1], before, me_d).start()

    for p in range(B):
        rows = pl.ds(p * N, N)
        start[rows, :] = mix[0, p] * clean[rows, :].astype(F32) + mix[1, p] * noise[rows, :].astype(F32)

    def ring_drain():
        for which in range(2):
            for side in range(2):
                for hop in range(sides[side][1]):
                    arrive(half_of(which, me_s, core), ring_ss.at[which, side, hop])
            for layer in range(S):
                @pl.when(layer != me_s)
                def _():
                    arrive(half_of(which, layer, core), sib_ss.at[which, layer])

    def unpack_messages(t):
        @pl.when(t != me_s)
        def _():
            arrive(half_of(0, t, 1 - core), sib_rs.at[0, t])

        wcat[t, pl.ds(0, DE), :] = wall_msg[t]

    def unpack_updates(t):
        @pl.when(t != me_s)
        def _():
            arrive(half_of(1, t, 1 - core), sib_rs.at[1, t])

        scat[t, pl.ds(0, DE), :] = wall_upd[t, pl.ds(0, DE), pl.ds(0, EP)]
        wo[t, pl.ds(0, DE), :] = wall_upd[t, pl.ds(0, DE), pl.ds(EP, EP)]
        wo[t, pl.ds(DE, N), :] = jnp.zeros((N, EP), BF16)
        eb1[t] = wall_upd[t, pl.ds(DE, 16), pl.ds(0, EP)]

    def rows_out(p, src, dst, ssem, rsem):
        for j in range(4):
            sec, dpi = worker_of(p, j)
            push(src.at[at(p, j * Q, Q)], dst, ssem, rsem, sec, dpi)

    def rows_drain(src, ssem):
        lax.cond(
            works_here,
            lambda: arrive(src.at[pl.ds(0, B * N - Q)], ssem),
            lambda: arrive(src, ssem),
        )

    def spread(rows, half, ref, layer, ssem, rsem, rows_sem):
        arrive(rows, rows_sem)
        for k in range(1, 4):
            _, sec, dpi = peer(k)
            far(rows.at[:, pl.ds(half, half)], ref.at[layer, quarter(q)], ssem, rsem, sec, dpi).start()
        ref[layer, own_rows, :] = rows[:, pl.ds(0, half)]
        ref[layer, quarter(q), :] = rows[:, pl.ds(half, half)]

    def spread_wait(ref, layer, sem):
        arrive(ref.at[layer, pl.ds(DE, 3 * Q)], sem)

    def share(group, src, dst):
        for c in range(C):
            push(src, dst.at[me_d], g_ss.at[group, c], g_rs.at[group, me_d], me_s, c)

    def share_wait(group, src, dst):
        for c in range(C):
            arrive(dst.at[c], g_rs.at[group, c])
            drain(src, g_ss.at[group, c], me_s, c)

    def share_near(group, src, dst):
        for c in range(C):
            @pl.when((c == pair) | (c == pair + 1) | (core == c % 2))
            def _():
                push(src, dst(me_d), g_ss.at[group, c], g_rs.at[group, me_d], me_s, c)

    def share_relay(group, src, dst):
        for c in range(C):
            @pl.when((c != me_d) & (core == c % 2))
            def _():
                arrive(dst(c), g_rs.at[group, c])
                far(dst(c), dst(c), relay_ss.at[group - 2, c // 2], g_rs.at[group, c], me_s, pair + 1 - core).start()

    def share_near_wait(group, src, dst):
        for c in range(C):
            @pl.when((c == me_d) | (core != c % 2))
            def _():
                arrive(dst(c), g_rs.at[group, c])

            @pl.when((c != me_d) & ((c == pair) | (c == pair + 1) | (core == c % 2)))
            def _():
                arrive(src, g_ss.at[group, c])

            @pl.when((c != me_d) & (core == c % 2))
            def _():
                arrive(dst(c), relay_ss.at[group - 2, c // 2])

    steps = 4
    KC = K // steps
    RC = KC * Q

    def messages(t):
        own = wcat[t, own_rows, :].astype(F32)
        total = jnp.zeros((Q, D), F32)
        for i in range(steps):
            pre = mm(ecat[t, pl.ds(i * RC, RC), :], wcat[t, pl.ds(0, top), :])
            for k in range(KC):
                total = total + gelu(pre[k * Q : (k + 1) * Q] + own)
        mb_s[...] = (total * (1.0 / K)).astype(BF16)

    def edge_update(t):
        own = scat[t, own_rows, :].astype(F32)
        bias = eb1[t, pl.ds(0, 1), :].astype(F32) + eb1[t, pl.ds(1, 1), :].astype(F32)
        for i in range(steps):
            pe = mm(ecat[t, pl.ds(i * RC, RC), :], scat[t, pl.ds(0, top), :])
            act_e = stacked([gelu(pe[k * Q : (k + 1) * Q] + own).astype(BF16) for k in range(KC)])
            z = mm(act_e, wo[t])
            for k in range(KC):
                rows = pl.ds(i * RC + k * Q, Q)
                ecat[t + 1, rows, :] = (ecat[t, rows, :].astype(F32) + z[k * Q : (k + 1) * Q] + bias).astype(BF16)

    chunks = 4
    FC = FF // chunks

    def node_forward(step):
        @pl.when(step < S)
        def _():
            arrive(pwn, nx_rs.at[0])
            arrive(parn, nx_rs.at[1])
            arrive(pw, nx_ss.at[0])
            arrive(par, nx_ss.at[1])

        @pl.when(step == 0)
        def _():
            hi_s[...] = start[...]

        @pl.when(step > 0)
        def _():
            arrive(hin_r, hop_rs)
            first = jnp.where(me_s == 0, 1.0, 0.0)
            for i in range(0, BN, RB):
                rows = pl.ds(i, RB)
                hi_s[rows, :] = hin_r[rows, :].astype(F32) + first * start[rows, :]

        later = lax.rem(me_s + 1, S)

        def turn(n, carry):
            p = lax.rem(near + n, B)
            whole = at(p, 0, N)
            arrive(mb_r.at[whole], mb_rs.at[p])
            mean = mm(mb_r[whole, :], mo[...])
            for i in range(0, N, RB):
                rows = at(p, i)
                h1 = hi_s[rows, :] + mean[i : i + RB] + node_b[1]
                h1_s[rows, :] = h1
                unit, scale = normed(h1)
                un1[rows, :] = unit
                sc1[rows, :] = scale
                fwd[rows, pl.ds(2 * D, D)] = (unit * gains[1] + shifts[1]).astype(BF16)
                fwd[rows, pl.ds(D, D)] = mb_r[rows, :]
            a2 = fwd[whole, pl.ds(2 * D, D)]
            y = jnp.zeros((N, D), F32)
            for c in range(chunks):
                cols = pl.ds(c * FC, FC)
                u = mm(a2, fi[:, cols])
                v = []
                for i in range(0, N, RB):
                    block = u[i : i + RB] + fb[:, cols]
                    u_s[at(p, i), cols] = block
                    v.append(gelu(block).astype(BF16))
                y = y + mm(stacked(v), fo[cols, :])
            last = jnp.where(me_s == S - 1, 1.0, 0.0)
            for i in range(0, N, RB):
                rows = at(p, i)
                h2 = h1_s[rows, :] + y[i : i + RB] + node_b[2]
                rounded = h2.astype(BF16)
                hst[rows, :] = rounded
                unit, scale = normed(h2)
                un2[rows, :] = unit
                sc2[rows, :] = scale
                fwd[rows, pl.ds(3 * D, D)] = (unit * gains[2] + shifts[2]).astype(BF16)
                pair_norm(rows, rounded.astype(F32) + last * start[rows, :], parn)
            rq = mm(fwd[whole, pl.ds(3 * D, D)], ep[...])
            for i in range(0, N, RB):
                rows = at(p, i)
                rq_s[rows, pl.ds(0, EP)] = (rq[i : i + RB, :EP] + eb0[...]).astype(BF16)
                rq_s[rows, pl.ds(EP, EP)] = rq[i : i + RB, EP:].astype(BF16)
            pair_rows(p, pwn, parn)

            @pl.when(me_s < S - 1)
            def _():
                rows_out(p, rq_s, rq_r, rq_ss, rq_rs)

            @pl.when(step < 2 * S - 1)
            def _():
                rows_out(p, pq_s, pq_r, pq_ss, pq_rs)

            @pl.when((n == 0) & works_here)
            def _():
                pass_on(step)

            return carry

        lax.fori_loop(0, B, turn, 0)

        @pl.when(step < 2 * S - 1)
        def _():
            far(hst, hin_r, hop_ss, hop_rs, later, me_d).start()

        @pl.when(step >= S)
        def _():
            act[...] = hst[...]
            for i in range(0, BN, RB):
                rows = pl.ds(i, RB)
                unit, scale = normed(hi_s[rows, :])
                hi_s[rows, :] = unit
                sci[rows, :] = scale
                fwd[rows, pl.ds(0, D)] = (unit * gains[0] + shifts[0]).astype(BF16)
                for c in range(chunks):
                    cols = pl.ds(c * FC, FC)
                    slope_s[rows, cols] = gelu_both(u_s[rows, cols])[1].astype(BF16)
            share(0, fwd, g_fwd)

    def pair_norm(rows, hidden, first):
        unit, scale = normed(hidden)
        un0[rows, :] = unit
        sc0[rows, :] = scale
        a1_s[rows, :] = (unit * first[pl.ds(0, 1), :] + first[pl.ds(1, 1), :]).astype(BF16)

    def pair_rows(p, weight, first):
        whole = at(p, 0, N)
        for half in range(2):
            cols = pl.ds(half * D, D)
            value = mm(a1_s[whole, :], weight[:, cols])
            if half == 0:
                value = value + first[pl.ds(2, 1), :]
            pq_s[whole, cols] = value.astype(BF16)

    def pass_on(step):
        t = lax.rem(step, S)

        @pl.when(t < S - 1)
        def _():
            spread(rq_r, EP, scat, t, ag2_ss, ag2_rs, rq_rs)

        @pl.when(step < 2 * S - 1)
        def _():
            spread(pq_r, D, wcat, lax.rem(step + 1, S), ag_ss, ag_rs, pq_rs)

    def node_forward_drain():
        arrive(hst, hop_ss)
        rows_drain(pq_s, pq_ss)

        @pl.when(me_s < S - 1)
        def _():
            rows_drain(rq_s, rq_ss)

    @pl.when(me_s == 0)
    def _():
        for i in range(0, BN, RB):
            rows = pl.ds(i, RB)
            pair_norm(rows, start[rows, :], par)
        for p in range(B):
            pair_rows(p, pw, par)
            rows_out(p, pq_s, pq_r, pq_ss, pq_rs)

    def message_slope(t):
        own = wcat[t, own_rows, :].astype(F32)
        for i in range(steps):
            pre = mm(ecat[t, pl.ds(i * RC, RC), :], wcat[t, pl.ds(0, top), :])
            for k in range(KC):
                gp[t, pl.ds(i * RC + k * Q, Q), :] = gelu_both(pre[k * Q : (k + 1) * Q] + own)[1].astype(BF16)

    def edge_slope(t):
        own = scat[t, own_rows, :].astype(F32)
        values = []
        for i in range(steps):
            pe = mm(ecat[t, pl.ds(i * RC, RC), :], scat[t, pl.ds(0, top), :])
            for k in range(KC):
                value, slope = gelu_both(pe[k * Q : (k + 1) * Q] + own)
                values.append(value.astype(BF16))
                gpe[t, pl.ds(i * RC + k * Q, Q), :] = slope.astype(BF16)
        act_t[t] = stacked(values).T

    def prepare(t):
        message_slope(t)
        edge_t[t] = ecat[t].T

        @pl.when(t > 0)
        def _():
            edge_slope(t - 1)

    def forward_step(step, carry):
        t = lax.rem(step, S)

        @pl.when(step < S)
        def _():
            unpack_messages(t)

        spread_wait(wcat, t, ag_rs)
        messages(t)
        spread_wait(wcat, t, ag_ss)
        push(mb_s, mb_r.at[pl.ds(my_row, Q)], mb_ss, mb_rs.at[slot], t, owner_d)

        for second in range(2):
            @pl.when(step == second)
            def _():
                ring_later(second == 1)

        @pl.when((step == 0) & (me_s == 0))
        def _():
            rows_drain(pq_s, pq_ss)

        @pl.when((step > 0) & (me_s == lax.rem(step + S - 1, S)))
        def _():
            node_forward_drain()

        @pl.when(me_s == t)
        def _():
            node_forward(step)

        @pl.when((me_s != t) & (step >= S))
        def _():
            prepare(t)

        @pl.when(jnp.logical_not((me_s == t) & works_here))
        def _():
            pass_on(step)

        @pl.when(t < S - 1)
        def _():
            @pl.when(step < S)
            def _():
                unpack_updates(t)

            spread_wait(scat, t, ag2_rs)
            edge_update(t)
            spread_wait(scat, t, ag2_ss)

        drain(mb_s, mb_ss, t, owner_d)
        return carry

    for hop, side in hops:
        if (hop, side) == (2, 0):
            edges_laid_out()
        ring_hop(0, side, hop)
    for side in range(2):
        ring_send(1, me_s, side, 0)
    spread(pq_r, D, wcat, 0, ag_ss, ag_rs, pq_rs)
    lax.fori_loop(0, 2 * S, forward_step, 0)
    ring_drain()

    @pl.when(me_s != S - 1)
    def _():
        arrive(half_of(1, S - 1, 1 - core), sib_rs.at[1, S - 1])

    def edge_back(t):
        b2, n2 = lax.rem(t, 2), lax.rem(t + 1, 2)
        total = jnp.zeros((Q, EP), F32)
        for i in range(steps):
            chunk = pl.ds(i * RC, RC)
            carry = mm_bt(dcat[b2, chunk, pl.ds(0, D)], wcat[t, pl.ds(0, top), :])
            low = []
            for k in range(KC):
                rows = pl.ds(i * RC + k * Q, Q)
                low.append((dacc[rows, :] + carry[k * Q : (k + 1) * Q]).astype(BF16))
                de[n2, rows, :] = low[-1]
            dw = mm_bt(stacked(low), wo[t - 1])
            for k in range(KC):
                rows = pl.ds(i * RC + k * Q, Q)
                d = (gpe[t - 1, rows, :].astype(F32) * dw[k * Q : (k + 1) * Q]).astype(BF16)
                total = total + d.astype(F32)
                dcat[n2, rows, pl.ds(D, EP)] = d
        row_s[:, pl.ds(2 * D, EP)] = total.astype(BF16)
        x_s[:, pl.ds(D, EP)] = mm(oht[...], dcat[n2, :, pl.ds(D, EP)]).astype(BF16)

    def edge_pass(t):
        b3 = lax.rem(t, 2)
        for i in range(steps):
            rows = pl.ds(i * RC, RC)
            d = dcat[b3, rows, pl.ds(D, EP)]
            dacc[rows, :] = de[b3, rows, :].astype(F32) + mm_bt(d, scat[t, pl.ds(0, top), :])

    blocks = 2 * C
    my_block = lax.rem(me_s, 2) * C + me_d
    BW, HM, HU = msg_o.shape[2], msg_o.shape[1], upd_o.shape[1]

    def block_of(t, half, c, size):
        return eg.at[t, half, pl.ds(0, size), pl.ds(pl.multiple_of(c * BW, BW), BW)]

    def blocks_out(t, size):
        for k in range(blocks):
            @pl.when(k != my_block)
            def _():
                far(
                    block_of(t, k // C, k % C, size), eg_r.at[t, my_block, pl.ds(0, size)],
                    e1_ss.at[t, k], e1_rs.at[t, my_block], 2 * w + k // C, k % C,
                ).start()

    def edge_grads(t):
        grad = mm(edge_t[t, pl.ds(0, DE), :], dcat[lax.rem(t, 2), :, pl.ds(0, D)]).astype(BF16)
        for half in range(2):
            eg[t, half, pl.ds(0, HM), :] = grad[half * HM : (half + 1) * HM]

        @pl.when(t > 0)
        def _():
            n2 = lax.rem(t + 1, 2)
            edges = mm(edge_t[t - 1, pl.ds(0, DE), :], dcat[n2, :, pl.ds(D, EP)])
            outs = mm(act_t[t - 1, pl.ds(0, DE), :], de[n2])
            bias = jnp.sum(de[n2].astype(F32), axis=0, keepdims=True)
            grad = jnp.concatenate([edges, outs], axis=1).astype(BF16)
            eg[t, 0, pl.ds(HM, HU), :] = grad[:HU]
            eg[t, 1, pl.ds(HM, DE - HU), :] = grad[HU:]
            eg[t, 1, pl.ds(HM + DE - HU, 16), pl.ds(0, EP)] = jnp.broadcast_to(bias, (16, EP)).astype(BF16)
            eg[t, 1, pl.ds(HM + DE - HU, 16), pl.ds(EP, EP)] = jnp.zeros((16, EP), BF16)
            eg[t, 1, pl.ds(HM + DE - HU + 16, 2 * HU - DE - 16), :] = jnp.zeros((2 * HU - DE - 16, 2 * EP), BF16)
            blocks_out(t, HM + HU)

        @pl.when(t == 0)
        def _():
            blocks_out(t, HM)

    def blocks_sum(t, size):
        eg_r[t, my_block, pl.ds(0, size), :] = block_of(t, lax.rem(me_s, 2), me_d, size)[...]
        for k in range(blocks):
            @pl.when(k != my_block)
            def _():
                arrive(eg_r.at[t, k, pl.ds(0, size)], e1_rs.at[t, k])
                arrive(block_of(t, k // C, k % C, size), e1_ss.at[t, k])
        total = eg_r[t, 0, pl.ds(0, size), :].astype(F32)
        for k in range(1, blocks):
            total = total + eg_r[t, k, pl.ds(0, size), :].astype(F32)
        eg_b[t, pl.ds(0, size), :] = total.astype(BF16)
        push(eg_b.at[t, pl.ds(0, HM)], msg_o.at[me_s], e2_ss.at[0, t], e2_rs.at[0, me_s], t, me_d)
        if size > HM:
            push(eg_b.at[t, pl.ds(HM, HU)], upd_o.at[me_s], e2_ss.at[1, t], e2_rs.at[1, me_s], t - 1, me_d)

    def gather_blocks():
        for k in range(1, 4):
            j, sec, dpi = peer(k)
            rows = pl.ds(pl.multiple_of(j * Q, Q), Q)
            far(x_s.at[rows], x_r.at[q], x_ss, x_rs, sec, dpi).start()
        x_r[q] = x_s[pl.ds(pl.multiple_of(q * Q, Q), Q), :]

    def gather_wait():
        arrive(x_r.at[pl.ds(0, 3)], x_rs)
        arrive(x_s.at[pl.ds(0, 3 * Q)], x_ss)
        total = x_r[0].astype(F32)
        for j in range(1, 4):
            total = total + x_r[j].astype(F32)
        return total

    def message_back(t):
        b2 = lax.rem(t, 2)
        dm = dmb_r[...].astype(F32)
        total = jnp.zeros((Q, D), F32)
        for k in range(K):
            rows = pl.ds(k * Q, Q)
            d = (gp[t, rows, :].astype(F32) * dm).astype(BF16)
            total = total + d.astype(F32)
            dcat[b2, rows, pl.ds(0, D)] = d
        row_s[:, pl.ds(0, D)] = total.astype(BF16)
        x_s[:, pl.ds(0, D)] = mm(oht[...], dcat[b2, :, pl.ds(0, D)]).astype(BF16)

    def node_backward():
        @pl.when(me_s < S - 1)
        def _():
            arrive(dh1_r, dh_rs)

        def turn(n, carry):
            p = lax.rem(near + n, B)
            whole = at(p, 0, N)

            @pl.when(me_s < S - 1)
            def _():
                arrive(row_r.at[whole], row_rs.at[p])
                dn0 = mm_bt(row_r[whole, pl.ds(0, 2 * D)], pwn[...])
                dn3 = mm_bt(row_r[whole, pl.ds(2 * D, 2 * EP)], ep[...])
                for i in range(0, N, RB):
                    rows = at(p, i)
                    dn = dn3[i : i + RB]
                    dn3_s[rows, :] = dn
                    first = norm_back(dn0[i : i + RB], un0[rows, :], sc0[rows, :], parn[pl.ds(0, 1), :])
                    dh = (dh1_r[rows, :].astype(F32) + first).astype(BF16).astype(F32)
                    dh2_s[rows, :] = dh + norm_back(dn, un2[rows, :], sc2[rows, :], gains[2])

            @pl.when(me_s == S - 1)
            def _():
                dh2_s[whole, :] = cot[whole, :].astype(F32)

            dy = dh2_s[whole, :].astype(BF16)
            bwd[whole, pl.ds(D, D)] = dy
            da2 = jnp.zeros((N, D), F32)
            for c in range(chunks):
                cols = pl.ds(c * FC, FC)
                dv = mm_bt(dy, fo[cols, :])
                du = stacked(
                    [(slope_s[at(p, i), cols].astype(F32) * dv[i : i + RB]).astype(BF16) for i in range(0, N, RB)]
                )
                da2 = da2 + mm_bt(du, fi[:, cols])
            for i in range(0, N, RB):
                rows = at(p, i)
                block = da2[i : i + RB]
                da2_s[rows, :] = block
                dh1 = dh2_s[rows, :] + norm_back(block, un1[rows, :], sc1[rows, :], gains[1])
                dh1_f[rows, :] = dh1
                bwd[rows, pl.ds(0, D)] = (dh1 * (1.0 / K)).astype(BF16)
            dmb_s[whole, :] = mm_bt(bwd[whole, pl.ds(0, D)], mo[...]).astype(BF16)
            rows_out(p, dmb_s, dmb_r, dmb_ss, dmb_rs)
            return carry

        lax.fori_loop(0, B, turn, 0)

        @pl.when(me_s > 0)
        def _():
            dh1_s[...] = dh1_f[...].astype(BF16)
            far(dh1_s, dh1_r, dh_ss, dh_rs, me_s - 1, me_d).start()

        @pl.when(me_s < S - 1)
        def _():
            far(row_r.at[:, pl.ds(0, 2 * D)], dpqo_r, fw_ss, dpqo_rs, me_s + 1, me_d).start()
            drs = row_r[:, pl.ds(2 * D, 2 * EP)]
            bwd[:, pl.ds(2 * D, 2 * EP)] = drs
            dn = dn3_s[...]
            sg[pl.ds(11, 1), :] = col_sum(dn * un2[...])
            sg[pl.ds(12, 1), :] = col_sum(dn)
            sg[pl.ds(16, 1), pl.ds(0, EP)] = col_sum(drs[:, :EP].astype(F32))

        @pl.when(me_s == S - 1)
        def _():
            bwd[:, pl.ds(2 * D, 2 * EP)] = jnp.zeros((B * N, 2 * EP), BF16)
            sg[pl.ds(11, 1), :] = jnp.zeros((1, D), F32)
            sg[pl.ds(12, 1), :] = jnp.zeros((1, D), F32)
            sg[pl.ds(16, 1), pl.ds(0, EP)] = jnp.zeros((1, EP), F32)

        share(1, bwd, g_bwd)
        sg[pl.ds(13, 1), :] = col_sum(dh2_s[...])
        sg[pl.ds(8, 1), :] = col_sum(da2_s[...] * un1[...])
        sg[pl.ds(9, 1), :] = col_sum(da2_s[...])
        sg[pl.ds(10, 1), :] = col_sum(dh1_f[...])

    def node_backward_drain():
        rows_drain(dmb_s, dmb_ss)

        @pl.when(me_s > 0)
        def _():
            arrive(dh1_s, dh_ss)

        @pl.when(me_s < S - 1)
        def _():
            arrive(row_r.at[:, pl.ds(0, 2 * D)], fw_ss)

    dacc[...] = jnp.zeros_like(dacc)

    def backward_step(step, carry):
        t = S - 1 - step

        @pl.when(me_s == t)
        def _():
            node_backward()

        @pl.when(((t == S - 1) & (me_s >= S - 2)) | (me_s == t - 2))
        def _():
            prepare(me_s)

        @pl.when(t < S - 1)
        def _():
            edge_pass(t)

        @pl.when(t + 2 < S)
        def _():
            blocks_sum(t + 2, HM + HU)

        @pl.when(t == 0)
        def _():
            blocks_sum(1, HM + HU)

        arrive(dmb_r, dmb_rs)
        message_back(t)

        @pl.when(t > 0)
        def _():
            edge_back(t)

        @pl.when(t == 0)
        def _():
            x_s[:, pl.ds(D, EP)] = jnp.zeros((N, EP), BF16)

        gather_blocks()
        other = gather_wait().astype(BF16)
        row_s[:, pl.ds(D, D)] = other[:, :D]
        row_s[:, pl.ds(2 * D + EP, EP)] = other[:, D:]
        dpq = row_s.at[:, pl.ds(0, 2 * D)]

        @pl.when(t > 0)
        def _():
            push(row_s, row_r.at[pl.ds(my_row, Q)], row_ss, row_rs.at[slot], t - 1, owner_d)

        @pl.when(t == 0)
        def _():
            push(dpq, dpqo_r.at[pl.ds(my_row, Q)], row_ss, dpqo_rs, t, owner_d)

        edge_grads(t)

        @pl.when(t > 0)
        def _():
            drain(row_s, row_ss, t - 1, owner_d)

        @pl.when(t == 0)
        def _():
            drain(dpq, row_ss, t, owner_d)

        @pl.when(me_s == t)
        def _():
            node_backward_drain()

        return carry

    lax.fori_loop(0, S, backward_step, 0)

    arrive(dpqo_r, dpqo_rs)
    across = [pl.ds(p * N, N) for p in range(B)]
    for p in range(B):
        share_near(2 + p, dpqo_r.at[across[p]], lambda c, p=p: g_dpq.at[c, across[p]])
    dpq = dpqo_r[...]
    sg[pl.ds(2, 1), :] = col_sum(dpq[:, :D].astype(F32))
    dn = mm_bt(dpq, pw[...])
    unit = hi_s[...]
    sg[pl.ds(0, 1), :] = col_sum(dn * unit)
    sg[pl.ds(1, 1), :] = col_sum(dn)
    share(2 + B, sg, g_small)
    ig[...] = (dh1_f[...] + norm_back(dn, unit, sci[...], gains[0])).astype(BF16)
    blocks_sum(0, HM)
    for p in range(B):
        share_relay(2 + p, dpqo_r.at[across[p]], lambda c, p=p: g_dpq.at[c, across[p]])
    def combine(kind, src, final):
        for sec in range(S):
            arrive(src.at[sec], e2_rs.at[kind, sec])
        for half in range(2):
            total = src[half].astype(F32)
            for sec in range(half + 2, S, 2):
                total = total + src[sec].astype(F32)
            final[half] = total.astype(BF16)

    @pl.when(me_s < S - 1)
    def _():
        combine(1, upd_o, upd_f)

    @pl.when(me_s == S - 1)
    def _():
        upd_f[...] = jnp.zeros_like(upd_f)

    share(4 + B, upd_f, g_upd)
    combine(0, msg_o, msg_f)
    share(3 + B, msg_f, g_msg)
    for t in range(S):
        drain(eg_b.at[t, pl.ds(0, HM)], e2_ss.at[0, t], t, me_d)
        if t > 0:
            drain(eg_b.at[t, pl.ds(HM, HU)], e2_ss.at[1, t], t - 1, me_d)
    share_wait(0, fwd, g_fwd)
    share_wait(1, bwd, g_bwd)
    for p in range(B):
        share_near_wait(2 + p, dpqo_r.at[across[p]], lambda c, p=p: g_dpq.at[c, across[p]])
    share_wait(2 + B, sg, g_small)
    share_wait(3 + B, msg_f, g_msg)
    share_wait(4 + B, upd_f, g_upd)


def run_relay(dims, operands):
    S, B, N, K, Q, D, DE, EP, FF, C = dims
    R = K * Q
    BN = B * N
    tall = DE + N + Q
    vm = pl.BlockSpec(memory_space=pltpu.VMEM)
    hbm = pl.BlockSpec(memory_space=pl.ANY)
    dma = pltpu.SemaphoreType.DMA
    sds = jax.ShapeDtypeStruct
    BW = D // C
    tile = 32
    held = -(-(DE + 16) // tile) * tile
    scratch = [
        pltpu.VMEM((D, 2 * EP), BF16),
        pltpu.VMEM((K, Q, DE), BF16),
        pltpu.VMEM((Q, K), jnp.int32),
        pltpu.VMEM((N, R), BF16),
        pltpu.VMEM((BN, D), F32),
        pltpu.VMEM((8, D), F32),
        pltpu.VMEM((1, EP), F32),
        pltpu.VMEM((S, DE, D), BF16),
        pltpu.VMEM((S, held, 2 * EP), BF16),
        pltpu.VMEM((BN, 4 * D), BF16),
        pltpu.VMEM((BN, 2 * D + 2 * EP), BF16),
        pltpu.VMEM((24, D), F32),
        pltpu.VMEM((S, 2, (DE + held) // 2, D), BF16),
        pltpu.VMEM((S, 2 * C, (DE + held) // 2, BW), BF16),
        pltpu.VMEM((S, (DE + held) // 2, BW), BF16),
        pltpu.VMEM((S, DE // 2, BW), BF16),
        pltpu.VMEM((2, DE // 2, BW), BF16),
        pltpu.VMEM((S, held // 2, BW), BF16),
        pltpu.VMEM((2, held // 2, BW), BF16),
        pltpu.VMEM((S, EP, EP), BF16),
        pltpu.VMEM((S, 16, EP), BF16),
        pltpu.VMEM((S, R, EP), BF16),
        pltpu.VMEM((S, tall, D), BF16),
        pltpu.VMEM((S, tall, EP), BF16),
        pltpu.VMEM((D, 2 * D), BF16),
        pltpu.VMEM((8, D), F32),
        pltpu.VMEM((BN, D), BF16),
        pltpu.VMEM((BN, D), BF16),
        pltpu.VMEM((Q, D), BF16),
        pltpu.VMEM((BN, D), BF16),
        pltpu.VMEM((BN, 2 * D), BF16),
        pltpu.VMEM((Q, 2 * D), BF16),
        pltpu.VMEM((BN, 2 * EP), BF16),
        pltpu.VMEM((Q, 2 * EP), BF16),
        pltpu.VMEM((BN, D), F32),
        pltpu.VMEM((BN, D), F32),
        pltpu.VMEM((BN, D), F32),
        pltpu.VMEM((BN, D), F32),
        pltpu.VMEM((BN, 1), F32),
        pltpu.VMEM((BN, 1), F32),
        pltpu.VMEM((BN, 1), F32),
        pltpu.VMEM((BN, 1), F32),
        pltpu.VMEM((BN, FF), F32),
        pltpu.VMEM((BN, FF), BF16),
        pltpu.VMEM((2, R, EP), BF16),
        pltpu.VMEM((R, EP), F32),
        pltpu.VMEM((S, R, D), BF16),
        pltpu.VMEM((S, R, EP), BF16),
        pltpu.VMEM((2, R, D + EP), BF16),
        pltpu.VMEM((S, EP, R), BF16),
        pltpu.VMEM((S, EP, R), BF16),
        pltpu.VMEM((N, D + EP), BF16),
        pltpu.VMEM((4, Q, D + EP), BF16),
        pltpu.VMEM((Q, 2 * D + 2 * EP), BF16),
        pltpu.VMEM((BN, 2 * D + 2 * EP), BF16),
        pltpu.VMEM((BN, 2 * D), BF16),
        pltpu.VMEM((BN, D), BF16),
        pltpu.VMEM((Q, D), BF16),
        pltpu.VMEM((BN, D), BF16),
        pltpu.VMEM((BN, D), BF16),
        pltpu.VMEM((BN, D), F32),
        pltpu.VMEM((BN, D), F32),
        pltpu.VMEM((BN, D), F32),
        pltpu.VMEM((BN, D), F32),
        pltpu.VMEM((BN, D), F32),
        pltpu.VMEM((BN, D), BF16),
        dma((2,)), dma((2,)), dma((2,)), dma((2,)), dma, dma,
        dma, dma, dma, dma, dma, dma, dma, dma,
        dma, dma((B,)), dma, dma, dma, dma((B,)), dma,
        dma, dma, dma, dma, dma,
        dma((S, 2 * C)), dma((S, 2 * C)), dma((2, S)), dma((2, S)), dma((5 + B, C)), dma((5 + B, C)),
        dma((B, C // 2)), dma((2, 2, S // 2)), dma((2, S)), dma((2, S)), dma((2, S)),
    ]
    return pl.pallas_call(
        functools.partial(relay_kernel, dims),
        out_shape=(
            sds((BN, D), BF16),
            sds((BN, D), BF16),
            sds((C, BN, 4 * D), BF16),
            sds((C, BN, 2 * D + 2 * EP), BF16),
            sds((C, BN, 2 * D), BF16),
            sds((C, 24, D), F32),
            sds((C, 2, DE // 2, BW), BF16),
            sds((C, 2, held // 2, BW), BF16),
        ),
        in_specs=[hbm, hbm, pl.BlockSpec(memory_space=pltpu.SMEM)] + [vm] * 16,
        out_specs=(vm,) * 2 + (hbm,) * 6,
        scratch_shapes=scratch,
        compiler_params=pltpu.CompilerParams(
            collective_id=0, has_side_effects=True, vmem_limit_bytes=62 * 1024 * 1024
        ),
    )(*operands)


def gradient_kernel(
    dims,
    fwd, bwd, dpq, small, edge, upd, fi, fo, fb, act, ig,
    g_pair, g_edge, g_out, g_fi, g_fo, g_ep, g_self, g_eout, g_gain, g_shift, g_nb, g_fb, g_eb, act_out, ig_out,
    fwd_v, bwd_v, dpq_v, fi_v, fo_v, gfi_v, gfo_v, pair_v, out_v, edge_v, upd_v, in_sems, sems,
):
    S, B, N, K, Q, D, DE, EP, FF, C = dims
    chunks = 4
    FC = FF // chunks

    def part(c, size=D):
        return pl.ds(c * size, size)

    loads = {}

    def load(name, src, dst):
        loads[name] = pltpu.make_async_copy(src, dst, in_sems.at[len(loads)])
        loads[name].start()

    load("a2", fwd.at[:, part(2)], fwd_v.at[2])
    load("dy", bwd.at[:, part(1)], bwd_v.at[1])
    for c in range(chunks):
        load(("fi", c), fi.at[:, part(c, FC)], fi_v.at[c])
        load(("fo", c), fo.at[part(c, FC)], fo_v.at[c])
    load("a1", fwd.at[:, part(0)], fwd_v.at[0])
    load("dpq0", dpq.at[:, part(0)], dpq_v.at[0])
    load("dpq1", dpq.at[:, part(1)], dpq_v.at[1])
    load("mbar", fwd.at[:, part(1)], fwd_v.at[1])
    load("dmsg", bwd.at[:, part(0)], bwd_v.at[0])
    load("a3", fwd.at[:, part(3)], fwd_v.at[3])
    load("drs", bwd.at[:, part(2)], bwd_v.at[2])
    load("edge", edge, edge_v)
    load("upd", upd, upd_v)
    stores = []

    def out(src, dst):
        copy = pltpu.make_async_copy(src, dst, sems.at[len(stores)])
        copy.start()
        stores.append(copy)

    out(act, act_out)
    out(ig, ig_out)
    loads["a2"].wait()
    loads["dy"].wait()
    a2 = fwd_v[2]
    dy = bwd_v[1]
    for c in range(chunks):
        cols = part(c, FC)
        loads["fi", c].wait()
        loads["fo", c].wait()
        value, slope = gelu_both(mm(a2, fi_v[c]) + fb[:, cols])
        du = (slope * mm_bt(dy, fo_v[c])).astype(BF16)
        g_fb[:, cols] = col_sum(du.astype(F32))
        gfi_v[c] = mm_at(a2, du)
        out(gfi_v.at[c], g_fi.at[0, :, cols])
        gfo_v[c] = mm_at(value.astype(BF16), dy)
        out(gfo_v.at[c], g_fo.at[0, cols])
    loads["a1"].wait()
    for c in range(2):
        loads["dpq%d" % c].wait()
        pair_v[c] = mm_at(fwd_v[0], dpq_v[c])
        out(pair_v.at[c], g_pair.at[0, :, part(c)])
    loads["mbar"].wait()
    loads["dmsg"].wait()
    out_v[...] = mm_at(fwd_v[1], bwd_v[0]) * float(K)
    out(out_v, g_out.at[0])
    loads["a3"].wait()
    loads["drs"].wait()
    ends = mm_at(fwd_v[3], bwd_v[2])
    g_ep[0] = jnp.concatenate([ends[:, :DE], ends[:, EP : EP + DE]], axis=1)
    total = small[0]
    for c in range(1, C):
        total = total + small[c]
    for i, rows in enumerate(((0, 1, 2), (8, 9, 10), (11, 12, 13))):
        g_gain[i] = total[rows[0] : rows[0] + 1]
        g_shift[i] = total[rows[1] : rows[1] + 1]
        g_nb[i] = total[rows[2] : rows[2] + 1]
    g_eb[0, pl.ds(0, 1), :] = total[16:17, :DE]
    loads["edge"].wait()
    loads["upd"].wait()
    BW = edge_v.shape[3]
    for c in range(C):
        for half in range(2):
            block = edge_v[c, half].astype(F32)
            g_edge[0, pl.ds(half * (DE // 2), DE // 2), pl.ds(c * BW, BW)] = block
        block = stacked([upd_v[c, 0], upd_v[c, 1]]).astype(F32)
        first = c * BW
        for array, begin in ((g_self, 0), (g_eout, EP)):
            low, high = max(first, begin), min(first + BW, begin + DE)
            if low < high:
                array[0, :, pl.ds(low - begin, high - low)] = block[:DE, low - first : high - first]
        low, high = first, min(first + BW, DE)
        if low < high:
            g_eb[0, pl.ds(1, 1), pl.ds(low, high - low)] = block[DE : DE + 1, low - first : high - first]
    for copy in stores:
        copy.wait()


def run_gradients(dims, operands):
    S, B, N, K, Q, D, DE, EP, FF, C = dims
    rows = C * B * N
    BW = D // C
    held = operands[5].shape[2]
    vm = pl.BlockSpec(memory_space=pltpu.VMEM)
    hbm = pl.BlockSpec(memory_space=pl.ANY)
    sds = jax.ShapeDtypeStruct
    shapes = (
        (1, D, 2 * D), (1, DE, D), (1, D, D), (1, D, FF), (1, FF, D), (1, D, 2 * DE), (1, DE, DE), (1, DE, DE),
        (3, 1, D), (3, 1, D), (3, 1, D), (1, FF), (1, 2, DE),
    )
    return pl.pallas_call(
        functools.partial(gradient_kernel, dims),
        out_shape=tuple(sds(shape, F32) for shape in shapes) + (sds((1, B, N, D), BF16),) * 2,
        in_specs=[hbm, hbm, hbm, vm, hbm, hbm, hbm, hbm, vm, hbm, hbm],
        out_specs=(hbm, vm, hbm, hbm, hbm) + (vm,) * 8 + (hbm,) * 2,
        scratch_shapes=[
            pltpu.VMEM((4, rows, D), BF16),
            pltpu.VMEM((3, rows, D), BF16),
            pltpu.VMEM((2, rows, D), BF16),
            pltpu.VMEM((4, D, FF // 4), BF16),
            pltpu.VMEM((4, FF // 4, D), BF16),
            pltpu.VMEM((4, D, FF // 4), F32),
            pltpu.VMEM((4, FF // 4, D), F32),
            pltpu.VMEM((2, D, D), F32),
            pltpu.VMEM((D, D), F32),
            pltpu.VMEM((C, 2, DE // 2, BW), BF16),
            pltpu.VMEM((C, 2, held, BW), BF16),
            pltpu.SemaphoreType.DMA((19,)),
            pltpu.SemaphoreType.DMA((13,)),
        ],
        compiler_params=pltpu.CompilerParams(vmem_limit_bytes=56 * 1024 * 1024),
    )(*operands)


def stationary(
    clean_nodes, noise_nodes, edge_feats, neighbours, time_bins, cotangent,
    pair_weight, message_edge, message_out, ffn_in, ffn_out, edge_pair, edge_self, edge_out,
    norm_gain, norm_shift, node_bias, ffn_bias, edge_bias,
):
    S = lax.axis_size("section")
    B, N, D = clean_nodes.shape
    K, DE = edge_feats.shape[2:]
    FF = ffn_in.shape[2]
    Q = N // 4
    EP = DE + N
    phase = (time_bins.astype(F32) + 0.5) * (math.pi * 0.5 / TBINS)
    mix = jnp.cos(phase[None] - jnp.array([[0.0], [math.pi * 0.5]], F32))

    def by_rows(array):
        return jnp.transpose(array, (1, 0, 2))

    C = lax.axis_size("dp")
    dims = (S, B, N, K, Q, D, DE, EP, FF, C)
    act, ig, g_fwd, g_bwd, g_dpq, g_small, g_msg, g_upd = run_relay(
        dims,
        (
            jnp.transpose(edge_feats, (0, 2, 1, 3)), neighbours, mix, clean_nodes.reshape(B * N, D), noise_nodes.reshape(B * N, D),
            cotangent.reshape(B * N, D), pair_weight[0], message_out[0], ffn_in[0], ffn_out[0], edge_pair[0],
            by_rows(norm_gain), by_rows(norm_shift), by_rows(node_bias), ffn_bias, edge_bias[0],
            message_edge[0], edge_self[0], edge_out[0],
        ),
    )
    grads = run_gradients(
        dims,
        (
            g_fwd.reshape(C * B * N, -1), g_bwd.reshape(C * B * N, -1), g_dpq.reshape(C * B * N, -1),
            g_small, g_msg, g_upd, ffn_in[0], ffn_out[0], ffn_bias, act.reshape(1, B, N, D), ig.reshape(1, B, N, D),
        ),
    )
    grads, outs = list(grads[:-2]), tuple(grads[-2:])
    grads[8:11] = [by_rows(array) for array in grads[8:11]]
    return outs + tuple(grads)


def solution(mesh):
    sections, copies = mesh.shape["section"], mesh.shape["dp"]

    def body(*args):
        B, N = args[0].shape[:2]
        fits = sections == 4 * B and copies % 2 == 0 and N % 64 == 0
        return stationary(*args) if fits else on_device(*args)

    placed = (
        P("dp", None, None),
        P("dp", None, None),
        P("dp", None, None, None),
        P("dp", None, None),
        P("dp"),
        P("dp", None, None),
        P("section", None, None),
        P("section", None, None),
        P("section", None, None),
        P("section", None, None),
        P("section", None, None),
        P("section", None, None),
        P("section", None, None),
        P("section", None, None),
        P("section", None, None),
        P("section", None, None),
        P("section", None, None),
        P("section", None),
        P("section", None, None),
    )
    return jax.shard_map(
        body,
        mesh=mesh,
        in_specs=placed,
        out_specs=(
            P("section", "dp", None, None),
            P("section", "dp", None, None),
            P("section", None, None),
            P("section", None, None),
            P("section", None, None),
            P("section", None, None),
            P("section", None, None),
            P("section", None, None),
            P("section", None, None),
            P("section", None, None),
            P("section", None, None),
            P("section", None, None),
            P("section", None, None),
            P("section", None),
            P("section", None, None),
        ),
        check_vma=False,
    )
```

```python
import functools
import math

import jax
import jax.numpy as jnp
from jax import lax
from jax.experimental import pallas as pl
from jax.experimental.pallas import tpu as pltpu
from jax.sharding import PartitionSpec as P

TBINS = 100


def from_behind(block, axis, distance):
    devices = range(lax.axis_size(axis))
    route = [(i - distance, i) for i in devices if i - distance in devices]
    return lax.ppermute(block, axis, route)


def for_sending(value):
    return jax.tree.map(lambda a: a.astype(jnp.bfloat16) if a.dtype == jnp.float32 else a, value)


def layer_norm(value, gain, shift):
    centre = jnp.mean(value, axis=-1, keepdims=True)
    centred = value - centre
    spread = jnp.mean(centred * centred, axis=-1, keepdims=True)
    return centred * lax.rsqrt(spread + 1e-05) * gain + shift


def forward_layer(weights, hidden, edge_state, nearest):
    (
        pair_w,
        msg_edge,
        msg_out,
        ffn_w_in,
        ffn_w_out,
        edge_pair_w,
        edge_self_w,
        edge_out_w,
        gains,
        shifts,
        node_b,
        ffn_b,
        edge_b,
    ) = weights
    width = msg_out.shape[0]
    edge_width = edge_self_w.shape[0]
    normed_one = layer_norm(hidden, gains[0], shifts[0]).astype(jnp.bfloat16)
    pair_out = jnp.dot(normed_one, pair_w, preferred_element_type=jnp.float32)
    before_act = (
        pair_out[:, None, :width]
        + jnp.take(pair_out[:, width:], nearest, axis=0)
        + jnp.einsum("nkc,cd->nkd", edge_state, msg_edge, preferred_element_type=jnp.float32)
        + node_b[0]
    )
    message_act = jax.nn.gelu(before_act).astype(jnp.bfloat16)
    message_all = jnp.einsum(
        "nkc,cd->nkd", message_act, msg_out, preferred_element_type=jnp.float32
    )
    after_msg = hidden + jnp.mean(message_all, axis=1) + node_b[1]
    normed_two = layer_norm(after_msg, gains[1], shifts[1]).astype(jnp.bfloat16)
    ffn_pre = jnp.dot(normed_two, ffn_w_in, preferred_element_type=jnp.float32) + ffn_b
    ffn_act = jax.nn.gelu(ffn_pre).astype(jnp.bfloat16)
    after_ffn = (
        after_msg + jnp.dot(ffn_act, ffn_w_out, preferred_element_type=jnp.float32) + node_b[2]
    )
    normed_three = layer_norm(after_ffn, gains[2], shifts[2]).astype(jnp.bfloat16)
    edge_pairs = jnp.dot(normed_three, edge_pair_w, preferred_element_type=jnp.float32)
    edge_pre = (
        edge_pairs[:, None, :edge_width]
        + jnp.take(edge_pairs[:, edge_width:], nearest, axis=0)
        + jnp.einsum("nkc,cd->nkd", edge_state, edge_self_w, preferred_element_type=jnp.float32)
        + edge_b[0]
    )
    edge_act = jax.nn.gelu(edge_pre).astype(jnp.bfloat16)
    edge_next = (
        edge_state.astype(jnp.float32)
        + jnp.einsum("nkc,cd->nkd", edge_act, edge_out_w, preferred_element_type=jnp.float32)
        + edge_b[1]
    )
    saved = (
        normed_one,
        before_act,
        message_act,
        after_msg,
        normed_two,
        ffn_pre,
        ffn_act,
        after_ffn,
        normed_three,
        edge_pre,
        edge_act,
    )
    return (after_ffn, edge_next, saved)


def backward_layer(weights, hidden, edge_state, nearest, grad_nodes_out, grad_edges_out):
    (
        pair_w,
        msg_edge,
        msg_out,
        ffn_w_in,
        ffn_w_out,
        edge_pair_w,
        edge_self_w,
        edge_out_w,
        gains,
        shifts,
        node_b,
        ffn_b,
        edge_b,
    ) = weights
    unused_nodes, unused_edges, saved = forward_layer(weights, hidden, edge_state, nearest)
    (
        normed_one,
        before_act,
        message_act,
        after_msg,
        normed_two,
        ffn_pre,
        ffn_act,
        after_ffn,
        normed_three,
        edge_pre,
        edge_act,
    ) = saved
    width = msg_out.shape[0]
    edge_width = edge_self_w.shape[0]
    count = nearest.shape[1]
    node_count = hidden.shape[0]
    one_hot = (
        nearest.reshape(-1)[None, :] == jnp.arange(node_count, dtype=jnp.int32)[:, None]
    ).astype(jnp.bfloat16)
    edge_grad_low = grad_edges_out.astype(jnp.bfloat16)
    grad_edge_b1 = jnp.sum(grad_edges_out, axis=(0, 1))
    grad_edge_out_w = jnp.einsum(
        "nkc,nkd->cd", edge_act, edge_grad_low, preferred_element_type=jnp.float32
    )
    edge_act_grad = jnp.einsum(
        "nkd,cd->nkc", edge_grad_low, edge_out_w, preferred_element_type=jnp.float32
    )
    unused_value, gelu_edge = jax.vjp(jax.nn.gelu, edge_pre)
    edge_pre_grad = gelu_edge(edge_act_grad)[0].astype(jnp.bfloat16)
    grad_edge_b0 = jnp.sum(edge_pre_grad, axis=(0, 1), dtype=jnp.float32)
    grad_edge_self_w = jnp.einsum(
        "nkc,nkd->cd", edge_state, edge_pre_grad, preferred_element_type=jnp.float32
    )
    edge_total = grad_edges_out + jnp.einsum(
        "nkd,cd->nkc", edge_pre_grad, edge_self_w, preferred_element_type=jnp.float32
    )
    own_edge = jnp.sum(edge_pre_grad, axis=1, dtype=jnp.float32)
    other_edge = jnp.dot(
        one_hot, edge_pre_grad.reshape(-1, edge_width), preferred_element_type=jnp.float32
    )
    pairs_grad = jnp.concatenate([own_edge, other_edge], axis=-1).astype(jnp.bfloat16)
    grad_edge_pair_w = jnp.einsum(
        "nc,nd->cd", normed_three, pairs_grad, preferred_element_type=jnp.float32
    )
    normed_three_grad = jnp.einsum(
        "nd,cd->nc", pairs_grad, edge_pair_w, preferred_element_type=jnp.float32
    )
    unused_value, norm_three_back = jax.vjp(layer_norm, after_ffn, gains[2], shifts[2])
    ffn_side, gain_three, shift_three = norm_three_back(normed_three_grad)
    after_ffn_grad = grad_nodes_out + ffn_side
    grad_node_b2 = jnp.sum(after_ffn_grad, axis=0)
    ffn_out_grad = after_ffn_grad.astype(jnp.bfloat16)
    grad_ffn_w_out = jnp.einsum(
        "nc,nd->cd", ffn_act, ffn_out_grad, preferred_element_type=jnp.float32
    )
    ffn_act_grad = jnp.einsum(
        "nd,cd->nc", ffn_out_grad, ffn_w_out, preferred_element_type=jnp.float32
    )
    unused_value, gelu_ffn = jax.vjp(jax.nn.gelu, ffn_pre)
    ffn_pre_grad = gelu_ffn(ffn_act_grad)[0].astype(jnp.bfloat16)
    grad_ffn_b = jnp.sum(ffn_pre_grad, axis=0, dtype=jnp.float32)
    grad_ffn_w_in = jnp.einsum(
        "nc,nd->cd", normed_two, ffn_pre_grad, preferred_element_type=jnp.float32
    )
    normed_two_grad = jnp.einsum(
        "nd,cd->nc", ffn_pre_grad, ffn_w_in, preferred_element_type=jnp.float32
    )
    unused_value, norm_two_back = jax.vjp(layer_norm, after_msg, gains[1], shifts[1])
    msg_side, gain_two, shift_two = norm_two_back(normed_two_grad)
    after_msg_grad = after_ffn_grad + msg_side
    grad_node_b1 = jnp.sum(after_msg_grad, axis=0)
    message_grad = (after_msg_grad / count).astype(jnp.bfloat16)
    grad_msg_out = jnp.einsum(
        "nkc,nd->cd", message_act, message_grad, preferred_element_type=jnp.float32
    )
    message_act_grad = jnp.einsum(
        "nd,cd->nc", message_grad, msg_out, preferred_element_type=jnp.float32
    )
    unused_value, gelu_msg = jax.vjp(jax.nn.gelu, before_act)
    before_grad = gelu_msg(jnp.broadcast_to(message_act_grad[:, None, :], before_act.shape))[
        0
    ].astype(jnp.bfloat16)
    grad_node_b0 = jnp.sum(before_grad, axis=(0, 1), dtype=jnp.float32)
    grad_msg_edge = jnp.einsum(
        "nkc,nkd->cd", edge_state, before_grad, preferred_element_type=jnp.float32
    )
    edge_total = edge_total + jnp.einsum(
        "nkd,cd->nkc", before_grad, msg_edge, preferred_element_type=jnp.float32
    )
    own_node = jnp.sum(before_grad, axis=1, dtype=jnp.float32)
    other_node = jnp.dot(
        one_hot, before_grad.reshape(-1, width), preferred_element_type=jnp.float32
    )
    pair_grad = jnp.concatenate([own_node, other_node], axis=-1).astype(jnp.bfloat16)
    grad_pair_w = jnp.einsum("nc,nd->cd", normed_one, pair_grad, preferred_element_type=jnp.float32)
    normed_one_grad = jnp.einsum("nd,cd->nc", pair_grad, pair_w, preferred_element_type=jnp.float32)
    unused_value, norm_one_back = jax.vjp(layer_norm, hidden, gains[0], shifts[0])
    input_side, gain_one, shift_one = norm_one_back(normed_one_grad)
    hidden_grad = after_msg_grad + input_side
    grads = (
        grad_pair_w,
        grad_msg_edge,
        grad_msg_out,
        grad_ffn_w_in,
        grad_ffn_w_out,
        grad_edge_pair_w,
        grad_edge_self_w,
        grad_edge_out_w,
        jnp.stack([gain_one, gain_two, gain_three]),
        jnp.stack([shift_one, shift_two, shift_three]),
        jnp.stack([grad_node_b0, grad_node_b1, grad_node_b2]),
        grad_ffn_b,
        jnp.stack([grad_edge_b0, grad_edge_b1]),
    )
    return (hidden_grad.astype(jnp.bfloat16), edge_total.astype(jnp.bfloat16), grads)


def on_device(
    clean_nodes,
    noise_nodes,
    edge_feats,
    neighbours,
    time_bins,
    cotangent,
    pair_weight,
    message_edge,
    message_out,
    ffn_in,
    ffn_out,
    edge_pair,
    edge_self,
    edge_out,
    norm_gain,
    norm_shift,
    node_bias,
    ffn_bias,
    edge_bias,
):
    sections = lax.axis_size("section")
    place = lax.axis_index("section")
    weights = tuple(
        (
            item[0]
            for item in (
                pair_weight,
                message_edge,
                message_out,
                ffn_in,
                ffn_out,
                edge_pair,
                edge_self,
                edge_out,
                norm_gain,
                norm_shift,
                node_bias,
                ffn_bias,
                edge_bias,
            )
        )
    )
    batches, node_count, width = clean_nodes.shape
    phase = (time_bins.astype(jnp.float32) + 0.5) * (math.pi * 0.5 / TBINS)
    start = jnp.cos(phase)[:, None, None] * clean_nodes.astype(jnp.float32) + jnp.sin(phase)[
        :, None, None
    ] * noise_nodes.astype(jnp.float32)
    zero_nodes = jnp.zeros((node_count, width), jnp.bfloat16)
    zero_edges = jnp.zeros(edge_feats.shape[1:], jnp.bfloat16)
    is_first = place == 0
    is_last = place == sections - 1

    def forward_step(step_index, carry):
        recv_nodes, recv_edges, back_nodes, kept_nodes, kept_edges, section_outs = carry
        item = step_index - place
        first_pass = (item >= 0) & (item < batches)
        second_pass = (item >= sections) & (item < sections + batches)
        index = jnp.clip(jnp.where(second_pass, item - sections, item), 0, batches - 1)
        predicted = back_nodes
        own_start = lax.dynamic_index_in_dim(start, index, 0, keepdims=False)
        lead_nodes = own_start + jnp.where(second_pass, predicted.astype(jnp.float32), 0.0)
        nodes_in = jnp.where(is_first, lead_nodes, recv_nodes.astype(jnp.float32))
        edges_in = jnp.where(
            is_first, lax.dynamic_index_in_dim(edge_feats, index, 0, keepdims=False), recv_edges
        )
        nearest = lax.dynamic_index_in_dim(neighbours, index, 0, keepdims=False)

        def run_layer(operand):
            after, edge_next, saved = forward_layer(weights, operand[0], operand[1], operand[2])
            return (after.astype(jnp.bfloat16), edge_next.astype(jnp.bfloat16))

        def skip_layer(operand):
            return (zero_nodes, zero_edges)

        out_nodes, out_edges = lax.cond(
            first_pass | second_pass, run_layer, skip_layer, (nodes_in, edges_in, nearest)
        )
        kept_nodes = lax.dynamic_update_index_in_dim(
            kept_nodes, jnp.where(second_pass, nodes_in, kept_nodes[index]), index, 0
        )
        kept_edges = lax.dynamic_update_index_in_dim(
            kept_edges, jnp.where(second_pass, edges_in, kept_edges[index]), index, 0
        )
        section_outs = lax.dynamic_update_index_in_dim(
            section_outs, jnp.where(second_pass, out_nodes, section_outs[index]), index, 0
        )
        recv_nodes, recv_edges = from_behind((out_nodes, out_edges), "section", 1)
        back_nodes = from_behind(out_nodes, "section", 1 - sections)
        return (recv_nodes, recv_edges, back_nodes, kept_nodes, kept_edges, section_outs)

    forward_init = (
        zero_nodes,
        zero_edges,
        zero_nodes,
        jnp.zeros((batches, node_count, width), jnp.float32),
        jnp.zeros_like(edge_feats),
        jnp.zeros((batches, node_count, width), jnp.bfloat16),
    )
    unused_nodes, unused_edges, unused_back, kept_nodes, kept_edges, section_outs = lax.fori_loop(
        0, 2 * sections + batches - 1, forward_step, forward_init
    )
    grads_zero = tuple((jnp.zeros(item.shape, jnp.float32) for item in weights))

    def backward_step(step_index, carry):
        recv_grad_nodes, recv_grad_edges, grads, input_grads = carry
        item = step_index - (sections - 1 - place)
        live = (item >= 0) & (item < batches)
        index = jnp.clip(item, 0, batches - 1)
        nodes_grad_out = jnp.where(
            is_last,
            lax.dynamic_index_in_dim(cotangent, index, 0, keepdims=False).astype(jnp.float32),
            recv_grad_nodes.astype(jnp.float32),
        )
        edges_grad_out = jnp.where(is_last, 0.0, recv_grad_edges.astype(jnp.float32))
        nearest = lax.dynamic_index_in_dim(neighbours, index, 0, keepdims=False)

        def run_back(operand):
            return backward_layer(
                weights, operand[0], operand[1], operand[2], operand[3], operand[4]
            )

        def skip_back(operand):
            return (zero_nodes, zero_edges, grads_zero)

        nodes_grad, edges_grad, terms = lax.cond(
            live,
            run_back,
            skip_back,
            (kept_nodes[index], kept_edges[index], nearest, nodes_grad_out, edges_grad_out),
        )
        grads = tuple((total + term for total, term in zip(grads, terms)))
        input_grads = lax.dynamic_update_index_in_dim(
            input_grads, jnp.where(live, nodes_grad, input_grads[index]), index, 0
        )
        recv_grad_nodes, recv_grad_edges = from_behind((nodes_grad, edges_grad), "section", -1)
        return (recv_grad_nodes, recv_grad_edges, grads, input_grads)

    backward_init = (
        zero_nodes,
        zero_edges,
        grads_zero,
        jnp.zeros((batches, node_count, width), jnp.bfloat16),
    )
    unused_grad_nodes, unused_grad_edges, grads, input_grads = lax.fori_loop(
        0, sections + batches - 1, backward_step, backward_init
    )
    totals = jax.tree.map(lambda part: part.astype(jnp.float32), lax.psum(for_sending(grads), "dp"))
    return (
        section_outs[None],
        input_grads[None],
        totals[0][None],
        totals[1][None],
        totals[2][None],
        totals[3][None],
        totals[4][None],
        totals[5][None],
        totals[6][None],
        totals[7][None],
        totals[8][None],
        totals[9][None],
        totals[10][None],
        totals[11][None],
        totals[12][None],
    )


BF16 = jnp.bfloat16
F32 = jnp.float32
MESH = pl.DeviceIdType.MESH
GELU_A = 0.7978845608028654
GELU_B = 0.044715


def gelu(x):
    return 0.5 * x * (1.0 + jnp.tanh(x * (GELU_A + (GELU_A * GELU_B) * (x * x))))


def gelu_both(x):
    square = x * x
    t = jnp.tanh(x * (GELU_A + (GELU_A * GELU_B) * square))
    half = 0.5 * (1.0 + t)
    slope = half + (0.5 * x) * (1.0 - t * t) * (GELU_A + (3.0 * GELU_A * GELU_B) * square)
    return x * half, slope


def mm(a, b):
    return jnp.dot(a, b, preferred_element_type=F32)


def mm_bt(a, b):
    return lax.dot_general(a, b, (((1,), (1,)), ((), ())), preferred_element_type=F32)


def mm_at(a, b):
    return lax.dot_general(a, b, (((0,), (0,)), ((), ())), preferred_element_type=F32)


def stacked(blocks):
    return jnp.concatenate(blocks, axis=0)


def row_mean(x):
    return jnp.mean(x, axis=-1, keepdims=True)


def normed(x):
    centred = x - row_mean(x)
    scale = lax.rsqrt(row_mean(centred * centred) + 1e-05)
    return centred * scale, scale


def norm_back(grad, unit, scale, gain):
    t = grad * gain
    return scale * (t - row_mean(t) - unit * row_mean(t * unit))


def col_sum(x):
    return jnp.sum(x, axis=0, keepdims=True)


def relay_kernel(
    dims,
    edges_in, near_in, mix, clean, noise, cot, pw_in, mo_in, fi_in, fo_in, ends, gains, shifts, node_b, fb, edge_b, we_own, ws_own, wo_own,
    act, ig, g_fwd, g_bwd, g_dpq, g_small, g_msg, g_upd,
    pw, mo, fi, fo, fwd_t, ep, e0, nb0, oht, start, par, eb0, wall_msg, wall_upd, fwd, bwd, sg,
    eg, eg_r, eg_b, msg_o, msg_f, upd_o, upd_f, wo, eb1,
    ecat, wcat, scat, pwn, parn, hin_r, hst, mb_s, mb_r, pq_s, pq_r, rq_s, rq_r,
    un0, un1, un2, hi_s, sc0, sc1, sc2, sci, u_s, slope_s, de, dacc, gp, gpe, dcat, act_t, edge_t,
    x_s, x_r, row_s, row_r, dpqo_r, dmb_s, dmb_r, dh1_s, dh1_r, dh1_f, dh2_s, dn3_s, da2_s, h1_s, a1_s,
    ld_sem, ld_ss, w_sem, nx_ss, nx_rs, hop_ss, hop_rs,
    pq_ss, pq_rs, ag_ss, ag_rs, rq_ss, rq_rs, ag2_ss, ag2_rs,
    mb_ss, mb_rs, x_ss, x_rs, row_ss, row_rs, dpqo_rs, fw_ss, dmb_ss, dmb_rs, dh_ss, dh_rs,
    e1_ss, e1_rs, e2_ss, e2_rs, g_ss, g_rs, relay_ss, ring_ss, ring_rs, sib_ss, sib_rs,
):
    S, B, N, K, Q, D, DE, EP, FF, C = dims
    BN = B * N
    RB = 16
    top = DE + N
    me_s = lax.axis_index("section")
    me_d = lax.axis_index("dp")
    core = lax.rem(me_d, 2)
    pair = me_d - core
    w = lax.div(me_s, 2)
    q = 2 * lax.rem(me_s, 2) + core
    owner_d = pair + lax.div(w, B)
    slot = lax.rem(w, B)
    my_row = pl.multiple_of(slot * N + q * Q, Q)
    own_rows = pl.ds(top, Q)

    def quarter(j):
        return pl.ds(pl.multiple_of(DE + j * Q, Q), Q)

    def is_me(sec, dpi):
        return (sec == me_s) & (dpi == me_d)

    def far(src, dst, ssem, rsem, sec, dpi):
        return pltpu.make_async_remote_copy(
            src_ref=src, dst_ref=dst, send_sem=ssem, recv_sem=rsem,
            device_id={"section": sec, "dp": dpi}, device_id_type=MESH,
        )

    def push(src, dst, ssem, rsem, sec, dpi):
        lax.cond(
            is_me(sec, dpi),
            lambda: pltpu.make_async_copy(src, dst, rsem).start(),
            lambda: far(src, dst, ssem, rsem, sec, dpi).start(),
        )

    def arrive(ref, sem):
        pltpu.make_async_copy(ref, ref, sem).wait()

    def drain(ref, sem, sec, dpi):
        @pl.when(jnp.logical_not(is_me(sec, dpi)))
        def _():
            arrive(ref, sem)

    def worker_of(p, j):
        return 2 * (core * B + p) + j // 2, pair + j % 2

    def peer(k):
        j = lax.rem(q + k, 4)
        return j, 2 * w + lax.div(j, 2), pair + lax.rem(j, 2)

    works_here = lax.div(w, B) == core

    def at(p, first=0, size=16):
        return pl.ds(pl.multiple_of(p * N + first, size), size)

    near = jnp.clip(w - core * B, 0, B - 1)

    weights = [
        pltpu.make_async_copy(src, dst, w_sem.at[n])
        for n, (src, dst) in enumerate(((pw_in, pw), (mo_in, mo), (fi_in, fi), (fo_in, fo)))
    ]
    for weight in weights:
        weight.start()
    barrier = pltpu.get_barrier_semaphore()
    for sec in range(S):
        for c in range(C):
            greeted = (c == pair) | (c == pair + 1) | (w == sec // 2)

            @pl.when(greeted & jnp.logical_not(is_me(sec, c)))
            def _():
                pl.semaphore_signal(
                    barrier, inc=1, device_id={"section": sec, "dp": c}, device_id_type=MESH
                )
    wall_msg[me_s] = we_own[...]
    wall_upd[me_s] = jnp.zeros(wall_upd.shape[1:], BF16)
    wall_upd[me_s, pl.ds(0, DE), pl.ds(0, DE)] = ws_own[...]
    wall_upd[me_s, pl.ds(0, DE), pl.ds(EP, DE)] = wo_own[...]
    bias = edge_b[pl.ds(1, 1), :]
    high = bias.astype(BF16).astype(F32)
    row = lax.broadcasted_iota(jnp.int32, (16, DE), 0)
    wall_upd[me_s, pl.ds(DE, 16), pl.ds(0, DE)] = jnp.where(
        row == 0, high, jnp.where(row == 1, bias - high, 0.0)
    ).astype(BF16)
    eb0[...] = jnp.zeros_like(eb0)
    eb0[:, pl.ds(0, DE)] = edge_b[pl.ds(0, 1), :]
    par[pl.ds(0, 1), :] = gains[0]
    par[pl.ds(1, 1), :] = shifts[0]
    par[pl.ds(2, 1), :] = node_b[0]
    par[pl.ds(3, 5), :] = jnp.zeros((5, D), F32)
    pl.semaphore_wait(barrier, 2 * S - 1 + 2 * (C - 2))

    def section_at(i):
        i = lax.rem(i + S, S)
        return jnp.where(i < S // 2, 2 * i, 2 * (S - i) - 1)

    place = jnp.where(lax.rem(me_s, 2) == 0, w, S - 1 - w)
    sides = ((section_at(place + 1), S // 2), (section_at(place - 1), S // 2 - 1))
    walls = (wall_msg, wall_upd)

    def half_of(which, layer, c):
        size = walls[which].shape[1] // 2
        return walls[which].at[layer, pl.ds(pl.multiple_of(c * size, size), size)]

    def ring_send(which, layer, side, hop):
        sec, reach = sides[side]
        if hop < reach:
            half = half_of(which, layer, core)
            far(half, half, ring_ss.at[which, side, hop], ring_rs.at[which, layer], sec, me_d).start()

    def ring_hop(which, side, hop):
        layer = section_at(place - hop if side == 0 else place + hop)
        half = half_of(which, layer, core)
        arrive(half, ring_rs.at[which, layer])
        ring_send(which, layer, side, hop)
        far(half, half, sib_ss.at[which, layer], sib_rs.at[which, layer], me_s, pair + 1 - core).start()

    hops = [(hop, side) for hop in range(1, S // 2 + 1) for side in range(2) if hop <= sides[side][1]]

    def ring_later(second):
        for hop, side in hops:
            early = (place > 0) & ((place >= hop) if side == 0 else (place + hop <= S))

            @pl.when(early != second)
            def _():
                ring_hop(1, side, hop)

    for side in range(2):
        ring_send(0, me_s, side, 0)

    ep[...] = jnp.zeros_like(ep)
    ep[:, pl.ds(0, DE)] = ends[:, pl.ds(0, DE)]
    ep[:, pl.ds(EP, DE)] = ends[...].astype(F32)[:, DE:].astype(BF16)

    arrays = ((edges_in, e0), (near_in, nb0))

    def quarter_of(n, j):
        rows = pl.ds(pl.multiple_of(j * Q, Q), Q)
        return edges_in.at[slot, :, rows] if n == 0 else near_in.at[slot, rows]

    @pl.when(works_here)
    def _():
        for n, (_, dst) in enumerate(arrays):
            pltpu.make_async_copy(quarter_of(n, q), dst, ld_sem.at[n]).start()
            other = q + 1 - 2 * core
            far(quarter_of(n, other), dst, ld_ss.at[n], ld_sem.at[n], me_s, pair + 1 - core).start()

    weights[0].wait()

    def edges_laid_out():
        for weight in weights[1:]:
            weight.wait()

        for n, (_, dst) in enumerate(arrays):
            arrive(dst, ld_sem.at[n])
        nearest = nb0[...]
        lane = lax.broadcasted_iota(jnp.int32, (Q, EP), 1) - DE
        for k in range(K):
            rows = pl.ds(k * Q, Q)
            ecat[0, rows, :] = jnp.where(lane == nearest[:, k : k + 1], 1.0, 0.0).astype(BF16)
            ecat[0, rows, pl.ds(0, DE)] = e0[k]
        node = lax.broadcasted_iota(jnp.int32, (N, EP), 0)
        lane = lax.broadcasted_iota(jnp.int32, (N, EP), 1) - DE
        chosen = jnp.where(lane == node, 1.0, 0.0).astype(BF16)
        oht[...] = mm_bt(chosen, ecat[0]).astype(BF16)

        @pl.when(works_here)
        def _():
            for n, (_, dst) in enumerate(arrays):
                arrive(dst, ld_ss.at[n])

    before = lax.rem(me_s + S - 1, S)
    far(pw_in, pwn, nx_ss.at[0], nx_rs.at[0], before, me_d).start()
    far(par, parn, nx_ss.at[1], nx_rs.at[1], before, me_d).start()

    for p in range(B):
        rows = pl.ds(p * N, N)
        start[rows, :] = mix[0, p] * clean[rows, :].astype(F32) + mix[1, p] * noise[rows, :].astype(F32)

    def ring_drain():
        for which in range(2):
            for side in range(2):
                for hop in range(sides[side][1]):
                    arrive(half_of(which, me_s, core), ring_ss.at[which, side, hop])
            for layer in range(S):
                @pl.when(layer != me_s)
                def _():
                    arrive(half_of(which, layer, core), sib_ss.at[which, layer])

    def unpack_messages(t):
        @pl.when(t != me_s)
        def _():
            arrive(half_of(0, t, 1 - core), sib_rs.at[0, t])

        wcat[t, pl.ds(0, DE), :] = wall_msg[t]

    def unpack_updates(t):
        @pl.when(t != me_s)
        def _():
            arrive(half_of(1, t, 1 - core), sib_rs.at[1, t])

        scat[t, pl.ds(0, DE), :] = wall_upd[t, pl.ds(0, DE), pl.ds(0, EP)]
        wo[t, pl.ds(0, DE), :] = wall_upd[t, pl.ds(0, DE), pl.ds(EP, EP)]
        wo[t, pl.ds(DE, N), :] = jnp.zeros((N, EP), BF16)
        eb1[t] = wall_upd[t, pl.ds(DE, 16), pl.ds(0, EP)]

    def rows_out(p, src, dst, ssem, rsem):
        for j in range(4):
            sec, dpi = worker_of(p, j)
            push(src.at[at(p, j * Q, Q)], dst, ssem, rsem, sec, dpi)

    def rows_drain(src, ssem):
        lax.cond(
            works_here,
            lambda: arrive(src.at[pl.ds(0, B * N - Q)], ssem),
            lambda: arrive(src, ssem),
        )

    def spread(rows, half, ref, layer, ssem, rsem, rows_sem):
        arrive(rows, rows_sem)
        for k in range(1, 4):
            _, sec, dpi = peer(k)
            far(rows.at[:, pl.ds(half, half)], ref.at[layer, quarter(q)], ssem, rsem, sec, dpi).start()
        ref[layer, own_rows, :] = rows[:, pl.ds(0, half)]
        ref[layer, quarter(q), :] = rows[:, pl.ds(half, half)]

    def spread_wait(ref, layer, sem):
        arrive(ref.at[layer, pl.ds(DE, 3 * Q)], sem)

    def share(group, src, dst):
        for c in range(C):
            push(src, dst.at[me_d], g_ss.at[group, c], g_rs.at[group, me_d], me_s, c)

    def share_wait(group, src, dst):
        for c in range(C):
            arrive(dst.at[c], g_rs.at[group, c])
            drain(src, g_ss.at[group, c], me_s, c)

    def share_near(group, src, dst):
        for c in range(C):
            @pl.when((c == pair) | (c == pair + 1) | (core == c % 2))
            def _():
                push(src, dst(me_d), g_ss.at[group, c], g_rs.at[group, me_d], me_s, c)

    def share_relay(group, src, dst):
        for c in range(C):
            @pl.when((c != me_d) & (core == c % 2))
            def _():
                arrive(dst(c), g_rs.at[group, c])
                far(dst(c), dst(c), relay_ss.at[group - 2, c // 2], g_rs.at[group, c], me_s, pair + 1 - core).start()

    def share_near_wait(group, src, dst):
        for c in range(C):
            @pl.when((c == me_d) | (core != c % 2))
            def _():
                arrive(dst(c), g_rs.at[group, c])

            @pl.when((c != me_d) & ((c == pair) | (c == pair + 1) | (core == c % 2)))
            def _():
                arrive(src, g_ss.at[group, c])

            @pl.when((c != me_d) & (core == c % 2))
            def _():
                arrive(dst(c), relay_ss.at[group - 2, c // 2])

    steps = 4
    KC = K // steps
    RC = KC * Q

    def messages(t):
        own = wcat[t, own_rows, :].astype(F32)
        total = jnp.zeros((Q, D), F32)
        for i in range(steps):
            pre = mm(ecat[t, pl.ds(i * RC, RC), :], wcat[t, pl.ds(0, top), :])
            for k in range(KC):
                total = total + gelu(pre[k * Q : (k + 1) * Q] + own)
        mb_s[...] = (total * (1.0 / K)).astype(BF16)

    def edge_update(t):
        own = scat[t, own_rows, :].astype(F32)
        bias = eb1[t, pl.ds(0, 1), :].astype(F32) + eb1[t, pl.ds(1, 1), :].astype(F32)
        for i in range(steps):
            pe = mm(ecat[t, pl.ds(i * RC, RC), :], scat[t, pl.ds(0, top), :])
            act_e = stacked([gelu(pe[k * Q : (k + 1) * Q] + own).astype(BF16) for k in range(KC)])
            z = mm(act_e, wo[t])
            for k in range(KC):
                rows = pl.ds(i * RC + k * Q, Q)
                ecat[t + 1, rows, :] = (ecat[t, rows, :].astype(F32) + z[k * Q : (k + 1) * Q] + bias).astype(BF16)

    chunks = 4
    FC = FF // chunks

    def node_forward(step):
        @pl.when(step < S)
        def _():
            arrive(pwn, nx_rs.at[0])
            arrive(parn, nx_rs.at[1])
            arrive(pw, nx_ss.at[0])
            arrive(par, nx_ss.at[1])

        @pl.when(step == 0)
        def _():
            hi_s[...] = start[...]

        @pl.when(step > 0)
        def _():
            arrive(hin_r, hop_rs)
            first = jnp.where(me_s == 0, 1.0, 0.0)
            for i in range(0, BN, RB):
                rows = pl.ds(i, RB)
                hi_s[rows, :] = hin_r[rows, :].astype(F32) + first * start[rows, :]

        later = lax.rem(me_s + 1, S)

        def turn(n, carry):
            p = lax.rem(near + n, B)
            whole = at(p, 0, N)
            arrive(mb_r.at[whole], mb_rs.at[p])
            mean = mm(mb_r[whole, :], mo[...])
            for i in range(0, N, RB):
                rows = at(p, i)
                h1 = hi_s[rows, :] + mean[i : i + RB] + node_b[1]
                h1_s[rows, :] = h1
                unit, scale = normed(h1)
                un1[rows, :] = unit
                sc1[rows, :] = scale
                fwd[rows, pl.ds(2 * D, D)] = (unit * gains[1] + shifts[1]).astype(BF16)
                fwd[rows, pl.ds(D, D)] = mb_r[rows, :]
            a2 = fwd[whole, pl.ds(2 * D, D)]
            y = jnp.zeros((N, D), F32)
            for c in range(chunks):
                cols = pl.ds(c * FC, FC)
                u = mm(a2, fi[:, cols])
                v = []
                for i in range(0, N, RB):
                    block = u[i : i + RB] + fb[:, cols]
                    u_s[at(p, i), cols] = block
                    v.append(gelu(block).astype(BF16))
                y = y + mm(stacked(v), fo[cols, :])
            last = jnp.where(me_s == S - 1, 1.0, 0.0)
            for i in range(0, N, RB):
                rows = at(p, i)
                h2 = h1_s[rows, :] + y[i : i + RB] + node_b[2]
                rounded = h2.astype(BF16)
                hst[rows, :] = rounded
                unit, scale = normed(h2)
                un2[rows, :] = unit
                sc2[rows, :] = scale
                fwd[rows, pl.ds(3 * D, D)] = (unit * gains[2] + shifts[2]).astype(BF16)
                pair_norm(rows, rounded.astype(F32) + last * start[rows, :], parn)
            rq = mm(fwd[whole, pl.ds(3 * D, D)], ep[...])
            for i in range(0, N, RB):
                rows = at(p, i)
                rq_s[rows, pl.ds(0, EP)] = (rq[i : i + RB, :EP] + eb0[...]).astype(BF16)
                rq_s[rows, pl.ds(EP, EP)] = rq[i : i + RB, EP:].astype(BF16)
            pair_rows(p, pwn, parn)

            @pl.when(me_s < S - 1)
            def _():
                rows_out(p, rq_s, rq_r, rq_ss, rq_rs)

            @pl.when(step < 2 * S - 1)
            def _():
                rows_out(p, pq_s, pq_r, pq_ss, pq_rs)

            @pl.when((n == 0) & works_here)
            def _():
                pass_on(step)

            return carry

        lax.fori_loop(0, B, turn, 0)

        @pl.when(step < 2 * S - 1)
        def _():
            far(hst, hin_r, hop_ss, hop_rs, later, me_d).start()

        @pl.when(step >= S)
        def _():
            act[...] = hst[...]
            for i in range(0, BN, RB):
                rows = pl.ds(i, RB)
                unit, scale = normed(hi_s[rows, :])
                hi_s[rows, :] = unit
                sci[rows, :] = scale
                fwd[rows, pl.ds(0, D)] = (unit * gains[0] + shifts[0]).astype(BF16)
                for c in range(chunks):
                    cols = pl.ds(c * FC, FC)
                    slope_s[rows, cols] = gelu_both(u_s[rows, cols])[1].astype(BF16)
            for n in range(4):
                fwd_t[pl.ds(n * D, D), :] = fwd[:, pl.ds(n * D, D)].T
            share(0, fwd_t, g_fwd)

    def pair_norm(rows, hidden, first):
        unit, scale = normed(hidden)
        un0[rows, :] = unit
        sc0[rows, :] = scale
        a1_s[rows, :] = (unit * first[pl.ds(0, 1), :] + first[pl.ds(1, 1), :]).astype(BF16)

    def pair_rows(p, weight, first):
        whole = at(p, 0, N)
        for half in range(2):
            cols = pl.ds(half * D, D)
            value = mm(a1_s[whole, :], weight[:, cols])
            if half == 0:
                value = value + first[pl.ds(2, 1), :]
            pq_s[whole, cols] = value.astype(BF16)

    def pass_on(step):
        t = lax.rem(step, S)

        @pl.when(t < S - 1)
        def _():
            spread(rq_r, EP, scat, t, ag2_ss, ag2_rs, rq_rs)

        @pl.when(step < 2 * S - 1)
        def _():
            spread(pq_r, D, wcat, lax.rem(step + 1, S), ag_ss, ag_rs, pq_rs)

    def node_forward_drain():
        arrive(hst, hop_ss)
        rows_drain(pq_s, pq_ss)

        @pl.when(me_s < S - 1)
        def _():
            rows_drain(rq_s, rq_ss)

    @pl.when(me_s == 0)
    def _():
        for i in range(0, BN, RB):
            rows = pl.ds(i, RB)
            pair_norm(rows, start[rows, :], par)
        for p in range(B):
            pair_rows(p, pw, par)
            rows_out(p, pq_s, pq_r, pq_ss, pq_rs)

    def message_slope(t):
        own = wcat[t, own_rows, :].astype(F32)
        for i in range(steps):
            pre = mm(ecat[t, pl.ds(i * RC, RC), :], wcat[t, pl.ds(0, top), :])
            for k in range(KC):
                gp[t, pl.ds(i * RC + k * Q, Q), :] = gelu_both(pre[k * Q : (k + 1) * Q] + own)[1].astype(BF16)

    def edge_slope(t):
        own = scat[t, own_rows, :].astype(F32)
        values = []
        for i in range(steps):
            pe = mm(ecat[t, pl.ds(i * RC, RC), :], scat[t, pl.ds(0, top), :])
            for k in range(KC):
                value, slope = gelu_both(pe[k * Q : (k + 1) * Q] + own)
                values.append(value.astype(BF16))
                gpe[t, pl.ds(i * RC + k * Q, Q), :] = slope.astype(BF16)
        act_t[t] = stacked(values).T

    def prepare(t):
        message_slope(t)
        edge_t[t] = ecat[t].T

        @pl.when(t > 0)
        def _():
            edge_slope(t - 1)

    def forward_step(step, carry):
        t = lax.rem(step, S)

        @pl.when(step < S)
        def _():
            unpack_messages(t)

        spread_wait(wcat, t, ag_rs)
        messages(t)
        spread_wait(wcat, t, ag_ss)
        push(mb_s, mb_r.at[pl.ds(my_row, Q)], mb_ss, mb_rs.at[slot], t, owner_d)

        for second in range(2):
            @pl.when(step == second)
            def _():
                ring_later(second == 1)

        @pl.when((step == 0) & (me_s == 0))
        def _():
            rows_drain(pq_s, pq_ss)

        @pl.when((step > 0) & (me_s == lax.rem(step + S - 1, S)))
        def _():
            node_forward_drain()

        @pl.when(me_s == t)
        def _():
            node_forward(step)

        @pl.when((me_s != t) & (step >= S))
        def _():
            prepare(t)

        @pl.when(jnp.logical_not((me_s == t) & works_here))
        def _():
            pass_on(step)

        @pl.when(t < S - 1)
        def _():
            @pl.when(step < S)
            def _():
                unpack_updates(t)

            spread_wait(scat, t, ag2_rs)
            edge_update(t)
            spread_wait(scat, t, ag2_ss)

        drain(mb_s, mb_ss, t, owner_d)
        return carry

    for hop, side in hops:
        if (hop, side) == (2, 0):
            edges_laid_out()
        ring_hop(0, side, hop)
    for side in range(2):
        ring_send(1, me_s, side, 0)
    spread(pq_r, D, wcat, 0, ag_ss, ag_rs, pq_rs)
    lax.fori_loop(0, 2 * S, forward_step, 0)
    ring_drain()

    @pl.when(me_s != S - 1)
    def _():
        arrive(half_of(1, S - 1, 1 - core), sib_rs.at[1, S - 1])

    def edge_back(t):
        b2, n2 = lax.rem(t, 2), lax.rem(t + 1, 2)
        total = jnp.zeros((Q, EP), F32)
        for i in range(steps):
            chunk = pl.ds(i * RC, RC)
            carry = mm_bt(dcat[b2, chunk, pl.ds(0, D)], wcat[t, pl.ds(0, top), :])
            low = []
            for k in range(KC):
                rows = pl.ds(i * RC + k * Q, Q)
                low.append((dacc[rows, :] + carry[k * Q : (k + 1) * Q]).astype(BF16))
                de[n2, rows, :] = low[-1]
            dw = mm_bt(stacked(low), wo[t - 1])
            for k in range(KC):
                rows = pl.ds(i * RC + k * Q, Q)
                d = (gpe[t - 1, rows, :].astype(F32) * dw[k * Q : (k + 1) * Q]).astype(BF16)
                total = total + d.astype(F32)
                dcat[n2, rows, pl.ds(D, EP)] = d
        row_s[:, pl.ds(2 * D, EP)] = total.astype(BF16)
        x_s[:, pl.ds(D, EP)] = mm(oht[...], dcat[n2, :, pl.ds(D, EP)]).astype(BF16)

    def edge_pass(t):
        b3 = lax.rem(t, 2)
        for i in range(steps):
            rows = pl.ds(i * RC, RC)
            d = dcat[b3, rows, pl.ds(D, EP)]
            dacc[rows, :] = de[b3, rows, :].astype(F32) + mm_bt(d, scat[t, pl.ds(0, top), :])

    blocks = 2 * C
    my_block = lax.rem(me_s, 2) * C + me_d
    BW, HM, HU = msg_o.shape[2], msg_o.shape[1], upd_o.shape[1]

    def block_of(t, half, c, size):
        return eg.at[t, half, pl.ds(0, size), pl.ds(pl.multiple_of(c * BW, BW), BW)]

    def blocks_out(t, size):
        for k in range(blocks):
            @pl.when(k != my_block)
            def _():
                far(
                    block_of(t, k // C, k % C, size), eg_r.at[t, my_block, pl.ds(0, size)],
                    e1_ss.at[t, k], e1_rs.at[t, my_block], 2 * w + k // C, k % C,
                ).start()

    def edge_grads(t):
        grad = mm(edge_t[t, pl.ds(0, DE), :], dcat[lax.rem(t, 2), :, pl.ds(0, D)]).astype(BF16)
        for half in range(2):
            eg[t, half, pl.ds(0, HM), :] = grad[half * HM : (half + 1) * HM]

        @pl.when(t > 0)
        def _():
            n2 = lax.rem(t + 1, 2)
            edges = mm(edge_t[t - 1, pl.ds(0, DE), :], dcat[n2, :, pl.ds(D, EP)])
            outs = mm(act_t[t - 1, pl.ds(0, DE), :], de[n2])
            bias = jnp.sum(de[n2].astype(F32), axis=0, keepdims=True)
            grad = jnp.concatenate([edges, outs], axis=1).astype(BF16)
            eg[t, 0, pl.ds(HM, HU), :] = grad[:HU]
            eg[t, 1, pl.ds(HM, DE - HU), :] = grad[HU:]
            eg[t, 1, pl.ds(HM + DE - HU, 16), pl.ds(0, EP)] = jnp.broadcast_to(bias, (16, EP)).astype(BF16)
            eg[t, 1, pl.ds(HM + DE - HU, 16), pl.ds(EP, EP)] = jnp.zeros((16, EP), BF16)
            eg[t, 1, pl.ds(HM + DE - HU + 16, 2 * HU - DE - 16), :] = jnp.zeros((2 * HU - DE - 16, 2 * EP), BF16)
            blocks_out(t, HM + HU)

        @pl.when(t == 0)
        def _():
            blocks_out(t, HM)

    def blocks_sum(t, size):
        eg_r[t, my_block, pl.ds(0, size), :] = block_of(t, lax.rem(me_s, 2), me_d, size)[...]
        for k in range(blocks):
            @pl.when(k != my_block)
            def _():
                arrive(eg_r.at[t, k, pl.ds(0, size)], e1_rs.at[t, k])
                arrive(block_of(t, k // C, k % C, size), e1_ss.at[t, k])
        total = eg_r[t, 0, pl.ds(0, size), :].astype(F32)
        for k in range(1, blocks):
            total = total + eg_r[t, k, pl.ds(0, size), :].astype(F32)
        eg_b[t, pl.ds(0, size), :] = total.astype(BF16)
        push(eg_b.at[t, pl.ds(0, HM)], msg_o.at[me_s], e2_ss.at[0, t], e2_rs.at[0, me_s], t, me_d)
        if size > HM:
            push(eg_b.at[t, pl.ds(HM, HU)], upd_o.at[me_s], e2_ss.at[1, t], e2_rs.at[1, me_s], t - 1, me_d)

    def gather_blocks():
        for k in range(1, 4):
            j, sec, dpi = peer(k)
            rows = pl.ds(pl.multiple_of(j * Q, Q), Q)
            far(x_s.at[rows], x_r.at[q], x_ss, x_rs, sec, dpi).start()
        x_r[q] = x_s[pl.ds(pl.multiple_of(q * Q, Q), Q), :]

    def gather_wait():
        arrive(x_r.at[pl.ds(0, 3)], x_rs)
        arrive(x_s.at[pl.ds(0, 3 * Q)], x_ss)
        total = x_r[0].astype(F32)
        for j in range(1, 4):
            total = total + x_r[j].astype(F32)
        return total

    def message_back(t):
        b2 = lax.rem(t, 2)
        dm = dmb_r[...].astype(F32)
        total = jnp.zeros((Q, D), F32)
        for k in range(K):
            rows = pl.ds(k * Q, Q)
            d = (gp[t, rows, :].astype(F32) * dm).astype(BF16)
            total = total + d.astype(F32)
            dcat[b2, rows, pl.ds(0, D)] = d
        row_s[:, pl.ds(0, D)] = total.astype(BF16)
        x_s[:, pl.ds(0, D)] = mm(oht[...], dcat[b2, :, pl.ds(0, D)]).astype(BF16)

    def node_backward():
        @pl.when(me_s < S - 1)
        def _():
            arrive(dh1_r, dh_rs)

        def turn(n, carry):
            p = lax.rem(near + n, B)
            whole = at(p, 0, N)

            @pl.when(me_s < S - 1)
            def _():
                arrive(row_r.at[whole], row_rs.at[p])
                dn0 = mm_bt(row_r[whole, pl.ds(0, 2 * D)], pwn[...])
                dn3 = mm_bt(row_r[whole, pl.ds(2 * D, 2 * EP)], ep[...])
                for i in range(0, N, RB):
                    rows = at(p, i)
                    dn = dn3[i : i + RB]
                    dn3_s[rows, :] = dn
                    first = norm_back(dn0[i : i + RB], un0[rows, :], sc0[rows, :], parn[pl.ds(0, 1), :])
                    dh = (dh1_r[rows, :].astype(F32) + first).astype(BF16).astype(F32)
                    dh2_s[rows, :] = dh + norm_back(dn, un2[rows, :], sc2[rows, :], gains[2])

            @pl.when(me_s == S - 1)
            def _():
                dh2_s[whole, :] = cot[whole, :].astype(F32)

            dy = dh2_s[whole, :].astype(BF16)
            bwd[whole, pl.ds(D, D)] = dy
            da2 = jnp.zeros((N, D), F32)
            for c in range(chunks):
                cols = pl.ds(c * FC, FC)
                dv = mm_bt(dy, fo[cols, :])
                du = stacked(
                    [(slope_s[at(p, i), cols].astype(F32) * dv[i : i + RB]).astype(BF16) for i in range(0, N, RB)]
                )
                da2 = da2 + mm_bt(du, fi[:, cols])
            for i in range(0, N, RB):
                rows = at(p, i)
                block = da2[i : i + RB]
                da2_s[rows, :] = block
                dh1 = dh2_s[rows, :] + norm_back(block, un1[rows, :], sc1[rows, :], gains[1])
                dh1_f[rows, :] = dh1
                bwd[rows, pl.ds(0, D)] = (dh1 * (1.0 / K)).astype(BF16)
            dmb_s[whole, :] = mm_bt(bwd[whole, pl.ds(0, D)], mo[...]).astype(BF16)
            rows_out(p, dmb_s, dmb_r, dmb_ss, dmb_rs)
            return carry

        lax.fori_loop(0, B, turn, 0)

        @pl.when(me_s > 0)
        def _():
            dh1_s[...] = dh1_f[...].astype(BF16)
            far(dh1_s, dh1_r, dh_ss, dh_rs, me_s - 1, me_d).start()

        @pl.when(me_s < S - 1)
        def _():
            far(row_r.at[:, pl.ds(0, 2 * D)], dpqo_r, fw_ss, dpqo_rs, me_s + 1, me_d).start()
            drs = row_r[:, pl.ds(2 * D, 2 * EP)]
            bwd[:, pl.ds(2 * D, 2 * EP)] = drs
            dn = dn3_s[...]
            sg[pl.ds(11, 1), :] = col_sum(dn * un2[...])
            sg[pl.ds(12, 1), :] = col_sum(dn)
            sg[pl.ds(16, 1), pl.ds(0, EP)] = col_sum(drs[:, :EP].astype(F32))

        @pl.when(me_s == S - 1)
        def _():
            bwd[:, pl.ds(2 * D, 2 * EP)] = jnp.zeros((B * N, 2 * EP), BF16)
            sg[pl.ds(11, 1), :] = jnp.zeros((1, D), F32)
            sg[pl.ds(12, 1), :] = jnp.zeros((1, D), F32)
            sg[pl.ds(16, 1), pl.ds(0, EP)] = jnp.zeros((1, EP), F32)

        share(1, bwd, g_bwd)
        sg[pl.ds(13, 1), :] = col_sum(dh2_s[...])
        sg[pl.ds(8, 1), :] = col_sum(da2_s[...] * un1[...])
        sg[pl.ds(9, 1), :] = col_sum(da2_s[...])
        sg[pl.ds(10, 1), :] = col_sum(dh1_f[...])

    def node_backward_drain():
        rows_drain(dmb_s, dmb_ss)

        @pl.when(me_s > 0)
        def _():
            arrive(dh1_s, dh_ss)

        @pl.when(me_s < S - 1)
        def _():
            arrive(row_r.at[:, pl.ds(0, 2 * D)], fw_ss)

    dacc[...] = jnp.zeros_like(dacc)

    def backward_step(step, carry):
        t = S - 1 - step

        @pl.when(me_s == t)
        def _():
            node_backward()

        @pl.when(((t == S - 1) & (me_s >= S - 2)) | (me_s == t - 2))
        def _():
            prepare(me_s)

        @pl.when(t < S - 1)
        def _():
            edge_pass(t)

        @pl.when(t + 2 < S)
        def _():
            blocks_sum(t + 2, HM + HU)

        @pl.when(t == 0)
        def _():
            blocks_sum(1, HM + HU)

        arrive(dmb_r, dmb_rs)
        message_back(t)

        @pl.when(t > 0)
        def _():
            edge_back(t)

        @pl.when(t == 0)
        def _():
            x_s[:, pl.ds(D, EP)] = jnp.zeros((N, EP), BF16)

        gather_blocks()
        other = gather_wait().astype(BF16)
        row_s[:, pl.ds(D, D)] = other[:, :D]
        row_s[:, pl.ds(2 * D + EP, EP)] = other[:, D:]
        dpq = row_s.at[:, pl.ds(0, 2 * D)]

        @pl.when(t > 0)
        def _():
            push(row_s, row_r.at[pl.ds(my_row, Q)], row_ss, row_rs.at[slot], t - 1, owner_d)

        @pl.when(t == 0)
        def _():
            push(dpq, dpqo_r.at[pl.ds(my_row, Q)], row_ss, dpqo_rs, t, owner_d)

        edge_grads(t)

        @pl.when(t > 0)
        def _():
            drain(row_s, row_ss, t - 1, owner_d)

        @pl.when(t == 0)
        def _():
            drain(dpq, row_ss, t, owner_d)

        @pl.when(me_s == t)
        def _():
            node_backward_drain()

        return carry

    lax.fori_loop(0, S, backward_step, 0)

    arrive(dpqo_r, dpqo_rs)
    across = [pl.ds(p * N, N) for p in range(B)]
    for p in range(B):
        share_near(2 + p, dpqo_r.at[across[p]], lambda c, p=p: g_dpq.at[c, across[p]])
    dpq = dpqo_r[...]
    sg[pl.ds(2, 1), :] = col_sum(dpq[:, :D].astype(F32))
    dn = mm_bt(dpq, pw[...])
    unit = hi_s[...]
    sg[pl.ds(0, 1), :] = col_sum(dn * unit)
    sg[pl.ds(1, 1), :] = col_sum(dn)
    share(2 + B, sg, g_small)
    ig[...] = (dh1_f[...] + norm_back(dn, unit, sci[...], gains[0])).astype(BF16)
    blocks_sum(0, HM)
    for p in range(B):
        share_relay(2 + p, dpqo_r.at[across[p]], lambda c, p=p: g_dpq.at[c, across[p]])
    def combine(kind, src, final):
        for sec in range(S):
            arrive(src.at[sec], e2_rs.at[kind, sec])
        for half in range(2):
            total = src[half].astype(F32)
            for sec in range(half + 2, S, 2):
                total = total + src[sec].astype(F32)
            final[half] = total.astype(BF16)

    @pl.when(me_s < S - 1)
    def _():
        combine(1, upd_o, upd_f)

    @pl.when(me_s == S - 1)
    def _():
        upd_f[...] = jnp.zeros_like(upd_f)

    share(4 + B, upd_f, g_upd)
    combine(0, msg_o, msg_f)
    share(3 + B, msg_f, g_msg)
    for t in range(S):
        drain(eg_b.at[t, pl.ds(0, HM)], e2_ss.at[0, t], t, me_d)
        if t > 0:
            drain(eg_b.at[t, pl.ds(HM, HU)], e2_ss.at[1, t], t - 1, me_d)
    share_wait(0, fwd_t, g_fwd)
    share_wait(1, bwd, g_bwd)
    for p in range(B):
        share_near_wait(2 + p, dpqo_r.at[across[p]], lambda c, p=p: g_dpq.at[c, across[p]])
    share_wait(2 + B, sg, g_small)
    share_wait(3 + B, msg_f, g_msg)
    share_wait(4 + B, upd_f, g_upd)


def run_relay(dims, operands):
    S, B, N, K, Q, D, DE, EP, FF, C = dims
    R = K * Q
    BN = B * N
    tall = DE + N + Q
    vm = pl.BlockSpec(memory_space=pltpu.VMEM)
    hbm = pl.BlockSpec(memory_space=pl.ANY)
    dma = pltpu.SemaphoreType.DMA
    sds = jax.ShapeDtypeStruct
    BW = D // C
    tile = 32
    held = -(-(DE + 16) // tile) * tile
    scratch = [
        pltpu.VMEM((D, 2 * D), BF16),
        pltpu.VMEM((D, D), BF16),
        pltpu.VMEM((D, FF), BF16),
        pltpu.VMEM((FF, D), BF16),
        pltpu.VMEM((4 * D, BN), BF16),
        pltpu.VMEM((D, 2 * EP), BF16),
        pltpu.VMEM((K, Q, DE), BF16),
        pltpu.VMEM((Q, K), jnp.int32),
        pltpu.VMEM((N, R), BF16),
        pltpu.VMEM((BN, D), F32),
        pltpu.VMEM((8, D), F32),
        pltpu.VMEM((1, EP), F32),
        pltpu.VMEM((S, DE, D), BF16),
        pltpu.VMEM((S, held, 2 * EP), BF16),
        pltpu.VMEM((BN, 4 * D), BF16),
        pltpu.VMEM((BN, 2 * D + 2 * EP), BF16),
        pltpu.VMEM((24, D), F32),
        pltpu.VMEM((S, 2, (DE + held) // 2, D), BF16),
        pltpu.VMEM((S, 2 * C, (DE + held) // 2, BW), BF16),
        pltpu.VMEM((S, (DE + held) // 2, BW), BF16),
        pltpu.VMEM((S, DE // 2, BW), BF16),
        pltpu.VMEM((2, DE // 2, BW), BF16),
        pltpu.VMEM((S, held // 2, BW), BF16),
        pltpu.VMEM((2, held // 2, BW), BF16),
        pltpu.VMEM((S, EP, EP), BF16),
        pltpu.VMEM((S, 16, EP), BF16),
        pltpu.VMEM((S, R, EP), BF16),
        pltpu.VMEM((S, tall, D), BF16),
        pltpu.VMEM((S, tall, EP), BF16),
        pltpu.VMEM((D, 2 * D), BF16),
        pltpu.VMEM((8, D), F32),
        pltpu.VMEM((BN, D), BF16),
        pltpu.VMEM((BN, D), BF16),
        pltpu.VMEM((Q, D), BF16),
        pltpu.VMEM((BN, D), BF16),
        pltpu.VMEM((BN, 2 * D), BF16),
        pltpu.VMEM((Q, 2 * D), BF16),
        pltpu.VMEM((BN, 2 * EP), BF16),
        pltpu.VMEM((Q, 2 * EP), BF16),
        pltpu.VMEM((BN, D), F32),
        pltpu.VMEM((BN, D), F32),
        pltpu.VMEM((BN, D), F32),
        pltpu.VMEM((BN, D), F32),
        pltpu.VMEM((BN, 1), F32),
        pltpu.VMEM((BN, 1), F32),
        pltpu.VMEM((BN, 1), F32),
        pltpu.VMEM((BN, 1), F32),
        pltpu.VMEM((BN, FF), F32),
        pltpu.VMEM((BN, FF), BF16),
        pltpu.VMEM((2, R, EP), BF16),
        pltpu.VMEM((R, EP), F32),
        pltpu.VMEM((S, R, D), BF16),
        pltpu.VMEM((S, R, EP), BF16),
        pltpu.VMEM((2, R, D + EP), BF16),
        pltpu.VMEM((S, EP, R), BF16),
        pltpu.VMEM((S, EP, R), BF16),
        pltpu.VMEM((N, D + EP), BF16),
        pltpu.VMEM((4, Q, D + EP), BF16),
        pltpu.VMEM((Q, 2 * D + 2 * EP), BF16),
        pltpu.VMEM((BN, 2 * D + 2 * EP), BF16),
        pltpu.VMEM((BN, 2 * D), BF16),
        pltpu.VMEM((BN, D), BF16),
        pltpu.VMEM((Q, D), BF16),
        pltpu.VMEM((BN, D), BF16),
        pltpu.VMEM((BN, D), BF16),
        pltpu.VMEM((BN, D), F32),
        pltpu.VMEM((BN, D), F32),
        pltpu.VMEM((BN, D), F32),
        pltpu.VMEM((BN, D), F32),
        pltpu.VMEM((BN, D), F32),
        pltpu.VMEM((BN, D), BF16),
        dma((2,)), dma((2,)), dma((4,)), dma((2,)), dma((2,)), dma, dma,
        dma, dma, dma, dma, dma, dma, dma, dma,
        dma, dma((B,)), dma, dma, dma, dma((B,)), dma,
        dma, dma, dma, dma, dma,
        dma((S, 2 * C)), dma((S, 2 * C)), dma((2, S)), dma((2, S)), dma((5 + B, C)), dma((5 + B, C)),
        dma((B, C // 2)), dma((2, 2, S // 2)), dma((2, S)), dma((2, S)), dma((2, S)),
    ]
    return pl.pallas_call(
        functools.partial(relay_kernel, dims),
        out_shape=(
            sds((BN, D), BF16),
            sds((BN, D), BF16),
            sds((C, 4 * D, BN), BF16),
            sds((C, BN, 2 * D + 2 * EP), BF16),
            sds((C, BN, 2 * D), BF16),
            sds((C, 24, D), F32),
            sds((C, 2, DE // 2, BW), BF16),
            sds((C, 2, held // 2, BW), BF16),
        ),
        in_specs=[hbm, hbm, pl.BlockSpec(memory_space=pltpu.SMEM)] + [vm] * 3 + [hbm] * 4 + [vm] * 9,
        out_specs=(vm,) * 2 + (hbm,) * 6,
        scratch_shapes=scratch,
        compiler_params=pltpu.CompilerParams(
            collective_id=0, has_side_effects=True, vmem_limit_bytes=62 * 1024 * 1024
        ),
    )(*operands)


def gradient_kernel(
    dims,
    fwd, bwd, dpq, small, edge, upd, fi, fo, fb, act, ig,
    g_pair, g_edge, g_out, g_fi, g_fo, g_ep, g_self, g_eout, g_gain, g_shift, g_nb, g_fb, g_eb, act_out, ig_out,
    fwd_v, bwd_v, dpq_v, fi_v, fo_v, gfi_v, gfo_v, pair_v, out_v, edge_v, upd_v, in_sems, sems,
):
    S, B, N, K, Q, D, DE, EP, FF, C = dims
    chunks = 4
    FC = FF // chunks

    def part(c, size=D):
        return pl.ds(c * size, size)

    loads = {}

    def load(name, src, dst):
        loads[name] = pltpu.make_async_copy(src, dst, in_sems.at[len(loads)])
        loads[name].start()

    BN = B * N

    def load_kept(n):
        for c in range(C):
            load((n, c), fwd.at[c, part(n)], fwd_v.at[n, :, part(c, BN)])

    def wait_kept(n):
        for c in range(C):
            loads[n, c].wait()
        return fwd_v[n]

    load_kept(2)
    load("dy", bwd.at[:, part(1)], bwd_v.at[1])
    for c in range(chunks):
        load(("fi", c), fi.at[:, part(c, FC)], fi_v.at[c])
        load(("fo", c), fo.at[part(c, FC)], fo_v.at[c])
    load_kept(0)
    load("dpq0", dpq.at[:, part(0)], dpq_v.at[0])
    load("dpq1", dpq.at[:, part(1)], dpq_v.at[1])
    load_kept(1)
    load("dmsg", bwd.at[:, part(0)], bwd_v.at[0])
    load_kept(3)
    load("drs", bwd.at[:, part(2)], bwd_v.at[2])
    load("edge", edge, edge_v)
    load("upd", upd, upd_v)
    stores = []

    def out(src, dst):
        copy = pltpu.make_async_copy(src, dst, sems.at[len(stores)])
        copy.start()
        stores.append(copy)

    out(act, act_out)
    out(ig, ig_out)
    a2_t = wait_kept(2)
    a2 = a2_t.T
    loads["dy"].wait()
    dy = bwd_v[1]
    for c in range(chunks):
        cols = part(c, FC)
        loads["fi", c].wait()
        loads["fo", c].wait()
        value, slope = gelu_both(mm(a2, fi_v[c]) + fb[:, cols])
        du = (slope * mm_bt(dy, fo_v[c])).astype(BF16)
        g_fb[:, cols] = col_sum(du.astype(F32))
        gfi_v[c] = mm(a2_t, du)
        out(gfi_v.at[c], g_fi.at[0, :, cols])
        gfo_v[c] = mm_at(value.astype(BF16), dy)
        out(gfo_v.at[c], g_fo.at[0, cols])
    a1_t = wait_kept(0)
    for c in range(2):
        loads["dpq%d" % c].wait()
        pair_v[c] = mm(a1_t, dpq_v[c])
        out(pair_v.at[c], g_pair.at[0, :, part(c)])
    loads["dmsg"].wait()
    out_v[...] = mm(wait_kept(1), bwd_v[0]) * float(K)
    out(out_v, g_out.at[0])
    loads["drs"].wait()
    ends = mm(wait_kept(3), bwd_v[2])
    g_ep[0] = jnp.concatenate([ends[:, :DE], ends[:, EP : EP + DE]], axis=1)
    total = small[0]
    for c in range(1, C):
        total = total + small[c]
    for i, rows in enumerate(((0, 1, 2), (8, 9, 10), (11, 12, 13))):
        g_gain[i] = total[rows[0] : rows[0] + 1]
        g_shift[i] = total[rows[1] : rows[1] + 1]
        g_nb[i] = total[rows[2] : rows[2] + 1]
    g_eb[0, pl.ds(0, 1), :] = total[16:17, :DE]
    loads["edge"].wait()
    loads["upd"].wait()
    BW = edge_v.shape[3]
    for c in range(C):
        for half in range(2):
            block = edge_v[c, half].astype(F32)
            g_edge[0, pl.ds(half * (DE // 2), DE // 2), pl.ds(c * BW, BW)] = block
        block = stacked([upd_v[c, 0], upd_v[c, 1]]).astype(F32)
        first = c * BW
        for array, begin in ((g_self, 0), (g_eout, EP)):
            low, high = max(first, begin), min(first + BW, begin + DE)
            if low < high:
                array[0, :, pl.ds(low - begin, high - low)] = block[:DE, low - first : high - first]
        low, high = first, min(first + BW, DE)
        if low < high:
            g_eb[0, pl.ds(1, 1), pl.ds(low, high - low)] = block[DE : DE + 1, low - first : high - first]
    for copy in stores:
        copy.wait()


def run_gradients(dims, operands):
    S, B, N, K, Q, D, DE, EP, FF, C = dims
    rows = C * B * N
    BW = D // C
    held = operands[5].shape[2]
    vm = pl.BlockSpec(memory_space=pltpu.VMEM)
    hbm = pl.BlockSpec(memory_space=pl.ANY)
    sds = jax.ShapeDtypeStruct
    shapes = (
        (1, D, 2 * D), (1, DE, D), (1, D, D), (1, D, FF), (1, FF, D), (1, D, 2 * DE), (1, DE, DE), (1, DE, DE),
        (3, 1, D), (3, 1, D), (3, 1, D), (1, FF), (1, 2, DE),
    )
    return pl.pallas_call(
        functools.partial(gradient_kernel, dims),
        out_shape=tuple(sds(shape, F32) for shape in shapes) + (sds((1, B, N, D), BF16),) * 2,
        in_specs=[hbm, hbm, hbm, vm, hbm, hbm, hbm, hbm, vm, hbm, hbm],
        out_specs=(hbm, vm, hbm, hbm, hbm) + (vm,) * 8 + (hbm,) * 2,
        scratch_shapes=[
            pltpu.VMEM((4, D, rows), BF16),
            pltpu.VMEM((3, rows, D), BF16),
            pltpu.VMEM((2, rows, D), BF16),
            pltpu.VMEM((4, D, FF // 4), BF16),
            pltpu.VMEM((4, FF // 4, D), BF16),
            pltpu.VMEM((4, D, FF // 4), F32),
            pltpu.VMEM((4, FF // 4, D), F32),
            pltpu.VMEM((2, D, D), F32),
            pltpu.VMEM((D, D), F32),
            pltpu.VMEM((C, 2, DE // 2, BW), BF16),
            pltpu.VMEM((C, 2, held, BW), BF16),
            pltpu.SemaphoreType.DMA((15 + 4 * C,)),
            pltpu.SemaphoreType.DMA((13,)),
        ],
        compiler_params=pltpu.CompilerParams(vmem_limit_bytes=56 * 1024 * 1024),
    )(*operands)


def stationary(
    clean_nodes, noise_nodes, edge_feats, neighbours, time_bins, cotangent,
    pair_weight, message_edge, message_out, ffn_in, ffn_out, edge_pair, edge_self, edge_out,
    norm_gain, norm_shift, node_bias, ffn_bias, edge_bias,
):
    S = lax.axis_size("section")
    B, N, D = clean_nodes.shape
    K, DE = edge_feats.shape[2:]
    FF = ffn_in.shape[2]
    Q = N // 4
    EP = DE + N
    phase = (time_bins.astype(F32) + 0.5) * (math.pi * 0.5 / TBINS)
    mix = jnp.cos(phase[None] - jnp.array([[0.0], [math.pi * 0.5]], F32))

    def by_rows(array):
        return jnp.transpose(array, (1, 0, 2))

    C = lax.axis_size("dp")
    dims = (S, B, N, K, Q, D, DE, EP, FF, C)
    act, ig, g_fwd, g_bwd, g_dpq, g_small, g_msg, g_upd = run_relay(
        dims,
        (
            jnp.transpose(edge_feats, (0, 2, 1, 3)), neighbours, mix, clean_nodes.reshape(B * N, D), noise_nodes.reshape(B * N, D),
            cotangent.reshape(B * N, D), pair_weight[0], message_out[0], ffn_in[0], ffn_out[0], edge_pair[0],
            by_rows(norm_gain), by_rows(norm_shift), by_rows(node_bias), ffn_bias, edge_bias[0],
            message_edge[0], edge_self[0], edge_out[0],
        ),
    )
    grads = run_gradients(
        dims,
        (
            g_fwd, g_bwd.reshape(C * B * N, -1), g_dpq.reshape(C * B * N, -1),
            g_small, g_msg, g_upd, ffn_in[0], ffn_out[0], ffn_bias, act.reshape(1, B, N, D), ig.reshape(1, B, N, D),
        ),
    )
    grads, outs = list(grads[:-2]), tuple(grads[-2:])
    grads[8:11] = [by_rows(array) for array in grads[8:11]]
    return outs + tuple(grads)


def solution(mesh):
    sections, copies = mesh.shape["section"], mesh.shape["dp"]

    def body(*args):
        B, N = args[0].shape[:2]
        fits = sections == 4 * B and copies % 2 == 0 and N % 64 == 0
        return stationary(*args) if fits else on_device(*args)

    placed = (
        P("dp", None, None),
        P("dp", None, None),
        P("dp", None, None, None),
        P("dp", None, None),
        P("dp"),
        P("dp", None, None),
        P("section", None, None),
        P("section", None, None),
        P("section", None, None),
        P("section", None, None),
        P("section", None, None),
        P("section", None, None),
        P("section", None, None),
        P("section", None, None),
        P("section", None, None),
        P("section", None, None),
        P("section", None, None),
        P("section", None),
        P("section", None, None),
    )
    return jax.shard_map(
        body,
        mesh=mesh,
        in_specs=placed,
        out_specs=(
            P("section", "dp", None, None),
            P("section", "dp", None, None),
            P("section", None, None),
            P("section", None, None),
            P("section", None, None),
            P("section", None, None),
            P("section", None, None),
            P("section", None, None),
            P("section", None, None),
            P("section", None, None),
            P("section", None, None),
            P("section", None, None),
            P("section", None, None),
            P("section", None),
            P("section", None, None),
        ),
        check_vma=False,
    )
```

```python
import functools
import math

import jax
import jax.numpy as jnp
from jax import lax
from jax.experimental import pallas as pl
from jax.experimental.pallas import tpu as pltpu
from jax.sharding import PartitionSpec as P

TBINS = 100


def from_behind(block, axis, distance):
    devices = range(lax.axis_size(axis))
    route = [(i - distance, i) for i in devices if i - distance in devices]
    return lax.ppermute(block, axis, route)


def for_sending(value):
    return jax.tree.map(lambda a: a.astype(jnp.bfloat16) if a.dtype == jnp.float32 else a, value)


def layer_norm(value, gain, shift):
    centre = jnp.mean(value, axis=-1, keepdims=True)
    centred = value - centre
    spread = jnp.mean(centred * centred, axis=-1, keepdims=True)
    return centred * lax.rsqrt(spread + 1e-05) * gain + shift


def forward_layer(weights, hidden, edge_state, nearest):
    (
        pair_w,
        msg_edge,
        msg_out,
        ffn_w_in,
        ffn_w_out,
        edge_pair_w,
        edge_self_w,
        edge_out_w,
        gains,
        shifts,
        node_b,
        ffn_b,
        edge_b,
    ) = weights
    width = msg_out.shape[0]
    edge_width = edge_self_w.shape[0]
    normed_one = layer_norm(hidden, gains[0], shifts[0]).astype(jnp.bfloat16)
    pair_out = jnp.dot(normed_one, pair_w, preferred_element_type=jnp.float32)
    before_act = (
        pair_out[:, None, :width]
        + jnp.take(pair_out[:, width:], nearest, axis=0)
        + jnp.einsum("nkc,cd->nkd", edge_state, msg_edge, preferred_element_type=jnp.float32)
        + node_b[0]
    )
    message_act = jax.nn.gelu(before_act).astype(jnp.bfloat16)
    message_all = jnp.einsum(
        "nkc,cd->nkd", message_act, msg_out, preferred_element_type=jnp.float32
    )
    after_msg = hidden + jnp.mean(message_all, axis=1) + node_b[1]
    normed_two = layer_norm(after_msg, gains[1], shifts[1]).astype(jnp.bfloat16)
    ffn_pre = jnp.dot(normed_two, ffn_w_in, preferred_element_type=jnp.float32) + ffn_b
    ffn_act = jax.nn.gelu(ffn_pre).astype(jnp.bfloat16)
    after_ffn = (
        after_msg + jnp.dot(ffn_act, ffn_w_out, preferred_element_type=jnp.float32) + node_b[2]
    )
    normed_three = layer_norm(after_ffn, gains[2], shifts[2]).astype(jnp.bfloat16)
    edge_pairs = jnp.dot(normed_three, edge_pair_w, preferred_element_type=jnp.float32)
    edge_pre = (
        edge_pairs[:, None, :edge_width]
        + jnp.take(edge_pairs[:, edge_width:], nearest, axis=0)
        + jnp.einsum("nkc,cd->nkd", edge_state, edge_self_w, preferred_element_type=jnp.float32)
        + edge_b[0]
    )
    edge_act = jax.nn.gelu(edge_pre).astype(jnp.bfloat16)
    edge_next = (
        edge_state.astype(jnp.float32)
        + jnp.einsum("nkc,cd->nkd", edge_act, edge_out_w, preferred_element_type=jnp.float32)
        + edge_b[1]
    )
    saved = (
        normed_one,
        before_act,
        message_act,
        after_msg,
        normed_two,
        ffn_pre,
        ffn_act,
        after_ffn,
        normed_three,
        edge_pre,
        edge_act,
    )
    return (after_ffn, edge_next, saved)


def backward_layer(weights, hidden, edge_state, nearest, grad_nodes_out, grad_edges_out):
    (
        pair_w,
        msg_edge,
        msg_out,
        ffn_w_in,
        ffn_w_out,
        edge_pair_w,
        edge_self_w,
        edge_out_w,
        gains,
        shifts,
        node_b,
        ffn_b,
        edge_b,
    ) = weights
    unused_nodes, unused_edges, saved = forward_layer(weights, hidden, edge_state, nearest)
    (
        normed_one,
        before_act,
        message_act,
        after_msg,
        normed_two,
        ffn_pre,
        ffn_act,
        after_ffn,
        normed_three,
        edge_pre,
        edge_act,
    ) = saved
    width = msg_out.shape[0]
    edge_width = edge_self_w.shape[0]
    count = nearest.shape[1]
    node_count = hidden.shape[0]
    one_hot = (
        nearest.reshape(-1)[None, :] == jnp.arange(node_count, dtype=jnp.int32)[:, None]
    ).astype(jnp.bfloat16)
    edge_grad_low = grad_edges_out.astype(jnp.bfloat16)
    grad_edge_b1 = jnp.sum(grad_edges_out, axis=(0, 1))
    grad_edge_out_w = jnp.einsum(
        "nkc,nkd->cd", edge_act, edge_grad_low, preferred_element_type=jnp.float32
    )
    edge_act_grad = jnp.einsum(
        "nkd,cd->nkc", edge_grad_low, edge_out_w, preferred_element_type=jnp.float32
    )
    unused_value, gelu_edge = jax.vjp(jax.nn.gelu, edge_pre)
    edge_pre_grad = gelu_edge(edge_act_grad)[0].astype(jnp.bfloat16)
    grad_edge_b0 = jnp.sum(edge_pre_grad, axis=(0, 1), dtype=jnp.float32)
    grad_edge_self_w = jnp.einsum(
        "nkc,nkd->cd", edge_state, edge_pre_grad, preferred_element_type=jnp.float32
    )
    edge_total = grad_edges_out + jnp.einsum(
        "nkd,cd->nkc", edge_pre_grad, edge_self_w, preferred_element_type=jnp.float32
    )
    own_edge = jnp.sum(edge_pre_grad, axis=1, dtype=jnp.float32)
    other_edge = jnp.dot(
        one_hot, edge_pre_grad.reshape(-1, edge_width), preferred_element_type=jnp.float32
    )
    pairs_grad = jnp.concatenate([own_edge, other_edge], axis=-1).astype(jnp.bfloat16)
    grad_edge_pair_w = jnp.einsum(
        "nc,nd->cd", normed_three, pairs_grad, preferred_element_type=jnp.float32
    )
    normed_three_grad = jnp.einsum(
        "nd,cd->nc", pairs_grad, edge_pair_w, preferred_element_type=jnp.float32
    )
    unused_value, norm_three_back = jax.vjp(layer_norm, after_ffn, gains[2], shifts[2])
    ffn_side, gain_three, shift_three = norm_three_back(normed_three_grad)
    after_ffn_grad = grad_nodes_out + ffn_side
    grad_node_b2 = jnp.sum(after_ffn_grad, axis=0)
    ffn_out_grad = after_ffn_grad.astype(jnp.bfloat16)
    grad_ffn_w_out = jnp.einsum(
        "nc,nd->cd", ffn_act, ffn_out_grad, preferred_element_type=jnp.float32
    )
    ffn_act_grad = jnp.einsum(
        "nd,cd->nc", ffn_out_grad, ffn_w_out, preferred_element_type=jnp.float32
    )
    unused_value, gelu_ffn = jax.vjp(jax.nn.gelu, ffn_pre)
    ffn_pre_grad = gelu_ffn(ffn_act_grad)[0].astype(jnp.bfloat16)
    grad_ffn_b = jnp.sum(ffn_pre_grad, axis=0, dtype=jnp.float32)
    grad_ffn_w_in = jnp.einsum(
        "nc,nd->cd", normed_two, ffn_pre_grad, preferred_element_type=jnp.float32
    )
    normed_two_grad = jnp.einsum(
        "nd,cd->nc", ffn_pre_grad, ffn_w_in, preferred_element_type=jnp.float32
    )
    unused_value, norm_two_back = jax.vjp(layer_norm, after_msg, gains[1], shifts[1])
    msg_side, gain_two, shift_two = norm_two_back(normed_two_grad)
    after_msg_grad = after_ffn_grad + msg_side
    grad_node_b1 = jnp.sum(after_msg_grad, axis=0)
    message_grad = (after_msg_grad / count).astype(jnp.bfloat16)
    grad_msg_out = jnp.einsum(
        "nkc,nd->cd", message_act, message_grad, preferred_element_type=jnp.float32
    )
    message_act_grad = jnp.einsum(
        "nd,cd->nc", message_grad, msg_out, preferred_element_type=jnp.float32
    )
    unused_value, gelu_msg = jax.vjp(jax.nn.gelu, before_act)
    before_grad = gelu_msg(jnp.broadcast_to(message_act_grad[:, None, :], before_act.shape))[
        0
    ].astype(jnp.bfloat16)
    grad_node_b0 = jnp.sum(before_grad, axis=(0, 1), dtype=jnp.float32)
    grad_msg_edge = jnp.einsum(
        "nkc,nkd->cd", edge_state, before_grad, preferred_element_type=jnp.float32
    )
    edge_total = edge_total + jnp.einsum(
        "nkd,cd->nkc", before_grad, msg_edge, preferred_element_type=jnp.float32
    )
    own_node = jnp.sum(before_grad, axis=1, dtype=jnp.float32)
    other_node = jnp.dot(
        one_hot, before_grad.reshape(-1, width), preferred_element_type=jnp.float32
    )
    pair_grad = jnp.concatenate([own_node, other_node], axis=-1).astype(jnp.bfloat16)
    grad_pair_w = jnp.einsum("nc,nd->cd", normed_one, pair_grad, preferred_element_type=jnp.float32)
    normed_one_grad = jnp.einsum("nd,cd->nc", pair_grad, pair_w, preferred_element_type=jnp.float32)
    unused_value, norm_one_back = jax.vjp(layer_norm, hidden, gains[0], shifts[0])
    input_side, gain_one, shift_one = norm_one_back(normed_one_grad)
    hidden_grad = after_msg_grad + input_side
    grads = (
        grad_pair_w,
        grad_msg_edge,
        grad_msg_out,
        grad_ffn_w_in,
        grad_ffn_w_out,
        grad_edge_pair_w,
        grad_edge_self_w,
        grad_edge_out_w,
        jnp.stack([gain_one, gain_two, gain_three]),
        jnp.stack([shift_one, shift_two, shift_three]),
        jnp.stack([grad_node_b0, grad_node_b1, grad_node_b2]),
        grad_ffn_b,
        jnp.stack([grad_edge_b0, grad_edge_b1]),
    )
    return (hidden_grad.astype(jnp.bfloat16), edge_total.astype(jnp.bfloat16), grads)


def on_device(
    clean_nodes,
    noise_nodes,
    edge_feats,
    neighbours,
    time_bins,
    cotangent,
    pair_weight,
    message_edge,
    message_out,
    ffn_in,
    ffn_out,
    edge_pair,
    edge_self,
    edge_out,
    norm_gain,
    norm_shift,
    node_bias,
    ffn_bias,
    edge_bias,
):
    sections = lax.axis_size("section")
    place = lax.axis_index("section")
    weights = tuple(
        (
            item[0]
            for item in (
                pair_weight,
                message_edge,
                message_out,
                ffn_in,
                ffn_out,
                edge_pair,
                edge_self,
                edge_out,
                norm_gain,
                norm_shift,
                node_bias,
                ffn_bias,
                edge_bias,
            )
        )
    )
    batches, node_count, width = clean_nodes.shape
    phase = (time_bins.astype(jnp.float32) + 0.5) * (math.pi * 0.5 / TBINS)
    start = jnp.cos(phase)[:, None, None] * clean_nodes.astype(jnp.float32) + jnp.sin(phase)[
        :, None, None
    ] * noise_nodes.astype(jnp.float32)
    zero_nodes = jnp.zeros((node_count, width), jnp.bfloat16)
    zero_edges = jnp.zeros(edge_feats.shape[1:], jnp.bfloat16)
    is_first = place == 0
    is_last = place == sections - 1

    def forward_step(step_index, carry):
        recv_nodes, recv_edges, back_nodes, kept_nodes, kept_edges, section_outs = carry
        item = step_index - place
        first_pass = (item >= 0) & (item < batches)
        second_pass = (item >= sections) & (item < sections + batches)
        index = jnp.clip(jnp.where(second_pass, item - sections, item), 0, batches - 1)
        predicted = back_nodes
        own_start = lax.dynamic_index_in_dim(start, index, 0, keepdims=False)
        lead_nodes = own_start + jnp.where(second_pass, predicted.astype(jnp.float32), 0.0)
        nodes_in = jnp.where(is_first, lead_nodes, recv_nodes.astype(jnp.float32))
        edges_in = jnp.where(
            is_first, lax.dynamic_index_in_dim(edge_feats, index, 0, keepdims=False), recv_edges
        )
        nearest = lax.dynamic_index_in_dim(neighbours, index, 0, keepdims=False)

        def run_layer(operand):
            after, edge_next, saved = forward_layer(weights, operand[0], operand[1], operand[2])
            return (after.astype(jnp.bfloat16), edge_next.astype(jnp.bfloat16))

        def skip_layer(operand):
            return (zero_nodes, zero_edges)

        out_nodes, out_edges = lax.cond(
            first_pass | second_pass, run_layer, skip_layer, (nodes_in, edges_in, nearest)
        )
        kept_nodes = lax.dynamic_update_index_in_dim(
            kept_nodes, jnp.where(second_pass, nodes_in, kept_nodes[index]), index, 0
        )
        kept_edges = lax.dynamic_update_index_in_dim(
            kept_edges, jnp.where(second_pass, edges_in, kept_edges[index]), index, 0
        )
        section_outs = lax.dynamic_update_index_in_dim(
            section_outs, jnp.where(second_pass, out_nodes, section_outs[index]), index, 0
        )
        recv_nodes, recv_edges = from_behind((out_nodes, out_edges), "section", 1)
        back_nodes = from_behind(out_nodes, "section", 1 - sections)
        return (recv_nodes, recv_edges, back_nodes, kept_nodes, kept_edges, section_outs)

    forward_init = (
        zero_nodes,
        zero_edges,
        zero_nodes,
        jnp.zeros((batches, node_count, width), jnp.float32),
        jnp.zeros_like(edge_feats),
        jnp.zeros((batches, node_count, width), jnp.bfloat16),
    )
    unused_nodes, unused_edges, unused_back, kept_nodes, kept_edges, section_outs = lax.fori_loop(
        0, 2 * sections + batches - 1, forward_step, forward_init
    )
    grads_zero = tuple((jnp.zeros(item.shape, jnp.float32) for item in weights))

    def backward_step(step_index, carry):
        recv_grad_nodes, recv_grad_edges, grads, input_grads = carry
        item = step_index - (sections - 1 - place)
        live = (item >= 0) & (item < batches)
        index = jnp.clip(item, 0, batches - 1)
        nodes_grad_out = jnp.where(
            is_last,
            lax.dynamic_index_in_dim(cotangent, index, 0, keepdims=False).astype(jnp.float32),
            recv_grad_nodes.astype(jnp.float32),
        )
        edges_grad_out = jnp.where(is_last, 0.0, recv_grad_edges.astype(jnp.float32))
        nearest = lax.dynamic_index_in_dim(neighbours, index, 0, keepdims=False)

        def run_back(operand):
            return backward_layer(
                weights, operand[0], operand[1], operand[2], operand[3], operand[4]
            )

        def skip_back(operand):
            return (zero_nodes, zero_edges, grads_zero)

        nodes_grad, edges_grad, terms = lax.cond(
            live,
            run_back,
            skip_back,
            (kept_nodes[index], kept_edges[index], nearest, nodes_grad_out, edges_grad_out),
        )
        grads = tuple((total + term for total, term in zip(grads, terms)))
        input_grads = lax.dynamic_update_index_in_dim(
            input_grads, jnp.where(live, nodes_grad, input_grads[index]), index, 0
        )
        recv_grad_nodes, recv_grad_edges = from_behind((nodes_grad, edges_grad), "section", -1)
        return (recv_grad_nodes, recv_grad_edges, grads, input_grads)

    backward_init = (
        zero_nodes,
        zero_edges,
        grads_zero,
        jnp.zeros((batches, node_count, width), jnp.bfloat16),
    )
    unused_grad_nodes, unused_grad_edges, grads, input_grads = lax.fori_loop(
        0, sections + batches - 1, backward_step, backward_init
    )
    totals = jax.tree.map(lambda part: part.astype(jnp.float32), lax.psum(for_sending(grads), "dp"))
    return (
        section_outs[None],
        input_grads[None],
        totals[0][None],
        totals[1][None],
        totals[2][None],
        totals[3][None],
        totals[4][None],
        totals[5][None],
        totals[6][None],
        totals[7][None],
        totals[8][None],
        totals[9][None],
        totals[10][None],
        totals[11][None],
        totals[12][None],
    )


BF16 = jnp.bfloat16
F32 = jnp.float32
MESH = pl.DeviceIdType.MESH
GELU_A = 0.7978845608028654
GELU_B = 0.044715


def gelu(x):
    return 0.5 * x * (1.0 + jnp.tanh(x * (GELU_A + (GELU_A * GELU_B) * (x * x))))


def gelu_both(x):
    square = x * x
    t = jnp.tanh(x * (GELU_A + (GELU_A * GELU_B) * square))
    half = 0.5 * (1.0 + t)
    slope = half + (0.5 * x) * (1.0 - t * t) * (GELU_A + (3.0 * GELU_A * GELU_B) * square)
    return x * half, slope


def mm(a, b):
    return jnp.dot(a, b, preferred_element_type=F32)


def mm_bt(a, b):
    return lax.dot_general(a, b, (((1,), (1,)), ((), ())), preferred_element_type=F32)


def mm_at(a, b):
    return lax.dot_general(a, b, (((0,), (0,)), ((), ())), preferred_element_type=F32)


def stacked(blocks):
    return jnp.concatenate(blocks, axis=0)


def row_mean(x):
    return jnp.mean(x, axis=-1, keepdims=True)


def normed(x):
    centred = x - row_mean(x)
    scale = lax.rsqrt(row_mean(centred * centred) + 1e-05)
    return centred * scale, scale


def norm_back(grad, unit, scale, gain):
    t = grad * gain
    return scale * (t - row_mean(t) - unit * row_mean(t * unit))


def col_sum(x):
    return jnp.sum(x, axis=0, keepdims=True)


def relay_kernel(
    dims,
    edges_in, near_in, bins, clean, noise, cot, pw_in, mo_in, fi_in, fo_in, ends, gains, shifts, node_b, fb, edge_b, we_own, ws_own, wo_own,
    act, ig, g_fwd, g_bwd, g_dpq, g_small, g_msg, g_upd,
    pw, mo, fi, fo, fwd_t, ep, e0, nb0, nb1, nb2, oht, start, par, eb0, wall_msg, wall_upd, fwd, bwd, sg,
    eg, eg_r, eg_b, msg_o, msg_f, upd_o, upd_f, wo, eb1,
    ecat, wcat, scat, pwn, parn, hin_r, hst, mb_s, mb_r, pq_s, pq_r, rq_s, rq_r,
    un0, un1, un2, hi_s, sc0, sc1, sc2, sci, u_s, slope_s, de, dacc, gp, gpe, dcat, act_t, edge_t,
    x_s, x_r, row_s, row_r, dpqo_r, dmb_s, dmb_r, dh1_s, dh1_r, dh1_f, dh2_s, dn3_s, da2_s, h1_s, a1_s,
    ld_sem, ld_ss, w_sem, nx_ss, nx_rs, hop_ss, hop_rs,
    pq_ss, pq_rs, ag_ss, ag_rs, rq_ss, rq_rs, ag2_ss, ag2_rs,
    mb_ss, mb_rs, x_ss, x_rs, row_ss, row_rs, dpqo_rs, fw_ss, dmb_ss, dmb_rs, dh_ss, dh_rs,
    e1_ss, e1_rs, e2_ss, e2_rs, g_ss, g_rs, relay_ss, ring_ss, ring_rs, sib_ss, sib_rs,
):
    S, B, N, K, Q, D, DE, EP, FF, C = dims
    BN = B * N
    RB = 16
    top = DE + N
    me_s = lax.axis_index("section")
    me_d = lax.axis_index("dp")
    core = lax.rem(me_d, 2)
    pair = me_d - core
    w = lax.div(me_s, 2)
    q = 2 * lax.rem(me_s, 2) + core
    owner_d = pair + lax.div(w, B)
    slot = lax.rem(w, B)
    my_row = pl.multiple_of(slot * N + q * Q, Q)
    own_rows = pl.ds(top, Q)

    def quarter(j):
        return pl.ds(pl.multiple_of(DE + j * Q, Q), Q)

    def is_me(sec, dpi):
        return (sec == me_s) & (dpi == me_d)

    def far(src, dst, ssem, rsem, sec, dpi):
        return pltpu.make_async_remote_copy(
            src_ref=src, dst_ref=dst, send_sem=ssem, recv_sem=rsem,
            device_id={"section": sec, "dp": dpi}, device_id_type=MESH,
        )

    def push(src, dst, ssem, rsem, sec, dpi):
        lax.cond(
            is_me(sec, dpi),
            lambda: pltpu.make_async_copy(src, dst, rsem).start(),
            lambda: far(src, dst, ssem, rsem, sec, dpi).start(),
        )

    def arrive(ref, sem):
        pltpu.make_async_copy(ref, ref, sem).wait()

    def drain(ref, sem, sec, dpi):
        @pl.when(jnp.logical_not(is_me(sec, dpi)))
        def _():
            arrive(ref, sem)

    def worker_of(p, j):
        return 2 * (core * B + p) + j // 2, pair + j % 2

    def peer(k):
        j = lax.rem(q + k, 4)
        return j, 2 * w + lax.div(j, 2), pair + lax.rem(j, 2)

    works_here = lax.div(w, B) == core

    def at(p, first=0, size=16):
        return pl.ds(pl.multiple_of(p * N + first, size), size)

    near = jnp.clip(w - core * B, 0, B - 1)

    weights = [
        pltpu.make_async_copy(src, dst, w_sem.at[n])
        for n, (src, dst) in enumerate(((pw_in, pw), (mo_in, mo), (fi_in, fi), (fo_in, fo)))
    ]
    for weight in weights:
        weight.start()
    barrier = pltpu.get_barrier_semaphore()
    for sec in range(S):
        for c in range(C):
            greeted = (c == pair) | (c == pair + 1) | (w == sec // 2)

            @pl.when(greeted & jnp.logical_not(is_me(sec, c)))
            def _():
                pl.semaphore_signal(
                    barrier, inc=1, device_id={"section": sec, "dp": c}, device_id_type=MESH
                )
    wall_msg[me_s] = we_own[...]
    wall_upd[me_s] = jnp.zeros(wall_upd.shape[1:], BF16)
    wall_upd[me_s, pl.ds(0, DE), pl.ds(0, DE)] = ws_own[...]
    wall_upd[me_s, pl.ds(0, DE), pl.ds(EP, DE)] = wo_own[...]
    bias = edge_b[pl.ds(1, 1), :]
    high = bias.astype(BF16).astype(F32)
    row = lax.broadcasted_iota(jnp.int32, (16, DE), 0)
    wall_upd[me_s, pl.ds(DE, 16), pl.ds(0, DE)] = jnp.where(
        row == 0, high, jnp.where(row == 1, bias - high, 0.0)
    ).astype(BF16)
    eb0[...] = jnp.zeros_like(eb0)
    eb0[:, pl.ds(0, DE)] = edge_b[pl.ds(0, 1), :]
    par[pl.ds(0, 1), :] = gains[0]
    par[pl.ds(1, 1), :] = shifts[0]
    par[pl.ds(2, 1), :] = node_b[0]
    par[pl.ds(3, 5), :] = jnp.zeros((5, D), F32)
    pl.semaphore_wait(barrier, 2 * S - 1 + 2 * (C - 2))

    def section_at(i):
        i = lax.rem(i + S, S)
        return jnp.where(i < S // 2, 2 * i, 2 * (S - i) - 1)

    place = jnp.where(lax.rem(me_s, 2) == 0, w, S - 1 - w)
    sides = ((section_at(place + 1), S // 2), (section_at(place - 1), S // 2 - 1))
    walls = (wall_msg, wall_upd)

    def half_of(which, layer, c):
        size = walls[which].shape[1] // 2
        return walls[which].at[layer, pl.ds(pl.multiple_of(c * size, size), size)]

    def ring_send(which, layer, side, hop):
        sec, reach = sides[side]
        if hop < reach:
            half = half_of(which, layer, core)
            far(half, half, ring_ss.at[which, side, hop], ring_rs.at[which, layer], sec, me_d).start()

    def ring_hop(which, side, hop):
        layer = section_at(place - hop if side == 0 else place + hop)
        half = half_of(which, layer, core)
        arrive(half, ring_rs.at[which, layer])
        ring_send(which, layer, side, hop)
        far(half, half, sib_ss.at[which, layer], sib_rs.at[which, layer], me_s, pair + 1 - core).start()

    hops = [(hop, side) for hop in range(1, S // 2 + 1) for side in range(2) if hop <= sides[side][1]]

    def ring_later(second):
        for hop, side in hops:
            early = (place > 0) & ((place >= hop) if side == 0 else (place + hop <= S))

            @pl.when(early != second)
            def _():
                ring_hop(1, side, hop)

    for side in range(2):
        ring_send(0, me_s, side, 0)

    ep[...] = jnp.zeros_like(ep)
    ep[:, pl.ds(0, DE)] = ends[:, pl.ds(0, DE)]
    ep[:, pl.ds(EP, DE)] = ends[...].astype(F32)[:, DE:].astype(BF16)

    arrays = ((edges_in, e0), (near_in, nb0))

    def quarter_of(n, j):
        return edges_in.at[slot, :, pl.ds(pl.multiple_of(j * Q, Q), Q)] if n == 0 else near_in

    @pl.when(works_here)
    def _():
        for n, (_, dst) in enumerate(arrays):
            pltpu.make_async_copy(quarter_of(n, q), dst, ld_sem.at[n]).start()
            other = q + 1 - 2 * core
            far(quarter_of(n, other), dst, ld_ss.at[n], ld_sem.at[n], me_s, pair + 1 - core).start()

    weights[0].wait()

    def edges_laid_out():
        for weight in weights[1:]:
            weight.wait()

        for n, (_, dst) in enumerate(arrays):
            arrive(dst, ld_sem.at[n])
        by_step = nb0[:, 0, :]
        for p in range(1, B):
            by_step = jnp.where(slot == p, nb0[:, p, :], by_step)
        nb1[...] = jnp.zeros_like(nb1)
        nb1[pl.ds(0, K), pl.ds(0, N)] = by_step.astype(F32)
        nb2[...] = nb1[...].T
        nearest = nb2[pl.ds(pl.multiple_of(q * Q, Q), Q), :]
        lane = (lax.broadcasted_iota(jnp.int32, (Q, EP), 1) - DE).astype(F32)
        for k in range(K):
            rows = pl.ds(k * Q, Q)
            ecat[0, rows, :] = jnp.where(lane == nearest[:, k : k + 1], 1.0, 0.0).astype(BF16)
            ecat[0, rows, pl.ds(0, DE)] = e0[k]
        node = lax.broadcasted_iota(jnp.int32, (N, EP), 0)
        lane = lax.broadcasted_iota(jnp.int32, (N, EP), 1) - DE
        chosen = jnp.where(lane == node, 1.0, 0.0).astype(BF16)
        oht[...] = mm_bt(chosen, ecat[0]).astype(BF16)

        @pl.when(works_here)
        def _():
            for n, (_, dst) in enumerate(arrays):
                arrive(dst, ld_ss.at[n])

    before = lax.rem(me_s + S - 1, S)
    far(pw_in, pwn, nx_ss.at[0], nx_rs.at[0], before, me_d).start()
    far(par, parn, nx_ss.at[1], nx_rs.at[1], before, me_d).start()

    for p in range(B):
        rows = pl.ds(p * N, N)
        phase = jnp.full((1, D), (bins[p].astype(F32) + 0.5) * (math.pi * 0.5 / TBINS), F32)
        start[rows, :] = jnp.cos(phase) * clean[rows, :].astype(F32) + jnp.sin(phase) * noise[rows, :].astype(F32)

    def ring_drain():
        for which in range(2):
            for side in range(2):
                for hop in range(sides[side][1]):
                    arrive(half_of(which, me_s, core), ring_ss.at[which, side, hop])
            for layer in range(S):
                @pl.when(layer != me_s)
                def _():
                    arrive(half_of(which, layer, core), sib_ss.at[which, layer])

    def unpack_messages(t):
        @pl.when(t != me_s)
        def _():
            arrive(half_of(0, t, 1 - core), sib_rs.at[0, t])

        wcat[t, pl.ds(0, DE), :] = wall_msg[t]

    def unpack_updates(t):
        @pl.when(t != me_s)
        def _():
            arrive(half_of(1, t, 1 - core), sib_rs.at[1, t])

        scat[t, pl.ds(0, DE), :] = wall_upd[t, pl.ds(0, DE), pl.ds(0, EP)]
        wo[t, pl.ds(0, DE), :] = wall_upd[t, pl.ds(0, DE), pl.ds(EP, EP)]
        wo[t, pl.ds(DE, N), :] = jnp.zeros((N, EP), BF16)
        eb1[t] = wall_upd[t, pl.ds(DE, 16), pl.ds(0, EP)]

    def rows_out(p, src, dst, ssem, rsem):
        for j in range(4):
            sec, dpi = worker_of(p, j)
            push(src.at[at(p, j * Q, Q)], dst, ssem, rsem, sec, dpi)

    def rows_drain(src, ssem):
        lax.cond(
            works_here,
            lambda: arrive(src.at[pl.ds(0, B * N - Q)], ssem),
            lambda: arrive(src, ssem),
        )

    def spread(rows, half, ref, layer, ssem, rsem, rows_sem):
        arrive(rows, rows_sem)
        for k in range(1, 4):
            _, sec, dpi = peer(k)
            far(rows.at[:, pl.ds(half, half)], ref.at[layer, quarter(q)], ssem, rsem, sec, dpi).start()
        ref[layer, own_rows, :] = rows[:, pl.ds(0, half)]
        ref[layer, quarter(q), :] = rows[:, pl.ds(half, half)]

    def spread_wait(ref, layer, sem):
        arrive(ref.at[layer, pl.ds(DE, 3 * Q)], sem)

    def share(group, src, dst):
        for c in range(C):
            push(src, dst.at[me_d], g_ss.at[group, c], g_rs.at[group, me_d], me_s, c)

    def share_wait(group, src, dst):
        for c in range(C):
            arrive(dst.at[c], g_rs.at[group, c])
            drain(src, g_ss.at[group, c], me_s, c)

    def share_near(group, src, dst):
        for c in range(C):
            @pl.when((c == pair) | (c == pair + 1) | (core == c % 2))
            def _():
                push(src, dst(me_d), g_ss.at[group, c], g_rs.at[group, me_d], me_s, c)

    def share_relay(group, src, dst):
        for c in range(C):
            @pl.when((c != me_d) & (core == c % 2))
            def _():
                arrive(dst(c), g_rs.at[group, c])
                far(dst(c), dst(c), relay_ss.at[group - 2, c // 2], g_rs.at[group, c], me_s, pair + 1 - core).start()

    def share_near_wait(group, src, dst):
        for c in range(C):
            @pl.when((c == me_d) | (core != c % 2))
            def _():
                arrive(dst(c), g_rs.at[group, c])

            @pl.when((c != me_d) & ((c == pair) | (c == pair + 1) | (core == c % 2)))
            def _():
                arrive(src, g_ss.at[group, c])

            @pl.when((c != me_d) & (core == c % 2))
            def _():
                arrive(dst(c), relay_ss.at[group - 2, c // 2])

    steps = 4
    KC = K // steps
    RC = KC * Q

    def messages(t):
        own = wcat[t, own_rows, :].astype(F32)
        total = jnp.zeros((Q, D), F32)
        for i in range(steps):
            pre = mm(ecat[t, pl.ds(i * RC, RC), :], wcat[t, pl.ds(0, top), :])
            for k in range(KC):
                total = total + gelu(pre[k * Q : (k + 1) * Q] + own)
        mb_s[...] = (total * (1.0 / K)).astype(BF16)

    def edge_update(t):
        own = scat[t, own_rows, :].astype(F32)
        bias = eb1[t, pl.ds(0, 1), :].astype(F32) + eb1[t, pl.ds(1, 1), :].astype(F32)
        for i in range(steps):
            pe = mm(ecat[t, pl.ds(i * RC, RC), :], scat[t, pl.ds(0, top), :])
            act_e = stacked([gelu(pe[k * Q : (k + 1) * Q] + own).astype(BF16) for k in range(KC)])
            z = mm(act_e, wo[t])
            for k in range(KC):
                rows = pl.ds(i * RC + k * Q, Q)
                ecat[t + 1, rows, :] = (ecat[t, rows, :].astype(F32) + z[k * Q : (k + 1) * Q] + bias).astype(BF16)

    chunks = 4
    FC = FF // chunks

    def node_forward(step):
        @pl.when(step < S)
        def _():
            arrive(pwn, nx_rs.at[0])
            arrive(parn, nx_rs.at[1])
            arrive(pw, nx_ss.at[0])
            arrive(par, nx_ss.at[1])

        @pl.when(step == 0)
        def _():
            hi_s[...] = start[...]

        @pl.when(step > 0)
        def _():
            arrive(hin_r, hop_rs)
            first = jnp.where(me_s == 0, 1.0, 0.0)
            for i in range(0, BN, RB):
                rows = pl.ds(i, RB)
                hi_s[rows, :] = hin_r[rows, :].astype(F32) + first * start[rows, :]

        later = lax.rem(me_s + 1, S)

        def turn(n, carry):
            p = lax.rem(near + n, B)
            whole = at(p, 0, N)
            arrive(mb_r.at[whole], mb_rs.at[p])
            mean = mm(mb_r[whole, :], mo[...])
            for i in range(0, N, RB):
                rows = at(p, i)
                h1 = hi_s[rows, :] + mean[i : i + RB] + node_b[1]
                h1_s[rows, :] = h1
                unit, scale = normed(h1)
                un1[rows, :] = unit
                sc1[rows, :] = scale
                fwd[rows, pl.ds(2 * D, D)] = (unit * gains[1] + shifts[1]).astype(BF16)
                fwd[rows, pl.ds(D, D)] = mb_r[rows, :]
            a2 = fwd[whole, pl.ds(2 * D, D)]
            y = jnp.zeros((N, D), F32)
            for c in range(chunks):
                cols = pl.ds(c * FC, FC)
                u = mm(a2, fi[:, cols])
                v = []
                for i in range(0, N, RB):
                    block = u[i : i + RB] + fb[:, cols]
                    u_s[at(p, i), cols] = block
                    v.append(gelu(block).astype(BF16))
                y = y + mm(stacked(v), fo[cols, :])
            last = jnp.where(me_s == S - 1, 1.0, 0.0)
            for i in range(0, N, RB):
                rows = at(p, i)
                h2 = h1_s[rows, :] + y[i : i + RB] + node_b[2]
                rounded = h2.astype(BF16)
                hst[rows, :] = rounded
                unit, scale = normed(h2)
                un2[rows, :] = unit
                sc2[rows, :] = scale
                fwd[rows, pl.ds(3 * D, D)] = (unit * gains[2] + shifts[2]).astype(BF16)
                pair_norm(rows, rounded.astype(F32) + last * start[rows, :], parn)
            rq = mm(fwd[whole, pl.ds(3 * D, D)], ep[...])
            for i in range(0, N, RB):
                rows = at(p, i)
                rq_s[rows, pl.ds(0, EP)] = (rq[i : i + RB, :EP] + eb0[...]).astype(BF16)
                rq_s[rows, pl.ds(EP, EP)] = rq[i : i + RB, EP:].astype(BF16)
            pair_rows(p, pwn, parn)

            @pl.when(me_s < S - 1)
            def _():
                rows_out(p, rq_s, rq_r, rq_ss, rq_rs)

            @pl.when(step < 2 * S - 1)
            def _():
                rows_out(p, pq_s, pq_r, pq_ss, pq_rs)

            @pl.when((n == 0) & works_here)
            def _():
                pass_on(step)

            return carry

        lax.fori_loop(0, B, turn, 0)

        @pl.when(step < 2 * S - 1)
        def _():
            far(hst, hin_r, hop_ss, hop_rs, later, me_d).start()

        @pl.when(step >= S)
        def _():
            act[...] = hst[...]
            for i in range(0, BN, RB):
                rows = pl.ds(i, RB)
                unit, scale = normed(hi_s[rows, :])
                hi_s[rows, :] = unit
                sci[rows, :] = scale
                fwd[rows, pl.ds(0, D)] = (unit * gains[0] + shifts[0]).astype(BF16)
                for c in range(chunks):
                    cols = pl.ds(c * FC, FC)
                    slope_s[rows, cols] = gelu_both(u_s[rows, cols])[1].astype(BF16)
            for n in range(4):
                fwd_t[pl.ds(n * D, D), :] = fwd[:, pl.ds(n * D, D)].T
            share(0, fwd_t, g_fwd)

    def pair_norm(rows, hidden, first):
        unit, scale = normed(hidden)
        un0[rows, :] = unit
        sc0[rows, :] = scale
        a1_s[rows, :] = (unit * first[pl.ds(0, 1), :] + first[pl.ds(1, 1), :]).astype(BF16)

    def pair_rows(p, weight, first):
        whole = at(p, 0, N)
        for half in range(2):
            cols = pl.ds(half * D, D)
            value = mm(a1_s[whole, :], weight[:, cols])
            if half == 0:
                value = value + first[pl.ds(2, 1), :]
            pq_s[whole, cols] = value.astype(BF16)

    def pass_on(step):
        t = lax.rem(step, S)

        @pl.when(t < S - 1)
        def _():
            spread(rq_r, EP, scat, t, ag2_ss, ag2_rs, rq_rs)

        @pl.when(step < 2 * S - 1)
        def _():
            spread(pq_r, D, wcat, lax.rem(step + 1, S), ag_ss, ag_rs, pq_rs)

    def node_forward_drain():
        arrive(hst, hop_ss)
        rows_drain(pq_s, pq_ss)

        @pl.when(me_s < S - 1)
        def _():
            rows_drain(rq_s, rq_ss)

    @pl.when(me_s == 0)
    def _():
        for i in range(0, BN, RB):
            rows = pl.ds(i, RB)
            pair_norm(rows, start[rows, :], par)
        for p in range(B):
            pair_rows(p, pw, par)
            rows_out(p, pq_s, pq_r, pq_ss, pq_rs)

    def message_slope(t):
        own = wcat[t, own_rows, :].astype(F32)
        for i in range(steps):
            pre = mm(ecat[t, pl.ds(i * RC, RC), :], wcat[t, pl.ds(0, top), :])
            for k in range(KC):
                gp[t, pl.ds(i * RC + k * Q, Q), :] = gelu_both(pre[k * Q : (k + 1) * Q] + own)[1].astype(BF16)

    def edge_slope(t):
        own = scat[t, own_rows, :].astype(F32)
        values = []
        for i in range(steps):
            pe = mm(ecat[t, pl.ds(i * RC, RC), :], scat[t, pl.ds(0, top), :])
            for k in range(KC):
                value, slope = gelu_both(pe[k * Q : (k + 1) * Q] + own)
                values.append(value.astype(BF16))
                gpe[t, pl.ds(i * RC + k * Q, Q), :] = slope.astype(BF16)
        act_t[t] = stacked(values).T

    def prepare(t):
        message_slope(t)
        edge_t[t] = ecat[t].T

        @pl.when(t > 0)
        def _():
            edge_slope(t - 1)

    def forward_step(step, carry):
        t = lax.rem(step, S)

        @pl.when(step < S)
        def _():
            unpack_messages(t)

        spread_wait(wcat, t, ag_rs)
        messages(t)
        spread_wait(wcat, t, ag_ss)
        push(mb_s, mb_r.at[pl.ds(my_row, Q)], mb_ss, mb_rs.at[slot], t, owner_d)

        for second in range(2):
            @pl.when(step == second)
            def _():
                ring_later(second == 1)

        @pl.when((step == 0) & (me_s == 0))
        def _():
            rows_drain(pq_s, pq_ss)

        @pl.when((step > 0) & (me_s == lax.rem(step + S - 1, S)))
        def _():
            node_forward_drain()

        @pl.when(me_s == t)
        def _():
            node_forward(step)

        @pl.when((me_s != t) & (step >= S))
        def _():
            prepare(t)

        @pl.when(jnp.logical_not((me_s == t) & works_here))
        def _():
            pass_on(step)

        @pl.when(t < S - 1)
        def _():
            @pl.when(step < S)
            def _():
                unpack_updates(t)

            spread_wait(scat, t, ag2_rs)
            edge_update(t)
            spread_wait(scat, t, ag2_ss)

        drain(mb_s, mb_ss, t, owner_d)
        return carry

    for hop, side in hops:
        if (hop, side) == (2, 0):
            edges_laid_out()
        ring_hop(0, side, hop)
    for side in range(2):
        ring_send(1, me_s, side, 0)
    spread(pq_r, D, wcat, 0, ag_ss, ag_rs, pq_rs)
    lax.fori_loop(0, 2 * S, forward_step, 0)
    ring_drain()

    @pl.when(me_s != S - 1)
    def _():
        arrive(half_of(1, S - 1, 1 - core), sib_rs.at[1, S - 1])

    def edge_back(t):
        b2, n2 = lax.rem(t, 2), lax.rem(t + 1, 2)
        total = jnp.zeros((Q, EP), F32)
        for i in range(steps):
            chunk = pl.ds(i * RC, RC)
            carry = mm_bt(dcat[b2, chunk, pl.ds(0, D)], wcat[t, pl.ds(0, top), :])
            low = []
            for k in range(KC):
                rows = pl.ds(i * RC + k * Q, Q)
                low.append((dacc[rows, :] + carry[k * Q : (k + 1) * Q]).astype(BF16))
                de[n2, rows, :] = low[-1]
            dw = mm_bt(stacked(low), wo[t - 1])
            for k in range(KC):
                rows = pl.ds(i * RC + k * Q, Q)
                d = (gpe[t - 1, rows, :].astype(F32) * dw[k * Q : (k + 1) * Q]).astype(BF16)
                total = total + d.astype(F32)
                dcat[n2, rows, pl.ds(D, EP)] = d
        row_s[:, pl.ds(2 * D, EP)] = total.astype(BF16)
        x_s[:, pl.ds(D, EP)] = mm(oht[...], dcat[n2, :, pl.ds(D, EP)]).astype(BF16)

    def edge_pass(t):
        b3 = lax.rem(t, 2)
        for i in range(steps):
            rows = pl.ds(i * RC, RC)
            d = dcat[b3, rows, pl.ds(D, EP)]
            dacc[rows, :] = de[b3, rows, :].astype(F32) + mm_bt(d, scat[t, pl.ds(0, top), :])

    blocks = 2 * C
    my_block = lax.rem(me_s, 2) * C + me_d
    BW, HM, HU = msg_o.shape[2], msg_o.shape[1], upd_o.shape[1]

    def block_of(t, half, c, size):
        return eg.at[t, half, pl.ds(0, size), pl.ds(pl.multiple_of(c * BW, BW), BW)]

    def blocks_out(t, size):
        for k in range(blocks):
            @pl.when(k != my_block)
            def _():
                far(
                    block_of(t, k // C, k % C, size), eg_r.at[t, my_block, pl.ds(0, size)],
                    e1_ss.at[t, k], e1_rs.at[t, my_block], 2 * w + k // C, k % C,
                ).start()

    def edge_grads(t):
        grad = mm(edge_t[t, pl.ds(0, DE), :], dcat[lax.rem(t, 2), :, pl.ds(0, D)]).astype(BF16)
        for half in range(2):
            eg[t, half, pl.ds(0, HM), :] = grad[half * HM : (half + 1) * HM]

        @pl.when(t > 0)
        def _():
            n2 = lax.rem(t + 1, 2)
            edges = mm(edge_t[t - 1, pl.ds(0, DE), :], dcat[n2, :, pl.ds(D, EP)])
            outs = mm(act_t[t - 1, pl.ds(0, DE), :], de[n2])
            bias = jnp.sum(de[n2].astype(F32), axis=0, keepdims=True)
            grad = jnp.concatenate([edges, outs], axis=1).astype(BF16)
            eg[t, 0, pl.ds(HM, HU), :] = grad[:HU]
            eg[t, 1, pl.ds(HM, DE - HU), :] = grad[HU:]
            eg[t, 1, pl.ds(HM + DE - HU, 16), pl.ds(0, EP)] = jnp.broadcast_to(bias, (16, EP)).astype(BF16)
            eg[t, 1, pl.ds(HM + DE - HU, 16), pl.ds(EP, EP)] = jnp.zeros((16, EP), BF16)
            eg[t, 1, pl.ds(HM + DE - HU + 16, 2 * HU - DE - 16), :] = jnp.zeros((2 * HU - DE - 16, 2 * EP), BF16)
            blocks_out(t, HM + HU)

        @pl.when(t == 0)
        def _():
            blocks_out(t, HM)

    def blocks_sum(t, size):
        eg_r[t, my_block, pl.ds(0, size), :] = block_of(t, lax.rem(me_s, 2), me_d, size)[...]
        for k in range(blocks):
            @pl.when(k != my_block)
            def _():
                arrive(eg_r.at[t, k, pl.ds(0, size)], e1_rs.at[t, k])
                arrive(block_of(t, k // C, k % C, size), e1_ss.at[t, k])
        total = eg_r[t, 0, pl.ds(0, size), :].astype(F32)
        for k in range(1, blocks):
            total = total + eg_r[t, k, pl.ds(0, size), :].astype(F32)
        eg_b[t, pl.ds(0, size), :] = total.astype(BF16)
        push(eg_b.at[t, pl.ds(0, HM)], msg_o.at[me_s], e2_ss.at[0, t], e2_rs.at[0, me_s], t, me_d)
        if size > HM:
            push(eg_b.at[t, pl.ds(HM, HU)], upd_o.at[me_s], e2_ss.at[1, t], e2_rs.at[1, me_s], t - 1, me_d)

    def gather_blocks():
        for k in range(1, 4):
            j, sec, dpi = peer(k)
            rows = pl.ds(pl.multiple_of(j * Q, Q), Q)
            far(x_s.at[rows], x_r.at[q], x_ss, x_rs, sec, dpi).start()
        x_r[q] = x_s[pl.ds(pl.multiple_of(q * Q, Q), Q), :]

    def gather_wait():
        arrive(x_r.at[pl.ds(0, 3)], x_rs)
        arrive(x_s.at[pl.ds(0, 3 * Q)], x_ss)
        total = x_r[0].astype(F32)
        for j in range(1, 4):
            total = total + x_r[j].astype(F32)
        return total

    def message_back(t):
        b2 = lax.rem(t, 2)
        dm = dmb_r[...].astype(F32)
        total = jnp.zeros((Q, D), F32)
        for k in range(K):
            rows = pl.ds(k * Q, Q)
            d = (gp[t, rows, :].astype(F32) * dm).astype(BF16)
            total = total + d.astype(F32)
            dcat[b2, rows, pl.ds(0, D)] = d
        row_s[:, pl.ds(0, D)] = total.astype(BF16)
        x_s[:, pl.ds(0, D)] = mm(oht[...], dcat[b2, :, pl.ds(0, D)]).astype(BF16)

    def node_backward():
        @pl.when(me_s < S - 1)
        def _():
            arrive(dh1_r, dh_rs)

        def turn(n, carry):
            p = lax.rem(near + n, B)
            whole = at(p, 0, N)

            @pl.when(me_s < S - 1)
            def _():
                arrive(row_r.at[whole], row_rs.at[p])
                dn0 = mm_bt(row_r[whole, pl.ds(0, 2 * D)], pwn[...])
                dn3 = mm_bt(row_r[whole, pl.ds(2 * D, 2 * EP)], ep[...])
                for i in range(0, N, RB):
                    rows = at(p, i)
                    dn = dn3[i : i + RB]
                    dn3_s[rows, :] = dn
                    first = norm_back(dn0[i : i + RB], un0[rows, :], sc0[rows, :], parn[pl.ds(0, 1), :])
                    dh = (dh1_r[rows, :].astype(F32) + first).astype(BF16).astype(F32)
                    dh2_s[rows, :] = dh + norm_back(dn, un2[rows, :], sc2[rows, :], gains[2])

            @pl.when(me_s == S - 1)
            def _():
                dh2_s[whole, :] = cot[whole, :].astype(F32)

            dy = dh2_s[whole, :].astype(BF16)
            bwd[whole, pl.ds(D, D)] = dy
            da2 = jnp.zeros((N, D), F32)
            for c in range(chunks):
                cols = pl.ds(c * FC, FC)
                dv = mm_bt(dy, fo[cols, :])
                du = stacked(
                    [(slope_s[at(p, i), cols].astype(F32) * dv[i : i + RB]).astype(BF16) for i in range(0, N, RB)]
                )
                da2 = da2 + mm_bt(du, fi[:, cols])
            for i in range(0, N, RB):
                rows = at(p, i)
                block = da2[i : i + RB]
                da2_s[rows, :] = block
                dh1 = dh2_s[rows, :] + norm_back(block, un1[rows, :], sc1[rows, :], gains[1])
                dh1_f[rows, :] = dh1
                bwd[rows, pl.ds(0, D)] = (dh1 * (1.0 / K)).astype(BF16)
            dmb_s[whole, :] = mm_bt(bwd[whole, pl.ds(0, D)], mo[...]).astype(BF16)
            rows_out(p, dmb_s, dmb_r, dmb_ss, dmb_rs)
            return carry

        lax.fori_loop(0, B, turn, 0)

        @pl.when(me_s > 0)
        def _():
            dh1_s[...] = dh1_f[...].astype(BF16)
            far(dh1_s, dh1_r, dh_ss, dh_rs, me_s - 1, me_d).start()

        @pl.when(me_s < S - 1)
        def _():
            far(row_r.at[:, pl.ds(0, 2 * D)], dpqo_r, fw_ss, dpqo_rs, me_s + 1, me_d).start()
            drs = row_r[:, pl.ds(2 * D, 2 * EP)]
            bwd[:, pl.ds(2 * D, 2 * EP)] = drs
            dn = dn3_s[...]
            sg[pl.ds(11, 1), :] = col_sum(dn * un2[...])
            sg[pl.ds(12, 1), :] = col_sum(dn)
            sg[pl.ds(16, 1), pl.ds(0, EP)] = col_sum(drs[:, :EP].astype(F32))

        @pl.when(me_s == S - 1)
        def _():
            bwd[:, pl.ds(2 * D, 2 * EP)] = jnp.zeros((B * N, 2 * EP), BF16)
            sg[pl.ds(11, 1), :] = jnp.zeros((1, D), F32)
            sg[pl.ds(12, 1), :] = jnp.zeros((1, D), F32)
            sg[pl.ds(16, 1), pl.ds(0, EP)] = jnp.zeros((1, EP), F32)

        share(1, bwd, g_bwd)
        sg[pl.ds(13, 1), :] = col_sum(dh2_s[...])
        sg[pl.ds(8, 1), :] = col_sum(da2_s[...] * un1[...])
        sg[pl.ds(9, 1), :] = col_sum(da2_s[...])
        sg[pl.ds(10, 1), :] = col_sum(dh1_f[...])

    def node_backward_drain():
        rows_drain(dmb_s, dmb_ss)

        @pl.when(me_s > 0)
        def _():
            arrive(dh1_s, dh_ss)

        @pl.when(me_s < S - 1)
        def _():
            arrive(row_r.at[:, pl.ds(0, 2 * D)], fw_ss)

    dacc[...] = jnp.zeros_like(dacc)

    def backward_step(step, carry):
        t = S - 1 - step

        @pl.when(me_s == t)
        def _():
            node_backward()

        @pl.when(((t == S - 1) & (me_s >= S - 2)) | (me_s == t - 2))
        def _():
            prepare(me_s)

        @pl.when(t < S - 1)
        def _():
            edge_pass(t)

        @pl.when(t + 2 < S)
        def _():
            blocks_sum(t + 2, HM + HU)

        @pl.when(t == 0)
        def _():
            blocks_sum(1, HM + HU)

        arrive(dmb_r, dmb_rs)
        message_back(t)

        @pl.when(t > 0)
        def _():
            edge_back(t)

        @pl.when(t == 0)
        def _():
            x_s[:, pl.ds(D, EP)] = jnp.zeros((N, EP), BF16)

        gather_blocks()
        other = gather_wait().astype(BF16)
        row_s[:, pl.ds(D, D)] = other[:, :D]
        row_s[:, pl.ds(2 * D + EP, EP)] = other[:, D:]
        dpq = row_s.at[:, pl.ds(0, 2 * D)]

        @pl.when(t > 0)
        def _():
            push(row_s, row_r.at[pl.ds(my_row, Q)], row_ss, row_rs.at[slot], t - 1, owner_d)

        @pl.when(t == 0)
        def _():
            push(dpq, dpqo_r.at[pl.ds(my_row, Q)], row_ss, dpqo_rs, t, owner_d)

        edge_grads(t)

        @pl.when(t > 0)
        def _():
            drain(row_s, row_ss, t - 1, owner_d)

        @pl.when(t == 0)
        def _():
            drain(dpq, row_ss, t, owner_d)

        @pl.when(me_s == t)
        def _():
            node_backward_drain()

        return carry

    lax.fori_loop(0, S, backward_step, 0)

    arrive(dpqo_r, dpqo_rs)
    across = [pl.ds(p * N, N) for p in range(B)]
    for p in range(B):
        share_near(2 + p, dpqo_r.at[across[p]], lambda c, p=p: g_dpq.at[c, across[p]])
    dpq = dpqo_r[...]
    sg[pl.ds(2, 1), :] = col_sum(dpq[:, :D].astype(F32))
    dn = mm_bt(dpq, pw[...])
    unit = hi_s[...]
    sg[pl.ds(0, 1), :] = col_sum(dn * unit)
    sg[pl.ds(1, 1), :] = col_sum(dn)
    share(2 + B, sg, g_small)
    ig[...] = (dh1_f[...] + norm_back(dn, unit, sci[...], gains[0])).astype(BF16)
    blocks_sum(0, HM)
    for p in range(B):
        share_relay(2 + p, dpqo_r.at[across[p]], lambda c, p=p: g_dpq.at[c, across[p]])
    def combine(kind, src, final):
        for sec in range(S):
            arrive(src.at[sec], e2_rs.at[kind, sec])
        for half in range(2):
            total = src[half].astype(F32)
            for sec in range(half + 2, S, 2):
                total = total + src[sec].astype(F32)
            final[half] = total.astype(BF16)

    @pl.when(me_s < S - 1)
    def _():
        combine(1, upd_o, upd_f)

    @pl.when(me_s == S - 1)
    def _():
        upd_f[...] = jnp.zeros_like(upd_f)

    share(4 + B, upd_f, g_upd)
    combine(0, msg_o, msg_f)
    share(3 + B, msg_f, g_msg)
    for t in range(S):
        drain(eg_b.at[t, pl.ds(0, HM)], e2_ss.at[0, t], t, me_d)
        if t > 0:
            drain(eg_b.at[t, pl.ds(HM, HU)], e2_ss.at[1, t], t - 1, me_d)
    share_wait(0, fwd_t, g_fwd)
    share_wait(1, bwd, g_bwd)
    for p in range(B):
        share_near_wait(2 + p, dpqo_r.at[across[p]], lambda c, p=p: g_dpq.at[c, across[p]])
    share_wait(2 + B, sg, g_small)
    share_wait(3 + B, msg_f, g_msg)
    share_wait(4 + B, upd_f, g_upd)


def run_relay(dims, operands):
    S, B, N, K, Q, D, DE, EP, FF, C = dims
    R = K * Q
    BN = B * N
    tall = DE + N + Q
    vm = pl.BlockSpec(memory_space=pltpu.VMEM)
    hbm = pl.BlockSpec(memory_space=pl.ANY)
    dma = pltpu.SemaphoreType.DMA
    sds = jax.ShapeDtypeStruct
    BW = D // C
    tile = 32
    held = -(-(DE + 16) // tile) * tile
    scratch = [
        pltpu.VMEM((D, 2 * D), BF16),
        pltpu.VMEM((D, D), BF16),
        pltpu.VMEM((D, FF), BF16),
        pltpu.VMEM((FF, D), BF16),
        pltpu.VMEM((4 * D, BN), BF16),
        pltpu.VMEM((D, 2 * EP), BF16),
        pltpu.VMEM((K, Q, DE), BF16),
        pltpu.VMEM((K, B, N), jnp.int32),
        pltpu.VMEM((128, 128), F32),
        pltpu.VMEM((128, 128), F32),
        pltpu.VMEM((N, R), BF16),
        pltpu.VMEM((BN, D), F32),
        pltpu.VMEM((8, D), F32),
        pltpu.VMEM((1, EP), F32),
        pltpu.VMEM((S, DE, D), BF16),
        pltpu.VMEM((S, held, 2 * EP), BF16),
        pltpu.VMEM((BN, 4 * D), BF16),
        pltpu.VMEM((BN, 2 * D + 2 * EP), BF16),
        pltpu.VMEM((24, D), F32),
        pltpu.VMEM((S, 2, (DE + held) // 2, D), BF16),
        pltpu.VMEM((S, 2 * C, (DE + held) // 2, BW), BF16),
        pltpu.VMEM((S, (DE + held) // 2, BW), BF16),
        pltpu.VMEM((S, DE // 2, BW), BF16),
        pltpu.VMEM((2, DE // 2, BW), BF16),
        pltpu.VMEM((S, held // 2, BW), BF16),
        pltpu.VMEM((2, held // 2, BW), BF16),
        pltpu.VMEM((S, EP, EP), BF16),
        pltpu.VMEM((S, 16, EP), BF16),
        pltpu.VMEM((S, R, EP), BF16),
        pltpu.VMEM((S, tall, D), BF16),
        pltpu.VMEM((S, tall, EP), BF16),
        pltpu.VMEM((D, 2 * D), BF16),
        pltpu.VMEM((8, D), F32),
        pltpu.VMEM((BN, D), BF16),
        pltpu.VMEM((BN, D), BF16),
        pltpu.VMEM((Q, D), BF16),
        pltpu.VMEM((BN, D), BF16),
        pltpu.VMEM((BN, 2 * D), BF16),
        pltpu.VMEM((Q, 2 * D), BF16),
        pltpu.VMEM((BN, 2 * EP), BF16),
        pltpu.VMEM((Q, 2 * EP), BF16),
        pltpu.VMEM((BN, D), F32),
        pltpu.VMEM((BN, D), F32),
        pltpu.VMEM((BN, D), F32),
        pltpu.VMEM((BN, D), F32),
        pltpu.VMEM((BN, 1), F32),
        pltpu.VMEM((BN, 1), F32),
        pltpu.VMEM((BN, 1), F32),
        pltpu.VMEM((BN, 1), F32),
        pltpu.VMEM((BN, FF), F32),
        pltpu.VMEM((BN, FF), BF16),
        pltpu.VMEM((2, R, EP), BF16),
        pltpu.VMEM((R, EP), F32),
        pltpu.VMEM((S, R, D), BF16),
        pltpu.VMEM((S, R, EP), BF16),
        pltpu.VMEM((2, R, D + EP), BF16),
        pltpu.VMEM((S, EP, R), BF16),
        pltpu.VMEM((S, EP, R), BF16),
        pltpu.VMEM((N, D + EP), BF16),
        pltpu.VMEM((4, Q, D + EP), BF16),
        pltpu.VMEM((Q, 2 * D + 2 * EP), BF16),
        pltpu.VMEM((BN, 2 * D + 2 * EP), BF16),
        pltpu.VMEM((BN, 2 * D), BF16),
        pltpu.VMEM((BN, D), BF16),
        pltpu.VMEM((Q, D), BF16),
        pltpu.VMEM((BN, D), BF16),
        pltpu.VMEM((BN, D), BF16),
        pltpu.VMEM((BN, D), F32),
        pltpu.VMEM((BN, D), F32),
        pltpu.VMEM((BN, D), F32),
        pltpu.VMEM((BN, D), F32),
        pltpu.VMEM((BN, D), F32),
        pltpu.VMEM((BN, D), BF16),
        dma((2,)), dma((2,)), dma((4,)), dma((2,)), dma((2,)), dma, dma,
        dma, dma, dma, dma, dma, dma, dma, dma,
        dma, dma((B,)), dma, dma, dma, dma((B,)), dma,
        dma, dma, dma, dma, dma,
        dma((S, 2 * C)), dma((S, 2 * C)), dma((2, S)), dma((2, S)), dma((5 + B, C)), dma((5 + B, C)),
        dma((B, C // 2)), dma((2, 2, S // 2)), dma((2, S)), dma((2, S)), dma((2, S)),
    ]
    return pl.pallas_call(
        functools.partial(relay_kernel, dims),
        out_shape=(
            sds((BN, D), BF16),
            sds((BN, D), BF16),
            sds((C, 4 * D, BN), BF16),
            sds((C, BN, 2 * D + 2 * EP), BF16),
            sds((C, BN, 2 * D), BF16),
            sds((C, 24, D), F32),
            sds((C, 2, DE // 2, BW), BF16),
            sds((C, 2, held // 2, BW), BF16),
        ),
        in_specs=[hbm, hbm, pl.BlockSpec(memory_space=pltpu.SMEM)] + [vm] * 3 + [hbm] * 4 + [vm] * 9,
        out_specs=(vm,) * 2 + (hbm,) * 6,
        scratch_shapes=scratch,
        compiler_params=pltpu.CompilerParams(
            collective_id=0, has_side_effects=True, vmem_limit_bytes=62 * 1024 * 1024
        ),
    )(*operands)


def gradient_kernel(
    dims,
    fwd, bwd, dpq, small, edge, upd, fi, fo, fb, act, ig,
    g_pair, g_edge, g_out, g_fi, g_fo, g_ep, g_self, g_eout, g_gain, g_shift, g_nb, g_fb, g_eb, act_out, ig_out,
    fwd_v, bwd_v, dpq_v, fi_v, fo_v, gfi_v, gfo_v, pair_v, out_v, edge_v, upd_v, in_sems, sems,
):
    S, B, N, K, Q, D, DE, EP, FF, C = dims
    chunks = 4
    FC = FF // chunks

    def part(c, size=D):
        return pl.ds(c * size, size)

    loads = {}

    def load(name, src, dst):
        loads[name] = pltpu.make_async_copy(src, dst, in_sems.at[len(loads)])
        loads[name].start()

    BN = B * N

    def load_kept(n):
        for c in range(C):
            load((n, c), fwd.at[c, part(n)], fwd_v.at[n, :, part(c, BN)])

    def wait_kept(n):
        for c in range(C):
            loads[n, c].wait()
        return fwd_v[n]

    load_kept(2)
    load("dy", bwd.at[:, part(1)], bwd_v.at[1])
    for c in range(chunks):
        load(("fi", c), fi.at[:, part(c, FC)], fi_v.at[c])
        load(("fo", c), fo.at[part(c, FC)], fo_v.at[c])
    load_kept(0)
    load("dpq0", dpq.at[:, part(0)], dpq_v.at[0])
    load("dpq1", dpq.at[:, part(1)], dpq_v.at[1])
    load_kept(1)
    load("dmsg", bwd.at[:, part(0)], bwd_v.at[0])
    load_kept(3)
    load("drs", bwd.at[:, part(2)], bwd_v.at[2])
    load("edge", edge, edge_v)
    load("upd", upd, upd_v)
    stores = []

    def out(src, dst):
        copy = pltpu.make_async_copy(src, dst, sems.at[len(stores)])
        copy.start()
        stores.append(copy)

    out(act, act_out)
    out(ig, ig_out)
    a2_t = wait_kept(2)
    a2 = a2_t.T
    loads["dy"].wait()
    dy = bwd_v[1]
    for c in range(chunks):
        cols = part(c, FC)
        loads["fi", c].wait()
        loads["fo", c].wait()
        u = mm(a2, fi_v[c])
        dv = mm_bt(dy, fo_v[c])
        v, du = [], []
        for i in range(0, C * BN, 16):
            value, slope = gelu_both(u[i : i + 16] + fb[:, cols])
            v.append(value.astype(BF16))
            du.append((slope * dv[i : i + 16]).astype(BF16))
        v, du = stacked(v), stacked(du)
        g_fb[:, cols] = col_sum(du.astype(F32))
        gfi_v[c] = mm(a2_t, du)
        out(gfi_v.at[c], g_fi.at[0, :, cols])
        gfo_v[c] = mm_at(v, dy)
        out(gfo_v.at[c], g_fo.at[0, cols])
    a1_t = wait_kept(0)
    for c in range(2):
        loads["dpq%d" % c].wait()
        pair_v[c] = mm(a1_t, dpq_v[c])
        out(pair_v.at[c], g_pair.at[0, :, part(c)])
    loads["dmsg"].wait()
    out_v[...] = mm(wait_kept(1), bwd_v[0]) * float(K)
    out(out_v, g_out.at[0])
    loads["drs"].wait()
    ends = mm(wait_kept(3), bwd_v[2])
    g_ep[0] = jnp.concatenate([ends[:, :DE], ends[:, EP : EP + DE]], axis=1)
    total = small[0]
    for c in range(1, C):
        total = total + small[c]
    for i, rows in enumerate(((0, 1, 2), (8, 9, 10), (11, 12, 13))):
        g_gain[i] = total[rows[0] : rows[0] + 1]
        g_shift[i] = total[rows[1] : rows[1] + 1]
        g_nb[i] = total[rows[2] : rows[2] + 1]
    g_eb[0, pl.ds(0, 1), :] = total[16:17, :DE]
    loads["edge"].wait()
    loads["upd"].wait()
    BW = edge_v.shape[3]
    for c in range(C):
        for half in range(2):
            block = edge_v[c, half].astype(F32)
            g_edge[0, pl.ds(half * (DE // 2), DE // 2), pl.ds(c * BW, BW)] = block
        block = stacked([upd_v[c, 0], upd_v[c, 1]]).astype(F32)
        first = c * BW
        for array, begin in ((g_self, 0), (g_eout, EP)):
            low, high = max(first, begin), min(first + BW, begin + DE)
            if low < high:
                array[0, :, pl.ds(low - begin, high - low)] = block[:DE, low - first : high - first]
        low, high = first, min(first + BW, DE)
        if low < high:
            g_eb[0, pl.ds(1, 1), pl.ds(low, high - low)] = block[DE : DE + 1, low - first : high - first]
    for copy in stores:
        copy.wait()


def run_gradients(dims, operands):
    S, B, N, K, Q, D, DE, EP, FF, C = dims
    rows = C * B * N
    BW = D // C
    held = operands[5].shape[2]
    vm = pl.BlockSpec(memory_space=pltpu.VMEM)
    hbm = pl.BlockSpec(memory_space=pl.ANY)
    sds = jax.ShapeDtypeStruct
    shapes = (
        (1, D, 2 * D), (1, DE, D), (1, D, D), (1, D, FF), (1, FF, D), (1, D, 2 * DE), (1, DE, DE), (1, DE, DE),
        (3, 1, D), (3, 1, D), (3, 1, D), (1, FF), (1, 2, DE),
    )
    return pl.pallas_call(
        functools.partial(gradient_kernel, dims),
        out_shape=tuple(sds(shape, F32) for shape in shapes) + (sds((1, B, N, D), BF16),) * 2,
        in_specs=[hbm, hbm, hbm, vm, hbm, hbm, hbm, hbm, vm, hbm, hbm],
        out_specs=(hbm, vm, hbm, hbm, hbm) + (vm,) * 8 + (hbm,) * 2,
        scratch_shapes=[
            pltpu.VMEM((4, D, rows), BF16),
            pltpu.VMEM((3, rows, D), BF16),
            pltpu.VMEM((2, rows, D), BF16),
            pltpu.VMEM((4, D, FF // 4), BF16),
            pltpu.VMEM((4, FF // 4, D), BF16),
            pltpu.VMEM((4, D, FF // 4), F32),
            pltpu.VMEM((4, FF // 4, D), F32),
            pltpu.VMEM((2, D, D), F32),
            pltpu.VMEM((D, D), F32),
            pltpu.VMEM((C, 2, DE // 2, BW), BF16),
            pltpu.VMEM((C, 2, held, BW), BF16),
            pltpu.SemaphoreType.DMA((15 + 4 * C,)),
            pltpu.SemaphoreType.DMA((13,)),
        ],
        compiler_params=pltpu.CompilerParams(vmem_limit_bytes=56 * 1024 * 1024),
    )(*operands)


def stationary(
    clean_nodes, noise_nodes, edge_feats, neighbours, time_bins, cotangent,
    pair_weight, message_edge, message_out, ffn_in, ffn_out, edge_pair, edge_self, edge_out,
    norm_gain, norm_shift, node_bias, ffn_bias, edge_bias,
):
    S = lax.axis_size("section")
    B, N, D = clean_nodes.shape
    K, DE = edge_feats.shape[2:]
    FF = ffn_in.shape[2]
    Q = N // 4
    EP = DE + N
    def by_rows(array):
        return jnp.transpose(array, (1, 0, 2))

    C = lax.axis_size("dp")
    dims = (S, B, N, K, Q, D, DE, EP, FF, C)
    act, ig, g_fwd, g_bwd, g_dpq, g_small, g_msg, g_upd = run_relay(
        dims,
        (
            jnp.transpose(edge_feats, (0, 2, 1, 3)), jnp.transpose(neighbours, (2, 0, 1)), time_bins,
            clean_nodes.reshape(B * N, D), noise_nodes.reshape(B * N, D),
            cotangent.reshape(B * N, D), pair_weight[0], message_out[0], ffn_in[0], ffn_out[0], edge_pair[0],
            by_rows(norm_gain), by_rows(norm_shift), by_rows(node_bias), ffn_bias, edge_bias[0],
            message_edge[0], edge_self[0], edge_out[0],
        ),
    )
    grads = run_gradients(
        dims,
        (
            g_fwd, g_bwd.reshape(C * B * N, -1), g_dpq.reshape(C * B * N, -1),
            g_small, g_msg, g_upd, ffn_in[0], ffn_out[0], ffn_bias, act.reshape(1, B, N, D), ig.reshape(1, B, N, D),
        ),
    )
    grads, outs = list(grads[:-2]), tuple(grads[-2:])
    grads[8:11] = [by_rows(array) for array in grads[8:11]]
    return outs + tuple(grads)


def solution(mesh):
    sections, copies = mesh.shape["section"], mesh.shape["dp"]

    def body(*args):
        B, N = args[0].shape[:2]
        fits = sections == 4 * B and copies % 2 == 0 and N % 64 == 0
        return stationary(*args) if fits else on_device(*args)

    placed = (
        P("dp", None, None),
        P("dp", None, None),
        P("dp", None, None, None),
        P("dp", None, None),
        P("dp"),
        P("dp", None, None),
        P("section", None, None),
        P("section", None, None),
        P("section", None, None),
        P("section", None, None),
        P("section", None, None),
        P("section", None, None),
        P("section", None, None),
        P("section", None, None),
        P("section", None, None),
        P("section", None, None),
        P("section", None, None),
        P("section", None),
        P("section", None, None),
    )
    return jax.shard_map(
        body,
        mesh=mesh,
        in_specs=placed,
        out_specs=(
            P("section", "dp", None, None),
            P("section", "dp", None, None),
            P("section", None, None),
            P("section", None, None),
            P("section", None, None),
            P("section", None, None),
            P("section", None, None),
            P("section", None, None),
            P("section", None, None),
            P("section", None, None),
            P("section", None, None),
            P("section", None, None),
            P("section", None, None),
            P("section", None),
            P("section", None, None),
        ),
        check_vma=False,
    )
```

```python
import functools
import math

import jax
import jax.numpy as jnp
from jax import lax
from jax.experimental import pallas as pl
from jax.experimental.pallas import tpu as pltpu
from jax.sharding import PartitionSpec as P

TBINS = 100


def from_behind(block, axis, distance):
    devices = range(lax.axis_size(axis))
    route = [(i - distance, i) for i in devices if i - distance in devices]
    return lax.ppermute(block, axis, route)


def for_sending(value):
    return jax.tree.map(lambda a: a.astype(jnp.bfloat16) if a.dtype == jnp.float32 else a, value)


def layer_norm(value, gain, shift):
    centre = jnp.mean(value, axis=-1, keepdims=True)
    centred = value - centre
    spread = jnp.mean(centred * centred, axis=-1, keepdims=True)
    return centred * lax.rsqrt(spread + 1e-05) * gain + shift


def forward_layer(weights, hidden, edge_state, nearest):
    (
        pair_w,
        msg_edge,
        msg_out,
        ffn_w_in,
        ffn_w_out,
        edge_pair_w,
        edge_self_w,
        edge_out_w,
        gains,
        shifts,
        node_b,
        ffn_b,
        edge_b,
    ) = weights
    width = msg_out.shape[0]
    edge_width = edge_self_w.shape[0]
    normed_one = layer_norm(hidden, gains[0], shifts[0]).astype(jnp.bfloat16)
    pair_out = jnp.dot(normed_one, pair_w, preferred_element_type=jnp.float32)
    before_act = (
        pair_out[:, None, :width]
        + jnp.take(pair_out[:, width:], nearest, axis=0)
        + jnp.einsum("nkc,cd->nkd", edge_state, msg_edge, preferred_element_type=jnp.float32)
        + node_b[0]
    )
    message_act = jax.nn.gelu(before_act).astype(jnp.bfloat16)
    message_all = jnp.einsum(
        "nkc,cd->nkd", message_act, msg_out, preferred_element_type=jnp.float32
    )
    after_msg = hidden + jnp.mean(message_all, axis=1) + node_b[1]
    normed_two = layer_norm(after_msg, gains[1], shifts[1]).astype(jnp.bfloat16)
    ffn_pre = jnp.dot(normed_two, ffn_w_in, preferred_element_type=jnp.float32) + ffn_b
    ffn_act = jax.nn.gelu(ffn_pre).astype(jnp.bfloat16)
    after_ffn = (
        after_msg + jnp.dot(ffn_act, ffn_w_out, preferred_element_type=jnp.float32) + node_b[2]
    )
    normed_three = layer_norm(after_ffn, gains[2], shifts[2]).astype(jnp.bfloat16)
    edge_pairs = jnp.dot(normed_three, edge_pair_w, preferred_element_type=jnp.float32)
    edge_pre = (
        edge_pairs[:, None, :edge_width]
        + jnp.take(edge_pairs[:, edge_width:], nearest, axis=0)
        + jnp.einsum("nkc,cd->nkd", edge_state, edge_self_w, preferred_element_type=jnp.float32)
        + edge_b[0]
    )
    edge_act = jax.nn.gelu(edge_pre).astype(jnp.bfloat16)
    edge_next = (
        edge_state.astype(jnp.float32)
        + jnp.einsum("nkc,cd->nkd", edge_act, edge_out_w, preferred_element_type=jnp.float32)
        + edge_b[1]
    )
    saved = (
        normed_one,
        before_act,
        message_act,
        after_msg,
        normed_two,
        ffn_pre,
        ffn_act,
        after_ffn,
        normed_three,
        edge_pre,
        edge_act,
    )
    return (after_ffn, edge_next, saved)


def backward_layer(weights, hidden, edge_state, nearest, grad_nodes_out, grad_edges_out):
    (
        pair_w,
        msg_edge,
        msg_out,
        ffn_w_in,
        ffn_w_out,
        edge_pair_w,
        edge_self_w,
        edge_out_w,
        gains,
        shifts,
        node_b,
        ffn_b,
        edge_b,
    ) = weights
    unused_nodes, unused_edges, saved = forward_layer(weights, hidden, edge_state, nearest)
    (
        normed_one,
        before_act,
        message_act,
        after_msg,
        normed_two,
        ffn_pre,
        ffn_act,
        after_ffn,
        normed_three,
        edge_pre,
        edge_act,
    ) = saved
    width = msg_out.shape[0]
    edge_width = edge_self_w.shape[0]
    count = nearest.shape[1]
    node_count = hidden.shape[0]
    one_hot = (
        nearest.reshape(-1)[None, :] == jnp.arange(node_count, dtype=jnp.int32)[:, None]
    ).astype(jnp.bfloat16)
    edge_grad_low = grad_edges_out.astype(jnp.bfloat16)
    grad_edge_b1 = jnp.sum(grad_edges_out, axis=(0, 1))
    grad_edge_out_w = jnp.einsum(
        "nkc,nkd->cd", edge_act, edge_grad_low, preferred_element_type=jnp.float32
    )
    edge_act_grad = jnp.einsum(
        "nkd,cd->nkc", edge_grad_low, edge_out_w, preferred_element_type=jnp.float32
    )
    unused_value, gelu_edge = jax.vjp(jax.nn.gelu, edge_pre)
    edge_pre_grad = gelu_edge(edge_act_grad)[0].astype(jnp.bfloat16)
    grad_edge_b0 = jnp.sum(edge_pre_grad, axis=(0, 1), dtype=jnp.float32)
    grad_edge_self_w = jnp.einsum(
        "nkc,nkd->cd", edge_state, edge_pre_grad, preferred_element_type=jnp.float32
    )
    edge_total = grad_edges_out + jnp.einsum(
        "nkd,cd->nkc", edge_pre_grad, edge_self_w, preferred_element_type=jnp.float32
    )
    own_edge = jnp.sum(edge_pre_grad, axis=1, dtype=jnp.float32)
    other_edge = jnp.dot(
        one_hot, edge_pre_grad.reshape(-1, edge_width), preferred_element_type=jnp.float32
    )
    pairs_grad = jnp.concatenate([own_edge, other_edge], axis=-1).astype(jnp.bfloat16)
    grad_edge_pair_w = jnp.einsum(
        "nc,nd->cd", normed_three, pairs_grad, preferred_element_type=jnp.float32
    )
    normed_three_grad = jnp.einsum(
        "nd,cd->nc", pairs_grad, edge_pair_w, preferred_element_type=jnp.float32
    )
    unused_value, norm_three_back = jax.vjp(layer_norm, after_ffn, gains[2], shifts[2])
    ffn_side, gain_three, shift_three = norm_three_back(normed_three_grad)
    after_ffn_grad = grad_nodes_out + ffn_side
    grad_node_b2 = jnp.sum(after_ffn_grad, axis=0)
    ffn_out_grad = after_ffn_grad.astype(jnp.bfloat16)
    grad_ffn_w_out = jnp.einsum(
        "nc,nd->cd", ffn_act, ffn_out_grad, preferred_element_type=jnp.float32
    )
    ffn_act_grad = jnp.einsum(
        "nd,cd->nc", ffn_out_grad, ffn_w_out, preferred_element_type=jnp.float32
    )
    unused_value, gelu_ffn = jax.vjp(jax.nn.gelu, ffn_pre)
    ffn_pre_grad = gelu_ffn(ffn_act_grad)[0].astype(jnp.bfloat16)
    grad_ffn_b = jnp.sum(ffn_pre_grad, axis=0, dtype=jnp.float32)
    grad_ffn_w_in = jnp.einsum(
        "nc,nd->cd", normed_two, ffn_pre_grad, preferred_element_type=jnp.float32
    )
    normed_two_grad = jnp.einsum(
        "nd,cd->nc", ffn_pre_grad, ffn_w_in, preferred_element_type=jnp.float32
    )
    unused_value, norm_two_back = jax.vjp(layer_norm, after_msg, gains[1], shifts[1])
    msg_side, gain_two, shift_two = norm_two_back(normed_two_grad)
    after_msg_grad = after_ffn_grad + msg_side
    grad_node_b1 = jnp.sum(after_msg_grad, axis=0)
    message_grad = (after_msg_grad / count).astype(jnp.bfloat16)
    grad_msg_out = jnp.einsum(
        "nkc,nd->cd", message_act, message_grad, preferred_element_type=jnp.float32
    )
    message_act_grad = jnp.einsum(
        "nd,cd->nc", message_grad, msg_out, preferred_element_type=jnp.float32
    )
    unused_value, gelu_msg = jax.vjp(jax.nn.gelu, before_act)
    before_grad = gelu_msg(jnp.broadcast_to(message_act_grad[:, None, :], before_act.shape))[
        0
    ].astype(jnp.bfloat16)
    grad_node_b0 = jnp.sum(before_grad, axis=(0, 1), dtype=jnp.float32)
    grad_msg_edge = jnp.einsum(
        "nkc,nkd->cd", edge_state, before_grad, preferred_element_type=jnp.float32
    )
    edge_total = edge_total + jnp.einsum(
        "nkd,cd->nkc", before_grad, msg_edge, preferred_element_type=jnp.float32
    )
    own_node = jnp.sum(before_grad, axis=1, dtype=jnp.float32)
    other_node = jnp.dot(
        one_hot, before_grad.reshape(-1, width), preferred_element_type=jnp.float32
    )
    pair_grad = jnp.concatenate([own_node, other_node], axis=-1).astype(jnp.bfloat16)
    grad_pair_w = jnp.einsum("nc,nd->cd", normed_one, pair_grad, preferred_element_type=jnp.float32)
    normed_one_grad = jnp.einsum("nd,cd->nc", pair_grad, pair_w, preferred_element_type=jnp.float32)
    unused_value, norm_one_back = jax.vjp(layer_norm, hidden, gains[0], shifts[0])
    input_side, gain_one, shift_one = norm_one_back(normed_one_grad)
    hidden_grad = after_msg_grad + input_side
    grads = (
        grad_pair_w,
        grad_msg_edge,
        grad_msg_out,
        grad_ffn_w_in,
        grad_ffn_w_out,
        grad_edge_pair_w,
        grad_edge_self_w,
        grad_edge_out_w,
        jnp.stack([gain_one, gain_two, gain_three]),
        jnp.stack([shift_one, shift_two, shift_three]),
        jnp.stack([grad_node_b0, grad_node_b1, grad_node_b2]),
        grad_ffn_b,
        jnp.stack([grad_edge_b0, grad_edge_b1]),
    )
    return (hidden_grad.astype(jnp.bfloat16), edge_total.astype(jnp.bfloat16), grads)


def on_device(
    clean_nodes,
    noise_nodes,
    edge_feats,
    neighbours,
    time_bins,
    cotangent,
    pair_weight,
    message_edge,
    message_out,
    ffn_in,
    ffn_out,
    edge_pair,
    edge_self,
    edge_out,
    norm_gain,
    norm_shift,
    node_bias,
    ffn_bias,
    edge_bias,
):
    sections = lax.axis_size("section")
    place = lax.axis_index("section")
    weights = tuple(
        (
            item[0]
            for item in (
                pair_weight,
                message_edge,
                message_out,
                ffn_in,
                ffn_out,
                edge_pair,
                edge_self,
                edge_out,
                norm_gain,
                norm_shift,
                node_bias,
                ffn_bias,
                edge_bias,
            )
        )
    )
    batches, node_count, width = clean_nodes.shape
    phase = (time_bins.astype(jnp.float32) + 0.5) * (math.pi * 0.5 / TBINS)
    start = jnp.cos(phase)[:, None, None] * clean_nodes.astype(jnp.float32) + jnp.sin(phase)[
        :, None, None
    ] * noise_nodes.astype(jnp.float32)
    zero_nodes = jnp.zeros((node_count, width), jnp.bfloat16)
    zero_edges = jnp.zeros(edge_feats.shape[1:], jnp.bfloat16)
    is_first = place == 0
    is_last = place == sections - 1

    def forward_step(step_index, carry):
        recv_nodes, recv_edges, back_nodes, kept_nodes, kept_edges, section_outs = carry
        item = step_index - place
        first_pass = (item >= 0) & (item < batches)
        second_pass = (item >= sections) & (item < sections + batches)
        index = jnp.clip(jnp.where(second_pass, item - sections, item), 0, batches - 1)
        predicted = back_nodes
        own_start = lax.dynamic_index_in_dim(start, index, 0, keepdims=False)
        lead_nodes = own_start + jnp.where(second_pass, predicted.astype(jnp.float32), 0.0)
        nodes_in = jnp.where(is_first, lead_nodes, recv_nodes.astype(jnp.float32))
        edges_in = jnp.where(
            is_first, lax.dynamic_index_in_dim(edge_feats, index, 0, keepdims=False), recv_edges
        )
        nearest = lax.dynamic_index_in_dim(neighbours, index, 0, keepdims=False)

        def run_layer(operand):
            after, edge_next, saved = forward_layer(weights, operand[0], operand[1], operand[2])
            return (after.astype(jnp.bfloat16), edge_next.astype(jnp.bfloat16))

        def skip_layer(operand):
            return (zero_nodes, zero_edges)

        out_nodes, out_edges = lax.cond(
            first_pass | second_pass, run_layer, skip_layer, (nodes_in, edges_in, nearest)
        )
        kept_nodes = lax.dynamic_update_index_in_dim(
            kept_nodes, jnp.where(second_pass, nodes_in, kept_nodes[index]), index, 0
        )
        kept_edges = lax.dynamic_update_index_in_dim(
            kept_edges, jnp.where(second_pass, edges_in, kept_edges[index]), index, 0
        )
        section_outs = lax.dynamic_update_index_in_dim(
            section_outs, jnp.where(second_pass, out_nodes, section_outs[index]), index, 0
        )
        recv_nodes, recv_edges = from_behind((out_nodes, out_edges), "section", 1)
        back_nodes = from_behind(out_nodes, "section", 1 - sections)
        return (recv_nodes, recv_edges, back_nodes, kept_nodes, kept_edges, section_outs)

    forward_init = (
        zero_nodes,
        zero_edges,
        zero_nodes,
        jnp.zeros((batches, node_count, width), jnp.float32),
        jnp.zeros_like(edge_feats),
        jnp.zeros((batches, node_count, width), jnp.bfloat16),
    )
    unused_nodes, unused_edges, unused_back, kept_nodes, kept_edges, section_outs = lax.fori_loop(
        0, 2 * sections + batches - 1, forward_step, forward_init
    )
    grads_zero = tuple((jnp.zeros(item.shape, jnp.float32) for item in weights))

    def backward_step(step_index, carry):
        recv_grad_nodes, recv_grad_edges, grads, input_grads = carry
        item = step_index - (sections - 1 - place)
        live = (item >= 0) & (item < batches)
        index = jnp.clip(item, 0, batches - 1)
        nodes_grad_out = jnp.where(
            is_last,
            lax.dynamic_index_in_dim(cotangent, index, 0, keepdims=False).astype(jnp.float32),
            recv_grad_nodes.astype(jnp.float32),
        )
        edges_grad_out = jnp.where(is_last, 0.0, recv_grad_edges.astype(jnp.float32))
        nearest = lax.dynamic_index_in_dim(neighbours, index, 0, keepdims=False)

        def run_back(operand):
            return backward_layer(
                weights, operand[0], operand[1], operand[2], operand[3], operand[4]
            )

        def skip_back(operand):
            return (zero_nodes, zero_edges, grads_zero)

        nodes_grad, edges_grad, terms = lax.cond(
            live,
            run_back,
            skip_back,
            (kept_nodes[index], kept_edges[index], nearest, nodes_grad_out, edges_grad_out),
        )
        grads = tuple((total + term for total, term in zip(grads, terms)))
        input_grads = lax.dynamic_update_index_in_dim(
            input_grads, jnp.where(live, nodes_grad, input_grads[index]), index, 0
        )
        recv_grad_nodes, recv_grad_edges = from_behind((nodes_grad, edges_grad), "section", -1)
        return (recv_grad_nodes, recv_grad_edges, grads, input_grads)

    backward_init = (
        zero_nodes,
        zero_edges,
        grads_zero,
        jnp.zeros((batches, node_count, width), jnp.bfloat16),
    )
    unused_grad_nodes, unused_grad_edges, grads, input_grads = lax.fori_loop(
        0, sections + batches - 1, backward_step, backward_init
    )
    totals = jax.tree.map(lambda part: part.astype(jnp.float32), lax.psum(for_sending(grads), "dp"))
    return (
        section_outs[None],
        input_grads[None],
        totals[0][None],
        totals[1][None],
        totals[2][None],
        totals[3][None],
        totals[4][None],
        totals[5][None],
        totals[6][None],
        totals[7][None],
        totals[8][None],
        totals[9][None],
        totals[10][None],
        totals[11][None],
        totals[12][None],
    )


BF16 = jnp.bfloat16
F32 = jnp.float32
MESH = pl.DeviceIdType.MESH
GELU_A = 0.7978845608028654
GELU_B = 0.044715


def gelu(x):
    return 0.5 * x * (1.0 + jnp.tanh(x * (GELU_A + (GELU_A * GELU_B) * (x * x))))


def gelu_both(x):
    square = x * x
    t = jnp.tanh(x * (GELU_A + (GELU_A * GELU_B) * square))
    half = 0.5 * (1.0 + t)
    slope = half + (0.5 * x) * (1.0 - t * t) * (GELU_A + (3.0 * GELU_A * GELU_B) * square)
    return x * half, slope


def mm(a, b):
    return jnp.dot(a, b, preferred_element_type=F32)


def mm_bt(a, b):
    return lax.dot_general(a, b, (((1,), (1,)), ((), ())), preferred_element_type=F32)


def mm_at(a, b):
    return lax.dot_general(a, b, (((0,), (0,)), ((), ())), preferred_element_type=F32)


def stacked(blocks):
    return jnp.concatenate(blocks, axis=0)


def row_mean(x):
    return jnp.mean(x, axis=-1, keepdims=True)


def normed(x):
    centred = x - row_mean(x)
    scale = lax.rsqrt(row_mean(centred * centred) + 1e-05)
    return centred * scale, scale


def norm_back(grad, unit, scale, gain):
    t = grad * gain
    return scale * (t - row_mean(t) - unit * row_mean(t * unit))


def col_sum(x):
    return jnp.sum(x, axis=0, keepdims=True)


def relay_kernel(
    dims,
    edges_in, near_in, bins, clean, noise, cot, pw_in, mo_in, fi_in, fo_in, ends, gains, shifts, node_b, fb, edge_b, we_own, ws_own, wo_own,
    act, ig, g_fwd, g_bwd, g_dpq, g_small, g_msg, g_upd,
    pw, mo, fi, fo, fwd_t, ep, e0, nb0, nb1, nb2, oht, start, par, eb0, wall_msg, wall_upd, fwd, bwd, sg,
    eg, eg_r, eg_b, msg_o, msg_f, upd_o, upd_f, wo, eb1,
    ecat, wcat, scat, pwn, parn, hin_r, hst, mb_s, mb_r, pq_s, pq_r, rq_s, rq_r,
    un0, un1, un2, hi_s, sc0, sc1, sc2, sci, u_s, slope_s, de, dacc, gp, gpe, dcat, act_t, edge_t,
    x_s, x_r, row_s, row_r, dpqo_r, dmb_s, dmb_r, dh1_s, dh1_r, dh1_f, dh2_s, dn3_s, da2_s, h1_s, a1_s,
    ld_sem, ld_ss, w_sem, nx_ss, nx_rs, hop_ss, hop_rs,
    pq_ss, pq_rs, ag_ss, ag_rs, rq_ss, rq_rs, ag2_ss, ag2_rs,
    mb_ss, mb_rs, x_ss, x_rs, row_ss, row_rs, dpqo_rs, fw_ss, dmb_ss, dmb_rs, dh_ss, dh_rs,
    e1_ss, e1_rs, e2_ss, e2_rs, g_ss, g_rs, relay_ss, ring_ss, ring_rs, sib_ss, sib_rs,
):
    S, B, N, K, Q, D, DE, EP, FF, C = dims
    BN = B * N
    RB = 16
    top = DE + N
    me_s = lax.axis_index("section")
    me_d = lax.axis_index("dp")
    core = lax.rem(me_d, 2)
    pair = me_d - core
    w = lax.div(me_s, 2)
    q = 2 * lax.rem(me_s, 2) + core
    owner_d = pair + lax.div(w, B)
    slot = lax.rem(w, B)
    my_row = pl.multiple_of(slot * N + q * Q, Q)
    own_rows = pl.ds(top, Q)

    def quarter(j):
        return pl.ds(pl.multiple_of(DE + j * Q, Q), Q)

    def is_me(sec, dpi):
        return (sec == me_s) & (dpi == me_d)

    def far(src, dst, ssem, rsem, sec, dpi):
        return pltpu.make_async_remote_copy(
            src_ref=src, dst_ref=dst, send_sem=ssem, recv_sem=rsem,
            device_id={"section": sec, "dp": dpi}, device_id_type=MESH,
        )

    def push(src, dst, ssem, rsem, sec, dpi):
        lax.cond(
            is_me(sec, dpi),
            lambda: pltpu.make_async_copy(src, dst, rsem).start(),
            lambda: far(src, dst, ssem, rsem, sec, dpi).start(),
        )

    def arrive(ref, sem):
        pltpu.make_async_copy(ref, ref, sem).wait()

    def drain(ref, sem, sec, dpi):
        @pl.when(jnp.logical_not(is_me(sec, dpi)))
        def _():
            arrive(ref, sem)

    def worker_of(p, j):
        return 2 * (core * B + p) + j // 2, pair + j % 2

    def peer(k):
        j = lax.rem(q + k, 4)
        return j, 2 * w + lax.div(j, 2), pair + lax.rem(j, 2)

    works_here = lax.div(w, B) == core

    def at(p, first=0, size=16):
        return pl.ds(pl.multiple_of(p * N + first, size), size)

    near = jnp.clip(w - core * B, 0, B - 1)
    leading = jnp.where(lax.div(w, B) == core, near, B - 1 - near)

    weights = [
        pltpu.make_async_copy(src, dst, w_sem.at[n])
        for n, (src, dst) in enumerate(((pw_in, pw), (mo_in, mo), (fi_in, fi), (fo_in, fo)))
    ]
    for weight in weights:
        weight.start()
    barrier = pltpu.get_barrier_semaphore()
    for sec in range(S):
        for c in range(C):
            greeted = (c == pair) | (c == pair + 1) | (w == sec // 2)

            @pl.when(greeted & jnp.logical_not(is_me(sec, c)))
            def _():
                pl.semaphore_signal(
                    barrier, inc=1, device_id={"section": sec, "dp": c}, device_id_type=MESH
                )
    wall_msg[me_s] = we_own[...]
    wall_upd[me_s] = jnp.zeros(wall_upd.shape[1:], BF16)
    wall_upd[me_s, pl.ds(0, DE), pl.ds(0, DE)] = ws_own[...]
    wall_upd[me_s, pl.ds(0, DE), pl.ds(EP, DE)] = wo_own[...]
    bias = edge_b[pl.ds(1, 1), :]
    high = bias.astype(BF16).astype(F32)
    row = lax.broadcasted_iota(jnp.int32, (16, DE), 0)
    wall_upd[me_s, pl.ds(DE, 16), pl.ds(0, DE)] = jnp.where(
        row == 0, high, jnp.where(row == 1, bias - high, 0.0)
    ).astype(BF16)
    eb0[...] = jnp.zeros_like(eb0)
    eb0[:, pl.ds(0, DE)] = edge_b[pl.ds(0, 1), :]
    par[pl.ds(0, 1), :] = gains[0]
    par[pl.ds(1, 1), :] = shifts[0]
    par[pl.ds(2, 1), :] = node_b[0]
    par[pl.ds(3, 5), :] = jnp.zeros((5, D), F32)
    pl.semaphore_wait(barrier, 2 * S - 1 + 2 * (C - 2))

    def section_at(i):
        i = lax.rem(i + S, S)
        return jnp.where(i < S // 2, 2 * i, 2 * (S - i) - 1)

    place = jnp.where(lax.rem(me_s, 2) == 0, w, S - 1 - w)
    sides = ((section_at(place + 1), S // 2), (section_at(place - 1), S // 2 - 1))
    walls = (wall_msg, wall_upd)

    def half_of(which, layer, c):
        size = walls[which].shape[1] // 2
        return walls[which].at[layer, pl.ds(pl.multiple_of(c * size, size), size)]

    def ring_send(which, layer, side, hop):
        sec, reach = sides[side]
        if hop < reach:
            half = half_of(which, layer, core)
            far(half, half, ring_ss.at[which, side, hop], ring_rs.at[which, layer], sec, me_d).start()

    def ring_hop(which, side, hop):
        layer = section_at(place - hop if side == 0 else place + hop)
        half = half_of(which, layer, core)
        arrive(half, ring_rs.at[which, layer])
        ring_send(which, layer, side, hop)
        far(half, half, sib_ss.at[which, layer], sib_rs.at[which, layer], me_s, pair + 1 - core).start()

    hops = [(hop, side) for hop in range(1, S // 2 + 1) for side in range(2) if hop <= sides[side][1]]

    def ring_later(second):
        for hop, side in hops:
            early = (place > 0) & ((place >= hop) if side == 0 else (place + hop <= S))

            @pl.when(early != second)
            def _():
                ring_hop(1, side, hop)

    for side in range(2):
        ring_send(0, me_s, side, 0)

    ep[...] = jnp.zeros_like(ep)
    ep[:, pl.ds(0, DE)] = ends[:, pl.ds(0, DE)]
    ep[:, pl.ds(EP, DE)] = ends[...].astype(F32)[:, DE:].astype(BF16)

    arrays = ((edges_in, e0), (near_in, nb0))

    def quarter_of(n, j):
        return edges_in.at[slot, :, pl.ds(pl.multiple_of(j * Q, Q), Q)] if n == 0 else near_in

    @pl.when(works_here)
    def _():
        for n, (_, dst) in enumerate(arrays):
            pltpu.make_async_copy(quarter_of(n, q), dst, ld_sem.at[n]).start()
            other = q + 1 - 2 * core
            far(quarter_of(n, other), dst, ld_ss.at[n], ld_sem.at[n], me_s, pair + 1 - core).start()

    weights[0].wait()

    def edges_laid_out():
        for weight in weights[1:]:
            weight.wait()

        for n, (_, dst) in enumerate(arrays):
            arrive(dst, ld_sem.at[n])
        by_step = nb0[:, 0, :]
        for p in range(1, B):
            by_step = jnp.where(slot == p, nb0[:, p, :], by_step)
        nb1[...] = jnp.zeros_like(nb1)
        nb1[pl.ds(0, K), pl.ds(0, N)] = by_step.astype(F32)
        nb2[...] = nb1[...].T
        nearest = nb2[pl.ds(pl.multiple_of(q * Q, Q), Q), :]
        lane = (lax.broadcasted_iota(jnp.int32, (Q, EP), 1) - DE).astype(F32)
        for k in range(K):
            rows = pl.ds(k * Q, Q)
            ecat[0, rows, :] = jnp.where(lane == nearest[:, k : k + 1], 1.0, 0.0).astype(BF16)
            ecat[0, rows, pl.ds(0, DE)] = e0[k]
        node = lax.broadcasted_iota(jnp.int32, (N, EP), 0)
        lane = lax.broadcasted_iota(jnp.int32, (N, EP), 1) - DE
        chosen = jnp.where(lane == node, 1.0, 0.0).astype(BF16)
        oht[...] = mm_bt(chosen, ecat[0]).astype(BF16)

        @pl.when(works_here)
        def _():
            for n, (_, dst) in enumerate(arrays):
                arrive(dst, ld_ss.at[n])

    before = lax.rem(me_s + S - 1, S)
    far(pw_in, pwn, nx_ss.at[0], nx_rs.at[0], before, me_d).start()
    far(par, parn, nx_ss.at[1], nx_rs.at[1], before, me_d).start()

    for p in range(B):
        rows = pl.ds(p * N, N)
        phase = jnp.full((1, D), (bins[p].astype(F32) + 0.5) * (math.pi * 0.5 / TBINS), F32)
        start[rows, :] = jnp.cos(phase) * clean[rows, :].astype(F32) + jnp.sin(phase) * noise[rows, :].astype(F32)

    def ring_drain():
        for which in range(2):
            for side in range(2):
                for hop in range(sides[side][1]):
                    arrive(half_of(which, me_s, core), ring_ss.at[which, side, hop])
            for layer in range(S):
                @pl.when(layer != me_s)
                def _():
                    arrive(half_of(which, layer, core), sib_ss.at[which, layer])

    def unpack_messages(t):
        @pl.when(t != me_s)
        def _():
            arrive(half_of(0, t, 1 - core), sib_rs.at[0, t])

        wcat[t, pl.ds(0, DE), :] = wall_msg[t]

    def unpack_updates(t):
        @pl.when(t != me_s)
        def _():
            arrive(half_of(1, t, 1 - core), sib_rs.at[1, t])

        scat[t, pl.ds(0, DE), :] = wall_upd[t, pl.ds(0, DE), pl.ds(0, EP)]
        wo[t, pl.ds(0, DE), :] = wall_upd[t, pl.ds(0, DE), pl.ds(EP, EP)]
        wo[t, pl.ds(DE, N), :] = jnp.zeros((N, EP), BF16)
        eb1[t] = wall_upd[t, pl.ds(DE, 16), pl.ds(0, EP)]

    def rows_out(p, src, dst, ssem, rsem):
        for j in range(4):
            sec, dpi = worker_of(p, j)
            push(src.at[at(p, j * Q, Q)], dst, ssem, rsem, sec, dpi)

    def rows_drain(src, ssem):
        lax.cond(
            works_here,
            lambda: arrive(src.at[pl.ds(0, B * N - Q)], ssem),
            lambda: arrive(src, ssem),
        )

    def spread(rows, half, ref, layer, ssem, rsem, rows_sem):
        arrive(rows, rows_sem)
        for k in range(1, 4):
            _, sec, dpi = peer(k)
            far(rows.at[:, pl.ds(half, half)], ref.at[layer, quarter(q)], ssem, rsem, sec, dpi).start()
        ref[layer, own_rows, :] = rows[:, pl.ds(0, half)]
        ref[layer, quarter(q), :] = rows[:, pl.ds(half, half)]

    def spread_wait(ref, layer, sem):
        arrive(ref.at[layer, pl.ds(DE, 3 * Q)], sem)

    def share(group, src, dst):
        for c in range(C):
            push(src, dst.at[me_d], g_ss.at[group, c], g_rs.at[group, me_d], me_s, c)

    def share_wait(group, src, dst):
        for c in range(C):
            arrive(dst.at[c], g_rs.at[group, c])
            drain(src, g_ss.at[group, c], me_s, c)

    def share_near(group, src, dst):
        for c in range(C):
            @pl.when((c == pair) | (c == pair + 1) | (core == c % 2))
            def _():
                push(src, dst(me_d), g_ss.at[group, c], g_rs.at[group, me_d], me_s, c)

    def share_relay(group, src, dst):
        for c in range(C):
            @pl.when((c != me_d) & (core == c % 2))
            def _():
                arrive(dst(c), g_rs.at[group, c])
                far(dst(c), dst(c), relay_ss.at[group - 2, c // 2], g_rs.at[group, c], me_s, pair + 1 - core).start()

    def share_near_wait(group, src, dst):
        for c in range(C):
            @pl.when((c == me_d) | (core != c % 2))
            def _():
                arrive(dst(c), g_rs.at[group, c])

            @pl.when((c != me_d) & ((c == pair) | (c == pair + 1) | (core == c % 2)))
            def _():
                arrive(src, g_ss.at[group, c])

            @pl.when((c != me_d) & (core == c % 2))
            def _():
                arrive(dst(c), relay_ss.at[group - 2, c // 2])

    steps = 4
    KC = K // steps
    RC = KC * Q

    def messages(t):
        own = wcat[t, own_rows, :].astype(F32)
        total = jnp.zeros((Q, D), F32)
        for i in range(steps):
            pre = mm(ecat[t, pl.ds(i * RC, RC), :], wcat[t, pl.ds(0, top), :])
            for k in range(KC):
                total = total + gelu(pre[k * Q : (k + 1) * Q] + own)
        mb_s[...] = (total * (1.0 / K)).astype(BF16)

    def edge_update(t):
        own = scat[t, own_rows, :].astype(F32)
        bias = eb1[t, pl.ds(0, 1), :].astype(F32) + eb1[t, pl.ds(1, 1), :].astype(F32)
        for i in range(steps):
            pe = mm(ecat[t, pl.ds(i * RC, RC), :], scat[t, pl.ds(0, top), :])
            act_e = stacked([gelu(pe[k * Q : (k + 1) * Q] + own).astype(BF16) for k in range(KC)])
            z = mm(act_e, wo[t])
            for k in range(KC):
                rows = pl.ds(i * RC + k * Q, Q)
                ecat[t + 1, rows, :] = (ecat[t, rows, :].astype(F32) + z[k * Q : (k + 1) * Q] + bias).astype(BF16)

    chunks = 4
    FC = FF // chunks

    def node_forward(step):
        @pl.when(step < S)
        def _():
            arrive(pwn, nx_rs.at[0])
            arrive(parn, nx_rs.at[1])
            arrive(pw, nx_ss.at[0])
            arrive(par, nx_ss.at[1])

        @pl.when(step == 0)
        def _():
            hi_s[...] = start[...]

        @pl.when(step > 0)
        def _():
            arrive(hin_r, hop_rs)
            first = jnp.where(me_s == 0, 1.0, 0.0)
            for i in range(0, BN, RB):
                rows = pl.ds(i, RB)
                hi_s[rows, :] = hin_r[rows, :].astype(F32) + first * start[rows, :]

        later = lax.rem(me_s + 1, S)

        def turn(n, carry):
            p = lax.rem(leading + n, B)
            whole = at(p, 0, N)
            arrive(mb_r.at[whole], mb_rs.at[p])
            mean = mm(mb_r[whole, :], mo[...])
            for i in range(0, N, RB):
                rows = at(p, i)
                h1 = hi_s[rows, :] + mean[i : i + RB] + node_b[1]
                h1_s[rows, :] = h1
                unit, scale = normed(h1)
                un1[rows, :] = unit
                sc1[rows, :] = scale
                fwd[rows, pl.ds(2 * D, D)] = (unit * gains[1] + shifts[1]).astype(BF16)
                fwd[rows, pl.ds(D, D)] = mb_r[rows, :]
            a2 = fwd[whole, pl.ds(2 * D, D)]
            y = jnp.zeros((N, D), F32)
            for c in range(chunks):
                cols = pl.ds(c * FC, FC)
                u = mm(a2, fi[:, cols])
                v = []
                for i in range(0, N, RB):
                    block = u[i : i + RB] + fb[:, cols]
                    u_s[at(p, i), cols] = block
                    v.append(gelu(block).astype(BF16))
                y = y + mm(stacked(v), fo[cols, :])
            last = jnp.where(me_s == S - 1, 1.0, 0.0)
            for i in range(0, N, RB):
                rows = at(p, i)
                h2 = h1_s[rows, :] + y[i : i + RB] + node_b[2]
                rounded = h2.astype(BF16)
                hst[rows, :] = rounded
                unit, scale = normed(h2)
                un2[rows, :] = unit
                sc2[rows, :] = scale
                fwd[rows, pl.ds(3 * D, D)] = (unit * gains[2] + shifts[2]).astype(BF16)
                pair_norm(rows, rounded.astype(F32) + last * start[rows, :], parn)
            rq = mm(fwd[whole, pl.ds(3 * D, D)], ep[...])
            for i in range(0, N, RB):
                rows = at(p, i)
                rq_s[rows, pl.ds(0, EP)] = (rq[i : i + RB, :EP] + eb0[...]).astype(BF16)
                rq_s[rows, pl.ds(EP, EP)] = rq[i : i + RB, EP:].astype(BF16)
            pair_rows(p, pwn, parn)

            @pl.when(me_s < S - 1)
            def _():
                rows_out(p, rq_s, rq_r, rq_ss, rq_rs)

            @pl.when(step < 2 * S - 1)
            def _():
                rows_out(p, pq_s, pq_r, pq_ss, pq_rs)

            @pl.when((n == 0) & works_here)
            def _():
                pass_on(step)

            return carry

        lax.fori_loop(0, B, turn, 0)

        @pl.when(step < 2 * S - 1)
        def _():
            far(hst, hin_r, hop_ss, hop_rs, later, me_d).start()

        @pl.when(step >= S)
        def _():
            act[...] = hst[...]
            for i in range(0, BN, RB):
                rows = pl.ds(i, RB)
                unit, scale = normed(hi_s[rows, :])
                hi_s[rows, :] = unit
                sci[rows, :] = scale
                fwd[rows, pl.ds(0, D)] = (unit * gains[0] + shifts[0]).astype(BF16)
                for c in range(chunks):
                    cols = pl.ds(c * FC, FC)
                    slope_s[rows, cols] = gelu_both(u_s[rows, cols])[1].astype(BF16)
            for n in range(4):
                fwd_t[pl.ds(n * D, D), :] = fwd[:, pl.ds(n * D, D)].T
            share(0, fwd_t, g_fwd)

    def pair_norm(rows, hidden, first):
        unit, scale = normed(hidden)
        un0[rows, :] = unit
        sc0[rows, :] = scale
        a1_s[rows, :] = (unit * first[pl.ds(0, 1), :] + first[pl.ds(1, 1), :]).astype(BF16)

    def pair_rows(p, weight, first):
        whole = at(p, 0, N)
        for half in range(2):
            cols = pl.ds(half * D, D)
            value = mm(a1_s[whole, :], weight[:, cols])
            if half == 0:
                value = value + first[pl.ds(2, 1), :]
            pq_s[whole, cols] = value.astype(BF16)

    def pass_on(step):
        t = lax.rem(step, S)

        @pl.when(t < S - 1)
        def _():
            spread(rq_r, EP, scat, t, ag2_ss, ag2_rs, rq_rs)

        @pl.when(step < 2 * S - 1)
        def _():
            spread(pq_r, D, wcat, lax.rem(step + 1, S), ag_ss, ag_rs, pq_rs)

    def node_forward_drain():
        arrive(hst, hop_ss)
        rows_drain(pq_s, pq_ss)

        @pl.when(me_s < S - 1)
        def _():
            rows_drain(rq_s, rq_ss)

    @pl.when(me_s == 0)
    def _():
        for i in range(0, BN, RB):
            rows = pl.ds(i, RB)
            pair_norm(rows, start[rows, :], par)
        for p in range(B):
            pair_rows(p, pw, par)
            rows_out(p, pq_s, pq_r, pq_ss, pq_rs)

    def message_slope(t):
        own = wcat[t, own_rows, :].astype(F32)
        for i in range(steps):
            pre = mm(ecat[t, pl.ds(i * RC, RC), :], wcat[t, pl.ds(0, top), :])
            for k in range(KC):
                gp[t, pl.ds(i * RC + k * Q, Q), :] = gelu_both(pre[k * Q : (k + 1) * Q] + own)[1].astype(BF16)

    def edge_slope(t):
        own = scat[t, own_rows, :].astype(F32)
        values = []
        for i in range(steps):
            pe = mm(ecat[t, pl.ds(i * RC, RC), :], scat[t, pl.ds(0, top), :])
            for k in range(KC):
                value, slope = gelu_both(pe[k * Q : (k + 1) * Q] + own)
                values.append(value.astype(BF16))
                gpe[t, pl.ds(i * RC + k * Q, Q), :] = slope.astype(BF16)
        act_t[t] = stacked(values).T

    def prepare(t):
        message_slope(t)
        edge_t[t] = ecat[t].T

        @pl.when(t > 0)
        def _():
            edge_slope(t - 1)

    def forward_step(step, carry):
        t = lax.rem(step, S)

        @pl.when(step < S)
        def _():
            unpack_messages(t)

        spread_wait(wcat, t, ag_rs)
        messages(t)
        spread_wait(wcat, t, ag_ss)
        push(mb_s, mb_r.at[pl.ds(my_row, Q)], mb_ss, mb_rs.at[slot], t, owner_d)

        for second in range(2):
            @pl.when(step == second)
            def _():
                ring_later(second == 1)

        @pl.when((step == 0) & (me_s == 0))
        def _():
            rows_drain(pq_s, pq_ss)

        @pl.when((step > 0) & (me_s == lax.rem(step + S - 1, S)))
        def _():
            node_forward_drain()

        @pl.when(me_s == t)
        def _():
            node_forward(step)

        @pl.when((me_s != t) & (step >= S))
        def _():
            prepare(t)

        @pl.when(jnp.logical_not((me_s == t) & works_here))
        def _():
            pass_on(step)

        @pl.when(t < S - 1)
        def _():
            @pl.when(step < S)
            def _():
                unpack_updates(t)

            spread_wait(scat, t, ag2_rs)
            edge_update(t)
            spread_wait(scat, t, ag2_ss)

        drain(mb_s, mb_ss, t, owner_d)
        return carry

    for hop, side in hops:
        if (hop, side) == (2, 0):
            edges_laid_out()
        ring_hop(0, side, hop)
    for side in range(2):
        ring_send(1, me_s, side, 0)
    spread(pq_r, D, wcat, 0, ag_ss, ag_rs, pq_rs)
    lax.fori_loop(0, 2 * S, forward_step, 0)
    ring_drain()

    @pl.when(me_s != S - 1)
    def _():
        arrive(half_of(1, S - 1, 1 - core), sib_rs.at[1, S - 1])

    def edge_back(t):
        b2, n2 = lax.rem(t, 2), lax.rem(t + 1, 2)
        total = jnp.zeros((Q, EP), F32)
        for i in range(steps):
            chunk = pl.ds(i * RC, RC)
            carry = mm_bt(dcat[b2, chunk, pl.ds(0, D)], wcat[t, pl.ds(0, top), :])
            low = []
            for k in range(KC):
                rows = pl.ds(i * RC + k * Q, Q)
                low.append((dacc[rows, :] + carry[k * Q : (k + 1) * Q]).astype(BF16))
                de[n2, rows, :] = low[-1]
            dw = mm_bt(stacked(low), wo[t - 1])
            for k in range(KC):
                rows = pl.ds(i * RC + k * Q, Q)
                d = (gpe[t - 1, rows, :].astype(F32) * dw[k * Q : (k + 1) * Q]).astype(BF16)
                total = total + d.astype(F32)
                dcat[n2, rows, pl.ds(D, EP)] = d
        row_s[:, pl.ds(2 * D, EP)] = total.astype(BF16)
        x_s[:, pl.ds(D, EP)] = mm(oht[...], dcat[n2, :, pl.ds(D, EP)]).astype(BF16)

    def edge_pass(t):
        b3 = lax.rem(t, 2)
        for i in range(steps):
            rows = pl.ds(i * RC, RC)
            d = dcat[b3, rows, pl.ds(D, EP)]
            dacc[rows, :] = de[b3, rows, :].astype(F32) + mm_bt(d, scat[t, pl.ds(0, top), :])

    blocks = 2 * C
    my_block = lax.rem(me_s, 2) * C + me_d
    BW, HM, HU = msg_o.shape[2], msg_o.shape[1], upd_o.shape[1]

    def block_of(t, half, c, size):
        return eg.at[t, half, pl.ds(0, size), pl.ds(pl.multiple_of(c * BW, BW), BW)]

    def blocks_out(t, size):
        for k in range(blocks):
            @pl.when(k != my_block)
            def _():
                far(
                    block_of(t, k // C, k % C, size), eg_r.at[t, my_block, pl.ds(0, size)],
                    e1_ss.at[t, k], e1_rs.at[t, my_block], 2 * w + k // C, k % C,
                ).start()

    def edge_grads(t):
        grad = mm(edge_t[t, pl.ds(0, DE), :], dcat[lax.rem(t, 2), :, pl.ds(0, D)]).astype(BF16)
        for half in range(2):
            eg[t, half, pl.ds(0, HM), :] = grad[half * HM : (half + 1) * HM]

        @pl.when(t > 0)
        def _():
            n2 = lax.rem(t + 1, 2)
            edges = mm(edge_t[t - 1, pl.ds(0, DE), :], dcat[n2, :, pl.ds(D, EP)])
            outs = mm(act_t[t - 1, pl.ds(0, DE), :], de[n2])
            bias = jnp.sum(de[n2].astype(F32), axis=0, keepdims=True)
            grad = jnp.concatenate([edges, outs], axis=1).astype(BF16)
            eg[t, 0, pl.ds(HM, HU), :] = grad[:HU]
            eg[t, 1, pl.ds(HM, DE - HU), :] = grad[HU:]
            eg[t, 1, pl.ds(HM + DE - HU, 16), pl.ds(0, EP)] = jnp.broadcast_to(bias, (16, EP)).astype(BF16)
            eg[t, 1, pl.ds(HM + DE - HU, 16), pl.ds(EP, EP)] = jnp.zeros((16, EP), BF16)
            eg[t, 1, pl.ds(HM + DE - HU + 16, 2 * HU - DE - 16), :] = jnp.zeros((2 * HU - DE - 16, 2 * EP), BF16)
            blocks_out(t, HM + HU)

        @pl.when(t == 0)
        def _():
            blocks_out(t, HM)

    def blocks_sum(t, size):
        eg_r[t, my_block, pl.ds(0, size), :] = block_of(t, lax.rem(me_s, 2), me_d, size)[...]
        for k in range(blocks):
            @pl.when(k != my_block)
            def _():
                arrive(eg_r.at[t, k, pl.ds(0, size)], e1_rs.at[t, k])
                arrive(block_of(t, k // C, k % C, size), e1_ss.at[t, k])
        total = eg_r[t, 0, pl.ds(0, size), :].astype(F32)
        for k in range(1, blocks):
            total = total + eg_r[t, k, pl.ds(0, size), :].astype(F32)
        eg_b[t, pl.ds(0, size), :] = total.astype(BF16)
        push(eg_b.at[t, pl.ds(0, HM)], msg_o.at[me_s], e2_ss.at[0, t], e2_rs.at[0, me_s], t, me_d)
        if size > HM:
            push(eg_b.at[t, pl.ds(HM, HU)], upd_o.at[me_s], e2_ss.at[1, t], e2_rs.at[1, me_s], t - 1, me_d)

    def gather_blocks():
        for k in range(1, 4):
            j, sec, dpi = peer(k)
            rows = pl.ds(pl.multiple_of(j * Q, Q), Q)
            far(x_s.at[rows], x_r.at[q], x_ss, x_rs, sec, dpi).start()
        x_r[q] = x_s[pl.ds(pl.multiple_of(q * Q, Q), Q), :]

    def gather_wait():
        arrive(x_r.at[pl.ds(0, 3)], x_rs)
        arrive(x_s.at[pl.ds(0, 3 * Q)], x_ss)
        total = x_r[0].astype(F32)
        for j in range(1, 4):
            total = total + x_r[j].astype(F32)
        return total

    def message_back(t):
        b2 = lax.rem(t, 2)
        dm = dmb_r[...].astype(F32)
        total = jnp.zeros((Q, D), F32)
        for k in range(K):
            rows = pl.ds(k * Q, Q)
            d = (gp[t, rows, :].astype(F32) * dm).astype(BF16)
            total = total + d.astype(F32)
            dcat[b2, rows, pl.ds(0, D)] = d
        row_s[:, pl.ds(0, D)] = total.astype(BF16)
        x_s[:, pl.ds(0, D)] = mm(oht[...], dcat[b2, :, pl.ds(0, D)]).astype(BF16)

    def node_backward():
        @pl.when(me_s < S - 1)
        def _():
            arrive(dh1_r, dh_rs)

        def turn(n, carry):
            p = lax.rem(near + n, B)
            whole = at(p, 0, N)

            @pl.when(me_s < S - 1)
            def _():
                arrive(row_r.at[whole], row_rs.at[p])
                dn0 = mm_bt(row_r[whole, pl.ds(0, 2 * D)], pwn[...])
                dn3 = mm_bt(row_r[whole, pl.ds(2 * D, 2 * EP)], ep[...])
                for i in range(0, N, RB):
                    rows = at(p, i)
                    dn = dn3[i : i + RB]
                    dn3_s[rows, :] = dn
                    first = norm_back(dn0[i : i + RB], un0[rows, :], sc0[rows, :], parn[pl.ds(0, 1), :])
                    dh = (dh1_r[rows, :].astype(F32) + first).astype(BF16).astype(F32)
                    dh2_s[rows, :] = dh + norm_back(dn, un2[rows, :], sc2[rows, :], gains[2])

            @pl.when(me_s == S - 1)
            def _():
                dh2_s[whole, :] = cot[whole, :].astype(F32)

            dy = dh2_s[whole, :].astype(BF16)
            bwd[whole, pl.ds(D, D)] = dy
            da2 = jnp.zeros((N, D), F32)
            for c in range(chunks):
                cols = pl.ds(c * FC, FC)
                dv = mm_bt(dy, fo[cols, :])
                du = stacked(
                    [(slope_s[at(p, i), cols].astype(F32) * dv[i : i + RB]).astype(BF16) for i in range(0, N, RB)]
                )
                da2 = da2 + mm_bt(du, fi[:, cols])
            for i in range(0, N, RB):
                rows = at(p, i)
                block = da2[i : i + RB]
                da2_s[rows, :] = block
                dh1 = dh2_s[rows, :] + norm_back(block, un1[rows, :], sc1[rows, :], gains[1])
                dh1_f[rows, :] = dh1
                bwd[rows, pl.ds(0, D)] = (dh1 * (1.0 / K)).astype(BF16)
            dmb_s[whole, :] = mm_bt(bwd[whole, pl.ds(0, D)], mo[...]).astype(BF16)
            rows_out(p, dmb_s, dmb_r, dmb_ss, dmb_rs)
            return carry

        lax.fori_loop(0, B, turn, 0)

        @pl.when(me_s > 0)
        def _():
            dh1_s[...] = dh1_f[...].astype(BF16)
            far(dh1_s, dh1_r, dh_ss, dh_rs, me_s - 1, me_d).start()

        @pl.when(me_s < S - 1)
        def _():
            far(row_r.at[:, pl.ds(0, 2 * D)], dpqo_r, fw_ss, dpqo_rs, me_s + 1, me_d).start()
            drs = row_r[:, pl.ds(2 * D, 2 * EP)]
            bwd[:, pl.ds(2 * D, 2 * EP)] = drs
            dn = dn3_s[...]
            sg[pl.ds(11, 1), :] = col_sum(dn * un2[...])
            sg[pl.ds(12, 1), :] = col_sum(dn)
            sg[pl.ds(16, 1), pl.ds(0, EP)] = col_sum(drs[:, :EP].astype(F32))

        @pl.when(me_s == S - 1)
        def _():
            bwd[:, pl.ds(2 * D, 2 * EP)] = jnp.zeros((B * N, 2 * EP), BF16)
            sg[pl.ds(11, 1), :] = jnp.zeros((1, D), F32)
            sg[pl.ds(12, 1), :] = jnp.zeros((1, D), F32)
            sg[pl.ds(16, 1), pl.ds(0, EP)] = jnp.zeros((1, EP), F32)

        share(1, bwd, g_bwd)
        sg[pl.ds(13, 1), :] = col_sum(dh2_s[...])
        sg[pl.ds(8, 1), :] = col_sum(da2_s[...] * un1[...])
        sg[pl.ds(9, 1), :] = col_sum(da2_s[...])
        sg[pl.ds(10, 1), :] = col_sum(dh1_f[...])

    def node_backward_drain():
        rows_drain(dmb_s, dmb_ss)

        @pl.when(me_s > 0)
        def _():
            arrive(dh1_s, dh_ss)

        @pl.when(me_s < S - 1)
        def _():
            arrive(row_r.at[:, pl.ds(0, 2 * D)], fw_ss)

    dacc[...] = jnp.zeros_like(dacc)

    def backward_step(step, carry):
        t = S - 1 - step

        @pl.when(me_s == t)
        def _():
            node_backward()

        @pl.when(((t == S - 1) & (me_s >= S - 2)) | (me_s == t - 2))
        def _():
            prepare(me_s)

        @pl.when(t < S - 1)
        def _():
            edge_pass(t)

        @pl.when(t + 2 < S)
        def _():
            blocks_sum(t + 2, HM + HU)

        @pl.when(t == 0)
        def _():
            blocks_sum(1, HM + HU)

        arrive(dmb_r, dmb_rs)
        message_back(t)

        @pl.when(t > 0)
        def _():
            edge_back(t)

        @pl.when(t == 0)
        def _():
            x_s[:, pl.ds(D, EP)] = jnp.zeros((N, EP), BF16)

        gather_blocks()
        other = gather_wait().astype(BF16)
        row_s[:, pl.ds(D, D)] = other[:, :D]
        row_s[:, pl.ds(2 * D + EP, EP)] = other[:, D:]
        dpq = row_s.at[:, pl.ds(0, 2 * D)]

        @pl.when(t > 0)
        def _():
            push(row_s, row_r.at[pl.ds(my_row, Q)], row_ss, row_rs.at[slot], t - 1, owner_d)

        @pl.when(t == 0)
        def _():
            push(dpq, dpqo_r.at[pl.ds(my_row, Q)], row_ss, dpqo_rs, t, owner_d)

        edge_grads(t)

        @pl.when(t > 0)
        def _():
            drain(row_s, row_ss, t - 1, owner_d)

        @pl.when(t == 0)
        def _():
            drain(dpq, row_ss, t, owner_d)

        @pl.when(me_s == t)
        def _():
            node_backward_drain()

        return carry

    lax.fori_loop(0, S, backward_step, 0)

    arrive(dpqo_r, dpqo_rs)
    across = [pl.ds(p * N, N) for p in range(B)]
    for p in range(B):
        share_near(2 + p, dpqo_r.at[across[p]], lambda c, p=p: g_dpq.at[c, across[p]])
    dpq = dpqo_r[...]
    sg[pl.ds(2, 1), :] = col_sum(dpq[:, :D].astype(F32))
    dn = mm_bt(dpq, pw[...])
    unit = hi_s[...]
    sg[pl.ds(0, 1), :] = col_sum(dn * unit)
    sg[pl.ds(1, 1), :] = col_sum(dn)
    share(2 + B, sg, g_small)
    ig[...] = (dh1_f[...] + norm_back(dn, unit, sci[...], gains[0])).astype(BF16)
    blocks_sum(0, HM)
    for p in range(B):
        share_relay(2 + p, dpqo_r.at[across[p]], lambda c, p=p: g_dpq.at[c, across[p]])
    def combine(kind, src, final):
        for sec in range(S):
            arrive(src.at[sec], e2_rs.at[kind, sec])
        for half in range(2):
            total = src[half].astype(F32)
            for sec in range(half + 2, S, 2):
                total = total + src[sec].astype(F32)
            final[half] = total.astype(BF16)

    @pl.when(me_s < S - 1)
    def _():
        combine(1, upd_o, upd_f)

    @pl.when(me_s == S - 1)
    def _():
        upd_f[...] = jnp.zeros_like(upd_f)

    share(4 + B, upd_f, g_upd)
    combine(0, msg_o, msg_f)
    share(3 + B, msg_f, g_msg)
    for t in range(S):
        drain(eg_b.at[t, pl.ds(0, HM)], e2_ss.at[0, t], t, me_d)
        if t > 0:
            drain(eg_b.at[t, pl.ds(HM, HU)], e2_ss.at[1, t], t - 1, me_d)
    share_wait(0, fwd_t, g_fwd)
    share_wait(1, bwd, g_bwd)
    for p in range(B):
        share_near_wait(2 + p, dpqo_r.at[across[p]], lambda c, p=p: g_dpq.at[c, across[p]])
    share_wait(2 + B, sg, g_small)
    share_wait(3 + B, msg_f, g_msg)
    share_wait(4 + B, upd_f, g_upd)


def run_relay(dims, operands):
    S, B, N, K, Q, D, DE, EP, FF, C = dims
    R = K * Q
    BN = B * N
    tall = DE + N + Q
    vm = pl.BlockSpec(memory_space=pltpu.VMEM)
    hbm = pl.BlockSpec(memory_space=pl.ANY)
    dma = pltpu.SemaphoreType.DMA
    sds = jax.ShapeDtypeStruct
    BW = D // C
    tile = 32
    held = -(-(DE + 16) // tile) * tile
    scratch = [
        pltpu.VMEM((D, 2 * D), BF16),
        pltpu.VMEM((D, D), BF16),
        pltpu.VMEM((D, FF), BF16),
        pltpu.VMEM((FF, D), BF16),
        pltpu.VMEM((4 * D, BN), BF16),
        pltpu.VMEM((D, 2 * EP), BF16),
        pltpu.VMEM((K, Q, DE), BF16),
        pltpu.VMEM((K, B, N), jnp.int32),
        pltpu.VMEM((128, 128), F32),
        pltpu.VMEM((128, 128), F32),
        pltpu.VMEM((N, R), BF16),
        pltpu.VMEM((BN, D), F32),
        pltpu.VMEM((8, D), F32),
        pltpu.VMEM((1, EP), F32),
        pltpu.VMEM((S, DE, D), BF16),
        pltpu.VMEM((S, held, 2 * EP), BF16),
        pltpu.VMEM((BN, 4 * D), BF16),
        pltpu.VMEM((BN, 2 * D + 2 * EP), BF16),
        pltpu.VMEM((24, D), F32),
        pltpu.VMEM((S, 2, (DE + held) // 2, D), BF16),
        pltpu.VMEM((S, 2 * C, (DE + held) // 2, BW), BF16),
        pltpu.VMEM((S, (DE + held) // 2, BW), BF16),
        pltpu.VMEM((S, DE // 2, BW), BF16),
        pltpu.VMEM((2, DE // 2, BW), BF16),
        pltpu.VMEM((S, held // 2, BW), BF16),
        pltpu.VMEM((2, held // 2, BW), BF16),
        pltpu.VMEM((S, EP, EP), BF16),
        pltpu.VMEM((S, 16, EP), BF16),
        pltpu.VMEM((S, R, EP), BF16),
        pltpu.VMEM((S, tall, D), BF16),
        pltpu.VMEM((S, tall, EP), BF16),
        pltpu.VMEM((D, 2 * D), BF16),
        pltpu.VMEM((8, D), F32),
        pltpu.VMEM((BN, D), BF16),
        pltpu.VMEM((BN, D), BF16),
        pltpu.VMEM((Q, D), BF16),
        pltpu.VMEM((BN, D), BF16),
        pltpu.VMEM((BN, 2 * D), BF16),
        pltpu.VMEM((Q, 2 * D), BF16),
        pltpu.VMEM((BN, 2 * EP), BF16),
        pltpu.VMEM((Q, 2 * EP), BF16),
        pltpu.VMEM((BN, D), F32),
        pltpu.VMEM((BN, D), F32),
        pltpu.VMEM((BN, D), F32),
        pltpu.VMEM((BN, D), F32),
        pltpu.VMEM((BN, 1), F32),
        pltpu.VMEM((BN, 1), F32),
        pltpu.VMEM((BN, 1), F32),
        pltpu.VMEM((BN, 1), F32),
        pltpu.VMEM((BN, FF), F32),
        pltpu.VMEM((BN, FF), BF16),
        pltpu.VMEM((2, R, EP), BF16),
        pltpu.VMEM((R, EP), F32),
        pltpu.VMEM((S, R, D), BF16),
        pltpu.VMEM((S, R, EP), BF16),
        pltpu.VMEM((2, R, D + EP), BF16),
        pltpu.VMEM((S, EP, R), BF16),
        pltpu.VMEM((S, EP, R), BF16),
        pltpu.VMEM((N, D + EP), BF16),
        pltpu.VMEM((4, Q, D + EP), BF16),
        pltpu.VMEM((Q, 2 * D + 2 * EP), BF16),
        pltpu.VMEM((BN, 2 * D + 2 * EP), BF16),
        pltpu.VMEM((BN, 2 * D), BF16),
        pltpu.VMEM((BN, D), BF16),
        pltpu.VMEM((Q, D), BF16),
        pltpu.VMEM((BN, D), BF16),
        pltpu.VMEM((BN, D), BF16),
        pltpu.VMEM((BN, D), F32),
        pltpu.VMEM((BN, D), F32),
        pltpu.VMEM((BN, D), F32),
        pltpu.VMEM((BN, D), F32),
        pltpu.VMEM((BN, D), F32),
        pltpu.VMEM((BN, D), BF16),
        dma((2,)), dma((2,)), dma((4,)), dma((2,)), dma((2,)), dma, dma,
        dma, dma, dma, dma, dma, dma, dma, dma,
        dma, dma((B,)), dma, dma, dma, dma((B,)), dma,
        dma, dma, dma, dma, dma,
        dma((S, 2 * C)), dma((S, 2 * C)), dma((2, S)), dma((2, S)), dma((5 + B, C)), dma((5 + B, C)),
        dma((B, C // 2)), dma((2, 2, S // 2)), dma((2, S)), dma((2, S)), dma((2, S)),
    ]
    return pl.pallas_call(
        functools.partial(relay_kernel, dims),
        out_shape=(
            sds((BN, D), BF16),
            sds((BN, D), BF16),
            sds((C, 4 * D, BN), BF16),
            sds((C, BN, 2 * D + 2 * EP), BF16),
            sds((C, BN, 2 * D), BF16),
            sds((C, 24, D), F32),
            sds((C, 2, DE // 2, BW), BF16),
            sds((C, 2, held // 2, BW), BF16),
        ),
        in_specs=[hbm, hbm, pl.BlockSpec(memory_space=pltpu.SMEM)] + [vm] * 3 + [hbm] * 4 + [vm] * 9,
        out_specs=(vm,) * 2 + (hbm,) * 6,
        scratch_shapes=scratch,
        compiler_params=pltpu.CompilerParams(
            collective_id=0, has_side_effects=True, vmem_limit_bytes=62 * 1024 * 1024
        ),
    )(*operands)


def gradient_kernel(
    dims,
    fwd, bwd, dpq, small, edge, upd, fi, fo, fb, act, ig,
    g_pair, g_edge, g_out, g_fi, g_fo, g_ep, g_self, g_eout, g_gain, g_shift, g_nb, g_fb, g_eb, act_out, ig_out,
    fwd_v, bwd_v, dpq_v, fi_v, fo_v, gfi_v, gfo_v, pair_v, out_v, edge_v, upd_v, in_sems, sems,
):
    S, B, N, K, Q, D, DE, EP, FF, C = dims
    chunks = 4
    FC = FF // chunks

    def part(c, size=D):
        return pl.ds(c * size, size)

    loads = {}

    def load(name, src, dst):
        loads[name] = pltpu.make_async_copy(src, dst, in_sems.at[len(loads)])
        loads[name].start()

    BN = B * N

    def load_kept(n):
        for c in range(C):
            load((n, c), fwd.at[c, part(n)], fwd_v.at[n, :, part(c, BN)])

    def wait_kept(n):
        for c in range(C):
            loads[n, c].wait()
        return fwd_v[n]

    load_kept(2)
    load("dy", bwd.at[:, part(1)], bwd_v.at[1])
    for c in range(chunks):
        load(("fi", c), fi.at[:, part(c, FC)], fi_v.at[c])
        load(("fo", c), fo.at[part(c, FC)], fo_v.at[c])
    load_kept(0)
    load("dpq0", dpq.at[:, part(0)], dpq_v.at[0])
    load("dpq1", dpq.at[:, part(1)], dpq_v.at[1])
    load_kept(1)
    load("dmsg", bwd.at[:, part(0)], bwd_v.at[0])
    load_kept(3)
    load("drs", bwd.at[:, part(2)], bwd_v.at[2])
    load("edge", edge, edge_v)
    load("upd", upd, upd_v)
    stores = []

    def out(src, dst):
        copy = pltpu.make_async_copy(src, dst, sems.at[len(stores)])
        copy.start()
        stores.append(copy)

    out(act, act_out)
    out(ig, ig_out)
    a2_t = wait_kept(2)
    a2 = a2_t.T
    loads["dy"].wait()
    dy = bwd_v[1]
    for c in range(chunks):
        cols = part(c, FC)
        loads["fi", c].wait()
        loads["fo", c].wait()
        u = mm(a2, fi_v[c])
        dv = mm_bt(dy, fo_v[c])
        v, du = [], []
        for i in range(0, C * BN, 16):
            value, slope = gelu_both(u[i : i + 16] + fb[:, cols])
            v.append(value.astype(BF16))
            du.append((slope * dv[i : i + 16]).astype(BF16))
        v, du = stacked(v), stacked(du)
        g_fb[:, cols] = col_sum(du.astype(F32))
        gfi_v[c] = mm(a2_t, du)
        out(gfi_v.at[c], g_fi.at[0, :, cols])
        gfo_v[c] = mm_at(v, dy)
        out(gfo_v.at[c], g_fo.at[0, cols])
    a1_t = wait_kept(0)
    for c in range(2):
        loads["dpq%d" % c].wait()
        pair_v[c] = mm(a1_t, dpq_v[c])
        out(pair_v.at[c], g_pair.at[0, :, part(c)])
    loads["dmsg"].wait()
    out_v[...] = mm(wait_kept(1), bwd_v[0]) * float(K)
    out(out_v, g_out.at[0])
    loads["drs"].wait()
    ends = mm(wait_kept(3), bwd_v[2])
    g_ep[0] = jnp.concatenate([ends[:, :DE], ends[:, EP : EP + DE]], axis=1)
    total = small[0]
    for c in range(1, C):
        total = total + small[c]
    for i, rows in enumerate(((0, 1, 2), (8, 9, 10), (11, 12, 13))):
        g_gain[i] = total[rows[0] : rows[0] + 1]
        g_shift[i] = total[rows[1] : rows[1] + 1]
        g_nb[i] = total[rows[2] : rows[2] + 1]
    g_eb[0, pl.ds(0, 1), :] = total[16:17, :DE]
    loads["edge"].wait()
    loads["upd"].wait()
    BW = edge_v.shape[3]
    for c in range(C):
        for half in range(2):
            block = edge_v[c, half].astype(F32)
            g_edge[0, pl.ds(half * (DE // 2), DE // 2), pl.ds(c * BW, BW)] = block
        block = stacked([upd_v[c, 0], upd_v[c, 1]]).astype(F32)
        first = c * BW
        for array, begin in ((g_self, 0), (g_eout, EP)):
            low, high = max(first, begin), min(first + BW, begin + DE)
            if low < high:
                array[0, :, pl.ds(low - begin, high - low)] = block[:DE, low - first : high - first]
        low, high = first, min(first + BW, DE)
        if low < high:
            g_eb[0, pl.ds(1, 1), pl.ds(low, high - low)] = block[DE : DE + 1, low - first : high - first]
    for copy in stores:
        copy.wait()


def run_gradients(dims, operands):
    S, B, N, K, Q, D, DE, EP, FF, C = dims
    rows = C * B * N
    BW = D // C
    held = operands[5].shape[2]
    vm = pl.BlockSpec(memory_space=pltpu.VMEM)
    hbm = pl.BlockSpec(memory_space=pl.ANY)
    sds = jax.ShapeDtypeStruct
    shapes = (
        (1, D, 2 * D), (1, DE, D), (1, D, D), (1, D, FF), (1, FF, D), (1, D, 2 * DE), (1, DE, DE), (1, DE, DE),
        (3, 1, D), (3, 1, D), (3, 1, D), (1, FF), (1, 2, DE),
    )
    return pl.pallas_call(
        functools.partial(gradient_kernel, dims),
        out_shape=tuple(sds(shape, F32) for shape in shapes) + (sds((1, B, N, D), BF16),) * 2,
        in_specs=[hbm, hbm, hbm, vm, hbm, hbm, hbm, hbm, vm, hbm, hbm],
        out_specs=(hbm, vm, hbm, hbm, hbm) + (vm,) * 8 + (hbm,) * 2,
        scratch_shapes=[
            pltpu.VMEM((4, D, rows), BF16),
            pltpu.VMEM((3, rows, D), BF16),
            pltpu.VMEM((2, rows, D), BF16),
            pltpu.VMEM((4, D, FF // 4), BF16),
            pltpu.VMEM((4, FF // 4, D), BF16),
            pltpu.VMEM((4, D, FF // 4), F32),
            pltpu.VMEM((4, FF // 4, D), F32),
            pltpu.VMEM((2, D, D), F32),
            pltpu.VMEM((D, D), F32),
            pltpu.VMEM((C, 2, DE // 2, BW), BF16),
            pltpu.VMEM((C, 2, held, BW), BF16),
            pltpu.SemaphoreType.DMA((15 + 4 * C,)),
            pltpu.SemaphoreType.DMA((13,)),
        ],
        compiler_params=pltpu.CompilerParams(vmem_limit_bytes=56 * 1024 * 1024),
    )(*operands)


def stationary(
    clean_nodes, noise_nodes, edge_feats, neighbours, time_bins, cotangent,
    pair_weight, message_edge, message_out, ffn_in, ffn_out, edge_pair, edge_self, edge_out,
    norm_gain, norm_shift, node_bias, ffn_bias, edge_bias,
):
    S = lax.axis_size("section")
    B, N, D = clean_nodes.shape
    K, DE = edge_feats.shape[2:]
    FF = ffn_in.shape[2]
    Q = N // 4
    EP = DE + N
    def by_rows(array):
        return jnp.transpose(array, (1, 0, 2))

    C = lax.axis_size("dp")
    dims = (S, B, N, K, Q, D, DE, EP, FF, C)
    act, ig, g_fwd, g_bwd, g_dpq, g_small, g_msg, g_upd = run_relay(
        dims,
        (
            jnp.transpose(edge_feats, (0, 2, 1, 3)), jnp.transpose(neighbours, (2, 0, 1)), time_bins,
            clean_nodes.reshape(B * N, D), noise_nodes.reshape(B * N, D),
            cotangent.reshape(B * N, D), pair_weight[0], message_out[0], ffn_in[0], ffn_out[0], edge_pair[0],
            by_rows(norm_gain), by_rows(norm_shift), by_rows(node_bias), ffn_bias, edge_bias[0],
            message_edge[0], edge_self[0], edge_out[0],
        ),
    )
    grads = run_gradients(
        dims,
        (
            g_fwd, g_bwd.reshape(C * B * N, -1), g_dpq.reshape(C * B * N, -1),
            g_small, g_msg, g_upd, ffn_in[0], ffn_out[0], ffn_bias, act.reshape(1, B, N, D), ig.reshape(1, B, N, D),
        ),
    )
    grads, outs = list(grads[:-2]), tuple(grads[-2:])
    grads[8:11] = [by_rows(array) for array in grads[8:11]]
    return outs + tuple(grads)


def solution(mesh):
    sections, copies = mesh.shape["section"], mesh.shape["dp"]

    def body(*args):
        B, N = args[0].shape[:2]
        fits = sections == 4 * B and copies % 2 == 0 and N % 64 == 0
        return stationary(*args) if fits else on_device(*args)

    placed = (
        P("dp", None, None),
        P("dp", None, None),
        P("dp", None, None, None),
        P("dp", None, None),
        P("dp"),
        P("dp", None, None),
        P("section", None, None),
        P("section", None, None),
        P("section", None, None),
        P("section", None, None),
        P("section", None, None),
        P("section", None, None),
        P("section", None, None),
        P("section", None, None),
        P("section", None, None),
        P("section", None, None),
        P("section", None, None),
        P("section", None),
        P("section", None, None),
    )
    return jax.shard_map(
        body,
        mesh=mesh,
        in_specs=placed,
        out_specs=(
            P("section", "dp", None, None),
            P("section", "dp", None, None),
            P("section", None, None),
            P("section", None, None),
            P("section", None, None),
            P("section", None, None),
            P("section", None, None),
            P("section", None, None),
            P("section", None, None),
            P("section", None, None),
            P("section", None, None),
            P("section", None, None),
            P("section", None, None),
            P("section", None),
            P("section", None, None),
        ),
        check_vma=False,
    )
```
